32 devices in a mesh: ctx: 8 (over z, x), head: 4 (over y, core).
Axes of the slice: x: 2, y: 2, z: 4, core: 2. Of those that a mesh axis runs over, the one named last changes fastest.
Arguments:
- inputs: bfloat16 [4096, 8192], P(('ctx', 'head')), may hold values from -1.75 to 1.75
- grad_out: bfloat16 [4096, 8192], P(('ctx', 'head')), may hold values from -1.75 to 1.75
- steps: bfloat16 [4096, 128], P(('ctx', 'head')), may hold values from 0.049804688 to 0.19921875
- log_decay: bfloat16 [4096, 128], P(('ctx', 'head')), may hold values from -0.52 to 0
- input_map: bfloat16 [4096, 128], P(('ctx', 'head')), may hold values from -0.5 to 0.5
- output_map: bfloat16 [4096, 128], P(('ctx', 'head')), may hold values from -0.5 to 0.5
- skip_gain: float32 [128], P('head'), may hold values from 0.5 to 1.5
Outputs:
- grad_inputs: bfloat16 [4096, 8192], P(('ctx', 'head'))
- grad_steps: bfloat16 [4096, 128], P(('ctx', 'head'))
- grad_decay: bfloat16 [4096, 128], P(('ctx', 'head'))
- grad_input_map: float32 [4096, 128], P(('ctx', 'head'))
- grad_output_map: float32 [4096, 128], P(('ctx', 'head'))
The draws below stay inside these ranges and needn't reach their ends.
All inputs are finite; a program needn't handle non-finite values.
Results may differ from the reference program's by a relative error of at most 0.004.
Values may be sent and summed in bfloat16 or wider, within the bound.
No kernel may reach another device: no remote copies, remote signals or barrier semaphores. Data moves between devices by JAX's collectives and lax.ppermute only.
A program may use at most 128 MiB of HBM per device.

```python
import math
import jax
import jax.numpy as jnp
from jax import lax

HEADS = 128
HEAD_DIM = 64
STATE = 128
SPAN = 256
L_DEV = 512
INNER = 8192
TOKENS = 4096


def draw_log_decay(key, part):
    key_kind, key_fast, key_slow, key_rough, key_block, key_spot, key_loss = jax.random.split(key, 7)
    slow_share = 0.5
    slow_head = jax.random.uniform(key_kind, (HEADS,)) < slow_share
    fast_rate = jnp.exp(jax.random.uniform(key_fast, (HEADS,), minval=jnp.log(1.0 / 50.0), maxval=jnp.log(1.0 / 30.0)))
    slow_rate = jnp.exp(jax.random.uniform(key_slow, (HEADS,), minval=jnp.log(0.1), maxval=jnp.log(0.5))) / TOKENS
    head_rate_value = jnp.where(slow_head, slow_rate, fast_rate)
    coarse_estimate = jnp.exp(jax.random.uniform(key_rough, (TOKENS, HEADS), minval=jnp.log(0.5), maxval=jnp.log(2.0)))
    block_factor = jnp.exp(jax.random.uniform(key_block, (TOKENS // L_DEV, HEADS), minval=jnp.log(0.5), maxval=jnp.log(2.0)))
    block_complete = jnp.repeat(block_factor, L_DEV, axis=0)
    sample_locations = jax.random.randint(key_spot, (2,), 0, TOKENS)
    token_positions = lax.broadcasted_iota(jnp.int32, (TOKENS, 1), 0)
    sudden_spike = jnp.any(token_positions == sample_locations[None, :], axis=1)
    retained_items = jax.random.uniform(key_loss, (TOKENS, HEADS), minval=0.6, maxval=0.8)
    value_rows = jnp.where(sudden_spike[:, None], jnp.log(retained_items), -head_rate_value[None, :] * coarse_estimate * block_complete)
    return value_rows.astype(jnp.bfloat16)


def levels(own_key, dims, cuts, smallest, largest):
    loudness = 1.0
    for dim, blocks in cuts:
        draws = jax.random.uniform(jax.random.fold_in(jax.random.fold_in(own_key, 6), dim), (blocks,), jnp.float32, smallest / len(cuts), largest / len(cuts))
        loudness = loudness * jnp.repeat(jnp.exp(draws), dims[dim] // blocks).reshape((-1,) + (1,) * (len(dims) - 1 - dim))
    return loudness


def noise(stream_key, shape, deviation, most, cuts=(), kind=jnp.bfloat16):
    values = jax.random.normal(stream_key, shape, jnp.float32) * deviation
    if len(cuts) > 0:
        values = levels(stream_key, shape, cuts, -0.22, 0.18) * values
    return jnp.clip(values, min=-most, max=most).astype(kind)


def setup_inputs(seed: int = 0) -> dict:
    keys = jax.random.split(jax.random.key(seed), 8)
    inputs = noise(keys[0], (TOKENS, INNER), 0.3, 1.75, ((0, 32),))
    grad_out = noise(keys[1], (TOKENS, INNER), 0.3, 1.75, ((0, 32),))
    steps = jnp.clip(jnp.exp(math.log(0.19921875) - 1.3862944 * jax.random.uniform(keys[2], (TOKENS, HEADS), jnp.float32) ** levels(keys[2], (TOKENS, HEADS), ((0, 32),), -0.2, 0.2)), 0.049804688, 0.19921875).astype(jnp.bfloat16)
    log_decay = draw_log_decay(jax.random.fold_in(keys[7], 71), 0)
    input_map = noise(keys[4], (TOKENS, STATE), STATE ** -0.5, 0.5, ((0, 32),))
    output_map = noise(keys[5], (TOKENS, STATE), STATE ** -0.5, 0.5, ((0, 32),))
    skip_gain = jnp.clip(0.5 + 1.0 * jax.random.uniform(keys[6], (HEADS,), jnp.float32) ** levels(keys[6], (HEADS,), ((0, 4),), -0.2, 0.2), 0.5, 1.5)
    return dict(inputs=inputs, grad_out=grad_out, steps=steps, log_decay=log_decay, input_map=input_map, output_map=output_map, skip_gain=skip_gain)


def local_forward(value_rows, step_sizes, log_steps, key_rows, query_rows, skip_local, start_state, span_len):
    length, groups, head_width = value_rows.shape
    blocks = length // span_len
    highest = lax.Precision.HIGHEST
    plain = lax.Precision.DEFAULT
    scaled = (value_rows * step_sizes[:, :, None]).reshape(blocks, span_len, groups, head_width)
    cumlog = jnp.cumsum(log_steps.reshape(blocks, span_len, groups).transpose(0, 2, 1), axis=2)
    row_index = lax.broadcasted_iota(jnp.int32, (span_len, span_len), 0)
    col_index = lax.broadcasted_iota(jnp.int32, (span_len, span_len), 1)
    below_diag = row_index >= col_index
    spread = cumlog[:, :, :, None] - cumlog[:, :, None, :]
    decays = jnp.exp(jnp.where(below_diag, spread, 0.0)) * below_diag.astype(jnp.float32)
    keys_blk = key_rows.reshape(blocks, span_len, key_rows.shape[1])
    queries_blk = query_rows.reshape(blocks, span_len, query_rows.shape[1])
    intersection = jnp.einsum('cqn,ckn->cqk', queries_blk, keys_blk, precision=plain)
    scores = intersection[:, None, :, :] * decays
    diag_out = jnp.einsum('cgqk,ckgp->cqgp', scores, scaled, precision=highest)
    to_end = jnp.exp(cumlog[:, :, -1:] - cumlog)
    weighted = scaled * to_end.transpose(0, 2, 1)[:, :, :, None]
    block_states = jnp.einsum('ckn,ckgp->cgpn', keys_blk, weighted, precision=highest)
    block_decay = jnp.exp(cumlog[:, :, -1])

    def advance(carry_state, link_pair):
        decay_now, added_state = link_pair
        return (decay_now[:, None, None] * carry_state + added_state, carry_state)
    final_state, start_states = lax.scan(advance, start_state, (block_decay, block_states))
    carried = jnp.einsum('cqn,cgpn->cqgp', queries_blk, start_states, precision=highest)
    carried = carried * jnp.exp(cumlog).transpose(0, 2, 1)[:, :, :, None]
    outputs = (diag_out + carried).reshape(length, groups, head_width) + skip_local[None, :, None] * value_rows
    return (outputs, final_state)

def reference(inputs, grad_out, steps, log_decay, input_map, output_map, skip_gain):
    token_count = inputs.shape[0]
    group_size = 8
    group_count = HEADS // group_size
    group_inputs = inputs.astype(jnp.float32).reshape(token_count, group_count, group_size, HEAD_DIM).transpose(1, 0, 2, 3)
    group_cotan = grad_out.astype(jnp.float32).reshape(token_count, group_count, group_size, HEAD_DIM).transpose(1, 0, 2, 3)
    group_steps = steps.astype(jnp.float32).reshape(token_count, group_count, group_size).transpose(1, 0, 2)
    group_decay = log_decay.astype(jnp.float32).reshape(token_count, group_count, group_size).transpose(1, 0, 2)
    group_skip = skip_gain.reshape(group_count, group_size)
    key_rows = input_map.astype(jnp.float32)
    query_rows = output_map.astype(jnp.float32)
    zero_state = jnp.zeros((group_size, HEAD_DIM, STATE), jnp.float32)

    def per_group(running, pieces):
        piece_inputs, piece_cotan, piece_steps, piece_decay, piece_skip = pieces

        def forward(value_rows, step_sizes, log_steps, keys_in, queries_in):
            return local_forward(value_rows, step_sizes, log_steps, keys_in, queries_in, piece_skip, zero_state, SPAN)[0]
        unused, pullback = jax.vjp(forward, piece_inputs, piece_steps, piece_decay, key_rows, query_rows)
        grad_values, grad_sizes, grad_logs, grad_keys, grad_queries = pullback(piece_cotan)
        return ((running[0] + grad_keys, running[1] + grad_queries), (grad_values, grad_sizes, grad_logs))
    start = (jnp.zeros((token_count, STATE), jnp.float32), jnp.zeros((token_count, STATE), jnp.float32))
    sums, stacked = lax.scan(per_group, start, (group_inputs, group_cotan, group_steps, group_decay, group_skip))
    grad_values, grad_sizes, grad_logs = stacked
    grad_inputs = grad_values.transpose(1, 0, 2, 3).reshape(token_count, HEADS * HEAD_DIM).astype(jnp.bfloat16)
    grad_steps = grad_sizes.transpose(1, 0, 2).reshape(token_count, HEADS).astype(jnp.bfloat16)
    grad_decay = grad_logs.transpose(1, 0, 2).reshape(token_count, HEADS).astype(jnp.bfloat16)
    return (grad_inputs, grad_steps, grad_decay, sums[0], sums[1])
```

```python
import functools

import jax
import jax.numpy as jnp
from jax import lax
from jax.experimental import pallas as pl
from jax.experimental.pallas import tpu as pltpu
from jax.sharding import PartitionSpec as P

F32 = jnp.float32
BF16 = jnp.bfloat16
LANES = 128
WIDTH = 64
COLS = 256
LOG2E = 1.4426950408889634
NT = (((1,), (1,)), ((), ()))
VMEM_LIMIT = 48 * 1024 * 1024


def dot(a, b):
    return jnp.dot(a, b, preferred_element_type=F32)


def dot_nt(a, b):
    return lax.dot_general(a, b, NT, preferred_element_type=F32)


def pieces(a, count):
    terms = []
    for _ in range(count):
        term = a.astype(BF16)
        terms.append(term)
        a = a - term.astype(F32)
    return terms


def selector(rows, cols, first):
    row = lax.broadcasted_iota(jnp.int32, (rows, cols), 0)
    col = lax.broadcasted_iota(jnp.int32, (rows, cols), 1)
    return jnp.where((col // WIDTH) + first == row, 1.0, 0.0).astype(BF16)


def spread(a, select, count=2):
    return sum(dot(term, select) for term in pieces(a, count))


def gather(a, select, count=2):
    return sum(dot_nt(term, select) for term in pieces(a, count))


def params(semantics=1):
    return pltpu.CompilerParams(
        dimension_semantics=("arbitrary",) * semantics, vmem_limit_bytes=VMEM_LIMIT
    )


def cost(flops, moved, exps=0):
    return pl.CostEstimate(flops=int(flops), bytes_accessed=int(moved), transcendentals=int(exps))


def whole(*shape):
    return pl.BlockSpec(shape, lambda *g: (0,) * len(shape))


def columns(rows):
    return pl.BlockSpec((rows, COLS), lambda g: (0, g))


def prepare_kernel(heads, at_ref, small_ref, col_ref, row_ref, in_ref, out_ref, dt_ref, tot_ref, bt_ref, ct_ref):
    length = small_ref.shape[0]
    shift = lax.rem(LANES - at_ref[0] * heads, LANES)
    steps = pltpu.roll(small_ref[:, 0:LANES].astype(F32), shift, 1)
    logs = pltpu.roll(small_ref[:, LANES : 2 * LANES].astype(F32), shift, 1)
    row = lax.broadcasted_iota(jnp.int32, (length, length), 0)
    col = lax.broadcasted_iota(jnp.int32, (length, length), 1)
    lower = jnp.where(row >= col, 1.0, 0.0).astype(BF16)
    cum = dot(lower, logs.astype(BF16)) * LOG2E
    total = cum[length - 1 : length, :]
    col_part = cum - jnp.log(steps) * LOG2E
    col_ref[...] = col_part
    turned = cum.T
    per_group = row_ref.shape[1]
    for group in range(row_ref.shape[0]):
        row_ref[group] = turned[group * per_group : (group + 1) * per_group, :]
    in_ref[...] = jnp.exp2(total - cum) * steps
    out_ref[...] = jnp.exp2(cum)
    dt_ref[...] = steps
    tot_ref[...] = jnp.broadcast_to(total, tot_ref.shape)
    bt_ref[...] = small_ref[:, 2 * LANES : 3 * LANES].astype(F32).T.astype(BF16)
    ct_ref[...] = small_ref[:, 3 * LANES : 4 * LANES].astype(F32).T.astype(BF16)


def prepare(at, small, heads):
    length = small.shape[0]
    tall = jax.ShapeDtypeStruct((length, LANES), F32)
    flat = jax.ShapeDtypeStruct((LANES, length), BF16)
    return pl.pallas_call(
        functools.partial(prepare_kernel, heads),
        out_shape=(
            tall,
            jax.ShapeDtypeStruct((heads * WIDTH // COLS, COLS // WIDTH, length), F32),
            tall,
            tall,
            tall,
            jax.ShapeDtypeStruct((8, LANES), F32),
            flat,
            flat,
        ),
        in_specs=[pl.BlockSpec(memory_space=pltpu.SMEM), pl.BlockSpec(memory_space=pltpu.VMEM)],
        compiler_params=pltpu.CompilerParams(vmem_limit_bytes=VMEM_LIMIT),
        cost_estimate=cost(2 * length * length * LANES, 3e6),
        name="prepare",
    )(at, small)


def state_kernel(weight_ref, rows_ref, map_ref, out_ref):
    select = selector(LANES, COLS, pl.program_id(0) * (COLS // WIDTH))
    weighted = rows_ref[...].astype(F32) * spread(weight_ref[...], select)
    out_ref[...] = sum(dot(map_ref[...], term) for term in pieces(weighted, 2)).astype(BF16)


def block_state(weight, rows, map_t):
    length, inner = rows.shape
    return pl.pallas_call(
        state_kernel,
        grid=(inner // COLS,),
        out_shape=jax.ShapeDtypeStruct((LANES, inner), BF16),
        in_specs=[whole(length, LANES), columns(length), whole(LANES, length)],
        out_specs=columns(LANES),
        compiler_params=params(),
        cost_estimate=cost(8 * length * inner * LANES, 2 * length * inner),
        name="block_state",
    )(weight, rows, map_t)


def scan_kernel(reverse, tot_ref, in_ref, out_ref):
    peers, rows, inner = in_ref.shape
    select = selector(LANES, inner, 0)
    decay = spread(jnp.exp2(tot_ref[...]), select, 3)
    running = jnp.zeros((rows, inner), F32)
    order = range(peers - 1, -1, -1) if reverse else range(peers)
    for at in order:
        out_ref[at] = running.astype(BF16)
        running = decay[at * 8 : at * 8 + 1, :] * running + in_ref[at].astype(F32)


def scan_blocks(totals, parts, reverse):
    peers, rows, inner = parts.shape
    return pl.pallas_call(
        functools.partial(scan_kernel, reverse),
        out_shape=jax.ShapeDtypeStruct(parts.shape, BF16),
        compiler_params=pltpu.CompilerParams(vmem_limit_bytes=VMEM_LIMIT),
        cost_estimate=cost(6 * 8 * peers * LANES * inner, 4 * peers * rows * inner),
        name="scan_blocks",
    )(totals.reshape(peers * 8, LANES), parts)


def carried_in(state, totals, reverse):
    peers = totals.shape[0]
    state_size, inner = state.shape
    parts = state.reshape(peers, state_size // peers, inner)
    parts = lax.all_to_all(parts, "ctx", split_axis=0, concat_axis=0, tiled=True)
    parts = scan_blocks(totals, parts, reverse)
    parts = lax.all_to_all(parts, "ctx", split_axis=0, concat_axis=0, tiled=True)
    return parts.reshape(state_size, inner)


def inside_kernel(
    x_ref, dy_ref, b_ref, c_ref, col_ref, row_ref, dx_ref, u_ref, v_ref, db_ref, dc_ref, s_ref, ds_ref
):
    length = x_ref.shape[0]
    tiles = length // LANES
    heads = COLS // WIDTH
    group = pl.program_id(0)
    from_k = lax.broadcasted_iota(jnp.int32, (length, length), 0)
    to_q = lax.broadcasted_iota(jnp.int32, (length, length), 1)

    @pl.when(group == 0)
    def _():
        s_ref[...] = jnp.where(to_q >= from_k, dot_nt(b_ref[...], c_ref[...]), 0.0)
        ds_ref[...] = jnp.zeros_like(ds_ref)
        v_ref[...] = jnp.zeros_like(v_ref)

    turned = pltpu.roll(col_ref[...], lax.rem(LANES - group * heads, LANES), 1)
    lane = lax.broadcasted_iota(jnp.int32, (LANES, LANES), 1)
    for j in range(tiles):
        low = j * LANES
        here = slice(low, low + LANES)
        for pair in range(heads // 2):
            across = slice(pair * LANES, (pair + 1) * LANES)
            xs = x_ref[here, across]
            dys = dy_ref[low:, across]
            side = lax.broadcasted_iota(jnp.int32, dys.shape, 1) // WIDTH
            total = None
            for half in range(2):
                local = pair * 2 + half
                head = group * heads + local
                own_x = jnp.where(lane // WIDTH == half, xs, jnp.zeros_like(xs))
                own_dy = jnp.where(side == half, dys, jnp.zeros_like(dys))
                products = dot_nt(own_x, dys)
                behind = turned[here, local : local + 1]
                kept = []
                v_sum = None
                for i in range(j, tiles):
                    there = slice(i * LANES, (i + 1) * LANES)
                    ahead = row_ref[0, local : local + 1, there]
                    decay = jnp.exp2(jnp.minimum(ahead - behind, 64.0))
                    product = products[:, (i - j) * LANES : (i - j + 1) * LANES]
                    score = s_ref[here, there] * decay
                    kept.append(score.astype(BF16))
                    ds_ref[here, there] += decay * product
                    both = score * product
                    v_sum = both if v_sum is None else v_sum + both
                    u_sum = jnp.sum(both, axis=0, keepdims=True)
                    if j > 0:
                        u_sum += u_ref[0, local : local + 1, there]
                    u_ref[0, local : local + 1, there] = u_sum
                v_col = jnp.sum(v_sum, axis=1, keepdims=True)
                v_ref[here, :] = jnp.where(lane == head, v_col, v_ref[here, :])
                scores = jnp.concatenate(kept, axis=1) if len(kept) > 1 else kept[0]
                part = dot(scores, own_dy)
                total = part if total is None else total + part
            dx_ref[here, across] = total

    @pl.when(group == pl.num_programs(0) - 1)
    def _():
        grads = jnp.where(to_q >= from_k, ds_ref[...], 0.0)
        db_ref[...] = sum(dot(term, c_ref[...]) for term in pieces(grads, 2))
        dc_ref[...] = sum(dot(term, b_ref[...]) for term in pieces(grads.T, 2))


def inside(x, dy, b, c, col_part, row_part):
    length, inner = x.shape
    tall = jax.ShapeDtypeStruct((length, LANES), F32)
    pairs = length * length * inner
    by_group = pl.BlockSpec((1,) + row_part.shape[1:], lambda g: (g, 0, 0))
    return pl.pallas_call(
        inside_kernel,
        grid=(inner // COLS,),
        out_shape=(
            jax.ShapeDtypeStruct((length, inner), F32),
            jax.ShapeDtypeStruct(row_part.shape, F32),
            tall,
            tall,
            tall,
        ),
        in_specs=[
            columns(length),
            columns(length),
            whole(length, LANES),
            whole(length, LANES),
            whole(length, LANES),
            by_group,
        ],
        out_specs=(
            columns(length),
            by_group,
            whole(length, LANES),
            whole(length, LANES),
            whole(length, LANES),
        ),
        scratch_shapes=[pltpu.VMEM((length, length), F32), pltpu.VMEM((length, length), F32)],
        compiler_params=params(),
        cost_estimate=cost(16 * pairs, 8 * length * inner, pairs // WIDTH),
        name="inside",
    )(x, dy, b, c, col_part, row_part)


def before_kernel(dy_ref, state_ref, weight_ref, c_ref, dci_ref, dc_ref, u_ref):
    group = pl.program_id(0)

    @pl.when(group == 0)
    def _():
        dc_ref[...] = dci_ref[...]
        u_ref[...] = jnp.zeros_like(u_ref)

    select = selector(LANES, COLS, group * (COLS // WIDTH))
    weighted = dy_ref[...].astype(F32) * spread(weight_ref[...], select)
    state = state_ref[...]
    dc_ref[...] += sum(dot_nt(term, state) for term in pieces(weighted, 2))
    u_ref[...] += gather(weighted * dot(c_ref[...], state), select)


def before(dy, state, weight, c, dc_inside):
    length, inner = dy.shape
    tall = jax.ShapeDtypeStruct((length, LANES), F32)
    return pl.pallas_call(
        before_kernel,
        grid=(inner // COLS,),
        out_shape=(tall, tall),
        in_specs=[
            columns(length),
            columns(LANES),
            whole(length, LANES),
            whole(length, LANES),
            whole(length, LANES),
        ],
        out_specs=(whole(length, LANES), whole(length, LANES)),
        compiler_params=params(),
        cost_estimate=cost(14 * length * inner * LANES, 3 * length * inner),
        name="before",
    )(dy, state, weight, c, dc_inside)


def after_kernel(
    heads,
    x_ref,
    dy_ref,
    dxi_ref,
    adjoint_ref,
    state_ref,
    weight_ref,
    b_ref,
    dt_ref,
    tot_ref,
    skip_ref,
    ui_ref,
    vi_ref,
    uc_ref,
    dbi_ref,
    dx_ref,
    small_ref,
    db_ref,
    vc_ref,
    link_ref,
):
    length = x_ref.shape[0]
    group = pl.program_id(0)

    @pl.when(group == 0)
    def _():
        db_ref[...] = dbi_ref[...]
        vc_ref[...] = jnp.zeros_like(vc_ref)
        link_ref[...] = jnp.zeros_like(link_ref)

    select = selector(LANES, COLS, group * (COLS // WIDTH))
    weight = spread(weight_ref[...], select)
    x = x_ref[...].astype(F32)
    adjoint = adjoint_ref[...]
    carried = weight * dot(b_ref[...], adjoint)
    gain = spread(skip_ref[...], select, 3)[0:1, :]
    dx_ref[...] = (dxi_ref[...] + carried + gain * dy_ref[...].astype(F32)).astype(BF16)
    db_ref[...] += sum(dot_nt(term, adjoint) for term in pieces(x * weight, 2))
    vc_ref[...] += gather(x * carried, select)
    through = jnp.sum(adjoint.astype(F32) * state_ref[...].astype(F32), axis=0, keepdims=True)
    link_ref[...] += gather(jnp.broadcast_to(through, (8, COLS)), select, 3)

    @pl.when(group == pl.num_programs(0) - 1)
    def _():
        inner_v, outer_v = vi_ref[...], vc_ref[...]
        steps = (inner_v + outer_v) / dt_ref[...]
        rows = [ui_ref[at] for at in range(ui_ref.shape[0])]
        rows.append(jnp.zeros((LANES - heads, length), F32))
        net = jnp.concatenate(rows, axis=0).T + uc_ref[...] - inner_v - outer_v
        row = lax.broadcasted_iota(jnp.int32, (length, length), 0)
        col = lax.broadcasted_iota(jnp.int32, (length, length), 1)
        upper = jnp.where(col >= row, 1.0, 0.0).astype(BF16)
        later = sum(dot(upper, term) for term in pieces(net, 3))
        whole_block = jnp.sum(outer_v, axis=0, keepdims=True)
        logs = later + whole_block + jnp.exp2(tot_ref[0:1, :]) * link_ref[0:1, :]
        lane = lax.broadcasted_iota(jnp.int32, (length, LANES), 1)
        small_ref[...] = jnp.where(lane < heads, steps, pltpu.roll(logs, heads, 1)).astype(BF16)


def after(heads, x, dy, dxi, adjoint, state, weight, b, dt, tot, skip, ui, vi, uc, dbi):
    length, inner = x.shape
    tall = whole(length, LANES)
    return pl.pallas_call(
        functools.partial(after_kernel, heads),
        grid=(inner // COLS,),
        out_shape=(
            jax.ShapeDtypeStruct((length, inner), BF16),
            jax.ShapeDtypeStruct((length, LANES), BF16),
            jax.ShapeDtypeStruct((length, LANES), F32),
        ),
        in_specs=[
            columns(length),
            columns(length),
            columns(length),
            columns(LANES),
            columns(LANES),
            tall,
            tall,
            tall,
            whole(8, LANES),
            whole(8, LANES),
            whole(*ui.shape),
            tall,
            tall,
            tall,
        ],
        out_specs=(columns(length), tall, tall),
        scratch_shapes=[pltpu.VMEM((length, LANES), F32), pltpu.VMEM((8, LANES), F32)],
        compiler_params=params(),
        cost_estimate=cost(14 * length * inner * LANES, 10 * length * inner),
        name="after",
    )(x, dy, dxi, adjoint, state, weight, b, dt, tot, skip, ui, vi, uc, dbi)


def exchange(parts, axis):
    return lax.all_to_all(parts, axis, split_axis=0, concat_axis=0, tiled=True)


def body(inputs, grad_out, steps, log_decay, input_map, output_map, skip_gain):
    blocks, peers = lax.axis_size("ctx"), lax.axis_size("head")
    tokens, channels = inputs.shape
    length = tokens * peers
    inner = channels // peers
    heads = steps.shape[1] // peers

    small = jnp.concatenate([steps, log_decay, input_map, output_map], axis=1)
    small = exchange(jnp.broadcast_to(small[None], (peers,) + small.shape), "head")
    small = small.reshape(length, 4 * LANES)

    def to_heads(rows):
        parts = rows.reshape(tokens, peers, inner).transpose(1, 0, 2)
        return exchange(parts, "head").reshape(length, inner)

    x = to_heads(inputs)
    dy = to_heads(grad_out)

    at = lax.axis_index("head").astype(jnp.int32).reshape(1)
    col_part, row_part, into, out_of, dt, tot, b_t, c_t = prepare(at, small, heads)
    b = small[:, 2 * LANES : 3 * LANES]
    c = small[:, 3 * LANES : 4 * LANES]
    totals = exchange(jnp.broadcast_to(tot[None], (blocks,) + tot.shape), "ctx")

    state = carried_in(block_state(into, x, b_t), totals, False)
    adjoint = carried_in(block_state(out_of, dy, c_t), totals, True)
    dxi, ui, vi, dbi, dci = inside(x, dy, b, c, col_part, row_part)
    dc, uc = before(dy, state, out_of, c, dci)
    skip = jnp.broadcast_to(jnp.pad(skip_gain, (0, LANES - heads))[None], (8, LANES))
    dx, thin, db = after(
        heads, x, dy, dxi, adjoint, state, into, b, dt, tot, skip, ui, vi, uc, dbi
    )

    dx = exchange(dx.reshape(peers, tokens, inner), "head")
    thin = exchange(thin.reshape(peers, tokens, LANES), "head")
    maps = exchange(jnp.concatenate([db, dc], axis=1).reshape(peers, tokens, 2 * LANES), "head")
    maps = jnp.sum(maps, axis=0)

    def from_heads(parts):
        return parts.transpose(1, 0, 2).reshape(tokens, -1)

    return (
        from_heads(dx),
        from_heads(thin[:, :, :heads]),
        from_heads(thin[:, :, heads : 2 * heads]),
        maps[:, :LANES],
        maps[:, LANES:],
    )


def solution(mesh):
    rows = P(("ctx", "head"), None)
    return jax.shard_map(
        body,
        mesh=mesh,
        in_specs=(rows,) * 6 + (P("head"),),
        out_specs=(rows,) * 5,
        check_vma=False,
    )
```

```python
import functools

import jax
import jax.numpy as jnp
from jax import lax
from jax.experimental import pallas as pl
from jax.experimental.pallas import tpu as pltpu
from jax.sharding import PartitionSpec as P

F32 = jnp.float32
BF16 = jnp.bfloat16
LANES = 128
WIDTH = 64
COLS = 256
LOG2E = 1.4426950408889634
NT = (((1,), (1,)), ((), ()))
VMEM_LIMIT = 48 * 1024 * 1024


def dot(a, b):
    return jnp.dot(a, b, preferred_element_type=F32)


def dot_nt(a, b):
    return lax.dot_general(a, b, NT, preferred_element_type=F32)


def pieces(a, count):
    terms = []
    for _ in range(count):
        term = a.astype(BF16)
        terms.append(term)
        a = a - term.astype(F32)
    return terms


def selector(rows, cols, first):
    row = lax.broadcasted_iota(jnp.int32, (rows, cols), 0)
    col = lax.broadcasted_iota(jnp.int32, (rows, cols), 1)
    return jnp.where((col // WIDTH) + first == row, 1.0, 0.0).astype(BF16)


def spread(a, select, count=2):
    return sum(dot(term, select) for term in pieces(a, count))


def gather(a, select, count=2):
    return sum(dot_nt(term, select) for term in pieces(a, count))


def params(semantics=1):
    return pltpu.CompilerParams(
        dimension_semantics=("arbitrary",) * semantics, vmem_limit_bytes=VMEM_LIMIT
    )


def cost(flops, moved, exps=0):
    return pl.CostEstimate(flops=int(flops), bytes_accessed=int(moved), transcendentals=int(exps))


def whole(*shape):
    return pl.BlockSpec(shape, lambda *g: (0,) * len(shape))


def columns(rows):
    return pl.BlockSpec((rows, COLS), lambda g: (0, g))


def smem():
    return pl.BlockSpec(memory_space=pltpu.SMEM)


def anywhere():
    return pl.BlockSpec(memory_space=pl.ANY)


def vmem():
    return pl.BlockSpec(memory_space=pltpu.VMEM)


def one_step():
    return pltpu.CompilerParams(vmem_limit_bytes=VMEM_LIMIT)


def swap(parts):
    peers = lax.axis_size("head")
    got = [parts[0]] + [None] * (peers - 1)
    for r in range(peers - 1, 0, -1):
        got[r] = lax.ppermute(parts[r], "head", [(i, i ^ r) for i in range(peers)])
    return got


def pack_kernel(peers, first, at_ref, x_ref, dy_ref, *rest):
    outs, sems = rest[:peers], rest[peers]
    width = outs[0].shape[2]
    inner = x_ref.shape[1] // peers
    copies = []
    for r in range(peers):
        start = pl.multiple_of((at_ref[0] ^ r) * inner + first, LANES)
        for k, source in enumerate((x_ref, dy_ref)):
            copies.append(
                pltpu.make_async_copy(
                    source.at[:, pl.ds(start, width)], outs[r].at[k], sems.at[r, k]
                )
            )
    for copy in copies:
        copy.start()
    for copy in copies:
        copy.wait()


def pack(at, x, dy, peers, first, width):
    tokens = x.shape[0]
    return pl.pallas_call(
        functools.partial(pack_kernel, peers, first),
        out_shape=[jax.ShapeDtypeStruct((2, tokens, width), BF16)] * peers,
        in_specs=[smem(), anywhere(), anywhere()],
        out_specs=[anywhere()] * peers,
        scratch_shapes=[pltpu.SemaphoreType.DMA((peers, 2))],
        compiler_params=one_step(),
        cost_estimate=cost(0, 8 * tokens * width * peers),
        name="pack",
    )(at, x, dy)


def prepare_kernel(heads, peers, at_ref, *rest):
    parts = rest[:peers]
    col_ref, row_ref, in_ref, out_ref, dt_ref, tot_ref, b_ref, c_ref, bt_ref, ct_ref, small_ref = rest[peers:]
    tokens = parts[0].shape[0]
    length = tokens * peers
    for r in range(peers):
        start = pl.multiple_of((at_ref[0] ^ r) * tokens, tokens)
        small_ref[pl.ds(start, tokens), :] = parts[r][...].astype(F32)
    shift = lax.rem(LANES - at_ref[0] * heads, LANES)
    steps = pltpu.roll(small_ref[:, 0:LANES], shift, 1)
    logs = pltpu.roll(small_ref[:, LANES : 2 * LANES], shift, 1)
    row = lax.broadcasted_iota(jnp.int32, (length, length), 0)
    col = lax.broadcasted_iota(jnp.int32, (length, length), 1)
    lower = jnp.where(row >= col, 1.0, 0.0).astype(BF16)
    cum = dot(lower, logs.astype(BF16)) * LOG2E
    total = cum[length - 1 : length, :]
    col_ref[...] = cum - jnp.log(steps) * LOG2E
    turned = cum.T
    per_group = row_ref.shape[1]
    for group in range(row_ref.shape[0]):
        row_ref[group] = turned[group * per_group : (group + 1) * per_group, :]
    in_ref[...] = jnp.exp2(total - cum) * steps
    out_ref[...] = jnp.exp2(cum)
    dt_ref[...] = steps
    tot_ref[...] = jnp.broadcast_to(total, tot_ref.shape)
    b = small_ref[:, 2 * LANES : 3 * LANES]
    c = small_ref[:, 3 * LANES : 4 * LANES]
    b_ref[...] = b.astype(BF16)
    c_ref[...] = c.astype(BF16)
    bt_ref[...] = b.T.astype(BF16)
    ct_ref[...] = c.T.astype(BF16)


def prepare(at, parts, heads):
    peers = len(parts)
    length = parts[0].shape[0] * peers
    tall = jax.ShapeDtypeStruct((length, LANES), F32)
    thin = jax.ShapeDtypeStruct((length, LANES), BF16)
    flat = jax.ShapeDtypeStruct((LANES, length), BF16)
    groups = jax.ShapeDtypeStruct((heads * WIDTH // COLS, COLS // WIDTH, length), F32)
    return pl.pallas_call(
        functools.partial(prepare_kernel, heads, peers),
        out_shape=(
            tall,
            groups,
            tall,
            tall,
            tall,
            jax.ShapeDtypeStruct((8, LANES), F32),
            thin,
            thin,
            flat,
            flat,
        ),
        in_specs=[smem()] + [vmem()] * peers,
        scratch_shapes=[pltpu.VMEM((length, 4 * LANES), F32)],
        compiler_params=one_step(),
        cost_estimate=cost(2 * length * length * LANES, 3e6),
        name="prepare",
    )(at, *parts)


def states_kernel(peers, first, at_ref, in_ref, out_ref, bt_ref, ct_ref, *rest):
    parts, (x_ref, dy_ref, sum_ref, sems) = rest[:peers], rest[peers:]
    tokens = parts[0].shape[1]
    blocks, rows, inner = sum_ref.shape
    rows //= 2
    copies = []
    for r in range(peers):
        start = pl.multiple_of((at_ref[0] ^ r) * tokens, tokens)
        for k, target in enumerate((x_ref, dy_ref)):
            copies.append(
                pltpu.make_async_copy(
                    parts[r].at[k], target.at[pl.ds(start, tokens), :], sems.at[r, k]
                )
            )
    for copy in copies:
        copy.start()
    weights = [pieces(in_ref[...], 2), pieces(out_ref[...], 2)]
    for copy in copies:
        copy.wait()
    for group in range(inner // COLS):
        here = slice(group * COLS, (group + 1) * COLS)
        select = selector(LANES, COLS, first + group * (COLS // WIDTH))
        for k, (source, map_ref) in enumerate(((x_ref, bt_ref), (dy_ref, ct_ref))):
            weight = sum(dot(term, select) for term in weights[k])
            weighted = source[:, here].astype(F32) * weight
            added = sum(dot(map_ref[...], term) for term in pieces(weighted, 2)).astype(BF16)
            for block in range(blocks):
                sum_ref[block, k * rows : (k + 1) * rows, here] = added[
                    block * rows : (block + 1) * rows, :
                ]


def states(at, into, out_of, b_t, c_t, parts, blocks, first):
    peers = len(parts)
    tokens, inner = parts[0].shape[1:]
    length = tokens * peers
    rows = jax.ShapeDtypeStruct((length, inner), BF16)
    return pl.pallas_call(
        functools.partial(states_kernel, peers, first),
        out_shape=(
            rows,
            rows,
            jax.ShapeDtypeStruct((blocks, 2 * LANES // blocks, inner), BF16),
        ),
        in_specs=[smem()] + [vmem()] * 4 + [anywhere()] * peers,
        scratch_shapes=[pltpu.SemaphoreType.DMA((peers, 2))],
        compiler_params=one_step(),
        cost_estimate=cost(16 * length * inner * LANES, 8 * length * inner),
        name="states",
    )(at, into, out_of, b_t, c_t, *parts)


def scan_kernel(first, tot_ref, in_ref, out_ref, kept_ref):
    blocks, rows, inner = in_ref.shape
    rows //= 2
    select = selector(LANES, inner, first)
    decay = spread(jnp.exp2(tot_ref[...]), select, 3)
    through = []
    for k, order in enumerate((range(blocks), range(blocks - 1, -1, -1))):
        here = slice(k * rows, (k + 1) * rows)
        running = jnp.zeros((rows, inner), F32)
        for block in order:
            out_ref[block, here, 0:inner] = running.astype(BF16)
            if k == 0:
                kept_ref[block] = running
            else:
                through.append(jnp.sum(kept_ref[block] * running, axis=0, keepdims=True))
            step = decay[block * 8 : block * 8 + 1, :]
            running = step * running + in_ref[block, here, :].astype(F32)
    link = gather(jnp.concatenate(through[::-1], axis=0), select, 3)
    high, low = (term.astype(F32) for term in pieces(link, 2))
    row = lax.broadcasted_iota(jnp.int32, (2 * rows, LANES), 0)
    for block in range(blocks):
        here = slice(block, block + 1)
        both = jnp.where(row == 0, high[here, :], jnp.where(row == 1, low[here, :], 0.0))
        out_ref[block, :, inner:] = both.astype(BF16)


def carried_in(sums, totals, first):
    blocks, rows, inner = sums.shape
    sums = lax.all_to_all(sums, "ctx", split_axis=0, concat_axis=0, tiled=True)
    sums = pl.pallas_call(
        functools.partial(scan_kernel, first),
        out_shape=jax.ShapeDtypeStruct((blocks, rows, inner + LANES), BF16),
        scratch_shapes=[pltpu.VMEM((blocks, rows // 2, inner), F32)],
        compiler_params=one_step(),
        cost_estimate=cost(6 * 8 * blocks * LANES * inner, 4 * blocks * rows * inner),
        name="scan_blocks",
    )(totals.reshape(blocks * 8, LANES), sums)
    return lax.all_to_all(sums, "ctx", split_axis=0, concat_axis=0, tiled=True)


def stacked(ref, k):
    blocks, rows, _ = ref.shape
    rows //= 2
    return jnp.concatenate(
        [ref[block, k * rows : (k + 1) * rows, :] for block in range(blocks)], axis=0
    )


def inside_kernel(first, x_ref, dy_ref, b_ref, c_ref, col_ref, row_ref, *rest):
    added, (dx_ref, u_ref, v_ref, db_ref, dc_ref, s_ref, ds_ref) = rest[:-7], rest[-7:]
    length = x_ref.shape[0]
    tiles = length // LANES
    heads = COLS // WIDTH
    group = pl.program_id(0)
    from_k = lax.broadcasted_iota(jnp.int32, (length, length), 0)
    to_q = lax.broadcasted_iota(jnp.int32, (length, length), 1)

    @pl.when(group == 0)
    def _():
        s_ref[...] = jnp.where(to_q >= from_k, dot_nt(b_ref[...], c_ref[...]), 0.0)
        ds_ref[...] = jnp.zeros_like(ds_ref)
        v_ref[...] = jnp.zeros_like(v_ref)

    turned = pltpu.roll(col_ref[...], lax.rem(LANES - first - group * heads, LANES), 1)
    lane = lax.broadcasted_iota(jnp.int32, (LANES, LANES), 1)
    for j in range(tiles):
        low = j * LANES
        here = slice(low, low + LANES)
        for pair in range(heads // 2):
            across = slice(pair * LANES, (pair + 1) * LANES)
            xs = x_ref[here, across]
            dys = dy_ref[low:, across]
            side = lax.broadcasted_iota(jnp.int32, dys.shape, 1) // WIDTH
            total = None
            for half in range(2):
                local = pair * 2 + half
                head = first + group * heads + local
                own_x = jnp.where(lane // WIDTH == half, xs, jnp.zeros_like(xs))
                own_dy = jnp.where(side == half, dys, jnp.zeros_like(dys))
                products = dot_nt(own_x, dys)
                behind = turned[here, local : local + 1]
                kept = []
                v_sum = None
                for i in range(j, tiles):
                    there = slice(i * LANES, (i + 1) * LANES)
                    ahead = row_ref[0, local : local + 1, there]
                    decay = jnp.exp2(jnp.minimum(ahead - behind, 64.0))
                    product = products[:, (i - j) * LANES : (i - j + 1) * LANES]
                    score = s_ref[here, there] * decay
                    kept.append(score.astype(BF16))
                    ds_ref[here, there] += decay * product
                    both = score * product
                    v_sum = both if v_sum is None else v_sum + both
                    u_sum = jnp.sum(both, axis=0, keepdims=True)
                    if j > 0:
                        u_sum += u_ref[0, local : local + 1, there]
                    u_ref[0, local : local + 1, there] = u_sum
                v_col = jnp.sum(v_sum, axis=1, keepdims=True)
                v_ref[here, :] = jnp.where(lane == head, v_col, v_ref[here, :])
                scores = jnp.concatenate(kept, axis=1) if len(kept) > 1 else kept[0]
                part = dot(scores, own_dy)
                total = part if total is None else total + part
            dx_ref[here, across] = total

    @pl.when(group == pl.num_programs(0) - 1)
    def _():
        grads = jnp.where(to_q >= from_k, ds_ref[...], 0.0)
        db = sum(dot(term, c_ref[...]) for term in pieces(grads, 2))
        dc = sum(dot(term, b_ref[...]) for term in pieces(grads.T, 2))
        db_ref[...] = db + added[0][...] if added else db
        dc_ref[...] = dc + added[1][...] if added else dc


def inside(x, dy, b, c, col_part, row_part, first, *added):
    added = [a for a in added if a is not None]
    length, inner = x.shape
    tall = jax.ShapeDtypeStruct((length, LANES), F32)
    pairs = length * length * inner
    offset = first * WIDTH // COLS
    by_group = pl.BlockSpec((1,) + row_part.shape[1:], lambda g: (g + offset, 0, 0))
    own_group = pl.BlockSpec((1,) + row_part.shape[1:], lambda g: (g, 0, 0))
    return pl.pallas_call(
        functools.partial(inside_kernel, first),
        grid=(inner // COLS,),
        out_shape=(
            jax.ShapeDtypeStruct((length, inner), F32),
            jax.ShapeDtypeStruct((inner // COLS,) + row_part.shape[1:], F32),
            tall,
            tall,
            tall,
        ),
        in_specs=[
            columns(length),
            columns(length),
            whole(length, LANES),
            whole(length, LANES),
            whole(length, LANES),
            by_group,
        ]
        + [whole(length, LANES)] * len(added),
        out_specs=(
            columns(length),
            own_group,
            whole(length, LANES),
            whole(length, LANES),
            whole(length, LANES),
        ),
        scratch_shapes=[pltpu.VMEM((length, length), F32), pltpu.VMEM((length, length), F32)],
        compiler_params=params(),
        cost_estimate=cost(16 * pairs, 8 * length * inner, pairs // WIDTH),
        name="inside",
    )(x, dy, b, c, col_part, row_part, *added)


def before_kernel(first, dy_ref, carry_ref, weight_ref, c_ref, dc_ref, u_ref):
    group = pl.program_id(0)

    @pl.when(group == 0)
    def _():
        dc_ref[...] = jnp.zeros_like(dc_ref)
        u_ref[...] = jnp.zeros_like(u_ref)

    select = selector(LANES, COLS, first + group * (COLS // WIDTH))
    weighted = dy_ref[...].astype(F32) * spread(weight_ref[...], select)
    state = stacked(carry_ref, 0)
    dc_ref[...] += sum(dot_nt(term, state) for term in pieces(weighted, 2))
    u_ref[...] += gather(weighted * dot(c_ref[...], state), select)


def by_columns(shape):
    return pl.BlockSpec(shape[:2] + (COLS,), lambda g: (0, 0, g))


def before(dy, carry, weight, c, first):
    length, inner = dy.shape
    tall = jax.ShapeDtypeStruct((length, LANES), F32)
    return pl.pallas_call(
        functools.partial(before_kernel, first),
        grid=(inner // COLS,),
        out_shape=(tall, tall),
        in_specs=[
            columns(length),
            by_columns(carry.shape),
            whole(length, LANES),
            whole(length, LANES),
        ],
        out_specs=(whole(length, LANES), whole(length, LANES)),
        compiler_params=params(),
        cost_estimate=cost(14 * length * inner * LANES, 3 * length * inner),
        name="before",
    )(dy, carry, weight, c)


def after_kernel(
    heads,
    peers,
    first,
    last,
    at_ref,
    x_ref,
    dy_ref,
    dxi_ref,
    carry_ref,
    through_ref,
    weight_ref,
    b_ref,
    dt_ref,
    tot_ref,
    skip_ref,
    ui_ref,
    vi_ref,
    uc_ref,
    *rest,
):
    if last:
        others, rest = rest[:6], rest[6:]
    outs, tails, rest = rest[:peers], rest[peers : 2 * peers if last else peers + 2], rest[-4:]
    db_ref, vc_ref, dx_ref, tail_ref = rest
    length = x_ref.shape[0]
    tokens = length // peers
    group = pl.program_id(0)

    @pl.when(group == 0)
    def _():
        db_ref[...] = jnp.zeros_like(db_ref)
        vc_ref[...] = jnp.zeros_like(vc_ref)

    select = selector(LANES, COLS, first + group * (COLS // WIDTH))
    weight = spread(weight_ref[...], select)
    x = x_ref[...].astype(F32)
    adjoint = stacked(carry_ref, 1)
    carried = weight * dot(b_ref[...], adjoint)
    gain = spread(skip_ref[...], select, 3)[0:1, :]
    dx_ref[...] = (dxi_ref[...] + carried + gain * dy_ref[...].astype(F32)).astype(BF16)
    for r in range(peers):
        start = pl.multiple_of((at_ref[0] ^ r) * tokens, tokens)
        outs[r][...] = dx_ref[pl.ds(start, tokens), :]
    db_ref[...] += sum(dot_nt(term, adjoint) for term in pieces(x * weight, 2))
    vc_ref[...] += gather(x * carried, select)

    @pl.when(group == pl.num_programs(0) - 1)
    def _():
        inner_v, outer_v = vi_ref[...], vc_ref[...]
        steps = (inner_v + outer_v) / dt_ref[...]
        rows = [ui_ref[at] for at in range(ui_ref.shape[0])]
        if first > 0:
            rows.insert(0, jnp.zeros((first, length), F32))
        rows.append(jnp.zeros((LANES - sum(part.shape[0] for part in rows), length), F32))
        net = jnp.concatenate(rows, axis=0).T + uc_ref[...] - inner_v - outer_v
        row = lax.broadcasted_iota(jnp.int32, (length, length), 0)
        col = lax.broadcasted_iota(jnp.int32, (length, length), 1)
        upper = jnp.where(col >= row, 1.0, 0.0).astype(BF16)
        later = sum(dot(upper, term) for term in pieces(net, 3))
        whole_block = jnp.sum(outer_v, axis=0, keepdims=True)
        link = sum(through_ref[block].astype(F32) for block in range(through_ref.shape[0]))
        link = jnp.sum(link, axis=0, keepdims=True)
        logs = later + whole_block + jnp.exp2(tot_ref[0:1, :]) * link
        thin = steps + pltpu.roll(logs, heads, 1)
        if not last:
            tails[0][...] = thin
            tails[1][...] = db_ref[...]
        else:
            thin_ref, dbo_ref, dbi_ref, dci_ref, dca_ref, dcb_ref = others
            tail_ref[:, 0:LANES] = (thin + thin_ref[...]).astype(BF16)
            tail_ref[:, LANES : 2 * LANES] = (db_ref[...] + dbo_ref[...] + dbi_ref[...]).astype(BF16)
            tail_ref[:, 2 * LANES :] = (dci_ref[...] + dca_ref[...] + dcb_ref[...]).astype(BF16)
            for r in range(peers):
                start = pl.multiple_of((at_ref[0] ^ r) * tokens, tokens)
                tails[r][...] = tail_ref[pl.ds(start, tokens), :]


def after(heads, peers, first, at, x, dy, dxi, carry, weight, b, dt, tot, skip, ui, vi, uc, others):
    length, inner = x.shape
    tokens = length // peers
    tall = whole(length, LANES)
    last = len(others) > 0
    tall_shape = jax.ShapeDtypeStruct((length, LANES), F32)
    tail_shape = jax.ShapeDtypeStruct((tokens, 3 * LANES), BF16)
    return pl.pallas_call(
        functools.partial(after_kernel, heads, peers, first, last),
        grid=(inner // COLS,),
        out_shape=[jax.ShapeDtypeStruct((tokens, inner), BF16)] * peers
        + ([tail_shape] * peers if last else [tall_shape] * 2),
        in_specs=[
            smem(),
            columns(length),
            columns(length),
            columns(length),
            by_columns(carry.shape),
            pl.BlockSpec(carry.shape[:2] + (LANES,), lambda g: (0, 0, inner // LANES)),
            tall,
            tall,
            tall,
            whole(8, LANES),
            whole(8, LANES),
            whole(*ui.shape),
            tall,
            tall,
        ]
        + [tall] * len(others),
        out_specs=[columns(tokens)] * peers
        + ([whole(tokens, 3 * LANES)] * peers if last else [tall] * 2),
        scratch_shapes=[
            pltpu.VMEM((length, LANES), F32),
            pltpu.VMEM((length, LANES), F32),
            pltpu.VMEM((length, COLS), BF16),
            pltpu.VMEM((length, 3 * LANES), BF16),
        ],
        compiler_params=params(),
        cost_estimate=cost(14 * length * inner * LANES, 10 * length * inner),
        name="after",
    )(at, x, dy, dxi, carry, carry, weight, b, dt, tot, skip, ui, vi, uc, *others)


def finish_kernel(heads, peers, halves, at_ref, *rest):
    count = peers * halves
    sent, tails = rest[:count], rest[count : count + peers]
    dx_ref, steps_ref, logs_ref, db_ref, dc_ref, sems = rest[count + peers :]
    tokens, width = sent[0].shape
    copies = []
    for half in range(halves):
        for r in range(peers):
            start = pl.multiple_of(((at_ref[0] ^ r) * halves + half) * width, LANES)
            copies.append(
                pltpu.make_async_copy(
                    sent[half * peers + r], dx_ref.at[:, pl.ds(start, width)], sems.at[half, r]
                )
            )
    for copy in copies:
        copy.start()
    lane = lax.broadcasted_iota(jnp.int32, (tokens, LANES), 1)
    results = [jnp.zeros((tokens, LANES), F32) for _ in range(4)]
    for r in range(peers):
        source = at_ref[0] ^ r
        own = lane // heads == source
        thin = tails[r][:, 0:LANES].astype(F32)
        for k in range(2):
            shift = lax.rem((source - k) * heads + LANES, LANES)
            results[k] += jnp.where(own, pltpu.roll(thin, shift, 1), 0.0)
            results[2 + k] += tails[r][:, (k + 1) * LANES : (k + 2) * LANES].astype(F32)
    steps_ref[...] = results[0].astype(BF16)
    logs_ref[...] = results[1].astype(BF16)
    db_ref[...] = results[2]
    dc_ref[...] = results[3]
    for copy in copies:
        copy.wait()


def finish(heads, at, sent, tails):
    peers, halves = len(tails), len(sent)
    tokens, width = sent[0][0].shape
    thin = jax.ShapeDtypeStruct((tokens, LANES), BF16)
    wide = jax.ShapeDtypeStruct((tokens, LANES), F32)
    return pl.pallas_call(
        functools.partial(finish_kernel, heads, peers, halves),
        out_shape=(
            jax.ShapeDtypeStruct((tokens, width * halves * peers), BF16),
            thin,
            thin,
            wide,
            wide,
        ),
        in_specs=[smem()] + [anywhere()] * (peers * halves) + [vmem()] * peers,
        out_specs=(anywhere(), vmem(), vmem(), vmem(), vmem()),
        scratch_shapes=[pltpu.SemaphoreType.DMA((halves, peers))],
        compiler_params=one_step(),
        cost_estimate=cost(0, 4 * tokens * width * halves * peers),
        name="finish",
    )(at, *[part for group in sent for part in group], *tails)


HALVES = 2


def body(inputs, grad_out, steps, log_decay, input_map, output_map, skip_gain):
    blocks, peers = lax.axis_size("ctx"), lax.axis_size("head")
    inner = inputs.shape[1] // peers
    heads = steps.shape[1] // peers
    width = inner // HALVES
    at = lax.axis_index("head").astype(jnp.int32).reshape(1)

    small = jnp.concatenate([steps, log_decay, input_map, output_map], axis=1)
    small = swap([small] * peers)
    parts = [
        swap(pack(at, inputs, grad_out, peers, half * width, width)) for half in range(HALVES)
    ]
    col_part, row_part, into, out_of, dt, tot, b, c, b_t, c_t = prepare(at, small, heads)
    totals = jnp.broadcast_to(tot[None], (blocks,) + tot.shape)
    totals = lax.all_to_all(totals, "ctx", split_axis=0, concat_axis=0, tiled=True)
    skip = jnp.broadcast_to(jnp.pad(skip_gain, (0, LANES - heads))[None], (8, LANES))

    sent, others, dbi, dci, dca = [], [], None, None, None
    for half in range(HALVES):
        first = half * heads // HALVES
        x, dy, sums = states(at, into, out_of, b_t, c_t, parts[half], blocks, first)
        carry = carried_in(sums, totals, first)
        dxi, ui, vi, dbi, dci = inside(x, dy, b, c, col_part, row_part, first, dbi, dci)
        dc, uc = before(dy, carry, out_of, c, first)
        if half == HALVES - 1:
            others = [*others, dbi, dci, dca, dc]
        out = after(
            heads, peers, first, at, x, dy, dxi, carry, into, b, dt, tot, skip, ui, vi, uc, others
        )
        sent.append(swap(out[:peers]))
        others, dca = out[peers:], dc
    tails = swap(others)
    return tuple(finish(heads, at, sent, tails))


def solution(mesh):
    rows = P(("ctx", "head"), None)
    return jax.shard_map(
        body,
        mesh=mesh,
        in_specs=(rows,) * 6 + (P("head"),),
        out_specs=(rows,) * 5,
        check_vma=False,
    )
```

```python
import functools

import jax
import jax.numpy as jnp
from jax import lax
from jax.experimental import pallas as pl
from jax.experimental.pallas import tpu as pltpu
from jax.sharding import PartitionSpec as P

F32 = jnp.float32
BF16 = jnp.bfloat16
LANES = 128
WIDTH = 64
COLS = 256
LOG2E = 1.4426950408889634
NT = (((1,), (1,)), ((), ()))
MIB = 1024 * 1024


def dot(a, b):
    return jnp.dot(a, b, preferred_element_type=F32)


def dot_nt(a, b):
    return lax.dot_general(a, b, NT, preferred_element_type=F32)


def pieces(a, count):
    terms = []
    for _ in range(count):
        term = a.astype(BF16)
        terms.append(term)
        a = a - term.astype(F32)
    return terms


def selector(rows, cols, first):
    row = lax.broadcasted_iota(jnp.int32, (rows, cols), 0)
    col = lax.broadcasted_iota(jnp.int32, (rows, cols), 1)
    return jnp.where((col // WIDTH) + first == row, 1.0, 0.0).astype(BF16)


def spread(a, select, count=2):
    return sum(dot(term, select) for term in pieces(a, count))


def gather(a, select, count=2):
    return sum(dot_nt(term, select) for term in pieces(a, count))


def params(mib):
    return pltpu.CompilerParams(dimension_semantics=("arbitrary",), vmem_limit_bytes=mib * MIB)


def cost(flops, moved, exps=0):
    return pl.CostEstimate(flops=int(flops), bytes_accessed=int(moved), transcendentals=int(exps))


def whole(*shape):
    return pl.BlockSpec(shape, lambda *g: (0,) * len(shape))


def columns(rows):
    return pl.BlockSpec((rows, COLS), lambda g: (0, g))


def smem():
    return pl.BlockSpec(memory_space=pltpu.SMEM)


def anywhere():
    return pl.BlockSpec(memory_space=pl.ANY)


def vmem():
    return pl.BlockSpec(memory_space=pltpu.VMEM)


def one_step(mib):
    return pltpu.CompilerParams(vmem_limit_bytes=mib * MIB)


def swap(parts):
    peers = lax.axis_size("head")
    got = [parts[0]] + [None] * (peers - 1)
    for r in range(peers - 1, 0, -1):
        got[r] = lax.ppermute(parts[r], "head", [(i, i ^ r) for i in range(peers)])
    return got


def join_kernel(a_ref, b_ref, c_ref, d_ref, out_ref):
    for k, source in enumerate((a_ref, b_ref, c_ref, d_ref)):
        out_ref[:, k * LANES : (k + 1) * LANES] = source[...]


def join(*arrays):
    tokens = arrays[0].shape[0]
    return pl.pallas_call(
        join_kernel,
        out_shape=jax.ShapeDtypeStruct((tokens, 4 * LANES), BF16),
        compiler_params=one_step(4),
        cost_estimate=cost(0, 16 * tokens * LANES),
        name="join",
    )(*arrays)


def pack_kernel(peers, first, at_ref, x_ref, dy_ref, _, *rest):
    outs, (held, sems) = rest[:peers], rest[peers:]
    width = outs[0].shape[2]
    inner = x_ref.shape[1] // peers
    order = list(range(peers - 1, -1, -1))
    reads = {}
    for r in order:
        start = pl.multiple_of((at_ref[0] ^ r) * inner + first, LANES)
        for k, source in enumerate((x_ref, dy_ref)):
            reads[r, k] = pltpu.make_async_copy(
                source.at[:, pl.ds(start, width)], held.at[r, k], sems.at[0, r, k]
            )
            reads[r, k].start()
    writes = []
    for r in order:
        for k in range(2):
            reads[r, k].wait()
            writes.append(pltpu.make_async_copy(held.at[r, k], outs[r].at[k], sems.at[1, r, k]))
            writes[-1].start()
    for write in writes:
        write.wait()


def pack(at, x, dy, peers, first, width, behind):
    tokens = x.shape[0]
    return pl.pallas_call(
        functools.partial(pack_kernel, peers, first),
        out_shape=[jax.ShapeDtypeStruct((2, tokens, width), BF16)] * peers,
        in_specs=[smem(), anywhere(), anywhere(), anywhere()],
        out_specs=[anywhere()] * peers,
        scratch_shapes=[
            pltpu.VMEM((peers, 2, tokens, width), BF16),
            pltpu.SemaphoreType.DMA((2, peers, 2)),
        ],
        compiler_params=one_step(8),
        cost_estimate=cost(0, 8 * tokens * width * peers),
        name="pack",
    )(at, x, dy, behind)


def prepare_kernel(heads, peers, at_ref, _, *rest):
    parts = rest[:peers]
    col_ref, row_ref, in_ref, out_ref, dt_ref, tot_ref, b_ref, c_ref, bt_ref, ct_ref, small_ref = rest[peers:]
    tokens = parts[0].shape[0]
    length = tokens * peers
    for r in range(peers):
        start = pl.multiple_of((at_ref[0] ^ r) * tokens, tokens)
        small_ref[pl.ds(start, tokens), :] = parts[r][...].astype(F32)
    shift = lax.rem(LANES - at_ref[0] * heads, LANES)
    steps = pltpu.roll(small_ref[:, 0:LANES], shift, 1)
    logs = pltpu.roll(small_ref[:, LANES : 2 * LANES], shift, 1)
    row = lax.broadcasted_iota(jnp.int32, (length, length), 0)
    col = lax.broadcasted_iota(jnp.int32, (length, length), 1)
    lower = jnp.where(row >= col, 1.0, 0.0).astype(BF16)
    cum = dot(lower, logs.astype(BF16)) * LOG2E
    total = cum[length - 1 : length, :]
    col_ref[...] = cum - jnp.log(steps) * LOG2E
    turned = cum.T
    per_group = row_ref.shape[1]
    for group in range(row_ref.shape[0]):
        row_ref[group] = turned[group * per_group : (group + 1) * per_group, :]
    in_ref[...] = jnp.exp2(total - cum) * steps
    out_ref[...] = jnp.exp2(cum)
    dt_ref[...] = steps
    tot_ref[...] = jnp.broadcast_to(total, tot_ref.shape)
    b = small_ref[:, 2 * LANES : 3 * LANES]
    c = small_ref[:, 3 * LANES : 4 * LANES]
    b_ref[...] = b.astype(BF16)
    c_ref[...] = c.astype(BF16)
    bt_ref[...] = b.T.astype(BF16)
    ct_ref[...] = c.T.astype(BF16)


def prepare(at, parts, heads, behind):
    peers = len(parts)
    length = parts[0].shape[0] * peers
    tall = jax.ShapeDtypeStruct((length, LANES), F32)
    thin = jax.ShapeDtypeStruct((length, LANES), BF16)
    flat = jax.ShapeDtypeStruct((LANES, length), BF16)
    groups = jax.ShapeDtypeStruct((heads * WIDTH // COLS, COLS // WIDTH, length), F32)
    return pl.pallas_call(
        functools.partial(prepare_kernel, heads, peers),
        out_shape=(
            tall,
            groups,
            tall,
            tall,
            tall,
            jax.ShapeDtypeStruct((8, LANES), F32),
            thin,
            thin,
            flat,
            flat,
        ),
        in_specs=[smem(), anywhere()] + [vmem()] * peers,
        scratch_shapes=[pltpu.VMEM((length, 4 * LANES), F32)],
        compiler_params=one_step(16),
        cost_estimate=cost(2 * length * length * LANES, 3e6),
        name="prepare",
    )(at, behind, *parts)


def states_kernel(peers, first, at_ref, in_ref, out_ref, bt_ref, ct_ref, *rest):
    parts, (x_ref, dy_ref, sum_ref, sems) = rest[:peers], rest[peers:]
    tokens = parts[0].shape[1]
    blocks, rows, inner = sum_ref.shape
    rows //= 2
    copies = []
    for r in range(peers):
        start = pl.multiple_of((at_ref[0] ^ r) * tokens, tokens)
        for k, target in enumerate((x_ref, dy_ref)):
            copies.append(
                pltpu.make_async_copy(
                    parts[r].at[k], target.at[pl.ds(start, tokens), :], sems.at[r, k]
                )
            )
    for copy in copies:
        copy.start()
    weights = [pieces(in_ref[...], 2), pieces(out_ref[...], 2)]
    for copy in copies:
        copy.wait()
    for group in range(inner // COLS):
        here = slice(group * COLS, (group + 1) * COLS)
        select = selector(LANES, COLS, first + group * (COLS // WIDTH))
        for k, (source, map_ref) in enumerate(((x_ref, bt_ref), (dy_ref, ct_ref))):
            weight = sum(dot(term, select) for term in weights[k])
            weighted = source[:, here].astype(F32) * weight
            added = sum(dot(map_ref[...], term) for term in pieces(weighted, 2)).astype(BF16)
            for block in range(blocks):
                sum_ref[block, k * rows : (k + 1) * rows, here] = added[
                    block * rows : (block + 1) * rows, :
                ]


def states(at, into, out_of, b_t, c_t, parts, blocks, first):
    peers = len(parts)
    tokens, inner = parts[0].shape[1:]
    length = tokens * peers
    rows = jax.ShapeDtypeStruct((length, inner), BF16)
    return pl.pallas_call(
        functools.partial(states_kernel, peers, first),
        out_shape=(
            rows,
            rows,
            jax.ShapeDtypeStruct((blocks, 2 * LANES // blocks, inner), BF16),
        ),
        in_specs=[smem()] + [vmem()] * 4 + [anywhere()] * peers,
        scratch_shapes=[pltpu.SemaphoreType.DMA((peers, 2))],
        compiler_params=one_step(16),
        cost_estimate=cost(16 * length * inner * LANES, 8 * length * inner),
        name="states",
    )(at, into, out_of, b_t, c_t, *parts)


def scan_kernel(first, tot_ref, in_ref, _, out_ref, kept_ref):
    blocks, rows, inner = in_ref.shape
    rows //= 2
    select = selector(LANES, inner, first)
    decay = spread(jnp.exp2(tot_ref[...]), select, 3)
    through = []
    for k, order in enumerate((range(blocks), range(blocks - 1, -1, -1))):
        here = slice(k * rows, (k + 1) * rows)
        running = jnp.zeros((rows, inner), F32)
        for block in order:
            out_ref[block, here, 0:inner] = running.astype(BF16)
            if k == 0:
                kept_ref[block] = running
            else:
                through.append(jnp.sum(kept_ref[block] * running, axis=0, keepdims=True))
            step = decay[block * 8 : block * 8 + 1, :]
            running = step * running + in_ref[block, here, :].astype(F32)
    link = gather(jnp.concatenate(through[::-1], axis=0), select, 3)
    high, low = (term.astype(F32) for term in pieces(link, 2))
    row = lax.broadcasted_iota(jnp.int32, (2 * rows, LANES), 0)
    for block in range(blocks):
        here = slice(block, block + 1)
        both = jnp.where(row == 0, high[here, :], jnp.where(row == 1, low[here, :], 0.0))
        out_ref[block, :, inner:] = both.astype(BF16)


def carried_in(sums, totals, first, behind):
    blocks, rows, inner = sums.shape
    sums = lax.all_to_all(sums, "ctx", split_axis=0, concat_axis=0, tiled=True)
    sums = pl.pallas_call(
        functools.partial(scan_kernel, first),
        out_shape=jax.ShapeDtypeStruct((blocks, rows, inner + LANES), BF16),
        scratch_shapes=[pltpu.VMEM((blocks, rows // 2, inner), F32)],
        in_specs=[vmem(), vmem(), anywhere()],
        compiler_params=one_step(8),
        cost_estimate=cost(6 * 8 * blocks * LANES * inner, 4 * blocks * rows * inner),
        name="scan_blocks",
    )(totals.reshape(blocks * 8, LANES), sums, behind)
    return lax.all_to_all(sums, "ctx", split_axis=0, concat_axis=0, tiled=True)


def stacked(ref, k):
    blocks, rows, _ = ref.shape
    rows //= 2
    return jnp.concatenate(
        [ref[block, k * rows : (k + 1) * rows, :] for block in range(blocks)], axis=0
    )


def inside_kernel(first, x_ref, dy_ref, b_ref, c_ref, col_ref, row_ref, *rest):
    added, (dx_ref, u_ref, v_ref, db_ref, dc_ref, s_ref, ds_ref) = rest[:-7], rest[-7:]
    length = x_ref.shape[0]
    tiles = length // LANES
    heads = COLS // WIDTH
    group = pl.program_id(0)
    from_k = lax.broadcasted_iota(jnp.int32, (length, length), 0)
    to_q = lax.broadcasted_iota(jnp.int32, (length, length), 1)

    @pl.when(group == 0)
    def _():
        s_ref[...] = jnp.where(to_q >= from_k, dot_nt(b_ref[...], c_ref[...]), 0.0)
        ds_ref[...] = jnp.zeros_like(ds_ref)
        v_ref[...] = jnp.zeros_like(v_ref)

    turned = pltpu.roll(col_ref[...], lax.rem(LANES - first - group * heads, LANES), 1)
    lane = lax.broadcasted_iota(jnp.int32, (LANES, LANES), 1)
    for j in range(tiles):
        low = j * LANES
        here = slice(low, low + LANES)
        for pair in range(heads // 2):
            across = slice(pair * LANES, (pair + 1) * LANES)
            xs = x_ref[here, across]
            dys = dy_ref[low:, across]
            side = lax.broadcasted_iota(jnp.int32, dys.shape, 1) // WIDTH
            total = None
            for half in range(2):
                local = pair * 2 + half
                head = first + group * heads + local
                own_x = jnp.where(lane // WIDTH == half, xs, jnp.zeros_like(xs))
                own_dy = jnp.where(side == half, dys, jnp.zeros_like(dys))
                products = dot_nt(own_x, dys)
                behind = turned[here, local : local + 1]
                kept = []
                v_sum = None
                for i in range(j, tiles):
                    there = slice(i * LANES, (i + 1) * LANES)
                    ahead = row_ref[0, local : local + 1, there]
                    decay = jnp.exp2(jnp.minimum(ahead - behind, 64.0))
                    product = products[:, (i - j) * LANES : (i - j + 1) * LANES]
                    score = s_ref[here, there] * decay
                    kept.append(score.astype(BF16))
                    ds_ref[here, there] += decay * product
                    both = score * product
                    v_sum = both if v_sum is None else v_sum + both
                    u_sum = jnp.sum(both, axis=0, keepdims=True)
                    if j > 0:
                        u_sum += u_ref[0, local : local + 1, there]
                    u_ref[0, local : local + 1, there] = u_sum
                v_col = jnp.sum(v_sum, axis=1, keepdims=True)
                v_ref[here, :] = jnp.where(lane == head, v_col, v_ref[here, :])
                scores = jnp.concatenate(kept, axis=1) if len(kept) > 1 else kept[0]
                part = dot(scores, own_dy)
                total = part if total is None else total + part
            dx_ref[here, across] = total

    @pl.when(group == pl.num_programs(0) - 1)
    def _():
        grads = jnp.where(to_q >= from_k, ds_ref[...], 0.0)
        db = sum(dot(term, c_ref[...]) for term in pieces(grads, 2))
        dc = sum(dot(term, b_ref[...]) for term in pieces(grads.T, 2))
        db_ref[...] = db + added[0][...] if added else db
        dc_ref[...] = dc + added[1][...] if added else dc


def inside(x, dy, b, c, col_part, row_part, first, *added):
    added = [a for a in added if a is not None]
    length, inner = x.shape
    tall = jax.ShapeDtypeStruct((length, LANES), F32)
    pairs = length * length * inner
    offset = first * WIDTH // COLS
    by_group = pl.BlockSpec((1,) + row_part.shape[1:], lambda g: (g + offset, 0, 0))
    own_group = pl.BlockSpec((1,) + row_part.shape[1:], lambda g: (g, 0, 0))
    return pl.pallas_call(
        functools.partial(inside_kernel, first),
        grid=(inner // COLS,),
        out_shape=(
            jax.ShapeDtypeStruct((length, inner), F32),
            jax.ShapeDtypeStruct((inner // COLS,) + row_part.shape[1:], F32),
            tall,
            tall,
            tall,
        ),
        in_specs=[
            columns(length),
            columns(length),
            whole(length, LANES),
            whole(length, LANES),
            whole(length, LANES),
            by_group,
        ]
        + [whole(length, LANES)] * len(added),
        out_specs=(
            columns(length),
            own_group,
            whole(length, LANES),
            whole(length, LANES),
            whole(length, LANES),
        ),
        scratch_shapes=[pltpu.VMEM((length, length), F32), pltpu.VMEM((length, length), F32)],
        compiler_params=params(20),
        cost_estimate=cost(16 * pairs, 8 * length * inner, pairs // WIDTH),
        name="inside",
    )(x, dy, b, c, col_part, row_part, *added)


def by_columns(shape):
    return pl.BlockSpec(shape[:2] + (COLS,), lambda g: (0, 0, g))


def channels_kernel(peers, first, at_ref, dy_ref, dxi_ref, carry_ref, weight_ref, b_ref, skip_ref, *rest):
    outs, dx_ref = rest[-1 - peers : -1], rest[-1]
    tokens = dy_ref.shape[0] // peers
    select = selector(LANES, COLS, first + pl.program_id(0) * (COLS // WIDTH))
    carried = spread(weight_ref[...], select) * dot(b_ref[...], stacked(carry_ref, 1))
    gain = spread(skip_ref[...], select, 3)[0:1, :]
    dx_ref[...] = (dxi_ref[...] + carried + gain * dy_ref[...].astype(F32)).astype(BF16)
    for r in range(peers):
        start = pl.multiple_of((at_ref[0] ^ r) * tokens, tokens)
        outs[r][...] = dx_ref[pl.ds(start, tokens), :]


def channels(peers, first, at, dy, dxi, carry, weight, b, skip, behind):
    length, inner = dy.shape
    tokens = length // peers
    tall = whole(length, LANES)
    return pl.pallas_call(
        functools.partial(channels_kernel, peers, first),
        grid=(inner // COLS,),
        out_shape=[jax.ShapeDtypeStruct((tokens, inner), BF16)] * peers,
        in_specs=[
            smem(),
            columns(length),
            columns(length),
            by_columns(carry.shape),
            tall,
            tall,
            whole(8, LANES),
        ]
        + [anywhere()] * len(behind),
        out_specs=[columns(tokens)] * peers,
        scratch_shapes=[pltpu.VMEM((length, COLS), BF16)],
        compiler_params=params(12),
        cost_estimate=cost(6 * length * inner * LANES, 8 * length * inner),
        name="channels",
    )(at, dy, dxi, carry, weight, b, skip, *behind)


def others_kernel(
    heads,
    peers,
    first,
    last,
    at_ref,
    _,
    x_ref,
    dy_ref,
    carry_ref,
    through_ref,
    into_ref,
    out_of_ref,
    b_ref,
    c_ref,
    dt_ref,
    tot_ref,
    ui_ref,
    vi_ref,
    *rest,
):
    if last:
        added, rest = rest[:5], rest[5:]
    outs, (db_ref, dc_ref, u_ref, v_ref, tail_ref) = rest[:-5], rest[-5:]
    length = x_ref.shape[0]
    tokens = length // peers
    group = pl.program_id(0)

    @pl.when(group == 0)
    def _():
        db_ref[...] = jnp.zeros_like(db_ref)
        dc_ref[...] = jnp.zeros_like(dc_ref)
        u_ref[...] = jnp.zeros_like(u_ref)
        v_ref[...] = jnp.zeros_like(v_ref)

    select = selector(LANES, COLS, first + group * (COLS // WIDTH))
    for source, weight_ref, k, near_ref, sum_ref, head_ref in (
        (x_ref, into_ref, 1, b_ref, db_ref, v_ref),
        (dy_ref, out_of_ref, 0, c_ref, dc_ref, u_ref),
    ):
        weighted = source[...].astype(F32) * spread(weight_ref[...], select)
        far = stacked(carry_ref, k)
        sum_ref[...] += sum(dot_nt(term, far) for term in pieces(weighted, 2))
        head_ref[...] += gather(weighted * dot(near_ref[...], far), select)

    @pl.when(group == pl.num_programs(0) - 1)
    def _():
        inner_v, outer_v = vi_ref[...], v_ref[...]
        steps = (inner_v + outer_v) / dt_ref[...]
        rows = [ui_ref[at] for at in range(ui_ref.shape[0])]
        if first > 0:
            rows.insert(0, jnp.zeros((first, length), F32))
        rows.append(jnp.zeros((LANES - sum(part.shape[0] for part in rows), length), F32))
        net = jnp.concatenate(rows, axis=0).T + u_ref[...] - inner_v - outer_v
        row = lax.broadcasted_iota(jnp.int32, (length, length), 0)
        col = lax.broadcasted_iota(jnp.int32, (length, length), 1)
        upper = jnp.where(col >= row, 1.0, 0.0).astype(BF16)
        later = sum(dot(upper, term) for term in pieces(net, 3))
        whole_block = jnp.sum(outer_v, axis=0, keepdims=True)
        link = sum(through_ref[block].astype(F32) for block in range(through_ref.shape[0]))
        link = jnp.sum(link, axis=0, keepdims=True)
        logs = later + whole_block + jnp.exp2(tot_ref[0:1, :]) * link
        thin = steps + pltpu.roll(logs, heads, 1)
        if not last:
            outs[0][...] = thin
            outs[1][...] = db_ref[...]
            outs[2][...] = dc_ref[...]
        else:
            thin_ref, dbo_ref, dco_ref, dbi_ref, dci_ref = added
            tail_ref[:, 0:LANES] = (thin + thin_ref[...]).astype(BF16)
            tail_ref[:, LANES : 2 * LANES] = (db_ref[...] + dbo_ref[...] + dbi_ref[...]).astype(BF16)
            tail_ref[:, 2 * LANES :] = (dc_ref[...] + dco_ref[...] + dci_ref[...]).astype(BF16)
            for r in range(peers):
                start = pl.multiple_of((at_ref[0] ^ r) * tokens, tokens)
                outs[r][...] = tail_ref[pl.ds(start, tokens), :]


def others(heads, peers, first, at, x, dy, carry, into, out_of, b, c, dt, tot, ui, vi, added, behind):
    length, inner = x.shape
    tokens = length // peers
    tall = whole(length, LANES)
    last = len(added) > 0
    tall_shape = jax.ShapeDtypeStruct((length, LANES), F32)
    tail_shape = jax.ShapeDtypeStruct((tokens, 3 * LANES), BF16)
    return pl.pallas_call(
        functools.partial(others_kernel, heads, peers, first, last),
        grid=(inner // COLS,),
        out_shape=[tail_shape] * peers if last else [tall_shape] * 3,
        in_specs=[
            smem(),
            anywhere(),
            columns(length),
            columns(length),
            by_columns(carry.shape),
            pl.BlockSpec(carry.shape[:2] + (LANES,), lambda g: (0, 0, inner // LANES)),
            tall,
            tall,
            tall,
            tall,
            tall,
            whole(8, LANES),
            whole(*ui.shape),
            tall,
        ]
        + [tall] * len(added),
        out_specs=[whole(tokens, 3 * LANES)] * peers if last else [tall] * 3,
        scratch_shapes=[pltpu.VMEM((length, LANES), F32)] * 4
        + [pltpu.VMEM((length, 3 * LANES), BF16)],
        compiler_params=params(20),
        cost_estimate=cost(28 * length * inner * LANES, 6 * length * inner),
        name="others",
    )(at, behind, x, dy, carry, carry, into, out_of, b, c, dt, tot, ui, vi, *added)


def finish_kernel(heads, peers, halves, at_ref, *rest):
    count = peers * halves
    sent, tails = rest[:count], rest[count : count + peers]
    dx_ref, steps_ref, logs_ref, db_ref, dc_ref, sems = rest[count + peers :]
    tokens, width = sent[0].shape
    copies = []
    for half in range(halves):
        for r in range(peers):
            start = pl.multiple_of(((at_ref[0] ^ r) * halves + half) * width, LANES)
            copies.append(
                pltpu.make_async_copy(
                    sent[half * peers + r], dx_ref.at[:, pl.ds(start, width)], sems.at[half, r]
                )
            )
    for copy in copies:
        copy.start()
    lane = lax.broadcasted_iota(jnp.int32, (tokens, LANES), 1)
    results = [jnp.zeros((tokens, LANES), F32) for _ in range(4)]
    for r in range(peers):
        source = at_ref[0] ^ r
        own = lane // heads == source
        thin = tails[r][:, 0:LANES].astype(F32)
        for k in range(2):
            shift = lax.rem((source - k) * heads + LANES, LANES)
            results[k] += jnp.where(own, pltpu.roll(thin, shift, 1), 0.0)
            results[2 + k] += tails[r][:, (k + 1) * LANES : (k + 2) * LANES].astype(F32)
    steps_ref[...] = results[0].astype(BF16)
    logs_ref[...] = results[1].astype(BF16)
    db_ref[...] = results[2]
    dc_ref[...] = results[3]
    for copy in copies:
        copy.wait()


def finish(heads, at, sent, tails):
    peers, halves = len(tails), len(sent)
    tokens, width = sent[0][0].shape
    thin = jax.ShapeDtypeStruct((tokens, LANES), BF16)
    wide = jax.ShapeDtypeStruct((tokens, LANES), F32)
    return pl.pallas_call(
        functools.partial(finish_kernel, heads, peers, halves),
        out_shape=(
            jax.ShapeDtypeStruct((tokens, width * halves * peers), BF16),
            thin,
            thin,
            wide,
            wide,
        ),
        in_specs=[smem()] + [vmem()] * (peers * halves + peers),
        out_specs=(anywhere(), vmem(), vmem(), vmem(), vmem()),
        scratch_shapes=[pltpu.SemaphoreType.DMA((halves, peers))],
        compiler_params=one_step(8),
        cost_estimate=cost(0, 4 * tokens * width * halves * peers),
        name="finish",
    )(at, *[part for group in sent for part in group], *tails)


HALVES = 2


def body(inputs, grad_out, steps, log_decay, input_map, output_map, skip_gain):
    blocks, peers = lax.axis_size("ctx"), lax.axis_size("head")
    inner = inputs.shape[1] // peers
    heads = steps.shape[1] // peers
    width = inner // HALVES
    at = lax.axis_index("head").astype(jnp.int32).reshape(1)

    small = join(steps, log_decay, input_map, output_map)
    small_parts = swap([small] * peers)
    packed = []
    for half in range(HALVES):
        behind = packed[-1][0] if packed else small
        packed.append(pack(at, inputs, grad_out, peers, half * width, width, behind))
    parts = [swap(part) for part in packed]
    col_part, row_part, into, out_of, dt, tot, b, c, b_t, c_t = prepare(
        at, small_parts, heads, packed[-1][0]
    )
    totals = jnp.broadcast_to(tot[None], (blocks,) + tot.shape)
    totals = lax.all_to_all(totals, "ctx", split_axis=0, concat_axis=0, tiled=True)
    skip = jnp.broadcast_to(jnp.pad(skip_gain, (0, LANES - heads))[None], (8, LANES))

    rows, pairs, carries = [], [], []
    behind = None
    dbi = dci = None
    for half in range(HALVES):
        first = half * heads // HALVES
        x, dy, sums = states(at, into, out_of, b_t, c_t, parts[half], blocks, first)
        dxi, ui, vi, dbi, dci = inside(x, dy, b, c, col_part, row_part, first, dbi, dci)
        rows.append((x, dy))
        pairs.append((dxi, ui, vi))
        carries.append(sums)

    def back(half, behind):
        first = half * heads // HALVES
        (x, dy), (dxi, ui, vi) = rows[half], pairs[half]
        return channels(peers, first, at, dy, dxi, carries[half], into, b, skip, behind)

    def remain(half, added, behind):
        first = half * heads // HALVES
        (x, dy), (dxi, ui, vi) = rows[half], pairs[half]
        return others(
            heads, peers, first, at, x, dy, carries[half], into, out_of, b, c, dt, tot, ui, vi,
            added, behind,
        )

    carries[0] = carried_in(carries[0], totals, 0, pairs[0][0])
    dx_low = back(0, pairs[1][:1])
    sent = [swap(dx_low)]
    added = remain(0, [], dx_low[0])
    carries[1] = carried_in(carries[1], totals, heads // HALVES, added[0])
    dx_high = back(1, sent[0][1:])
    sent.append(swap(dx_high))
    tails = swap(remain(1, [*added, dbi, dci], dx_high[0]))
    return tuple(finish(heads, at, sent, tails))


def solution(mesh):
    rows = P(("ctx", "head"), None)
    return jax.shard_map(
        body,
        mesh=mesh,
        in_specs=(rows,) * 6 + (P("head"),),
        out_specs=(rows,) * 5,
        check_vma=False,
    )
```

```python
import functools

import jax
import jax.numpy as jnp
from jax import lax
from jax.experimental import pallas as pl
from jax.experimental.pallas import tpu as pltpu
from jax.sharding import PartitionSpec as P

F32 = jnp.float32
BF16 = jnp.bfloat16
LANES = 128
WIDTH = 64
COLS = 256
LOG2E = 1.4426950408889634
NT = (((1,), (1,)), ((), ()))
MIB = 1024 * 1024
LITTLE = pl.CostEstimate(flops=1000, bytes_accessed=1000, transcendentals=0)


def dot(a, b):
    return jnp.dot(a, b, preferred_element_type=F32)


def dot_nt(a, b):
    return lax.dot_general(a, b, NT, preferred_element_type=F32)


def pieces(a, count):
    terms = []
    for _ in range(count):
        term = a.astype(BF16)
        terms.append(term)
        a = a - term.astype(F32)
    return terms


def selector(rows, cols, first):
    row = lax.broadcasted_iota(jnp.int32, (rows, cols), 0)
    col = lax.broadcasted_iota(jnp.int32, (rows, cols), 1)
    return jnp.where((col // WIDTH) + first == row, 1.0, 0.0).astype(BF16)


def spread(a, select, count=2):
    return sum(dot(term, select) for term in pieces(a, count))


def gather(a, select, count=2):
    return sum(dot_nt(term, select) for term in pieces(a, count))


def params(mib):
    return pltpu.CompilerParams(dimension_semantics=("arbitrary",), vmem_limit_bytes=mib * MIB)


def whole(*shape):
    return pl.BlockSpec(shape, lambda *g: (0,) * len(shape))


def columns(rows):
    return pl.BlockSpec((rows, COLS), lambda g: (0, g))


def call(kernel, out_shape, operands, **options):
    operands = [
        a if a.dtype == jnp.int32 else pltpu.with_memory_space_constraint(a, pltpu.HBM)
        for a in operands
    ]
    out_shape = [pltpu.HBM(one.shape, one.dtype) for one in out_shape]
    return pl.pallas_call(kernel, out_shape=out_shape, **options)(*operands)


def smem():
    return pl.BlockSpec(memory_space=pltpu.SMEM)


def anywhere():
    return pl.BlockSpec(memory_space=pl.ANY)


def vmem():
    return pl.BlockSpec(memory_space=pltpu.VMEM)


def one_step(mib):
    return pltpu.CompilerParams(vmem_limit_bytes=mib * MIB)


def swap(parts):
    peers = lax.axis_size("head")
    got = [parts[0]] + [None] * (peers - 1)
    for r in range(peers - 1, 0, -1):
        got[r] = lax.ppermute(parts[r], "head", [(i, i ^ r) for i in range(peers)])
    return got


def pack_kernel(peers, first, width, at_ref, *rest):
    sources, outs, (held, sems) = rest[: -peers - 2], rest[-peers - 2 : -2], rest[-2:]
    inner = sources[0].shape[1] // peers
    order = list(range(peers - 1, -1, -1))
    parts, at = [], 0
    for k, source in enumerate(sources):
        size = width if k < 2 else source.shape[1]
        parts.append((source, at, size))
        at += size
    reads = {}
    for r in order:
        start = pl.multiple_of((at_ref[0] ^ r) * inner + first, LANES)
        for k, (source, at, size) in enumerate(parts):
            chosen = source.at[:, pl.ds(start, size)] if k < 2 else source
            reads[r, k] = pltpu.make_async_copy(
                chosen, held.at[r, :, pl.ds(at, size)], sems.at[0, r, k]
            )
            reads[r, k].start()
    writes = []
    for r in order:
        for k in range(len(parts)):
            reads[r, k].wait()
        writes.append(pltpu.make_async_copy(held.at[r], outs[r], sems.at[1, r, 0]))
        writes[-1].start()
    for write in writes:
        write.wait()


def pack(at, x, dy, riders, peers, first, width, behind):
    tokens = x.shape[0]
    full = 2 * width + sum(rider.shape[1] for rider in riders)
    count = 2 + len(riders)

    def kernel(at_ref, *rest):
        pack_kernel(peers, first, width, at_ref, *rest[:count], *rest[count + len(behind) :])

    return call(
        kernel,
        [jax.ShapeDtypeStruct((tokens, full), BF16)] * peers,
        (at, x, dy, *riders, *behind),
        in_specs=[smem()] + [anywhere()] * (count + len(behind)),
        out_specs=[anywhere()] * peers,
        scratch_shapes=[
            pltpu.VMEM((peers, tokens, full), BF16),
            pltpu.SemaphoreType.DMA((2, peers, count)),
        ],
        compiler_params=one_step(10),
        cost_estimate=LITTLE,
        name="pack",
    )


def prepare_kernel(heads, peers, at_ref, *rest):
    parts = rest[:peers]
    col_ref, row_ref, in_ref, out_ref, dt_ref, tot_ref, b_ref, c_ref, bt_ref, ct_ref = rest[peers:-3]
    small_ref, got, sems = rest[-3:]
    tokens, full = parts[0].shape
    length = tokens * peers
    copies = []
    for r in range(peers):
        chosen = parts[r].at[:, pl.ds(full - 4 * LANES, 4 * LANES)]
        copies.append(pltpu.make_async_copy(chosen, got.at[r], sems.at[r]))
        copies[-1].start()
    for r in range(peers):
        copies[r].wait()
        start = pl.multiple_of((at_ref[0] ^ r) * tokens, tokens)
        small_ref[pl.ds(start, tokens), :] = got[r].astype(F32)
    shift = lax.rem(LANES - at_ref[0] * heads, LANES)
    steps = pltpu.roll(small_ref[:, 0:LANES], shift, 1)
    logs = pltpu.roll(small_ref[:, LANES : 2 * LANES], shift, 1)
    row = lax.broadcasted_iota(jnp.int32, (length, length), 0)
    col = lax.broadcasted_iota(jnp.int32, (length, length), 1)
    lower = jnp.where(row >= col, 1.0, 0.0).astype(BF16)
    cum = dot(lower, logs.astype(BF16)) * LOG2E
    total = cum[length - 1 : length, :]
    col_ref[...] = cum - jnp.log(steps) * LOG2E
    turned = cum.T
    per_group = row_ref.shape[1]
    for group in range(row_ref.shape[0]):
        row_ref[group] = turned[group * per_group : (group + 1) * per_group, :]
    in_ref[...] = jnp.exp2(total - cum) * steps
    out_ref[...] = jnp.exp2(cum)
    dt_ref[...] = steps
    tot_ref[...] = jnp.broadcast_to(total, tot_ref.shape)
    b = small_ref[:, 2 * LANES : 3 * LANES]
    c = small_ref[:, 3 * LANES : 4 * LANES]
    b_ref[...] = b.astype(BF16)
    c_ref[...] = c.astype(BF16)
    bt_ref[...] = b.T.astype(BF16)
    ct_ref[...] = c.T.astype(BF16)


def prepare(at, parts, heads):
    peers = len(parts)
    length = parts[0].shape[0] * peers
    tall = jax.ShapeDtypeStruct((length, LANES), F32)
    thin = jax.ShapeDtypeStruct((length, LANES), BF16)
    flat = jax.ShapeDtypeStruct((LANES, length), BF16)
    groups = jax.ShapeDtypeStruct((heads * WIDTH // COLS, COLS // WIDTH, length), F32)
    return call(
        functools.partial(prepare_kernel, heads, peers),
        (
            tall,
            groups,
            tall,
            tall,
            tall,
            jax.ShapeDtypeStruct((8, LANES), F32),
            thin,
            thin,
            flat,
            flat,
        ),
        (at, *parts,),
        in_specs=[smem()] + [anywhere()] * peers,
        scratch_shapes=[
            pltpu.VMEM((length, 4 * LANES), F32),
            pltpu.VMEM((peers, parts[0].shape[0], 4 * LANES), BF16),
            pltpu.SemaphoreType.DMA((peers,)),
        ],
        compiler_params=one_step(16),
        cost_estimate=LITTLE,
        name="prepare",
    )


def states_kernel(peers, first, at_ref, in_ref, out_ref, bt_ref, ct_ref, tot_ref, *rest):
    parts, (x_ref, dy_ref, sum_ref, sems) = rest[:peers], rest[-4:]
    tokens = parts[0].shape[0]
    blocks, rows, inner = sum_ref.shape
    rows, inner = rows // 2, inner - LANES
    copies = []
    for r in range(peers):
        start = pl.multiple_of((at_ref[0] ^ r) * tokens, tokens)
        for k, target in enumerate((x_ref, dy_ref)):
            copies.append(
                pltpu.make_async_copy(
                    parts[r].at[:, pl.ds(k * inner, inner)],
                    target.at[pl.ds(start, tokens), :],
                    sems.at[r, k],
                )
            )
    for copy in copies:
        copy.start()
    row = lax.broadcasted_iota(jnp.int32, (2 * rows, LANES), 0)
    total = jnp.zeros((2 * rows, LANES), F32)
    for k, term in enumerate(pieces(tot_ref[0:1, :], 3)):
        total = jnp.where(row == k, term.astype(F32), total)
    for block in range(blocks):
        sum_ref[block, :, inner:] = total.astype(BF16)
    weights = [pieces(in_ref[...], 2), pieces(out_ref[...], 2)]
    for copy in copies:
        copy.wait()
    for group in range(inner // COLS):
        here = slice(group * COLS, (group + 1) * COLS)
        select = selector(LANES, COLS, first + group * (COLS // WIDTH))
        for k, (source, map_ref) in enumerate(((x_ref, bt_ref), (dy_ref, ct_ref))):
            weight = sum(dot(term, select) for term in weights[k])
            weighted = source[:, here].astype(F32) * weight
            added = sum(dot(map_ref[...], term) for term in pieces(weighted, 2)).astype(BF16)
            for block in range(blocks):
                sum_ref[block, k * rows : (k + 1) * rows, here] = added[
                    block * rows : (block + 1) * rows, :
                ]


def states(at, into, out_of, b_t, c_t, tot, parts, blocks, inner, first, behind):
    peers = len(parts)
    length = parts[0].shape[0] * peers
    rows = jax.ShapeDtypeStruct((length, inner), BF16)
    return call(
        functools.partial(states_kernel, peers, first),
        (
            rows,
            rows,
            jax.ShapeDtypeStruct((blocks, 2 * LANES // blocks, inner + LANES), BF16),
        ),
        (at, into, out_of, b_t, c_t, tot, *parts, *behind,),
        in_specs=[smem()] + [vmem()] * 5 + [anywhere()] * (peers + len(behind)),
        scratch_shapes=[pltpu.SemaphoreType.DMA((peers, 2))],
        compiler_params=one_step(16),
        cost_estimate=LITTLE,
        name="states",
    )


def scan_kernel(first, in_ref, _, out_ref, kept_ref):
    blocks, rows, inner = in_ref.shape
    rows, inner = rows // 2, inner - LANES
    select = selector(LANES, inner, first)
    totals = [
        jnp.sum(in_ref[block, :, inner:].astype(F32), axis=0, keepdims=True)
        for block in range(blocks)
    ]
    decay = spread(jnp.exp2(jnp.concatenate(totals, axis=0)), select, 3)
    through = []
    for k, order in enumerate((range(blocks), range(blocks - 1, -1, -1))):
        here = slice(k * rows, (k + 1) * rows)
        running = jnp.zeros((rows, inner), F32)
        for block in order:
            out_ref[block, here, 0:inner] = running.astype(BF16)
            if k == 0:
                kept_ref[block] = running
            else:
                through.append(jnp.sum(kept_ref[block] * running, axis=0, keepdims=True))
            step = decay[block : block + 1, :]
            running = step * running + in_ref[block, here, 0:inner].astype(F32)
    link = gather(jnp.concatenate(through[::-1], axis=0), select, 3)
    high, low = (term.astype(F32) for term in pieces(link, 2))
    row = lax.broadcasted_iota(jnp.int32, (2 * rows, LANES), 0)
    for block in range(blocks):
        here = slice(block, block + 1)
        both = jnp.where(row == 0, high[here, :], jnp.where(row == 1, low[here, :], 0.0))
        out_ref[block, :, inner:] = both.astype(BF16)


def scan_blocks(sums, first, behind):
    blocks, rows, inner = sums.shape
    return call(
        functools.partial(scan_kernel, first),
        [jax.ShapeDtypeStruct(sums.shape, BF16)],
        (sums, behind),
        scratch_shapes=[pltpu.VMEM((blocks, rows // 2, inner - LANES), F32)],
        in_specs=[vmem(), anywhere()],
        compiler_params=one_step(8),
        cost_estimate=LITTLE,
        name="scan_blocks",
    )[0]


def across(sums):
    return lax.all_to_all(sums, "ctx", split_axis=0, concat_axis=0, tiled=True)


def stacked(ref, k):
    blocks, rows, _ = ref.shape
    rows //= 2
    return jnp.concatenate(
        [ref[block, k * rows : (k + 1) * rows, :] for block in range(blocks)], axis=0
    )


def inside_kernel(first, x_ref, dy_ref, b_ref, c_ref, col_ref, row_ref, *rest):
    added, (dx_ref, u_ref, v_ref, db_ref, dc_ref, s_ref, ds_ref) = rest[:-7], rest[-7:]
    length = x_ref.shape[0]
    tiles = length // LANES
    heads = COLS // WIDTH
    group = pl.program_id(0)
    from_k = lax.broadcasted_iota(jnp.int32, (length, length), 0)
    to_q = lax.broadcasted_iota(jnp.int32, (length, length), 1)

    @pl.when(group == 0)
    def _():
        s_ref[...] = jnp.where(to_q >= from_k, dot_nt(b_ref[...], c_ref[...]), 0.0)
        ds_ref[...] = jnp.zeros_like(ds_ref)
        v_ref[...] = jnp.zeros_like(v_ref)

    turned = pltpu.roll(col_ref[...], lax.rem(LANES - first - group * heads, LANES), 1)
    lane = lax.broadcasted_iota(jnp.int32, (LANES, LANES), 1)
    for j in range(tiles):
        low = j * LANES
        here = slice(low, low + LANES)
        for pair in range(heads // 2):
            across = slice(pair * LANES, (pair + 1) * LANES)
            xs = x_ref[here, across]
            dys = dy_ref[low:, across]
            side = lax.broadcasted_iota(jnp.int32, dys.shape, 1) // WIDTH
            total = None
            for half in range(2):
                local = pair * 2 + half
                head = first + group * heads + local
                own_x = jnp.where(lane // WIDTH == half, xs, jnp.zeros_like(xs))
                own_dy = jnp.where(side == half, dys, jnp.zeros_like(dys))
                products = dot_nt(own_x, dys)
                behind = turned[here, local : local + 1]
                kept = []
                v_sum = None
                for i in range(j, tiles):
                    there = slice(i * LANES, (i + 1) * LANES)
                    ahead = row_ref[0, local : local + 1, there]
                    decay = jnp.exp2(jnp.minimum(ahead - behind, 64.0))
                    product = products[:, (i - j) * LANES : (i - j + 1) * LANES]
                    score = s_ref[here, there] * decay
                    kept.append(score.astype(BF16))
                    ds_ref[here, there] += decay * product
                    both = score * product
                    v_sum = both if v_sum is None else v_sum + both
                    u_sum = jnp.sum(both, axis=0, keepdims=True)
                    if j > 0:
                        u_sum += u_ref[0, local : local + 1, there]
                    u_ref[0, local : local + 1, there] = u_sum
                v_col = jnp.sum(v_sum, axis=1, keepdims=True)
                v_ref[here, :] = jnp.where(lane == head, v_col, v_ref[here, :])
                scores = jnp.concatenate(kept, axis=1) if len(kept) > 1 else kept[0]
                part = dot(scores, own_dy)
                total = part if total is None else total + part
            dx_ref[here, across] = total

    @pl.when(group == pl.num_programs(0) - 1)
    def _():
        grads = jnp.where(to_q >= from_k, ds_ref[...], 0.0)
        db = sum(dot(term, c_ref[...]) for term in pieces(grads, 2))
        dc = sum(dot(term, b_ref[...]) for term in pieces(grads.T, 2))
        db_ref[...] = db + added[0][...] if added else db
        dc_ref[...] = dc + added[1][...] if added else dc


def inside(x, dy, b, c, col_part, row_part, first, *added):
    added = [a for a in added if a is not None]
    length, inner = x.shape
    tall = jax.ShapeDtypeStruct((length, LANES), F32)
    pairs = length * length * inner
    offset = first * WIDTH // COLS
    by_group = pl.BlockSpec((1,) + row_part.shape[1:], lambda g: (g + offset, 0, 0))
    own_group = pl.BlockSpec((1,) + row_part.shape[1:], lambda g: (g, 0, 0))
    return call(
        functools.partial(inside_kernel, first),
        (
            jax.ShapeDtypeStruct((length, inner), F32),
            jax.ShapeDtypeStruct((inner // COLS,) + row_part.shape[1:], F32),
            tall,
            tall,
            tall,
        ),
        (x, dy, b, c, col_part, row_part, *added,),
        grid=(inner // COLS,),
        in_specs=[
            columns(length),
            columns(length),
            whole(length, LANES),
            whole(length, LANES),
            whole(length, LANES),
            by_group,
        ]
        + [whole(length, LANES)] * len(added),
        out_specs=(
            columns(length),
            own_group,
            whole(length, LANES),
            whole(length, LANES),
            whole(length, LANES),
        ),
        scratch_shapes=[pltpu.VMEM((length, length), F32), pltpu.VMEM((length, length), F32)],
        compiler_params=params(20),
        cost_estimate=LITTLE,
        name="inside",
    )


def by_columns(shape):
    return pl.BlockSpec(shape[:2] + (COLS,), lambda g: (0, 0, g))


def channels_kernel(peers, first, at_ref, dy_ref, dxi_ref, carry_ref, weight_ref, b_ref, skip_ref, *rest):
    outs, dx_ref = rest[-1 - peers : -1], rest[-1]
    tokens = dy_ref.shape[0] // peers
    select = selector(LANES, COLS, first + pl.program_id(0) * (COLS // WIDTH))
    carried = spread(weight_ref[...], select) * dot(b_ref[...], stacked(carry_ref, 1))
    gain = spread(skip_ref[...], select, 3)[0:1, :]
    dx_ref[...] = (dxi_ref[...] + carried + gain * dy_ref[...].astype(F32)).astype(BF16)
    for r in range(peers):
        start = pl.multiple_of((at_ref[0] ^ r) * tokens, tokens)
        outs[r][...] = dx_ref[pl.ds(start, tokens), :]


def channels(peers, first, at, dy, dxi, carry, weight, b, skip, behind):
    length, inner = dy.shape
    tokens = length // peers
    tall = whole(length, LANES)
    return call(
        functools.partial(channels_kernel, peers, first),
        [jax.ShapeDtypeStruct((tokens, inner), BF16)] * peers,
        (at, dy, dxi, carry, weight, b, skip, *behind,),
        grid=(inner // COLS,),
        in_specs=[
            smem(),
            columns(length),
            columns(length),
            by_columns(carry.shape),
            tall,
            tall,
            whole(8, LANES),
        ]
        + [anywhere()] * len(behind),
        out_specs=[columns(tokens)] * peers,
        scratch_shapes=[pltpu.VMEM((length, COLS), BF16)],
        compiler_params=params(12),
        cost_estimate=LITTLE,
        name="channels",
    )


def others_kernel(
    heads,
    peers,
    first,
    last,
    at_ref,
    _,
    x_ref,
    dy_ref,
    carry_ref,
    through_ref,
    into_ref,
    out_of_ref,
    b_ref,
    c_ref,
    dt_ref,
    tot_ref,
    ui_ref,
    vi_ref,
    *rest,
):
    if last:
        added, rest = rest[:5], rest[5:]
    outs, (db_ref, dc_ref, u_ref, v_ref, tail_ref) = rest[:-5], rest[-5:]
    length = x_ref.shape[0]
    tokens = length // peers
    group = pl.program_id(0)

    @pl.when(group == 0)
    def _():
        db_ref[...] = jnp.zeros_like(db_ref)
        dc_ref[...] = jnp.zeros_like(dc_ref)
        u_ref[...] = jnp.zeros_like(u_ref)
        v_ref[...] = jnp.zeros_like(v_ref)

    select = selector(LANES, COLS, first + group * (COLS // WIDTH))
    for source, weight_ref, k, near_ref, sum_ref, head_ref in (
        (x_ref, into_ref, 1, b_ref, db_ref, v_ref),
        (dy_ref, out_of_ref, 0, c_ref, dc_ref, u_ref),
    ):
        weighted = source[...].astype(F32) * spread(weight_ref[...], select)
        far = stacked(carry_ref, k)
        sum_ref[...] += sum(dot_nt(term, far) for term in pieces(weighted, 2))
        head_ref[...] += gather(weighted * dot(near_ref[...], far), select)

    @pl.when(group == pl.num_programs(0) - 1)
    def _():
        inner_v, outer_v = vi_ref[...], v_ref[...]
        steps = (inner_v + outer_v) / dt_ref[...]
        rows = [ui_ref[at] for at in range(ui_ref.shape[0])]
        if first > 0:
            rows.insert(0, jnp.zeros((first, length), F32))
        rows.append(jnp.zeros((LANES - sum(part.shape[0] for part in rows), length), F32))
        net = jnp.concatenate(rows, axis=0).T + u_ref[...] - inner_v - outer_v
        row = lax.broadcasted_iota(jnp.int32, (length, length), 0)
        col = lax.broadcasted_iota(jnp.int32, (length, length), 1)
        upper = jnp.where(col >= row, 1.0, 0.0).astype(BF16)
        later = sum(dot(upper, term) for term in pieces(net, 3))
        whole_block = jnp.sum(outer_v, axis=0, keepdims=True)
        link = sum(through_ref[block].astype(F32) for block in range(through_ref.shape[0]))
        link = jnp.sum(link, axis=0, keepdims=True)
        logs = later + whole_block + jnp.exp2(tot_ref[0:1, :]) * link
        thin = steps + pltpu.roll(logs, heads, 1)
        if not last:
            outs[0][...] = thin
            outs[1][...] = db_ref[...]
            outs[2][...] = dc_ref[...]
        else:
            thin_ref, dbo_ref, dco_ref, dbi_ref, dci_ref = added
            tail_ref[:, 0:LANES] = (thin + thin_ref[...]).astype(BF16)
            tail_ref[:, LANES : 2 * LANES] = (db_ref[...] + dbo_ref[...] + dbi_ref[...]).astype(BF16)
            tail_ref[:, 2 * LANES :] = (dc_ref[...] + dco_ref[...] + dci_ref[...]).astype(BF16)
            for r in range(peers):
                start = pl.multiple_of((at_ref[0] ^ r) * tokens, tokens)
                outs[r][...] = tail_ref[pl.ds(start, tokens), :]


def others(heads, peers, first, at, x, dy, carry, into, out_of, b, c, dt, tot, ui, vi, added, behind):
    length, inner = x.shape
    tokens = length // peers
    tall = whole(length, LANES)
    last = len(added) > 0
    tall_shape = jax.ShapeDtypeStruct((length, LANES), F32)
    tail_shape = jax.ShapeDtypeStruct((tokens, 3 * LANES), BF16)
    return call(
        functools.partial(others_kernel, heads, peers, first, last),
        [tail_shape] * peers if last else [tall_shape] * 3,
        (at, behind, x, dy, carry, carry, into, out_of, b, c, dt, tot, ui, vi, *added,),
        grid=(inner // COLS,),
        in_specs=[
            smem(),
            anywhere(),
            columns(length),
            columns(length),
            by_columns(carry.shape),
            pl.BlockSpec(carry.shape[:2] + (LANES,), lambda g: (0, 0, inner // LANES)),
            tall,
            tall,
            tall,
            tall,
            tall,
            whole(8, LANES),
            whole(*ui.shape),
            tall,
        ]
        + [tall] * len(added),
        out_specs=[whole(tokens, 3 * LANES)] * peers if last else [tall] * 3,
        scratch_shapes=[pltpu.VMEM((length, LANES), F32)] * 4
        + [pltpu.VMEM((length, 3 * LANES), BF16)],
        compiler_params=params(20),
        cost_estimate=LITTLE,
        name="others",
    )


def finish_kernel(heads, peers, halves, at_ref, *rest):
    count = peers * halves
    sent, tails = rest[:count], rest[count : count + peers]
    dx_ref, steps_ref, logs_ref, db_ref, dc_ref, sems = rest[count + peers :]
    tokens, width = sent[0].shape
    copies = []
    for half in range(halves):
        for r in range(peers):
            start = pl.multiple_of(((at_ref[0] ^ r) * halves + half) * width, LANES)
            copies.append(
                pltpu.make_async_copy(
                    sent[half * peers + r], dx_ref.at[:, pl.ds(start, width)], sems.at[half, r]
                )
            )
    for copy in copies:
        copy.start()
    lane = lax.broadcasted_iota(jnp.int32, (tokens, LANES), 1)
    results = [jnp.zeros((tokens, LANES), F32) for _ in range(4)]
    for r in range(peers):
        source = at_ref[0] ^ r
        own = lane // heads == source
        thin = tails[r][:, 0:LANES].astype(F32)
        for k in range(2):
            shift = lax.rem((source - k) * heads + LANES, LANES)
            results[k] += jnp.where(own, pltpu.roll(thin, shift, 1), 0.0)
            results[2 + k] += tails[r][:, (k + 1) * LANES : (k + 2) * LANES].astype(F32)
    steps_ref[...] = results[0].astype(BF16)
    logs_ref[...] = results[1].astype(BF16)
    db_ref[...] = results[2]
    dc_ref[...] = results[3]
    for copy in copies:
        copy.wait()


def finish(heads, at, sent, tails):
    peers, halves = len(tails), len(sent)
    tokens, width = sent[0][0].shape
    thin = jax.ShapeDtypeStruct((tokens, LANES), BF16)
    wide = jax.ShapeDtypeStruct((tokens, LANES), F32)
    return call(
        functools.partial(finish_kernel, heads, peers, halves),
        (
            jax.ShapeDtypeStruct((tokens, width * halves * peers), BF16),
            thin,
            thin,
            wide,
            wide,
        ),
        (at, *[part for group in sent for part in group], *tails,),
        in_specs=[smem()] + [vmem()] * (peers * halves + peers),
        out_specs=(anywhere(), vmem(), vmem(), vmem(), vmem()),
        scratch_shapes=[pltpu.SemaphoreType.DMA((halves, peers))],
        compiler_params=one_step(8),
        cost_estimate=LITTLE,
        name="finish",
    )


HALVES = 2


def body(inputs, grad_out, steps, log_decay, input_map, output_map, skip_gain):
    blocks, peers = lax.axis_size("ctx"), lax.axis_size("head")
    inner = inputs.shape[1] // peers
    heads = steps.shape[1] // peers
    width = inner // HALVES
    at = lax.axis_index("head").astype(jnp.int32).reshape(1)

    riders = (steps, log_decay, input_map, output_map)
    packed = [pack(at, inputs, grad_out, riders, peers, 0, width, ())]
    for half in range(1, HALVES):
        behind = (packed[-1][0],)
        packed.append(pack(at, inputs, grad_out, (), peers, half * width, width, behind))
    parts = [swap(part) for part in packed]
    col_part, row_part, into, out_of, dt, tot, b, c, b_t, c_t = prepare(at, parts[0], heads)
    skip = jnp.broadcast_to(jnp.pad(skip_gain, (0, LANES - heads))[None], (8, LANES))

    rows, pairs, sums = [], [], []
    dbi = dci = None

    def begin(half, behind):
        first = half * heads // HALVES
        x, dy, added = states(
            at, into, out_of, b_t, c_t, tot, parts[half], blocks, width, first, behind
        )
        rows.append((x, dy))
        return added

    def within(half, dbi, dci):
        first = half * heads // HALVES
        dxi, ui, vi, dbi, dci = inside(*rows[half], b, c, col_part, row_part, first, dbi, dci)
        pairs.append((dxi, ui, vi))
        return dbi, dci

    reached = across(begin(0, ()))
    dbi, dci = within(0, None, None)
    reached = scan_blocks(reached, 0, pairs[0][0])
    carries = [across(reached)]
    reached_high = across(begin(1, (reached,)))
    dbi, dci = within(1, dbi, dci)

    def back(half, behind):
        first = half * heads // HALVES
        (x, dy), (dxi, ui, vi) = rows[half], pairs[half]
        return channels(peers, first, at, dy, dxi, carries[half], into, b, skip, behind)

    def remain(half, added, behind):
        first = half * heads // HALVES
        (x, dy), (dxi, ui, vi) = rows[half], pairs[half]
        return others(
            heads, peers, first, at, x, dy, carries[half], into, out_of, b, c, dt, tot, ui, vi,
            added, behind,
        )

    dx_low = back(0, pairs[1][:1])
    sent = [swap(dx_low)]
    added = remain(0, [], dx_low[0])
    carries.append(across(scan_blocks(reached_high, heads // HALVES, added[0])))
    dx_high = back(1, sent[0][1:])
    sent.append(swap(dx_high))
    tails = swap(remain(1, [*added, dbi, dci], dx_high[0]))
    return tuple(finish(heads, at, sent, tails))


def solution(mesh):
    rows = P(("ctx", "head"), None)
    return jax.shard_map(
        body,
        mesh=mesh,
        in_specs=(rows,) * 6 + (P("head"),),
        out_specs=(rows,) * 5,
        check_vma=False,
    )
```

```python
import functools

import jax
import jax.numpy as jnp
from jax import lax
from jax.experimental import pallas as pl
from jax.experimental.pallas import tpu as pltpu
from jax.sharding import PartitionSpec as P

F32 = jnp.float32
BF16 = jnp.bfloat16
LANES = 128
WIDTH = 64
COLS = 256
LOG2E = 1.4426950408889634
NT = (((1,), (1,)), ((), ()))
MIB = 1024 * 1024
LITTLE = pl.CostEstimate(flops=1000, bytes_accessed=1000, transcendentals=0)


def dot(a, b):
    return jnp.dot(a, b, preferred_element_type=F32)


def dot_nt(a, b):
    return lax.dot_general(a, b, NT, preferred_element_type=F32)


def pieces(a, count):
    terms = []
    for _ in range(count):
        term = a.astype(BF16)
        terms.append(term)
        a = a - term.astype(F32)
    return terms


def selector(rows, cols, first):
    row = lax.broadcasted_iota(jnp.int32, (rows, cols), 0)
    col = lax.broadcasted_iota(jnp.int32, (rows, cols), 1)
    return jnp.where((col // WIDTH) + first == row, 1.0, 0.0).astype(BF16)


def spread(a, select, count=2):
    return sum(dot(term, select) for term in pieces(a, count))


def gather(a, select, count=2):
    return sum(dot_nt(term, select) for term in pieces(a, count))


def params(mib):
    return pltpu.CompilerParams(dimension_semantics=("arbitrary",), vmem_limit_bytes=mib * MIB)


def whole(*shape):
    return pl.BlockSpec(shape, lambda *g: (0,) * len(shape))


def columns(rows, first=0):
    return pl.BlockSpec((rows, COLS), lambda g: (0, g + first // COLS))


def call(kernel, out_shape, operands, **options):
    operands = [
        a if a.dtype == jnp.int32 else pltpu.with_memory_space_constraint(a, pltpu.HBM)
        for a in operands
    ]
    out_shape = [pltpu.HBM(one.shape, one.dtype) for one in out_shape]
    return pl.pallas_call(kernel, out_shape=out_shape, **options)(*operands)


def smem():
    return pl.BlockSpec(memory_space=pltpu.SMEM)


def anywhere():
    return pl.BlockSpec(memory_space=pl.ANY)


def vmem():
    return pl.BlockSpec(memory_space=pltpu.VMEM)


def one_step(mib):
    return pltpu.CompilerParams(vmem_limit_bytes=mib * MIB)


def swap(parts, axis):
    peers = lax.axis_size(axis)
    got = [parts[0]] + [None] * (peers - 1)
    for r in range(peers - 1, 0, -1):
        got[r] = lax.ppermute(parts[r], axis, [(i, i ^ r) for i in range(peers)])
    return got


def trade(parts):
    return lax.all_to_all(parts, "head", split_axis=0, concat_axis=0, tiled=True)


def pack_kernel(peers, first, width, sources, out_ref, held, sems):
    inner = sources[0].shape[1] // peers
    parts, at = [], 0
    for k, source in enumerate(sources):
        size = width if k < 2 else source.shape[1]
        parts.append((source, at, size))
        at += size
    reads, writes = {}, []
    for peer in range(peers):
        for k, (source, at, size) in enumerate(parts):
            chosen = source.at[:, pl.ds(peer * inner + first, size)] if k < 2 else source
            reads[peer, k] = pltpu.make_async_copy(
                chosen, held.at[peer, :, pl.ds(at, size)], sems.at[0, peer, k]
            )
            reads[peer, k].start()
    for peer in range(peers):
        for k in range(len(parts)):
            reads[peer, k].wait()
        writes.append(pltpu.make_async_copy(held.at[peer], out_ref.at[peer], sems.at[1, peer, 0]))
        writes[-1].start()
    for write in writes:
        write.wait()


def pack(x, dy, riders, peers, first, width, behind):
    tokens = x.shape[0]
    full = 2 * width + sum(rider.shape[1] for rider in riders)
    count = 2 + len(riders)

    def kernel(*refs):
        pack_kernel(peers, first, width, refs[:count], *refs[-3:])

    return call(
        kernel,
        [jax.ShapeDtypeStruct((peers, tokens, full), BF16)],
        (x, dy, *riders, *behind),
        in_specs=[anywhere()] * (count + len(behind)),
        out_specs=[anywhere()],
        scratch_shapes=[
            pltpu.VMEM((peers, tokens, full), BF16),
            pltpu.SemaphoreType.DMA((2, peers, count)),
        ],
        compiler_params=one_step(10),
        cost_estimate=LITTLE,
        name="pack",
    )[0]


def prepare(heads, at_ref, small_ref, outs):
    col_ref, row_ref, in_ref, out_ref, dt_ref, tot_ref, b_ref, c_ref, bt_ref, ct_ref = outs
    length = small_ref.shape[0]
    shift = lax.rem(LANES - at_ref[0] * heads, LANES)
    steps = pltpu.roll(small_ref[:, 0:LANES].astype(F32), shift, 1)
    logs = pltpu.roll(small_ref[:, LANES : 2 * LANES].astype(F32), shift, 1)
    row = lax.broadcasted_iota(jnp.int32, (length, length), 0)
    col = lax.broadcasted_iota(jnp.int32, (length, length), 1)
    lower = jnp.where(row >= col, 1.0, 0.0).astype(BF16)
    cum = dot(lower, logs.astype(BF16)) * LOG2E
    total = cum[length - 1 : length, :]
    col_ref[...] = cum - jnp.log(steps) * LOG2E
    turned = cum.T
    per_group = row_ref.shape[1]
    for group in range(row_ref.shape[0]):
        row_ref[group] = turned[group * per_group : (group + 1) * per_group, :]
    in_ref[...] = jnp.exp2(total - cum) * steps
    out_ref[...] = jnp.exp2(cum)
    dt_ref[...] = steps
    tot_ref[...] = jnp.broadcast_to(total, tot_ref.shape)
    b = small_ref[:, 2 * LANES : 3 * LANES]
    c = small_ref[:, 3 * LANES : 4 * LANES]
    b_ref[...] = b
    c_ref[...] = c
    bt_ref[...] = b.astype(F32).T.astype(BF16)
    ct_ref[...] = c.astype(F32).T.astype(BF16)


def prepared(length, heads):
    tall = jax.ShapeDtypeStruct((length, LANES), F32)
    thin = jax.ShapeDtypeStruct((length, LANES), BF16)
    flat = jax.ShapeDtypeStruct((LANES, length), BF16)
    groups = jax.ShapeDtypeStruct((heads * WIDTH // COLS, COLS // WIDTH, length), F32)
    total = jax.ShapeDtypeStruct((8, LANES), F32)
    return [tall, groups, tall, tall, tall, total, thin, thin, flat, flat]


def add_up(first, weight_refs, map_refs, tot_ref, at_ref, rows_ref, sum_refs, made_ref):
    blocks, rows, inner = made_ref.shape
    rows, inner = rows // 2, inner - LANES
    row = lax.broadcasted_iota(jnp.int32, (2 * rows, LANES), 0)
    total = jnp.zeros((2 * rows, LANES), F32)
    for k, term in enumerate(pieces(tot_ref[0:1, :], 3)):
        total = jnp.where(row == k, term.astype(F32), total)
    for block in range(blocks):
        made_ref[block, :, inner:] = total.astype(BF16)
    weights = [pieces(ref[...], 2) for ref in weight_refs]
    for group in range(inner // COLS):
        here = slice(group * COLS, (group + 1) * COLS)
        select = selector(LANES, COLS, first + group * (COLS // WIDTH))
        for k in range(2):
            there = slice(k * inner + group * COLS, k * inner + (group + 1) * COLS)
            weight = sum(dot(term, select) for term in weights[k])
            weighted = rows_ref[:, there].astype(F32) * weight
            added = sum(dot(map_refs[k][...], term) for term in pieces(weighted, 2)).astype(BF16)
            for block in range(blocks):
                made_ref[block, k * rows : (k + 1) * rows, here] = added[
                    block * rows : (block + 1) * rows, :
                ]
    for r in range(blocks):
        sum_refs[r][...] = made_ref[at_ref[0] ^ r]


def opening_kernel(heads, blocks, head_ref, at_ref, rows_ref, _, *rest):
    outs, sum_refs, made_ref = rest[:10], rest[10:-1], rest[-1]
    width = rows_ref.shape[1] - 4 * LANES
    prepare(heads, head_ref, rows_ref.at[:, width:], outs)
    _, _, in_ref, out_ref, _, tot_ref, _, _, bt_ref, ct_ref = outs
    add_up(0, (in_ref, out_ref), (bt_ref, ct_ref), tot_ref, at_ref, rows_ref, sum_refs, made_ref)


def state_shape(blocks, inner):
    return 2 * LANES // blocks, inner + LANES


def opening(head, at, rows, heads, blocks, inner, behind):
    shape = state_shape(blocks, inner)
    sums = [jax.ShapeDtypeStruct(shape, BF16)] * blocks
    got = call(
        functools.partial(opening_kernel, heads, blocks),
        prepared(rows.shape[0], heads) + sums,
        (head, at, rows, behind),
        in_specs=[smem(), smem(), vmem(), anywhere()],
        scratch_shapes=[pltpu.VMEM((blocks,) + shape, BF16)],
        compiler_params=one_step(20),
        cost_estimate=LITTLE,
        name="opening",
    )
    return got[:10], got[10:]


def states_kernel(first, at_ref, in_ref, out_ref, bt_ref, ct_ref, tot_ref, rows_ref, _, *rest):
    sum_refs, made_ref = rest[:-1], rest[-1]
    weights, maps = (in_ref, out_ref), (bt_ref, ct_ref)
    add_up(first, weights, maps, tot_ref, at_ref, rows_ref, sum_refs, made_ref)


def states(at, into, out_of, b_t, c_t, tot, rows, blocks, inner, first, behind):
    shape = state_shape(blocks, inner)
    return call(
        functools.partial(states_kernel, first),
        [jax.ShapeDtypeStruct(shape, BF16)] * blocks,
        (at, into, out_of, b_t, c_t, tot, rows, behind),
        in_specs=[smem()] + [vmem()] * 6 + [anywhere()],
        scratch_shapes=[pltpu.VMEM((blocks,) + shape, BF16)],
        compiler_params=one_step(16),
        cost_estimate=LITTLE,
        name="states",
    )


def scan_kernel(first, blocks, at_ref, *rest):
    parts, outs, (in_ref, out_ref, kept_ref) = rest[:blocks], rest[-3 - blocks : -3], rest[-3:]
    _, rows, inner = in_ref.shape
    rows, inner = rows // 2, inner - LANES
    for r in range(blocks):
        in_ref[at_ref[0] ^ r] = parts[r][...]
    select = selector(LANES, inner, first)
    totals = [
        jnp.sum(in_ref[block, :, inner:].astype(F32), axis=0, keepdims=True)
        for block in range(blocks)
    ]
    decay = spread(jnp.exp2(jnp.concatenate(totals, axis=0)), select, 3)
    through = []
    for k, order in enumerate((range(blocks), range(blocks - 1, -1, -1))):
        here = slice(k * rows, (k + 1) * rows)
        running = jnp.zeros((rows, inner), F32)
        for block in order:
            out_ref[block, here, 0:inner] = running.astype(BF16)
            if k == 0:
                kept_ref[block] = running
            else:
                through.append(jnp.sum(kept_ref[block] * running, axis=0, keepdims=True))
            step = decay[block : block + 1, :]
            running = step * running + in_ref[block, here, 0:inner].astype(F32)
    link = gather(jnp.concatenate(through[::-1], axis=0), select, 3)
    high, low = (term.astype(F32) for term in pieces(link, 2))
    row = lax.broadcasted_iota(jnp.int32, (2 * rows, LANES), 0)
    for block in range(blocks):
        here = slice(block, block + 1)
        both = jnp.where(row == 0, high[here, :], jnp.where(row == 1, low[here, :], 0.0))
        out_ref[block, :, inner:] = both.astype(BF16)
    for r in range(blocks):
        outs[r][...] = out_ref[at_ref[0] ^ r]


def scan_blocks(at, parts, first, behind):
    blocks = len(parts)
    rows, inner = parts[0].shape
    held = pltpu.VMEM((blocks, rows, inner), BF16)
    return call(
        functools.partial(scan_kernel, first, blocks),
        [jax.ShapeDtypeStruct((rows, inner), BF16)] * blocks,
        (at, *parts, *behind),
        scratch_shapes=[held, held, pltpu.VMEM((blocks, rows // 2, inner - LANES), F32)],
        in_specs=[smem()] + [vmem()] * blocks + [anywhere()] * len(behind),
        compiler_params=one_step(8),
        cost_estimate=LITTLE,
        name="scan_blocks",
    )


def ordered(at_ref, parts, held_ref):
    for r, part in enumerate(parts):
        held_ref[at_ref[0] ^ r] = part[...]


def stacked(ref, k):
    blocks, rows, _ = ref.shape
    rows //= 2
    return jnp.concatenate(
        [ref[block, k * rows : (k + 1) * rows, :] for block in range(blocks)], axis=0
    )


def inside_kernel(first, x_ref, dy_ref, b_ref, c_ref, col_ref, row_ref, *rest):
    added, (dx_ref, u_ref, v_ref, db_ref, dc_ref, s_ref, ds_ref) = rest[:-7], rest[-7:]
    length = x_ref.shape[0]
    tiles = length // LANES
    heads = COLS // WIDTH
    group = pl.program_id(0)
    from_k = lax.broadcasted_iota(jnp.int32, (length, length), 0)
    to_q = lax.broadcasted_iota(jnp.int32, (length, length), 1)

    @pl.when(group == 0)
    def _():
        s_ref[...] = jnp.where(to_q >= from_k, dot_nt(b_ref[...], c_ref[...]), 0.0)
        ds_ref[...] = jnp.zeros_like(ds_ref)
        v_ref[...] = jnp.zeros_like(v_ref)

    turned = pltpu.roll(col_ref[...], lax.rem(LANES - first - group * heads, LANES), 1)
    lane = lax.broadcasted_iota(jnp.int32, (LANES, LANES), 1)
    for j in range(tiles):
        low = j * LANES
        here = slice(low, low + LANES)
        for pair in range(heads // 2):
            across = slice(pair * LANES, (pair + 1) * LANES)
            xs = x_ref[here, across]
            dys = dy_ref[low:, across]
            side = lax.broadcasted_iota(jnp.int32, dys.shape, 1) // WIDTH
            total = None
            for half in range(2):
                local = pair * 2 + half
                head = first + group * heads + local
                own_x = jnp.where(lane // WIDTH == half, xs, jnp.zeros_like(xs))
                own_dy = jnp.where(side == half, dys, jnp.zeros_like(dys))
                products = dot_nt(own_x, dys)
                behind = turned[here, local : local + 1]
                kept = []
                v_sum = None
                for i in range(j, tiles):
                    there = slice(i * LANES, (i + 1) * LANES)
                    ahead = row_ref[0, local : local + 1, there]
                    decay = jnp.exp2(jnp.minimum(ahead - behind, 64.0))
                    product = products[:, (i - j) * LANES : (i - j + 1) * LANES]
                    score = s_ref[here, there] * decay
                    kept.append(score.astype(BF16))
                    ds_ref[here, there] += decay * product
                    both = score * product
                    v_sum = both if v_sum is None else v_sum + both
                    u_sum = jnp.sum(both, axis=0, keepdims=True)
                    if j > 0:
                        u_sum += u_ref[0, local : local + 1, there]
                    u_ref[0, local : local + 1, there] = u_sum
                v_col = jnp.sum(v_sum, axis=1, keepdims=True)
                v_ref[here, :] = jnp.where(lane == head, v_col, v_ref[here, :])
                scores = jnp.concatenate(kept, axis=1) if len(kept) > 1 else kept[0]
                part = dot(scores, own_dy)
                total = part if total is None else total + part
            dx_ref[here, across] = total

    @pl.when(group == pl.num_programs(0) - 1)
    def _():
        grads = jnp.where(to_q >= from_k, ds_ref[...], 0.0)
        db = sum(dot(term, c_ref[...]) for term in pieces(grads, 2))
        dc = sum(dot(term, b_ref[...]) for term in pieces(grads.T, 2))
        db_ref[...] = db + added[0][...] if added else db
        dc_ref[...] = dc + added[1][...] if added else dc


def inside(rows, inner, b, c, col_part, row_part, first, *added):
    added = [a for a in added if a is not None]
    length = rows.shape[0]
    tall = jax.ShapeDtypeStruct((length, LANES), F32)
    pairs = length * length * inner
    offset = first * WIDTH // COLS
    by_group = pl.BlockSpec((1,) + row_part.shape[1:], lambda g: (g + offset, 0, 0))
    own_group = pl.BlockSpec((1,) + row_part.shape[1:], lambda g: (g, 0, 0))
    return call(
        functools.partial(inside_kernel, first),
        (
            jax.ShapeDtypeStruct((length, inner), F32),
            jax.ShapeDtypeStruct((inner // COLS,) + row_part.shape[1:], F32),
            tall,
            tall,
            tall,
        ),
        (rows, rows, b, c, col_part, row_part, *added),
        grid=(inner // COLS,),
        in_specs=[
            columns(length),
            columns(length, inner),
            whole(length, LANES),
            whole(length, LANES),
            whole(length, LANES),
            by_group,
        ]
        + [whole(length, LANES)] * len(added),
        out_specs=(
            columns(length),
            own_group,
            whole(length, LANES),
            whole(length, LANES),
            whole(length, LANES),
        ),
        scratch_shapes=[pltpu.VMEM((length, length), F32), pltpu.VMEM((length, length), F32)],
        compiler_params=params(20),
        cost_estimate=LITTLE,
        name="inside",
    )


def by_columns(shape):
    return pl.BlockSpec((shape[0], COLS), lambda g: (0, g))


def channels_kernel(blocks, first, at_ref, dy_ref, dxi_ref, weight_ref, b_ref, skip_ref, *rest):
    carry_refs, (dx_ref, held_ref) = rest[:blocks], rest[-2:]
    ordered(at_ref, carry_refs, held_ref)
    select = selector(LANES, COLS, first + pl.program_id(0) * (COLS // WIDTH))
    carried = spread(weight_ref[...], select) * dot(b_ref[...], stacked(held_ref, 1))
    gain = spread(skip_ref[...], select, 3)[0:1, :]
    dx_ref[...] = (dxi_ref[...] + carried + gain * dy_ref[...].astype(F32)).astype(BF16)


def channels(first, at, rows, dxi, carry, weight, b, skip, behind):
    length, inner = dxi.shape
    tall = whole(length, LANES)
    blocks = len(carry)
    return call(
        functools.partial(channels_kernel, blocks, first),
        [jax.ShapeDtypeStruct((length, inner), BF16)],
        (at, rows, dxi, weight, b, skip, *carry, *behind),
        grid=(inner // COLS,),
        in_specs=[smem(), columns(length, inner), columns(length), tall, tall, whole(8, LANES)]
        + [by_columns(carry[0].shape)] * blocks
        + [anywhere()] * len(behind),
        out_specs=[columns(length)],
        scratch_shapes=[pltpu.VMEM((blocks, carry[0].shape[0], COLS), BF16)],
        compiler_params=params(12),
        cost_estimate=LITTLE,
        name="channels",
    )[0]


def others_kernel(
    heads,
    peers,
    blocks,
    first,
    last,
    head_ref,
    at_ref,
    _,
    x_ref,
    dy_ref,
    into_ref,
    out_of_ref,
    b_ref,
    c_ref,
    dt_ref,
    tot_ref,
    ui_ref,
    vi_ref,
    *rest,
):
    carry_refs, through_refs, rest = rest[:blocks], rest[blocks : 2 * blocks], rest[2 * blocks :]
    if last:
        added, rest = rest[:5], rest[5:]
    outs, (db_ref, dc_ref, u_ref, v_ref, tail_ref, held_ref) = rest[:-6], rest[-6:]
    length = x_ref.shape[0]
    tokens = length // peers
    group = pl.program_id(0)

    @pl.when(group == 0)
    def _():
        db_ref[...] = jnp.zeros_like(db_ref)
        dc_ref[...] = jnp.zeros_like(dc_ref)
        u_ref[...] = jnp.zeros_like(u_ref)
        v_ref[...] = jnp.zeros_like(v_ref)

    ordered(at_ref, carry_refs, held_ref)
    select = selector(LANES, COLS, first + group * (COLS // WIDTH))
    for source, weight_ref, k, near_ref, sum_ref, each_ref in (
        (x_ref, into_ref, 1, b_ref, db_ref, v_ref),
        (dy_ref, out_of_ref, 0, c_ref, dc_ref, u_ref),
    ):
        weighted = source[...].astype(F32) * spread(weight_ref[...], select)
        far = stacked(held_ref, k)
        sum_ref[...] += sum(dot_nt(term, far) for term in pieces(weighted, 2))
        each_ref[...] += gather(weighted * dot(near_ref[...], far), select)

    @pl.when(group == pl.num_programs(0) - 1)
    def _():
        inner_v, outer_v = vi_ref[...], v_ref[...]
        steps = (inner_v + outer_v) / dt_ref[...]
        rows = [ui_ref[at] for at in range(ui_ref.shape[0])]
        if first > 0:
            rows.insert(0, jnp.zeros((first, length), F32))
        rows.append(jnp.zeros((LANES - sum(part.shape[0] for part in rows), length), F32))
        net = jnp.concatenate(rows, axis=0).T + u_ref[...] - inner_v - outer_v
        row = lax.broadcasted_iota(jnp.int32, (length, length), 0)
        col = lax.broadcasted_iota(jnp.int32, (length, length), 1)
        upper = jnp.where(col >= row, 1.0, 0.0).astype(BF16)
        later = sum(dot(upper, term) for term in pieces(net, 3))
        whole_block = jnp.sum(outer_v, axis=0, keepdims=True)
        link = sum(ref[...].astype(F32) for ref in through_refs)
        link = jnp.sum(link, axis=0, keepdims=True)
        logs = later + whole_block + jnp.exp2(tot_ref[0:1, :]) * link
        thin = steps + pltpu.roll(logs, heads, 1)
        if not last:
            outs[0][...] = thin
            outs[1][...] = db_ref[...]
            outs[2][...] = dc_ref[...]
        else:
            thin_ref, dbo_ref, dco_ref, dbi_ref, dci_ref = added
            tail_ref[:, 0:LANES] = (thin + thin_ref[...]).astype(BF16)
            tail_ref[:, LANES : 2 * LANES] = (db_ref[...] + dbo_ref[...] + dbi_ref[...]).astype(BF16)
            tail_ref[:, 2 * LANES :] = (dc_ref[...] + dco_ref[...] + dci_ref[...]).astype(BF16)
            for r in range(peers):
                start = pl.multiple_of((head_ref[0] ^ r) * tokens, tokens)
                outs[r][...] = tail_ref[pl.ds(start, tokens), :]


def others(
    heads, peers, first, head, at, rows, inner, carry, into, out_of, b, c, dt, tot, ui, vi, added,
    behind,
):
    length = rows.shape[0]
    tokens = length // peers
    tall = whole(length, LANES)
    last = len(added) > 0
    blocks = len(carry)
    tall_shape = jax.ShapeDtypeStruct((length, LANES), F32)
    tail_shape = jax.ShapeDtypeStruct((tokens, 3 * LANES), BF16)
    high = carry[0].shape[0]
    return call(
        functools.partial(others_kernel, heads, peers, blocks, first, last),
        [tail_shape] * peers if last else [tall_shape] * 3,
        (head, at, behind, rows, rows, into, out_of, b, c, dt, tot, ui, vi, *carry, *carry, *added),
        grid=(inner // COLS,),
        in_specs=[smem(), smem(), anywhere(), columns(length), columns(length, inner)]
        + [tall] * 5
        + [whole(8, LANES), whole(*ui.shape), tall]
        + [by_columns(carry[0].shape)] * blocks
        + [pl.BlockSpec((high, LANES), lambda g: (0, inner // LANES))] * blocks
        + [tall] * len(added),
        out_specs=[whole(tokens, 3 * LANES)] * peers if last else [tall] * 3,
        scratch_shapes=[pltpu.VMEM((length, LANES), F32)] * 4
        + [pltpu.VMEM((length, 3 * LANES), BF16), pltpu.VMEM((blocks, high, COLS), BF16)],
        compiler_params=params(20),
        cost_estimate=LITTLE,
        name="others",
    )


def finish_kernel(heads, halves, at_ref, *rest):
    sent, rest = rest[:halves], rest[halves:]
    tails, (dx_ref, steps_ref, logs_ref, db_ref, dc_ref, held_ref, sems) = rest[:-7], rest[-7:]
    peers, tokens, width = sent[0].shape
    reads, writes = [], []
    for half in range(halves):
        reads.append(pltpu.make_async_copy(sent[half], held_ref.at[half], sems.at[0, half, 0]))
        reads[-1].start()
    for half in range(halves):
        reads[half].wait()
        for peer in range(peers):
            there = pl.ds((peer * halves + half) * width, width)
            writes.append(
                pltpu.make_async_copy(
                    held_ref.at[half, peer], dx_ref.at[:, there], sems.at[1, half, peer]
                )
            )
            writes[-1].start()
    lane = lax.broadcasted_iota(jnp.int32, (tokens, LANES), 1)
    results = [jnp.zeros((tokens, LANES), F32) for _ in range(4)]
    for r in range(peers):
        source = at_ref[0] ^ r
        own = lane // heads == source
        thin = tails[r][:, 0:LANES].astype(F32)
        for k in range(2):
            shift = lax.rem((source - k) * heads + LANES, LANES)
            results[k] += jnp.where(own, pltpu.roll(thin, shift, 1), 0.0)
            results[2 + k] += tails[r][:, (k + 1) * LANES : (k + 2) * LANES].astype(F32)
    steps_ref[...] = results[0].astype(BF16)
    logs_ref[...] = results[1].astype(BF16)
    db_ref[...] = results[2]
    dc_ref[...] = results[3]
    for write in writes:
        write.wait()


def finish(heads, at, sent, tails):
    halves = len(sent)
    peers, tokens, width = sent[0].shape
    thin = jax.ShapeDtypeStruct((tokens, LANES), BF16)
    wide = jax.ShapeDtypeStruct((tokens, LANES), F32)
    return call(
        functools.partial(finish_kernel, heads, halves),
        [jax.ShapeDtypeStruct((tokens, width * halves * peers), BF16), thin, thin, wide, wide],
        (at, *sent, *tails),
        in_specs=[smem()] + [anywhere()] * halves + [vmem()] * peers,
        out_specs=[anywhere(), vmem(), vmem(), vmem(), vmem()],
        scratch_shapes=[
            pltpu.VMEM((halves, peers, tokens, width), BF16),
            pltpu.SemaphoreType.DMA((2, halves, peers)),
        ],
        compiler_params=one_step(8),
        cost_estimate=LITTLE,
        name="finish",
    )


HALVES = 2


def body(inputs, grad_out, steps, log_decay, input_map, output_map, skip_gain):
    blocks, peers = lax.axis_size("ctx"), lax.axis_size("head")
    inner = inputs.shape[1] // peers
    heads = steps.shape[1] // peers
    width = inner // HALVES
    length = inputs.shape[0] * peers
    head = lax.axis_index("head").astype(jnp.int32).reshape(1)
    at = lax.axis_index("ctx").astype(jnp.int32).reshape(1)

    riders = (steps, log_decay, input_map, output_map)
    low = pack(inputs, grad_out, riders, peers, 0, width, ())
    high = pack(inputs, grad_out, (), peers, width, width, (low,))
    rows = [trade(part).reshape(length, part.shape[2]) for part in (low, high)]
    scalars, sums = opening(head, at, rows[0], heads, blocks, width, high)
    col_part, row_part, into, out_of, dt, tot, b, c, b_t, c_t = scalars
    skip = jnp.broadcast_to(jnp.pad(skip_gain, (0, LANES - heads))[None], (8, LANES))
    half = heads // HALVES

    reached = swap(sums, "ctx")
    dxi, ui, vi, dbi, dci = inside(rows[0], width, b, c, col_part, row_part, 0)
    begun = scan_blocks(at, reached, 0, (dxi, rows[1]))
    carry = swap(begun, "ctx")
    sums = states(at, into, out_of, b_t, c_t, tot, rows[1], blocks, width, half, begun[0])
    reached = swap(sums, "ctx")
    dxi_high, ui_high, vi_high, dbi, dci = inside(
        rows[1], width, b, c, col_part, row_part, half, dbi, dci
    )

    def back(dx):
        return trade(dx.reshape(peers, length // peers, width))

    dx_low = channels(0, at, rows[0], dxi, carry, into, b, skip, (dxi_high,))
    sent_low = back(dx_low)
    added = others(
        heads, peers, 0, head, at, rows[0], width, carry, into, out_of, b, c, dt, tot, ui, vi, [],
        dx_low,
    )
    begun = scan_blocks(at, reached, half, (added[0],))
    carry = swap(begun, "ctx")
    dx_high = channels(half, at, rows[1], dxi_high, carry, into, b, skip, (sent_low,))
    sent_high = back(dx_high)
    tails = others(
        heads, peers, half, head, at, rows[1], width, carry, into, out_of, b, c, dt, tot, ui_high,
        vi_high, [*added, dbi, dci], dx_high,
    )
    tails = swap(tails, "head")
    return tuple(finish(heads, head, (sent_low, sent_high), tails))


def solution(mesh):
    rows = P(("ctx", "head"), None)
    return jax.shard_map(
        body,
        mesh=mesh,
        in_specs=(rows,) * 6 + (P("head"),),
        out_specs=(rows,) * 5,
        check_vma=False,
    )
```

```python
import functools

import jax
import jax.numpy as jnp
from jax import lax
from jax.experimental import pallas as pl
from jax.experimental.pallas import tpu as pltpu
from jax.sharding import PartitionSpec as P

F32 = jnp.float32
BF16 = jnp.bfloat16
LANES = 128
WIDTH = 64
COLS = 256
LOG2E = 1.4426950408889634
NT = (((1,), (1,)), ((), ()))
MIB = 1024 * 1024
LITTLE = pl.CostEstimate(flops=1000, bytes_accessed=1000, transcendentals=0)


def dot(a, b):
    return jnp.dot(a, b, preferred_element_type=F32)


def dot_nt(a, b):
    return lax.dot_general(a, b, NT, preferred_element_type=F32)


def pieces(a, count):
    terms = []
    for _ in range(count):
        term = a.astype(BF16)
        terms.append(term)
        a = a - term.astype(F32)
    return terms


def selector(rows, cols, first):
    row = lax.broadcasted_iota(jnp.int32, (rows, cols), 0)
    col = lax.broadcasted_iota(jnp.int32, (rows, cols), 1)
    return jnp.where((col // WIDTH) + first == row, 1.0, 0.0).astype(BF16)


def spread(a, select, count=2):
    return sum(dot(term, select) for term in pieces(a, count))


def gather(a, select, count=2):
    return sum(dot_nt(term, select) for term in pieces(a, count))


def params(mib):
    return pltpu.CompilerParams(dimension_semantics=("arbitrary",), vmem_limit_bytes=mib * MIB)


def whole(*shape):
    return pl.BlockSpec(shape, lambda *g: (0,) * len(shape))


def columns(rows, first=0):
    return pl.BlockSpec((rows, COLS), lambda g: (0, g + first // COLS))


def call(kernel, out_shape, operands, **options):
    operands = [
        a if a.dtype == jnp.int32 else pltpu.with_memory_space_constraint(a, pltpu.HBM)
        for a in operands
    ]
    out_shape = [pltpu.HBM(one.shape, one.dtype) for one in out_shape]
    return pl.pallas_call(kernel, out_shape=out_shape, **options)(*operands)


def smem():
    return pl.BlockSpec(memory_space=pltpu.SMEM)


def anywhere():
    return pl.BlockSpec(memory_space=pl.ANY)


def vmem():
    return pl.BlockSpec(memory_space=pltpu.VMEM)


def one_step(mib):
    return pltpu.CompilerParams(vmem_limit_bytes=mib * MIB)


def swap(parts):
    peers = lax.axis_size("head")
    got = [parts[0]] + [None] * (peers - 1)
    for r in range(peers - 1, 0, -1):
        got[r] = lax.ppermute(parts[r], "head", [(i, i ^ r) for i in range(peers)])
    return got


def pack_kernel(peers, first, width, at_ref, *rest):
    sources, outs, (held, sems) = rest[: -peers - 2], rest[-peers - 2 : -2], rest[-2:]
    inner = sources[0].shape[1] // peers
    order = list(range(peers - 1, -1, -1))
    parts, at = [], 0
    for k, source in enumerate(sources):
        size = width if k < 2 else source.shape[1]
        parts.append((source, at, size))
        at += size
    reads = {}
    for r in order:
        start = pl.multiple_of((at_ref[0] ^ r) * inner + first, LANES)
        for k, (source, at, size) in enumerate(parts):
            chosen = source.at[:, pl.ds(start, size)] if k < 2 else source
            reads[r, k] = pltpu.make_async_copy(
                chosen, held.at[r, :, pl.ds(at, size)], sems.at[0, r, k]
            )
            reads[r, k].start()
    writes = []
    for r in order:
        for k in range(len(parts)):
            reads[r, k].wait()
        writes.append(pltpu.make_async_copy(held.at[r], outs[r], sems.at[1, r, 0]))
        writes[-1].start()
    for write in writes:
        write.wait()


def pack(at, x, dy, riders, peers, first, width, behind):
    tokens = x.shape[0]
    full = 2 * width + sum(rider.shape[1] for rider in riders)
    count = 2 + len(riders)

    def kernel(at_ref, *rest):
        pack_kernel(peers, first, width, at_ref, *rest[:count], *rest[count + len(behind) :])

    return call(
        kernel,
        [jax.ShapeDtypeStruct((tokens, full), BF16)] * peers,
        (at, x, dy, *riders, *behind),
        in_specs=[smem()] + [anywhere()] * (count + len(behind)),
        out_specs=[anywhere()] * peers,
        scratch_shapes=[
            pltpu.VMEM((peers, tokens, full), BF16),
            pltpu.SemaphoreType.DMA((2, peers, count)),
        ],
        compiler_params=one_step(10),
        cost_estimate=LITTLE,
        name="pack",
    )


def prepare(heads, at_ref, small_ref, outs):
    col_ref, row_ref, in_ref, out_ref, dt_ref, tot_ref, b_ref, c_ref, bt_ref, ct_ref = outs
    length = small_ref.shape[0]
    shift = lax.rem(LANES - at_ref[0] * heads, LANES)
    steps = pltpu.roll(small_ref[:, 0:LANES].astype(F32), shift, 1)
    logs = pltpu.roll(small_ref[:, LANES : 2 * LANES].astype(F32), shift, 1)
    row = lax.broadcasted_iota(jnp.int32, (length, length), 0)
    col = lax.broadcasted_iota(jnp.int32, (length, length), 1)
    lower = jnp.where(row >= col, 1.0, 0.0).astype(BF16)
    cum = dot(lower, logs.astype(BF16)) * LOG2E
    total = cum[length - 1 : length, :]
    col_ref[...] = cum - jnp.log(steps) * LOG2E
    turned = cum.T
    per_group = row_ref.shape[1]
    for group in range(row_ref.shape[0]):
        row_ref[group] = turned[group * per_group : (group + 1) * per_group, :]
    in_ref[...] = jnp.exp2(total - cum) * steps
    out_ref[...] = jnp.exp2(cum)
    dt_ref[...] = steps
    tot_ref[...] = jnp.broadcast_to(total, tot_ref.shape)
    b = small_ref[:, 2 * LANES : 3 * LANES]
    c = small_ref[:, 3 * LANES : 4 * LANES]
    b_ref[...] = b
    c_ref[...] = c
    bt_ref[...] = b.astype(F32).T.astype(BF16)
    ct_ref[...] = c.astype(F32).T.astype(BF16)


def prepared(length, heads):
    tall = jax.ShapeDtypeStruct((length, LANES), F32)
    thin = jax.ShapeDtypeStruct((length, LANES), BF16)
    flat = jax.ShapeDtypeStruct((LANES, length), BF16)
    groups = jax.ShapeDtypeStruct((heads * WIDTH // COLS, COLS // WIDTH, length), F32)
    total = jax.ShapeDtypeStruct((8, LANES), F32)
    return [tall, groups, tall, tall, tall, total, thin, thin, flat, flat]


def put_in_order(head_ref, parts, rows_ref, sems):
    tokens = parts[0].shape[0]
    copies = []
    for r, part in enumerate(parts):
        start = pl.multiple_of((head_ref[0] ^ r) * tokens, tokens)
        copies.append(pltpu.make_async_copy(part, rows_ref.at[pl.ds(start, tokens), :], sems.at[r]))
        copies[-1].start()
    for copy in copies:
        copy.wait()


def add_up(first, weight_refs, map_refs, tot_ref, rows_ref, sum_ref):
    blocks, rows, inner = sum_ref.shape
    rows, inner = rows // 2, inner - LANES
    row = lax.broadcasted_iota(jnp.int32, (2 * rows, LANES), 0)
    total = jnp.zeros((2 * rows, LANES), F32)
    for k, term in enumerate(pieces(tot_ref[0:1, :], 3)):
        total = jnp.where(row == k, term.astype(F32), total)
    for block in range(blocks):
        sum_ref[block, :, inner:] = total.astype(BF16)
    weights = [pieces(ref[...], 2) for ref in weight_refs]
    for group in range(inner // COLS):
        here = slice(group * COLS, (group + 1) * COLS)
        select = selector(LANES, COLS, first + group * (COLS // WIDTH))
        for k in range(2):
            there = slice(k * inner + group * COLS, k * inner + (group + 1) * COLS)
            weight = sum(dot(term, select) for term in weights[k])
            weighted = rows_ref[:, there].astype(F32) * weight
            added = sum(dot(map_refs[k][...], term) for term in pieces(weighted, 2)).astype(BF16)
            for block in range(blocks):
                sum_ref[block, k * rows : (k + 1) * rows, here] = added[
                    block * rows : (block + 1) * rows, :
                ]


def opening_kernel(heads, peers, head_ref, *rest):
    parts, (rows_ref, sum_ref, sems) = rest[:peers], rest[-3:]
    outs = rest[peers : peers + 10]
    width = rows_ref.shape[1] - 4 * LANES
    put_in_order(head_ref, parts, rows_ref, sems)
    prepare(heads, head_ref, rows_ref.at[:, width:], outs)
    _, _, in_ref, out_ref, _, tot_ref, _, _, bt_ref, ct_ref = outs
    add_up(0, (in_ref, out_ref), (bt_ref, ct_ref), tot_ref, rows_ref, sum_ref)


def sum_shape(blocks, inner):
    return jax.ShapeDtypeStruct((blocks, 2 * LANES // blocks, inner + LANES), BF16)


def opening(head, parts, heads, blocks, inner):
    peers = len(parts)
    tokens, full = parts[0].shape
    rows = jax.ShapeDtypeStruct((tokens * peers, full), BF16)
    got = call(
        functools.partial(opening_kernel, heads, peers),
        prepared(tokens * peers, heads) + [rows, sum_shape(blocks, inner)],
        (head, *parts),
        in_specs=[smem()] + [anywhere()] * peers,
        scratch_shapes=[pltpu.SemaphoreType.DMA((peers,))],
        compiler_params=one_step(20),
        cost_estimate=LITTLE,
        name="opening",
    )
    return got[:10], got[10], got[11]


def states_kernel(first, peers, head_ref, in_ref, out_ref, bt_ref, ct_ref, tot_ref, *rest):
    parts, (rows_ref, sum_ref, sems) = rest[:peers], rest[-3:]
    put_in_order(head_ref, parts, rows_ref, sems)
    add_up(first, (in_ref, out_ref), (bt_ref, ct_ref), tot_ref, rows_ref, sum_ref)


def states(head, into, out_of, b_t, c_t, tot, parts, blocks, inner, first, behind):
    peers = len(parts)
    tokens, full = parts[0].shape
    rows = jax.ShapeDtypeStruct((tokens * peers, full), BF16)
    return call(
        functools.partial(states_kernel, first, peers),
        [rows, sum_shape(blocks, inner)],
        (head, into, out_of, b_t, c_t, tot, *parts, *behind),
        in_specs=[smem()] + [vmem()] * 5 + [anywhere()] * (peers + len(behind)),
        scratch_shapes=[pltpu.SemaphoreType.DMA((peers,))],
        compiler_params=one_step(16),
        cost_estimate=LITTLE,
        name="states",
    )


def scan_kernel(first, in_ref, *rest):
    out_ref, kept_ref = rest[-2:]
    blocks, rows, inner = in_ref.shape
    rows, inner = rows // 2, inner - LANES
    select = selector(LANES, inner, first)
    totals = [
        jnp.sum(in_ref[block, :, inner:].astype(F32), axis=0, keepdims=True)
        for block in range(blocks)
    ]
    decay = spread(jnp.exp2(jnp.concatenate(totals, axis=0)), select, 3)
    through = []
    for k, order in enumerate((range(blocks), range(blocks - 1, -1, -1))):
        here = slice(k * rows, (k + 1) * rows)
        running = jnp.zeros((rows, inner), F32)
        for block in order:
            out_ref[block, here, 0:inner] = running.astype(BF16)
            if k == 0:
                kept_ref[block] = running
            else:
                through.append(jnp.sum(kept_ref[block] * running, axis=0, keepdims=True))
            step = decay[block : block + 1, :]
            running = step * running + in_ref[block, here, 0:inner].astype(F32)
    link = gather(jnp.concatenate(through[::-1], axis=0), select, 3)
    high, low = (term.astype(F32) for term in pieces(link, 2))
    row = lax.broadcasted_iota(jnp.int32, (2 * rows, LANES), 0)
    for block in range(blocks):
        here = slice(block, block + 1)
        both = jnp.where(row == 0, high[here, :], jnp.where(row == 1, low[here, :], 0.0))
        out_ref[block, :, inner:] = both.astype(BF16)


def scan_blocks(sums, first, behind):
    blocks, rows, inner = sums.shape
    return call(
        functools.partial(scan_kernel, first),
        [jax.ShapeDtypeStruct(sums.shape, BF16)],
        (sums, *behind),
        scratch_shapes=[pltpu.VMEM((blocks, rows // 2, inner - LANES), F32)],
        in_specs=[vmem()] + [anywhere()] * len(behind),
        compiler_params=one_step(8),
        cost_estimate=LITTLE,
        name="scan_blocks",
    )[0]


def across(sums):
    return lax.all_to_all(sums, "ctx", split_axis=0, concat_axis=0, tiled=True)


def stacked(ref, k):
    blocks, rows, _ = ref.shape
    rows //= 2
    return jnp.concatenate(
        [ref[block, k * rows : (k + 1) * rows, :] for block in range(blocks)], axis=0
    )


def inside_kernel(first, x_ref, dy_ref, b_ref, c_ref, col_ref, row_ref, *rest):
    added, (dx_ref, u_ref, v_ref, db_ref, dc_ref, s_ref, ds_ref) = rest[:-7], rest[-7:]
    length = x_ref.shape[0]
    tiles = length // LANES
    heads = COLS // WIDTH
    group = pl.program_id(0)
    from_k = lax.broadcasted_iota(jnp.int32, (length, length), 0)
    to_q = lax.broadcasted_iota(jnp.int32, (length, length), 1)

    @pl.when(group == 0)
    def _():
        s_ref[...] = jnp.where(to_q >= from_k, dot_nt(b_ref[...], c_ref[...]), 0.0)
        ds_ref[...] = jnp.zeros_like(ds_ref)
        v_ref[...] = jnp.zeros_like(v_ref)

    turned = pltpu.roll(col_ref[...], lax.rem(LANES - first - group * heads, LANES), 1)
    lane = lax.broadcasted_iota(jnp.int32, (LANES, LANES), 1)
    for j in range(tiles):
        low = j * LANES
        here = slice(low, low + LANES)
        for pair in range(heads // 2):
            across = slice(pair * LANES, (pair + 1) * LANES)
            xs = x_ref[here, across]
            dys = dy_ref[low:, across]
            side = lax.broadcasted_iota(jnp.int32, dys.shape, 1) // WIDTH
            total = None
            for half in range(2):
                local = pair * 2 + half
                head = first + group * heads + local
                own_x = jnp.where(lane // WIDTH == half, xs, jnp.zeros_like(xs))
                own_dy = jnp.where(side == half, dys, jnp.zeros_like(dys))
                products = dot_nt(own_x, dys)
                behind = turned[here, local : local + 1]
                kept = []
                v_sum = None
                for i in range(j, tiles):
                    there = slice(i * LANES, (i + 1) * LANES)
                    ahead = row_ref[0, local : local + 1, there]
                    decay = jnp.exp2(jnp.minimum(ahead - behind, 64.0))
                    product = products[:, (i - j) * LANES : (i - j + 1) * LANES]
                    score = s_ref[here, there] * decay
                    kept.append(score.astype(BF16))
                    ds_ref[here, there] += decay * product
                    both = score * product
                    v_sum = both if v_sum is None else v_sum + both
                    u_sum = jnp.sum(both, axis=0, keepdims=True)
                    if j > 0:
                        u_sum += u_ref[0, local : local + 1, there]
                    u_ref[0, local : local + 1, there] = u_sum
                v_col = jnp.sum(v_sum, axis=1, keepdims=True)
                v_ref[here, :] = jnp.where(lane == head, v_col, v_ref[here, :])
                scores = jnp.concatenate(kept, axis=1) if len(kept) > 1 else kept[0]
                part = dot(scores, own_dy)
                total = part if total is None else total + part
            dx_ref[here, across] = total

    @pl.when(group == pl.num_programs(0) - 1)
    def _():
        grads = jnp.where(to_q >= from_k, ds_ref[...], 0.0)
        db = sum(dot(term, c_ref[...]) for term in pieces(grads, 2))
        dc = sum(dot(term, b_ref[...]) for term in pieces(grads.T, 2))
        db_ref[...] = db + added[0][...] if added else db
        dc_ref[...] = dc + added[1][...] if added else dc


def inside(rows, inner, b, c, col_part, row_part, first, *added):
    added = [a for a in added if a is not None]
    length = rows.shape[0]
    tall = jax.ShapeDtypeStruct((length, LANES), F32)
    pairs = length * length * inner
    offset = first * WIDTH // COLS
    by_group = pl.BlockSpec((1,) + row_part.shape[1:], lambda g: (g + offset, 0, 0))
    own_group = pl.BlockSpec((1,) + row_part.shape[1:], lambda g: (g, 0, 0))
    return call(
        functools.partial(inside_kernel, first),
        (
            jax.ShapeDtypeStruct((length, inner), F32),
            jax.ShapeDtypeStruct((inner // COLS,) + row_part.shape[1:], F32),
            tall,
            tall,
            tall,
        ),
        (rows, rows, b, c, col_part, row_part, *added),
        grid=(inner // COLS,),
        in_specs=[
            columns(length),
            columns(length, inner),
            whole(length, LANES),
            whole(length, LANES),
            whole(length, LANES),
            by_group,
        ]
        + [whole(length, LANES)] * len(added),
        out_specs=(
            columns(length),
            own_group,
            whole(length, LANES),
            whole(length, LANES),
            whole(length, LANES),
        ),
        scratch_shapes=[pltpu.VMEM((length, length), F32), pltpu.VMEM((length, length), F32)],
        compiler_params=params(20),
        cost_estimate=LITTLE,
        name="inside",
    )


def by_columns(shape):
    return pl.BlockSpec(shape[:2] + (COLS,), lambda g: (0, 0, g))


def channels_kernel(peers, first, at_ref, dy_ref, dxi_ref, carry_ref, weight_ref, b_ref, skip_ref, *rest):
    outs, dx_ref = rest[-1 - peers : -1], rest[-1]
    tokens = dy_ref.shape[0] // peers
    select = selector(LANES, COLS, first + pl.program_id(0) * (COLS // WIDTH))
    carried = spread(weight_ref[...], select) * dot(b_ref[...], stacked(carry_ref, 1))
    gain = spread(skip_ref[...], select, 3)[0:1, :]
    dx_ref[...] = (dxi_ref[...] + carried + gain * dy_ref[...].astype(F32)).astype(BF16)
    for r in range(peers):
        start = pl.multiple_of((at_ref[0] ^ r) * tokens, tokens)
        outs[r][...] = dx_ref[pl.ds(start, tokens), :]


def channels(peers, first, at, rows, dxi, carry, weight, b, skip, behind):
    length, inner = dxi.shape
    tokens = length // peers
    tall = whole(length, LANES)
    return call(
        functools.partial(channels_kernel, peers, first),
        [jax.ShapeDtypeStruct((tokens, inner), BF16)] * peers,
        (at, rows, dxi, carry, weight, b, skip, *behind),
        grid=(inner // COLS,),
        in_specs=[
            smem(),
            columns(length, inner),
            columns(length),
            by_columns(carry.shape),
            tall,
            tall,
            whole(8, LANES),
        ]
        + [anywhere()] * len(behind),
        out_specs=[columns(tokens)] * peers,
        scratch_shapes=[pltpu.VMEM((length, COLS), BF16)],
        compiler_params=params(12),
        cost_estimate=LITTLE,
        name="channels",
    )


def others_kernel(
    heads,
    peers,
    first,
    last,
    at_ref,
    _,
    x_ref,
    dy_ref,
    carry_ref,
    through_ref,
    into_ref,
    out_of_ref,
    b_ref,
    c_ref,
    dt_ref,
    tot_ref,
    ui_ref,
    vi_ref,
    *rest,
):
    if last:
        added, rest = rest[:5], rest[5:]
    outs, (db_ref, dc_ref, u_ref, v_ref, tail_ref) = rest[:-5], rest[-5:]
    length = x_ref.shape[0]
    tokens = length // peers
    group = pl.program_id(0)

    @pl.when(group == 0)
    def _():
        db_ref[...] = jnp.zeros_like(db_ref)
        dc_ref[...] = jnp.zeros_like(dc_ref)
        u_ref[...] = jnp.zeros_like(u_ref)
        v_ref[...] = jnp.zeros_like(v_ref)

    select = selector(LANES, COLS, first + group * (COLS // WIDTH))
    for source, weight_ref, k, near_ref, sum_ref, head_ref in (
        (x_ref, into_ref, 1, b_ref, db_ref, v_ref),
        (dy_ref, out_of_ref, 0, c_ref, dc_ref, u_ref),
    ):
        weighted = source[...].astype(F32) * spread(weight_ref[...], select)
        far = stacked(carry_ref, k)
        sum_ref[...] += sum(dot_nt(term, far) for term in pieces(weighted, 2))
        head_ref[...] += gather(weighted * dot(near_ref[...], far), select)

    @pl.when(group == pl.num_programs(0) - 1)
    def _():
        inner_v, outer_v = vi_ref[...], v_ref[...]
        steps = (inner_v + outer_v) / dt_ref[...]
        rows = [ui_ref[at] for at in range(ui_ref.shape[0])]
        if first > 0:
            rows.insert(0, jnp.zeros((first, length), F32))
        rows.append(jnp.zeros((LANES - sum(part.shape[0] for part in rows), length), F32))
        net = jnp.concatenate(rows, axis=0).T + u_ref[...] - inner_v - outer_v
        row = lax.broadcasted_iota(jnp.int32, (length, length), 0)
        col = lax.broadcasted_iota(jnp.int32, (length, length), 1)
        upper = jnp.where(col >= row, 1.0, 0.0).astype(BF16)
        later = sum(dot(upper, term) for term in pieces(net, 3))
        whole_block = jnp.sum(outer_v, axis=0, keepdims=True)
        link = sum(through_ref[block].astype(F32) for block in range(through_ref.shape[0]))
        link = jnp.sum(link, axis=0, keepdims=True)
        logs = later + whole_block + jnp.exp2(tot_ref[0:1, :]) * link
        thin = steps + pltpu.roll(logs, heads, 1)
        if not last:
            outs[0][...] = thin
            outs[1][...] = db_ref[...]
            outs[2][...] = dc_ref[...]
        else:
            thin_ref, dbo_ref, dco_ref, dbi_ref, dci_ref = added
            tail_ref[:, 0:LANES] = (thin + thin_ref[...]).astype(BF16)
            tail_ref[:, LANES : 2 * LANES] = (db_ref[...] + dbo_ref[...] + dbi_ref[...]).astype(BF16)
            tail_ref[:, 2 * LANES :] = (dc_ref[...] + dco_ref[...] + dci_ref[...]).astype(BF16)
            for r in range(peers):
                start = pl.multiple_of((at_ref[0] ^ r) * tokens, tokens)
                outs[r][...] = tail_ref[pl.ds(start, tokens), :]


def others(
    heads, peers, first, at, rows, inner, carry, into, out_of, b, c, dt, tot, ui, vi, added, behind
):
    length = rows.shape[0]
    tokens = length // peers
    tall = whole(length, LANES)
    last = len(added) > 0
    tall_shape = jax.ShapeDtypeStruct((length, LANES), F32)
    tail_shape = jax.ShapeDtypeStruct((tokens, 3 * LANES), BF16)
    return call(
        functools.partial(others_kernel, heads, peers, first, last),
        [tail_shape] * peers if last else [tall_shape] * 3,
        (at, behind, rows, rows, carry, carry, into, out_of, b, c, dt, tot, ui, vi, *added,),
        grid=(inner // COLS,),
        in_specs=[
            smem(),
            anywhere(),
            columns(length),
            columns(length, inner),
            by_columns(carry.shape),
            pl.BlockSpec(carry.shape[:2] + (LANES,), lambda g: (0, 0, inner // LANES)),
            tall,
            tall,
            tall,
            tall,
            tall,
            whole(8, LANES),
            whole(*ui.shape),
            tall,
        ]
        + [tall] * len(added),
        out_specs=[whole(tokens, 3 * LANES)] * peers if last else [tall] * 3,
        scratch_shapes=[pltpu.VMEM((length, LANES), F32)] * 4
        + [pltpu.VMEM((length, 3 * LANES), BF16)],
        compiler_params=params(20),
        cost_estimate=LITTLE,
        name="others",
    )


def finish_kernel(heads, peers, halves, at_ref, *rest):
    count = peers * halves
    sent, tails = rest[:count], rest[count : count + peers]
    dx_ref, steps_ref, logs_ref, db_ref, dc_ref, sems = rest[count + peers :]
    tokens, width = sent[0].shape
    copies = []
    for half in range(halves):
        for r in range(peers):
            start = pl.multiple_of(((at_ref[0] ^ r) * halves + half) * width, LANES)
            copies.append(
                pltpu.make_async_copy(
                    sent[half * peers + r], dx_ref.at[:, pl.ds(start, width)], sems.at[half, r]
                )
            )
    for copy in copies:
        copy.start()
    lane = lax.broadcasted_iota(jnp.int32, (tokens, LANES), 1)
    results = [jnp.zeros((tokens, LANES), F32) for _ in range(4)]
    for r in range(peers):
        source = at_ref[0] ^ r
        own = lane // heads == source
        thin = tails[r][:, 0:LANES].astype(F32)
        for k in range(2):
            shift = lax.rem((source - k) * heads + LANES, LANES)
            results[k] += jnp.where(own, pltpu.roll(thin, shift, 1), 0.0)
            results[2 + k] += tails[r][:, (k + 1) * LANES : (k + 2) * LANES].astype(F32)
    steps_ref[...] = results[0].astype(BF16)
    logs_ref[...] = results[1].astype(BF16)
    db_ref[...] = results[2]
    dc_ref[...] = results[3]
    for copy in copies:
        copy.wait()


def finish(heads, at, sent, tails):
    peers, halves = len(tails), len(sent)
    tokens, width = sent[0][0].shape
    thin = jax.ShapeDtypeStruct((tokens, LANES), BF16)
    wide = jax.ShapeDtypeStruct((tokens, LANES), F32)
    return call(
        functools.partial(finish_kernel, heads, peers, halves),
        (
            jax.ShapeDtypeStruct((tokens, width * halves * peers), BF16),
            thin,
            thin,
            wide,
            wide,
        ),
        (at, *[part for group in sent for part in group], *tails,),
        in_specs=[smem()] + [vmem()] * (peers * halves + peers),
        out_specs=(anywhere(), vmem(), vmem(), vmem(), vmem()),
        scratch_shapes=[pltpu.SemaphoreType.DMA((halves, peers))],
        compiler_params=one_step(8),
        cost_estimate=LITTLE,
        name="finish",
    )


HALVES = 2


def body(inputs, grad_out, steps, log_decay, input_map, output_map, skip_gain):
    blocks, peers = lax.axis_size("ctx"), lax.axis_size("head")
    inner = inputs.shape[1] // peers
    heads = steps.shape[1] // peers
    width = inner // HALVES
    at = lax.axis_index("head").astype(jnp.int32).reshape(1)

    riders = (steps, log_decay, input_map, output_map)
    low = pack(at, inputs, grad_out, riders, peers, 0, width, ())
    high = pack(at, inputs, grad_out, (), peers, width, width, (low[0],))
    low, high = swap(low), swap(high)
    skip = jnp.broadcast_to(jnp.pad(skip_gain, (0, LANES - heads))[None], (8, LANES))
    half = heads // HALVES

    def begin(low):
        scalars, rows, sums = opening(at, low, heads, blocks, width)
        col_part, row_part, b, c = scalars[0], scalars[1], scalars[6], scalars[7]
        reached = across(sums)
        pairs = inside(rows, width, b, c, col_part, row_part, 0)
        return scalars, rows, pairs, scan_blocks(reached, 0, (pairs[0],))

    def empty(low):
        return jax.tree.map(lambda a: jnp.zeros(a.shape, a.dtype), jax.eval_shape(begin, low))

    scalars, rows, pairs, begun = lax.cond(at[0] < peers, begin, empty, low)
    col_part, row_part, into, out_of, dt, tot, b, c, b_t, c_t = scalars
    dxi, ui, vi, dbi, dci = pairs

    carry = across(begun)
    rows_high, sums = states(at, into, out_of, b_t, c_t, tot, high, blocks, width, half, (begun,))
    reached = across(sums)
    dxi_high, ui_high, vi_high, dbi, dci = inside(
        rows_high, width, b, c, col_part, row_part, half, dbi, dci
    )
    dx_low = channels(peers, 0, at, rows, dxi, carry, into, b, skip, (dxi_high,))
    sent_low = swap(dx_low)
    begun = scan_blocks(reached, half, (dx_low[0],))
    carry_high = across(begun)
    added = others(
        heads, peers, 0, at, rows, width, carry, into, out_of, b, c, dt, tot, ui, vi, [], begun
    )
    dx_high = channels(
        peers, half, at, rows_high, dxi_high, carry_high, into, b, skip, (added[0], *sent_low[1:])
    )
    sent_high = swap(dx_high)
    tails = others(
        heads, peers, half, at, rows_high, width, carry_high, into, out_of, b, c, dt, tot, ui_high,
        vi_high, [*added, dbi, dci], dx_high[0],
    )
    return tuple(finish(heads, at, (sent_low, sent_high), swap(tails)))


def solution(mesh):
    rows = P(("ctx", "head"), None)
    return jax.shard_map(
        body,
        mesh=mesh,
        in_specs=(rows,) * 6 + (P("head"),),
        out_specs=(rows,) * 5,
        check_vma=False,
    )
```

```python
import functools

import jax
import jax.numpy as jnp
from jax import lax
from jax.experimental import pallas as pl
from jax.experimental.pallas import tpu as pltpu
from jax.sharding import PartitionSpec as P

F32 = jnp.float32
BF16 = jnp.bfloat16
LANES = 128
WIDTH = 64
COLS = 256
LOG2E = 1.4426950408889634
NT = (((1,), (1,)), ((), ()))
MIB = 1024 * 1024
LITTLE = pl.CostEstimate(flops=1000, bytes_accessed=1000, transcendentals=0)


def dot(a, b):
    return jnp.dot(a, b, preferred_element_type=F32)


def dot_nt(a, b):
    return lax.dot_general(a, b, NT, preferred_element_type=F32)


def pieces(a, count):
    terms = []
    for _ in range(count):
        term = a.astype(BF16)
        terms.append(term)
        a = a - term.astype(F32)
    return terms


def selector(rows, cols, first):
    row = lax.broadcasted_iota(jnp.int32, (rows, cols), 0)
    col = lax.broadcasted_iota(jnp.int32, (rows, cols), 1)
    return jnp.where((col // WIDTH) + first == row, 1.0, 0.0).astype(BF16)


def spread(a, select, count=2):
    return sum(dot(term, select) for term in pieces(a, count))


def gather(a, select, count=2):
    return sum(dot_nt(term, select) for term in pieces(a, count))


def params(mib):
    return pltpu.CompilerParams(dimension_semantics=("arbitrary",), vmem_limit_bytes=mib * MIB)


def whole(*shape):
    return pl.BlockSpec(shape, lambda *g: (0,) * len(shape))


def columns(rows, first=0):
    return pl.BlockSpec((rows, COLS), lambda g: (0, g + first // COLS))


def call(kernel, out_shape, operands, **options):
    operands = [
        a if a.dtype == jnp.int32 else pltpu.with_memory_space_constraint(a, pltpu.HBM)
        for a in operands
    ]
    out_shape = [pltpu.HBM(one.shape, one.dtype) for one in out_shape]
    return pl.pallas_call(kernel, out_shape=out_shape, **options)(*operands)


def smem():
    return pl.BlockSpec(memory_space=pltpu.SMEM)


def anywhere():
    return pl.BlockSpec(memory_space=pl.ANY)


def vmem():
    return pl.BlockSpec(memory_space=pltpu.VMEM)


def one_step(mib):
    return pltpu.CompilerParams(vmem_limit_bytes=mib * MIB)


def swap(parts):
    peers = lax.axis_size("head")
    got = [parts[0]] + [None] * (peers - 1)
    for r in range(peers - 1, 0, -1):
        got[r] = lax.ppermute(parts[r], "head", [(i, i ^ r) for i in range(peers)])
    return got


def pack_kernel(peers, first, width, at_ref, *rest):
    sources, outs, (held, sems) = rest[: -peers - 2], rest[-peers - 2 : -2], rest[-2:]
    inner = sources[0].shape[1] // peers
    order = list(range(peers - 1, -1, -1))
    parts, at = [], 0
    for k, source in enumerate(sources):
        size = width if k < 2 else source.shape[1]
        parts.append((source, at, size))
        at += size
    reads = {}
    for r in order:
        start = pl.multiple_of((at_ref[0] ^ r) * inner + first, LANES)
        for k, (source, at, size) in enumerate(parts):
            chosen = source.at[:, pl.ds(start, size)] if k < 2 else source
            reads[r, k] = pltpu.make_async_copy(
                chosen, held.at[r, :, pl.ds(at, size)], sems.at[0, r, k]
            )
            reads[r, k].start()
    writes = []
    for r in order:
        for k in range(len(parts)):
            reads[r, k].wait()
        writes.append(pltpu.make_async_copy(held.at[r], outs[r], sems.at[1, r, 0]))
        writes[-1].start()
    for write in writes:
        write.wait()


def pack(at, x, dy, riders, peers, first, width, behind):
    tokens = x.shape[0]
    full = 2 * width + sum(rider.shape[1] for rider in riders)
    count = 2 + len(riders)

    def kernel(at_ref, *rest):
        pack_kernel(peers, first, width, at_ref, *rest[:count], *rest[count + len(behind) :])

    return call(
        kernel,
        [jax.ShapeDtypeStruct((tokens, full), BF16)] * peers,
        (at, x, dy, *riders, *behind),
        in_specs=[smem()] + [anywhere()] * (count + len(behind)),
        out_specs=[anywhere()] * peers,
        scratch_shapes=[
            pltpu.VMEM((peers, tokens, full), BF16),
            pltpu.SemaphoreType.DMA((2, peers, count)),
        ],
        compiler_params=one_step(10),
        cost_estimate=LITTLE,
        name="pack",
    )


def prepare(heads, at_ref, small_ref, outs):
    col_ref, row_ref, in_ref, out_ref, dt_ref, tot_ref, b_ref, c_ref, bt_ref, ct_ref = outs
    length = small_ref.shape[0]
    shift = lax.rem(LANES - at_ref[0] * heads, LANES)
    steps = pltpu.roll(small_ref[:, 0:LANES].astype(F32), shift, 1)
    logs = pltpu.roll(small_ref[:, LANES : 2 * LANES].astype(F32), shift, 1)
    row = lax.broadcasted_iota(jnp.int32, (length, length), 0)
    col = lax.broadcasted_iota(jnp.int32, (length, length), 1)
    lower = jnp.where(row >= col, 1.0, 0.0).astype(BF16)
    cum = dot(lower, logs.astype(BF16)) * LOG2E
    total = cum[length - 1 : length, :]
    col_ref[...] = cum - jnp.log(steps) * LOG2E
    turned = cum.T
    per_group = row_ref.shape[1]
    for group in range(row_ref.shape[0]):
        row_ref[group] = turned[group * per_group : (group + 1) * per_group, :]
    in_ref[...] = jnp.exp2(total - cum) * steps
    out_ref[...] = jnp.exp2(cum)
    dt_ref[...] = steps
    tot_ref[...] = jnp.broadcast_to(total, tot_ref.shape)
    b = small_ref[:, 2 * LANES : 3 * LANES]
    c = small_ref[:, 3 * LANES : 4 * LANES]
    b_ref[...] = b
    c_ref[...] = c
    bt_ref[...] = b.astype(F32).T.astype(BF16)
    ct_ref[...] = c.astype(F32).T.astype(BF16)


def prepared(length, heads):
    tall = jax.ShapeDtypeStruct((length, LANES), F32)
    thin = jax.ShapeDtypeStruct((length, LANES), BF16)
    flat = jax.ShapeDtypeStruct((LANES, length), BF16)
    groups = jax.ShapeDtypeStruct((heads * WIDTH // COLS, COLS // WIDTH, length), F32)
    total = jax.ShapeDtypeStruct((8, LANES), F32)
    return [tall, groups, tall, tall, tall, total, thin, thin, flat, flat]


def put_in_order(head_ref, parts, rows_ref, sems):
    tokens = parts[0].shape[0]
    copies = []
    for r, part in enumerate(parts):
        start = pl.multiple_of((head_ref[0] ^ r) * tokens, tokens)
        copies.append(pltpu.make_async_copy(part, rows_ref.at[pl.ds(start, tokens), :], sems.at[r]))
        copies[-1].start()
    for copy in copies:
        copy.wait()


def add_up(first, weight_refs, map_refs, tot_ref, rows_ref, sum_ref):
    blocks, rows, inner = sum_ref.shape
    rows, inner = rows // 2, inner - LANES
    row = lax.broadcasted_iota(jnp.int32, (2 * rows, LANES), 0)
    total = jnp.zeros((2 * rows, LANES), F32)
    for k, term in enumerate(pieces(tot_ref[0:1, :], 3)):
        total = jnp.where(row == k, term.astype(F32), total)
    for block in range(blocks):
        sum_ref[block, :, inner:] = total.astype(BF16)
    weights = [pieces(ref[...], 2) for ref in weight_refs]
    for group in range(inner // COLS):
        here = slice(group * COLS, (group + 1) * COLS)
        select = selector(LANES, COLS, first + group * (COLS // WIDTH))
        for k in range(2):
            there = slice(k * inner + group * COLS, k * inner + (group + 1) * COLS)
            weight = sum(dot(term, select) for term in weights[k])
            weighted = rows_ref[:, there].astype(F32) * weight
            added = sum(dot(map_refs[k][...], term) for term in pieces(weighted, 2)).astype(BF16)
            for block in range(blocks):
                sum_ref[block, k * rows : (k + 1) * rows, here] = added[
                    block * rows : (block + 1) * rows, :
                ]


def opening_kernel(heads, peers, head_ref, *rest):
    parts, (rows_ref, sum_ref, sems) = rest[:peers], rest[-3:]
    outs = rest[peers : peers + 10]
    width = rows_ref.shape[1] - 4 * LANES
    put_in_order(head_ref, parts, rows_ref, sems)
    prepare(heads, head_ref, rows_ref.at[:, width:], outs)
    _, _, in_ref, out_ref, _, tot_ref, _, _, bt_ref, ct_ref = outs
    add_up(0, (in_ref, out_ref), (bt_ref, ct_ref), tot_ref, rows_ref, sum_ref)


def sum_shape(blocks, inner):
    return jax.ShapeDtypeStruct((blocks, 2 * LANES // blocks, inner + LANES), BF16)


def opening(head, parts, heads, blocks, inner):
    peers = len(parts)
    tokens, full = parts[0].shape
    rows = jax.ShapeDtypeStruct((tokens * peers, full), BF16)
    got = call(
        functools.partial(opening_kernel, heads, peers),
        prepared(tokens * peers, heads) + [rows, sum_shape(blocks, inner)],
        (head, *parts),
        in_specs=[smem()] + [anywhere()] * peers,
        scratch_shapes=[pltpu.SemaphoreType.DMA((peers,))],
        compiler_params=one_step(20),
        cost_estimate=LITTLE,
        name="opening",
    )
    return got[:10], got[10], got[11]


def states_kernel(first, peers, head_ref, in_ref, out_ref, bt_ref, ct_ref, tot_ref, *rest):
    parts, (rows_ref, sum_ref, sems) = rest[:peers], rest[-3:]
    put_in_order(head_ref, parts, rows_ref, sems)
    add_up(first, (in_ref, out_ref), (bt_ref, ct_ref), tot_ref, rows_ref, sum_ref)


def states(head, into, out_of, b_t, c_t, tot, parts, blocks, inner, first, behind):
    peers = len(parts)
    tokens, full = parts[0].shape
    rows = jax.ShapeDtypeStruct((tokens * peers, full), BF16)
    return call(
        functools.partial(states_kernel, first, peers),
        [rows, sum_shape(blocks, inner)],
        (head, into, out_of, b_t, c_t, tot, *parts, *behind),
        in_specs=[smem()] + [vmem()] * 5 + [anywhere()] * (peers + len(behind)),
        scratch_shapes=[pltpu.SemaphoreType.DMA((peers,))],
        compiler_params=one_step(16),
        cost_estimate=LITTLE,
        name="states",
    )


def scan_kernel(first, in_ref, *rest):
    out_ref, kept_ref = rest[-2:]
    blocks, rows, inner = in_ref.shape
    rows, inner = rows // 2, inner - LANES
    select = selector(LANES, inner, first)
    totals = [
        jnp.sum(in_ref[block, :, inner:].astype(F32), axis=0, keepdims=True)
        for block in range(blocks)
    ]
    decay = spread(jnp.exp2(jnp.concatenate(totals, axis=0)), select, 3)
    through = []
    for k, order in enumerate((range(blocks), range(blocks - 1, -1, -1))):
        here = slice(k * rows, (k + 1) * rows)
        running = jnp.zeros((rows, inner), F32)
        for block in order:
            out_ref[block, here, 0:inner] = running.astype(BF16)
            if k == 0:
                kept_ref[block] = running
            else:
                through.append(jnp.sum(kept_ref[block] * running, axis=0, keepdims=True))
            step = decay[block : block + 1, :]
            running = step * running + in_ref[block, here, 0:inner].astype(F32)
    link = gather(jnp.concatenate(through[::-1], axis=0), select, 3)
    high, low = (term.astype(F32) for term in pieces(link, 2))
    row = lax.broadcasted_iota(jnp.int32, (2 * rows, LANES), 0)
    for block in range(blocks):
        here = slice(block, block + 1)
        both = jnp.where(row == 0, high[here, :], jnp.where(row == 1, low[here, :], 0.0))
        out_ref[block, :, inner:] = both.astype(BF16)


def scan_blocks(sums, first, behind):
    blocks, rows, inner = sums.shape
    return call(
        functools.partial(scan_kernel, first),
        [jax.ShapeDtypeStruct(sums.shape, BF16)],
        (sums, *behind),
        scratch_shapes=[pltpu.VMEM((blocks, rows // 2, inner - LANES), F32)],
        in_specs=[vmem()] + [anywhere()] * len(behind),
        compiler_params=one_step(8),
        cost_estimate=LITTLE,
        name="scan_blocks",
    )[0]


def across(sums):
    return lax.all_to_all(sums, "ctx", split_axis=0, concat_axis=0, tiled=True)


def stacked(ref, k):
    blocks, rows, _ = ref.shape
    rows //= 2
    return jnp.concatenate(
        [ref[block, k * rows : (k + 1) * rows, :] for block in range(blocks)], axis=0
    )


def inside_kernel(first, x_ref, dy_ref, b_ref, c_ref, col_ref, row_ref, *rest):
    added, (dx_ref, u_ref, v_ref, db_ref, dc_ref, s_ref, ds_ref) = rest[:-7], rest[-7:]
    length = x_ref.shape[0]
    tiles = length // LANES
    heads = COLS // WIDTH
    group = pl.program_id(0)
    from_k = lax.broadcasted_iota(jnp.int32, (length, length), 0)
    to_q = lax.broadcasted_iota(jnp.int32, (length, length), 1)

    @pl.when(group == 0)
    def _():
        s_ref[...] = jnp.where(to_q >= from_k, dot_nt(b_ref[...], c_ref[...]), 0.0)
        ds_ref[...] = jnp.zeros_like(ds_ref)
        v_ref[...] = jnp.zeros_like(v_ref)

    turned = pltpu.roll(col_ref[...], lax.rem(LANES - first - group * heads, LANES), 1)
    lane = lax.broadcasted_iota(jnp.int32, (LANES, LANES), 1)
    for j in range(tiles):
        low = j * LANES
        here = slice(low, low + LANES)
        for pair in range(heads // 2):
            across = slice(pair * LANES, (pair + 1) * LANES)
            xs = x_ref[here, across]
            dys = dy_ref[low:, across]
            side = lax.broadcasted_iota(jnp.int32, dys.shape, 1) // WIDTH
            total = None
            for half in range(2):
                local = pair * 2 + half
                head = first + group * heads + local
                own_x = jnp.where(lane // WIDTH == half, xs, jnp.zeros_like(xs))
                own_dy = jnp.where(side == half, dys, jnp.zeros_like(dys))
                products = dot_nt(own_x, dys)
                behind = turned[here, local : local + 1]
                kept = []
                v_sum = None
                for i in range(j, tiles):
                    there = slice(i * LANES, (i + 1) * LANES)
                    ahead = row_ref[0, local : local + 1, there]
                    decay = jnp.exp2(jnp.minimum(ahead - behind, 64.0))
                    product = products[:, (i - j) * LANES : (i - j + 1) * LANES]
                    score = s_ref[here, there] * decay
                    kept.append(score.astype(BF16))
                    ds_ref[here, there] += decay * product
                    both = score * product
                    v_sum = both if v_sum is None else v_sum + both
                    u_sum = jnp.sum(both, axis=0, keepdims=True)
                    if j > 0:
                        u_sum += u_ref[0, local : local + 1, there]
                    u_ref[0, local : local + 1, there] = u_sum
                v_col = jnp.sum(v_sum, axis=1, keepdims=True)
                v_ref[here, :] = jnp.where(lane == head, v_col, v_ref[here, :])
                scores = jnp.concatenate(kept, axis=1) if len(kept) > 1 else kept[0]
                part = dot(scores, own_dy)
                total = part if total is None else total + part
            dx_ref[here, across] = total

    @pl.when(group == pl.num_programs(0) - 1)
    def _():
        grads = jnp.where(to_q >= from_k, ds_ref[...], 0.0)
        db = sum(dot(term, c_ref[...]) for term in pieces(grads, 2))
        dc = sum(dot(term, b_ref[...]) for term in pieces(grads.T, 2))
        db_ref[...] = db + added[0][...] if added else db
        dc_ref[...] = dc + added[1][...] if added else dc


def inside(rows, inner, b, c, col_part, row_part, first, *added):
    added = [a for a in added if a is not None]
    length = rows.shape[0]
    tall = jax.ShapeDtypeStruct((length, LANES), F32)
    pairs = length * length * inner
    offset = first * WIDTH // COLS
    by_group = pl.BlockSpec((1,) + row_part.shape[1:], lambda g: (g + offset, 0, 0))
    own_group = pl.BlockSpec((1,) + row_part.shape[1:], lambda g: (g, 0, 0))
    return call(
        functools.partial(inside_kernel, first),
        (
            jax.ShapeDtypeStruct((length, inner), F32),
            jax.ShapeDtypeStruct((inner // COLS,) + row_part.shape[1:], F32),
            tall,
            tall,
            tall,
        ),
        (rows, rows, b, c, col_part, row_part, *added),
        grid=(inner // COLS,),
        in_specs=[
            columns(length),
            columns(length, inner),
            whole(length, LANES),
            whole(length, LANES),
            whole(length, LANES),
            by_group,
        ]
        + [whole(length, LANES)] * len(added),
        out_specs=(
            columns(length),
            own_group,
            whole(length, LANES),
            whole(length, LANES),
            whole(length, LANES),
        ),
        scratch_shapes=[pltpu.VMEM((length, length), F32), pltpu.VMEM((length, length), F32)],
        compiler_params=params(20),
        cost_estimate=LITTLE,
        name="inside",
    )


def by_columns(shape):
    return pl.BlockSpec(shape[:2] + (COLS,), lambda g: (0, 0, g))


def channels_kernel(peers, first, at_ref, dy_ref, dxi_ref, carry_ref, weight_ref, b_ref, skip_ref, *rest):
    outs, dx_ref = rest[-1 - peers : -1], rest[-1]
    tokens = dy_ref.shape[0] // peers
    select = selector(LANES, COLS, first + pl.program_id(0) * (COLS // WIDTH))
    carried = spread(weight_ref[...], select) * dot(b_ref[...], stacked(carry_ref, 1))
    gain = spread(skip_ref[...], select, 3)[0:1, :]
    dx_ref[...] = (dxi_ref[...] + carried + gain * dy_ref[...].astype(F32)).astype(BF16)
    for r in range(peers):
        start = pl.multiple_of((at_ref[0] ^ r) * tokens, tokens)
        outs[r][...] = dx_ref[pl.ds(start, tokens), :]


def channels(peers, first, at, rows, dxi, carry, weight, b, skip, behind):
    length, inner = dxi.shape
    tokens = length // peers
    tall = whole(length, LANES)
    return call(
        functools.partial(channels_kernel, peers, first),
        [jax.ShapeDtypeStruct((tokens, inner), BF16)] * peers,
        (at, rows, dxi, carry, weight, b, skip, *behind),
        grid=(inner // COLS,),
        in_specs=[
            smem(),
            columns(length, inner),
            columns(length),
            by_columns(carry.shape),
            tall,
            tall,
            whole(8, LANES),
        ]
        + [anywhere()] * len(behind),
        out_specs=[columns(tokens)] * peers,
        scratch_shapes=[pltpu.VMEM((length, COLS), BF16)],
        compiler_params=params(12),
        cost_estimate=LITTLE,
        name="channels",
    )


def others_kernel(
    heads,
    peers,
    first,
    last,
    at_ref,
    _,
    x_ref,
    dy_ref,
    carry_ref,
    through_ref,
    into_ref,
    out_of_ref,
    b_ref,
    c_ref,
    dt_ref,
    tot_ref,
    ui_ref,
    vi_ref,
    *rest,
):
    if last:
        added, rest = rest[:5], rest[5:]
    outs, (db_ref, dc_ref, u_ref, v_ref, tail_ref) = rest[:-5], rest[-5:]
    length = x_ref.shape[0]
    tokens = length // peers
    group = pl.program_id(0)

    @pl.when(group == 0)
    def _():
        db_ref[...] = jnp.zeros_like(db_ref)
        dc_ref[...] = jnp.zeros_like(dc_ref)
        u_ref[...] = jnp.zeros_like(u_ref)
        v_ref[...] = jnp.zeros_like(v_ref)

    select = selector(LANES, COLS, first + group * (COLS // WIDTH))
    for source, weight_ref, k, near_ref, sum_ref, head_ref in (
        (x_ref, into_ref, 1, b_ref, db_ref, v_ref),
        (dy_ref, out_of_ref, 0, c_ref, dc_ref, u_ref),
    ):
        weighted = source[...].astype(F32) * spread(weight_ref[...], select)
        far = stacked(carry_ref, k)
        sum_ref[...] += sum(dot_nt(term, far) for term in pieces(weighted, 2))
        head_ref[...] += gather(weighted * dot(near_ref[...], far), select)

    @pl.when(group == pl.num_programs(0) - 1)
    def _():
        inner_v, outer_v = vi_ref[...], v_ref[...]
        steps = (inner_v + outer_v) / dt_ref[...]
        rows = [ui_ref[at] for at in range(ui_ref.shape[0])]
        if first > 0:
            rows.insert(0, jnp.zeros((first, length), F32))
        rows.append(jnp.zeros((LANES - sum(part.shape[0] for part in rows), length), F32))
        net = jnp.concatenate(rows, axis=0).T + u_ref[...] - inner_v - outer_v
        row = lax.broadcasted_iota(jnp.int32, (length, length), 0)
        col = lax.broadcasted_iota(jnp.int32, (length, length), 1)
        upper = jnp.where(col >= row, 1.0, 0.0).astype(BF16)
        later = sum(dot(upper, term) for term in pieces(net, 3))
        whole_block = jnp.sum(outer_v, axis=0, keepdims=True)
        link = sum(through_ref[block].astype(F32) for block in range(through_ref.shape[0]))
        link = jnp.sum(link, axis=0, keepdims=True)
        logs = later + whole_block + jnp.exp2(tot_ref[0:1, :]) * link
        thin = steps + pltpu.roll(logs, heads, 1)
        if not last:
            outs[0][...] = thin
            outs[1][...] = db_ref[...]
            outs[2][...] = dc_ref[...]
        else:
            thin_ref, dbo_ref, dco_ref, dbi_ref, dci_ref = added
            tail_ref[:, 0:LANES] = (thin + thin_ref[...]).astype(BF16)
            tail_ref[:, LANES : 2 * LANES] = (db_ref[...] + dbo_ref[...] + dbi_ref[...]).astype(BF16)
            tail_ref[:, 2 * LANES :] = (dc_ref[...] + dco_ref[...] + dci_ref[...]).astype(BF16)
            for r in range(peers):
                start = pl.multiple_of((at_ref[0] ^ r) * tokens, tokens)
                outs[r][...] = tail_ref[pl.ds(start, tokens), :]


def others(
    heads, peers, first, at, rows, inner, carry, into, out_of, b, c, dt, tot, ui, vi, added, behind
):
    length = rows.shape[0]
    tokens = length // peers
    tall = whole(length, LANES)
    last = len(added) > 0
    tall_shape = jax.ShapeDtypeStruct((length, LANES), F32)
    tail_shape = jax.ShapeDtypeStruct((tokens, 3 * LANES), BF16)
    return call(
        functools.partial(others_kernel, heads, peers, first, last),
        [tail_shape] * peers if last else [tall_shape] * 3,
        (at, behind, rows, rows, carry, carry, into, out_of, b, c, dt, tot, ui, vi, *added,),
        grid=(inner // COLS,),
        in_specs=[
            smem(),
            anywhere(),
            columns(length),
            columns(length, inner),
            by_columns(carry.shape),
            pl.BlockSpec(carry.shape[:2] + (LANES,), lambda g: (0, 0, inner // LANES)),
            tall,
            tall,
            tall,
            tall,
            tall,
            whole(8, LANES),
            whole(*ui.shape),
            tall,
        ]
        + [tall] * len(added),
        out_specs=[whole(tokens, 3 * LANES)] * peers if last else [tall] * 3,
        scratch_shapes=[pltpu.VMEM((length, LANES), F32)] * 4
        + [pltpu.VMEM((length, 3 * LANES), BF16)],
        compiler_params=params(20),
        cost_estimate=LITTLE,
        name="others",
    )


def finish_kernel(heads, peers, halves, at_ref, *rest):
    count = peers * halves
    sent, tails = rest[:count], rest[count : count + peers]
    dx_ref, steps_ref, logs_ref, db_ref, dc_ref, sems = rest[count + peers :]
    tokens, width = sent[0].shape
    copies = []
    for half in range(halves):
        for r in range(peers):
            start = pl.multiple_of(((at_ref[0] ^ r) * halves + half) * width, LANES)
            copies.append(
                pltpu.make_async_copy(
                    sent[half * peers + r], dx_ref.at[:, pl.ds(start, width)], sems.at[half, r]
                )
            )
    for copy in copies:
        copy.start()
    lane = lax.broadcasted_iota(jnp.int32, (tokens, LANES), 1)
    results = [jnp.zeros((tokens, LANES), F32) for _ in range(4)]
    for r in range(peers):
        source = at_ref[0] ^ r
        own = lane // heads == source
        thin = tails[r][:, 0:LANES].astype(F32)
        for k in range(2):
            shift = lax.rem((source - k) * heads + LANES, LANES)
            results[k] += jnp.where(own, pltpu.roll(thin, shift, 1), 0.0)
            results[2 + k] += tails[r][:, (k + 1) * LANES : (k + 2) * LANES].astype(F32)
    steps_ref[...] = results[0].astype(BF16)
    logs_ref[...] = results[1].astype(BF16)
    db_ref[...] = results[2]
    dc_ref[...] = results[3]
    for copy in copies:
        copy.wait()


def finish(heads, at, sent, tails):
    peers, halves = len(tails), len(sent)
    tokens, width = sent[0][0].shape
    thin = jax.ShapeDtypeStruct((tokens, LANES), BF16)
    wide = jax.ShapeDtypeStruct((tokens, LANES), F32)
    return call(
        functools.partial(finish_kernel, heads, peers, halves),
        (
            jax.ShapeDtypeStruct((tokens, width * halves * peers), BF16),
            thin,
            thin,
            wide,
            wide,
        ),
        (at, *[part for group in sent for part in group], *tails,),
        in_specs=[smem()] + [vmem()] * (peers * halves + peers),
        out_specs=(anywhere(), vmem(), vmem(), vmem(), vmem()),
        scratch_shapes=[pltpu.SemaphoreType.DMA((halves, peers))],
        compiler_params=one_step(8),
        cost_estimate=LITTLE,
        name="finish",
    )


HALVES = 2


def body(inputs, grad_out, steps, log_decay, input_map, output_map, skip_gain):
    blocks, peers = lax.axis_size("ctx"), lax.axis_size("head")
    inner = inputs.shape[1] // peers
    heads = steps.shape[1] // peers
    width = inner // HALVES
    at = lax.axis_index("head").astype(jnp.int32).reshape(1)

    riders = (steps, log_decay, input_map, output_map)
    low = pack(at, inputs, grad_out, riders, peers, 0, width, ())
    high = pack(at, inputs, grad_out, (), peers, width, width, (low[0],))
    low, high = swap(low), swap(high)
    skip = jnp.broadcast_to(jnp.pad(skip_gain, (0, LANES - heads))[None], (8, LANES))
    half = heads // HALVES

    def begin(low):
        scalars, rows, sums = opening(at, low, heads, blocks, width)
        col_part, row_part, b, c = scalars[0], scalars[1], scalars[6], scalars[7]
        reached = across(sums)
        pairs = inside(rows, width, b, c, col_part, row_part, 0)
        return scalars, rows, pairs, reached

    def empty(low):
        return jax.tree.map(lambda a: jnp.zeros(a.shape, a.dtype), jax.eval_shape(begin, low))

    scalars, rows, pairs, reached = lax.cond(at[0] < peers, begin, empty, low)
    col_part, row_part, into, out_of, dt, tot, b, c, b_t, c_t = scalars
    dxi, ui, vi, dbi, dci = pairs

    begun = scan_blocks(reached, 0, (dxi, *high[1:]))
    carry = across(begun)
    rows_high, sums = states(at, into, out_of, b_t, c_t, tot, high, blocks, width, half, (begun,))
    reached = across(sums)
    dxi_high, ui_high, vi_high, dbi, dci = inside(
        rows_high, width, b, c, col_part, row_part, half, dbi, dci
    )
    dx_low = channels(peers, 0, at, rows, dxi, carry, into, b, skip, (dxi_high,))
    sent_low = swap(dx_low)
    begun = scan_blocks(reached, half, (dx_low[0],))
    carry_high = across(begun)
    added = others(
        heads, peers, 0, at, rows, width, carry, into, out_of, b, c, dt, tot, ui, vi, [], begun
    )
    dx_high = channels(
        peers, half, at, rows_high, dxi_high, carry_high, into, b, skip, (added[0], *sent_low[1:])
    )
    sent_high = swap(dx_high)
    tails = others(
        heads, peers, half, at, rows_high, width, carry_high, into, out_of, b, c, dt, tot, ui_high,
        vi_high, [*added, dbi, dci], dx_high[0],
    )
    return tuple(finish(heads, at, (sent_low, sent_high), swap(tails)))


def solution(mesh):
    rows = P(("ctx", "head"), None)
    return jax.shard_map(
        body,
        mesh=mesh,
        in_specs=(rows,) * 6 + (P("head"),),
        out_specs=(rows,) * 5,
        check_vma=False,
    )
```

```python
import functools

import jax
import jax.numpy as jnp
from jax import lax
from jax.experimental import pallas as pl
from jax.experimental.pallas import tpu as pltpu
from jax.sharding import PartitionSpec as P

F32 = jnp.float32
BF16 = jnp.bfloat16
LANES = 128
WIDTH = 64
COLS = 256
WIDE = 512
LOG2E = 1.4426950408889634
NT = (((1,), (1,)), ((), ()))
MIB = 1024 * 1024
LITTLE = pl.CostEstimate(flops=1000, bytes_accessed=1000, transcendentals=0)


def dot(a, b):
    return jnp.dot(a, b, preferred_element_type=F32)


def dot_nt(a, b):
    return lax.dot_general(a, b, NT, preferred_element_type=F32)


def pieces(a, count):
    terms = []
    for _ in range(count):
        term = a.astype(BF16)
        terms.append(term)
        a = a - term.astype(F32)
    return terms


def selector(rows, cols, first):
    row = lax.broadcasted_iota(jnp.int32, (rows, cols), 0)
    col = lax.broadcasted_iota(jnp.int32, (rows, cols), 1)
    return jnp.where((col // WIDTH) + first == row, 1.0, 0.0).astype(BF16)


def spread(a, select, count=2):
    return sum(dot(term, select) for term in pieces(a, count))


def gather(a, select, count=2):
    return sum(dot_nt(term, select) for term in pieces(a, count))


def params(mib):
    return pltpu.CompilerParams(dimension_semantics=("arbitrary",), vmem_limit_bytes=mib * MIB)


def whole(*shape):
    return pl.BlockSpec(shape, lambda *g: (0,) * len(shape))


def columns(rows, first=0, cols=COLS):
    return pl.BlockSpec((rows, cols), lambda g: (0, g + first // cols))


def call(kernel, out_shape, operands, **options):
    operands = [
        a if a.dtype == jnp.int32 else pltpu.with_memory_space_constraint(a, pltpu.HBM)
        for a in operands
    ]
    out_shape = [pltpu.HBM(one.shape, one.dtype) for one in out_shape]
    return pl.pallas_call(kernel, out_shape=out_shape, **options)(*operands)


def smem():
    return pl.BlockSpec(memory_space=pltpu.SMEM)


def anywhere():
    return pl.BlockSpec(memory_space=pl.ANY)


def vmem():
    return pl.BlockSpec(memory_space=pltpu.VMEM)


def one_step(mib):
    return pltpu.CompilerParams(vmem_limit_bytes=mib * MIB)


def swap(parts):
    peers = lax.axis_size("head")
    got = [parts[0]] + [None] * (peers - 1)
    for r in range(peers - 1, 0, -1):
        got[r] = lax.ppermute(parts[r], "head", [(i, i ^ r) for i in range(peers)])
    return got


def pack_kernel(peers, first, width, at_ref, *rest):
    sources, outs, (held, sems) = rest[: -peers - 2], rest[-peers - 2 : -2], rest[-2:]
    inner = sources[0].shape[1] // peers
    order = list(range(peers - 1, -1, -1))
    parts, at = [], 0
    for k, source in enumerate(sources):
        size = width if k < 2 else source.shape[1]
        parts.append((source, at, size))
        at += size
    reads = {}
    for r in order:
        start = pl.multiple_of((at_ref[0] ^ r) * inner + first, LANES)
        for k, (source, at, size) in enumerate(parts):
            chosen = source.at[:, pl.ds(start, size)] if k < 2 else source
            reads[r, k] = pltpu.make_async_copy(
                chosen, held.at[r, :, pl.ds(at, size)], sems.at[0, r, k]
            )
            reads[r, k].start()
    writes = []
    for r in order:
        for k in range(len(parts)):
            reads[r, k].wait()
        writes.append(pltpu.make_async_copy(held.at[r], outs[r], sems.at[1, r, 0]))
        writes[-1].start()
    for write in writes:
        write.wait()


def pack(at, x, dy, riders, peers, first, width, behind):
    tokens = x.shape[0]
    full = 2 * width + sum(rider.shape[1] for rider in riders)
    count = 2 + len(riders)

    def kernel(at_ref, *rest):
        pack_kernel(peers, first, width, at_ref, *rest[:count], *rest[count + len(behind) :])

    return call(
        kernel,
        [jax.ShapeDtypeStruct((tokens, full), BF16)] * peers,
        (at, x, dy, *riders, *behind),
        in_specs=[smem()] + [anywhere()] * (count + len(behind)),
        out_specs=[anywhere()] * peers,
        scratch_shapes=[
            pltpu.VMEM((peers, tokens, full), BF16),
            pltpu.SemaphoreType.DMA((2, peers, count)),
        ],
        compiler_params=one_step(10),
        cost_estimate=LITTLE,
        name="pack",
    )


def prepare(heads, at_ref, small_ref, outs):
    col_ref, row_ref, in_ref, out_ref, dt_ref, tot_ref, b_ref, c_ref, bt_ref, ct_ref = outs
    length = small_ref.shape[0]
    shift = lax.rem(LANES - at_ref[0] * heads, LANES)
    steps = pltpu.roll(small_ref[:, 0:LANES].astype(F32), shift, 1)
    logs = pltpu.roll(small_ref[:, LANES : 2 * LANES].astype(F32), shift, 1)
    row = lax.broadcasted_iota(jnp.int32, (length, length), 0)
    col = lax.broadcasted_iota(jnp.int32, (length, length), 1)
    lower = jnp.where(row >= col, 1.0, 0.0).astype(BF16)
    cum = dot(lower, logs.astype(BF16)) * LOG2E
    total = cum[length - 1 : length, :]
    col_ref[...] = cum - jnp.log(steps) * LOG2E
    turned = cum.T
    per_group = row_ref.shape[1]
    for group in range(row_ref.shape[0]):
        row_ref[group] = turned[group * per_group : (group + 1) * per_group, :]
    in_ref[...] = jnp.exp2(total - cum) * steps
    out_ref[...] = jnp.exp2(cum)
    dt_ref[...] = steps
    tot_ref[...] = jnp.broadcast_to(total, tot_ref.shape)
    b = small_ref[:, 2 * LANES : 3 * LANES]
    c = small_ref[:, 3 * LANES : 4 * LANES]
    b_ref[...] = b
    c_ref[...] = c
    bt_ref[...] = b.astype(F32).T.astype(BF16)
    ct_ref[...] = c.astype(F32).T.astype(BF16)


def prepared(length, heads):
    tall = jax.ShapeDtypeStruct((length, LANES), F32)
    thin = jax.ShapeDtypeStruct((length, LANES), BF16)
    flat = jax.ShapeDtypeStruct((LANES, length), BF16)
    groups = jax.ShapeDtypeStruct((heads * WIDTH // COLS, COLS // WIDTH, length), F32)
    total = jax.ShapeDtypeStruct((8, LANES), F32)
    return [tall, groups, tall, tall, tall, total, thin, thin, flat, flat]


def put_in_order(head_ref, parts, rows_ref, sems):
    tokens = parts[0].shape[0]
    copies = []
    for r, part in enumerate(parts):
        start = pl.multiple_of((head_ref[0] ^ r) * tokens, tokens)
        copies.append(pltpu.make_async_copy(part, rows_ref.at[pl.ds(start, tokens), :], sems.at[r]))
        copies[-1].start()
    for copy in copies:
        copy.wait()


def add_up(first, weight_refs, map_refs, tot_ref, rows_ref, sum_ref):
    blocks, rows, inner = sum_ref.shape
    rows, inner = rows // 2, inner - LANES
    row = lax.broadcasted_iota(jnp.int32, (2 * rows, LANES), 0)
    total = jnp.zeros((2 * rows, LANES), F32)
    for k, term in enumerate(pieces(tot_ref[0:1, :], 3)):
        total = jnp.where(row == k, term.astype(F32), total)
    for block in range(blocks):
        sum_ref[block, :, inner:] = total.astype(BF16)
    weights = [pieces(ref[...], 2) for ref in weight_refs]
    for group in range(inner // COLS):
        here = slice(group * COLS, (group + 1) * COLS)
        select = selector(LANES, COLS, first + group * (COLS // WIDTH))
        for k in range(2):
            there = slice(k * inner + group * COLS, k * inner + (group + 1) * COLS)
            weight = sum(dot(term, select) for term in weights[k])
            weighted = rows_ref[:, there].astype(F32) * weight
            added = sum(dot(map_refs[k][...], term) for term in pieces(weighted, 2)).astype(BF16)
            for block in range(blocks):
                sum_ref[block, k * rows : (k + 1) * rows, here] = added[
                    block * rows : (block + 1) * rows, :
                ]


def opening_kernel(heads, peers, head_ref, *rest):
    parts, (rows_ref, sum_ref, sems) = rest[:peers], rest[-3:]
    outs = rest[peers : peers + 10]
    width = rows_ref.shape[1] - 4 * LANES
    put_in_order(head_ref, parts, rows_ref, sems)
    prepare(heads, head_ref, rows_ref.at[:, width:], outs)
    _, _, in_ref, out_ref, _, tot_ref, _, _, bt_ref, ct_ref = outs
    add_up(0, (in_ref, out_ref), (bt_ref, ct_ref), tot_ref, rows_ref, sum_ref)


def sum_shape(blocks, inner):
    return jax.ShapeDtypeStruct((blocks, 2 * LANES // blocks, inner + LANES), BF16)


def opening(head, parts, heads, blocks, inner):
    peers = len(parts)
    tokens, full = parts[0].shape
    rows = jax.ShapeDtypeStruct((tokens * peers, full), BF16)
    got = call(
        functools.partial(opening_kernel, heads, peers),
        prepared(tokens * peers, heads) + [rows, sum_shape(blocks, inner)],
        (head, *parts),
        in_specs=[smem()] + [anywhere()] * peers,
        scratch_shapes=[pltpu.SemaphoreType.DMA((peers,))],
        compiler_params=one_step(20),
        cost_estimate=LITTLE,
        name="opening",
    )
    return got[:10], got[10], got[11]


def states_kernel(first, peers, head_ref, in_ref, out_ref, bt_ref, ct_ref, tot_ref, *rest):
    parts, (rows_ref, sum_ref, sems) = rest[:peers], rest[-3:]
    put_in_order(head_ref, parts, rows_ref, sems)
    add_up(first, (in_ref, out_ref), (bt_ref, ct_ref), tot_ref, rows_ref, sum_ref)


def states(head, into, out_of, b_t, c_t, tot, parts, blocks, inner, first, behind):
    peers = len(parts)
    tokens, full = parts[0].shape
    rows = jax.ShapeDtypeStruct((tokens * peers, full), BF16)
    return call(
        functools.partial(states_kernel, first, peers),
        [rows, sum_shape(blocks, inner)],
        (head, into, out_of, b_t, c_t, tot, *parts, *behind),
        in_specs=[smem()] + [vmem()] * 5 + [anywhere()] * (peers + len(behind)),
        scratch_shapes=[pltpu.SemaphoreType.DMA((peers,))],
        compiler_params=one_step(16),
        cost_estimate=LITTLE,
        name="states",
    )


def scan_kernel(first, in_ref, *rest):
    out_ref, kept_ref = rest[-2:]
    blocks, rows, inner = in_ref.shape
    rows, inner = rows // 2, inner - LANES
    select = selector(LANES, inner, first)
    totals = [
        jnp.sum(in_ref[block, :, inner:].astype(F32), axis=0, keepdims=True)
        for block in range(blocks)
    ]
    decay = spread(jnp.exp2(jnp.concatenate(totals, axis=0)), select, 3)
    through = []
    for k, order in enumerate((range(blocks), range(blocks - 1, -1, -1))):
        here = slice(k * rows, (k + 1) * rows)
        running = jnp.zeros((rows, inner), F32)
        for block in order:
            out_ref[block, here, 0:inner] = running.astype(BF16)
            if k == 0:
                kept_ref[block] = running
            else:
                through.append(jnp.sum(kept_ref[block] * running, axis=0, keepdims=True))
            step = decay[block : block + 1, :]
            running = step * running + in_ref[block, here, 0:inner].astype(F32)
    link = gather(jnp.concatenate(through[::-1], axis=0), select, 3)
    high, low = (term.astype(F32) for term in pieces(link, 2))
    row = lax.broadcasted_iota(jnp.int32, (2 * rows, LANES), 0)
    for block in range(blocks):
        here = slice(block, block + 1)
        both = jnp.where(row == 0, high[here, :], jnp.where(row == 1, low[here, :], 0.0))
        out_ref[block, :, inner:] = both.astype(BF16)


def scan_blocks(sums, first, behind):
    blocks, rows, inner = sums.shape
    return call(
        functools.partial(scan_kernel, first),
        [jax.ShapeDtypeStruct(sums.shape, BF16)],
        (sums, *behind),
        scratch_shapes=[pltpu.VMEM((blocks, rows // 2, inner - LANES), F32)],
        in_specs=[vmem()] + [anywhere()] * len(behind),
        compiler_params=one_step(8),
        cost_estimate=LITTLE,
        name="scan_blocks",
    )[0]


def across(sums):
    return lax.all_to_all(sums, "ctx", split_axis=0, concat_axis=0, tiled=True)


def stacked(ref, k):
    blocks, rows, _ = ref.shape
    rows //= 2
    return jnp.concatenate(
        [ref[block, k * rows : (k + 1) * rows, :] for block in range(blocks)], axis=0
    )


def inside_kernel(first, x_ref, dy_ref, b_ref, c_ref, col_ref, row_ref, *rest):
    added, (dx_ref, u_ref, v_ref, db_ref, dc_ref, s_ref, ds_ref) = rest[:-7], rest[-7:]
    length = x_ref.shape[0]
    tiles = length // LANES
    heads = COLS // WIDTH
    group = pl.program_id(0)
    from_k = lax.broadcasted_iota(jnp.int32, (length, length), 0)
    to_q = lax.broadcasted_iota(jnp.int32, (length, length), 1)

    @pl.when(group == 0)
    def _():
        s_ref[...] = jnp.where(to_q >= from_k, dot_nt(b_ref[...], c_ref[...]), 0.0)
        ds_ref[...] = jnp.zeros_like(ds_ref)
        v_ref[...] = jnp.zeros_like(v_ref)

    turned = pltpu.roll(col_ref[...], lax.rem(LANES - first - group * heads, LANES), 1)
    lane = lax.broadcasted_iota(jnp.int32, (LANES, LANES), 1)
    for j in range(tiles):
        low = j * LANES
        here = slice(low, low + LANES)
        for pair in range(heads // 2):
            across = slice(pair * LANES, (pair + 1) * LANES)
            xs = x_ref[here, across]
            dys = dy_ref[low:, across]
            side = lax.broadcasted_iota(jnp.int32, dys.shape, 1) // WIDTH
            total = None
            for half in range(2):
                local = pair * 2 + half
                head = first + group * heads + local
                own_x = jnp.where(lane // WIDTH == half, xs, jnp.zeros_like(xs))
                own_dy = jnp.where(side == half, dys, jnp.zeros_like(dys))
                products = dot_nt(own_x, dys)
                behind = turned[here, local : local + 1]
                kept = []
                v_sum = None
                for i in range(j, tiles):
                    there = slice(i * LANES, (i + 1) * LANES)
                    ahead = row_ref[0, local : local + 1, there]
                    decay = jnp.exp2(jnp.minimum(ahead - behind, 64.0))
                    product = products[:, (i - j) * LANES : (i - j + 1) * LANES]
                    score = s_ref[here, there] * decay
                    kept.append(score.astype(BF16))
                    ds_ref[here, there] += decay * product
                    both = score * product
                    v_sum = both if v_sum is None else v_sum + both
                    u_sum = jnp.sum(both, axis=0, keepdims=True)
                    if j > 0:
                        u_sum += u_ref[0, local : local + 1, there]
                    u_ref[0, local : local + 1, there] = u_sum
                v_col = jnp.sum(v_sum, axis=1, keepdims=True)
                v_ref[here, :] = jnp.where(lane == head, v_col, v_ref[here, :])
                scores = jnp.concatenate(kept, axis=1) if len(kept) > 1 else kept[0]
                part = dot(scores, own_dy)
                total = part if total is None else total + part
            dx_ref[here, across] = total

    @pl.when(group == pl.num_programs(0) - 1)
    def _():
        grads = jnp.where(to_q >= from_k, ds_ref[...], 0.0)
        db = sum(dot(term, c_ref[...]) for term in pieces(grads, 2))
        dc = sum(dot(term, b_ref[...]) for term in pieces(grads.T, 2))
        db_ref[...] = db + added[0][...] if added else db
        dc_ref[...] = dc + added[1][...] if added else dc


def inside(rows, inner, b, c, col_part, row_part, first, *added):
    added = [a for a in added if a is not None]
    length = rows.shape[0]
    tall = jax.ShapeDtypeStruct((length, LANES), F32)
    pairs = length * length * inner
    offset = first * WIDTH // COLS
    by_group = pl.BlockSpec((1,) + row_part.shape[1:], lambda g: (g + offset, 0, 0))
    own_group = pl.BlockSpec((1,) + row_part.shape[1:], lambda g: (g, 0, 0))
    return call(
        functools.partial(inside_kernel, first),
        (
            jax.ShapeDtypeStruct((length, inner), F32),
            jax.ShapeDtypeStruct((inner // COLS,) + row_part.shape[1:], F32),
            tall,
            tall,
            tall,
        ),
        (rows, rows, b, c, col_part, row_part, *added),
        grid=(inner // COLS,),
        in_specs=[
            columns(length),
            columns(length, inner),
            whole(length, LANES),
            whole(length, LANES),
            whole(length, LANES),
            by_group,
        ]
        + [whole(length, LANES)] * len(added),
        out_specs=(
            columns(length),
            own_group,
            whole(length, LANES),
            whole(length, LANES),
            whole(length, LANES),
        ),
        scratch_shapes=[pltpu.VMEM((length, length), F32), pltpu.VMEM((length, length), F32)],
        compiler_params=params(20),
        cost_estimate=LITTLE,
        name="inside",
    )


def by_columns(shape):
    return pl.BlockSpec(shape[:2] + (WIDE,), lambda g: (0, 0, g))


def channels_kernel(peers, first, at_ref, dy_ref, dxi_ref, carry_ref, weight_ref, b_ref, skip_ref, *rest):
    outs, dx_ref = rest[-1 - peers : -1], rest[-1]
    tokens = dy_ref.shape[0] // peers
    select = selector(LANES, WIDE, first + pl.program_id(0) * (WIDE // WIDTH))
    carried = spread(weight_ref[...], select) * dot(b_ref[...], stacked(carry_ref, 1))
    gain = spread(skip_ref[...], select, 3)[0:1, :]
    dx_ref[...] = (dxi_ref[...] + carried + gain * dy_ref[...].astype(F32)).astype(BF16)
    for r in range(peers):
        start = pl.multiple_of((at_ref[0] ^ r) * tokens, tokens)
        outs[r][...] = dx_ref[pl.ds(start, tokens), :]


def channels(peers, first, at, rows, dxi, carry, weight, b, skip, behind):
    length, inner = dxi.shape
    tokens = length // peers
    tall = whole(length, LANES)
    return call(
        functools.partial(channels_kernel, peers, first),
        [jax.ShapeDtypeStruct((tokens, inner), BF16)] * peers,
        (at, rows, dxi, carry, weight, b, skip, *behind),
        grid=(inner // WIDE,),
        in_specs=[
            smem(),
            columns(length, inner, WIDE),
            columns(length, 0, WIDE),
            by_columns(carry.shape),
            tall,
            tall,
            whole(8, LANES),
        ]
        + [anywhere()] * len(behind),
        out_specs=[columns(tokens, 0, WIDE)] * peers,
        scratch_shapes=[pltpu.VMEM((length, WIDE), BF16)],
        compiler_params=params(16),
        cost_estimate=LITTLE,
        name="channels",
    )


def others_kernel(
    heads,
    peers,
    first,
    last,
    at_ref,
    _,
    x_ref,
    dy_ref,
    carry_ref,
    through_ref,
    into_ref,
    out_of_ref,
    b_ref,
    c_ref,
    dt_ref,
    tot_ref,
    ui_ref,
    vi_ref,
    *rest,
):
    if last:
        added, rest = rest[:5], rest[5:]
    outs, (db_ref, dc_ref, u_ref, v_ref, tail_ref) = rest[:-5], rest[-5:]
    length = x_ref.shape[0]
    tokens = length // peers
    group = pl.program_id(0)

    @pl.when(group == 0)
    def _():
        db_ref[...] = jnp.zeros_like(db_ref)
        dc_ref[...] = jnp.zeros_like(dc_ref)
        u_ref[...] = jnp.zeros_like(u_ref)
        v_ref[...] = jnp.zeros_like(v_ref)

    select = selector(LANES, WIDE, first + group * (WIDE // WIDTH))
    for source, weight_ref, k, near_ref, sum_ref, head_ref in (
        (x_ref, into_ref, 1, b_ref, db_ref, v_ref),
        (dy_ref, out_of_ref, 0, c_ref, dc_ref, u_ref),
    ):
        weighted = source[...].astype(F32) * spread(weight_ref[...], select)
        far = stacked(carry_ref, k)
        sum_ref[...] += dot_nt(weighted.astype(BF16), far)
        head_ref[...] += gather(weighted * dot(near_ref[...], far), select)

    @pl.when(group == pl.num_programs(0) - 1)
    def _():
        inner_v, outer_v = vi_ref[...], v_ref[...]
        steps = (inner_v + outer_v) / dt_ref[...]
        rows = [ui_ref[at] for at in range(ui_ref.shape[0])]
        if first > 0:
            rows.insert(0, jnp.zeros((first, length), F32))
        rows.append(jnp.zeros((LANES - sum(part.shape[0] for part in rows), length), F32))
        net = jnp.concatenate(rows, axis=0).T + u_ref[...] - inner_v - outer_v
        row = lax.broadcasted_iota(jnp.int32, (length, length), 0)
        col = lax.broadcasted_iota(jnp.int32, (length, length), 1)
        upper = jnp.where(col >= row, 1.0, 0.0).astype(BF16)
        later = sum(dot(upper, term) for term in pieces(net, 3))
        whole_block = jnp.sum(outer_v, axis=0, keepdims=True)
        link = sum(through_ref[block].astype(F32) for block in range(through_ref.shape[0]))
        link = jnp.sum(link, axis=0, keepdims=True)
        logs = later + whole_block + jnp.exp2(tot_ref[0:1, :]) * link
        thin = steps + pltpu.roll(logs, heads, 1)
        if not last:
            outs[0][...] = thin
            outs[1][...] = db_ref[...]
            outs[2][...] = dc_ref[...]
        else:
            thin_ref, dbo_ref, dco_ref, dbi_ref, dci_ref = added
            tail_ref[:, 0:LANES] = (thin + thin_ref[...]).astype(BF16)
            tail_ref[:, LANES : 2 * LANES] = (db_ref[...] + dbo_ref[...] + dbi_ref[...]).astype(BF16)
            tail_ref[:, 2 * LANES :] = (dc_ref[...] + dco_ref[...] + dci_ref[...]).astype(BF16)
            for r in range(peers):
                start = pl.multiple_of((at_ref[0] ^ r) * tokens, tokens)
                outs[r][...] = tail_ref[pl.ds(start, tokens), :]


def others(
    heads, peers, first, at, rows, inner, carry, into, out_of, b, c, dt, tot, ui, vi, added, behind
):
    length = rows.shape[0]
    tokens = length // peers
    tall = whole(length, LANES)
    last = len(added) > 0
    tall_shape = jax.ShapeDtypeStruct((length, LANES), F32)
    tail_shape = jax.ShapeDtypeStruct((tokens, 3 * LANES), BF16)
    return call(
        functools.partial(others_kernel, heads, peers, first, last),
        [tail_shape] * peers if last else [tall_shape] * 3,
        (at, behind, rows, rows, carry, carry, into, out_of, b, c, dt, tot, ui, vi, *added,),
        grid=(inner // WIDE,),
        in_specs=[
            smem(),
            anywhere(),
            columns(length, 0, WIDE),
            columns(length, inner, WIDE),
            by_columns(carry.shape),
            pl.BlockSpec(carry.shape[:2] + (LANES,), lambda g: (0, 0, inner // LANES)),
            tall,
            tall,
            tall,
            tall,
            tall,
            whole(8, LANES),
            whole(*ui.shape),
            tall,
        ]
        + [tall] * len(added),
        out_specs=[whole(tokens, 3 * LANES)] * peers if last else [tall] * 3,
        scratch_shapes=[pltpu.VMEM((length, LANES), F32)] * 4
        + [pltpu.VMEM((length, 3 * LANES), BF16)],
        compiler_params=params(24),
        cost_estimate=LITTLE,
        name="others",
    )


def put_columns(peers, half, head_ref, sent, held_ref, dx_ref, sems):
    width = sent[0].shape[1]
    reads = [
        pltpu.make_async_copy(sent[r], held_ref.at[r], sems.at[0, r]) for r in range(peers)
    ]
    for read in reads:
        read.start()
    writes = []
    for r in range(peers):
        reads[r].wait()
        start = pl.multiple_of(((head_ref[0] ^ r) * HALVES + half) * width, LANES)
        writes.append(
            pltpu.make_async_copy(
                held_ref.at[r], dx_ref.at[:, pl.ds(start, width)], sems.at[1, r]
            )
        )
        writes[-1].start()
    return writes


def place_kernel(peers, head_ref, *rest):
    dx_ref, held_ref, sems = rest[-3:]
    for write in put_columns(peers, 0, head_ref, rest[:peers], held_ref, dx_ref, sems):
        write.wait()


def place(head, sent, behind):
    peers = len(sent)
    tokens, width = sent[0].shape
    return call(
        functools.partial(place_kernel, peers),
        [jax.ShapeDtypeStruct((tokens, width * HALVES * peers), BF16)],
        (head, *sent, behind),
        in_specs=[smem()] + [anywhere()] * (peers + 1),
        out_specs=[anywhere()],
        scratch_shapes=[
            pltpu.VMEM((peers, tokens, width), BF16),
            pltpu.SemaphoreType.DMA((2, peers)),
        ],
        compiler_params=one_step(8),
        cost_estimate=LITTLE,
        name="place",
    )[0]


def finish_kernel(heads, peers, head_ref, _, *rest):
    sent, tails = rest[:peers], rest[peers : 2 * peers]
    dx_ref, steps_ref, logs_ref, db_ref, dc_ref, held_ref, sems = rest[2 * peers :]
    tokens = sent[0].shape[0]
    writes = put_columns(peers, 1, head_ref, sent, held_ref, dx_ref, sems)
    lane = lax.broadcasted_iota(jnp.int32, (tokens, LANES), 1)
    results = [jnp.zeros((tokens, LANES), F32) for _ in range(4)]
    for r in range(peers):
        source = head_ref[0] ^ r
        own = lane // heads == source
        thin = tails[r][:, 0:LANES].astype(F32)
        for k in range(2):
            shift = lax.rem((source - k) * heads + LANES, LANES)
            results[k] += jnp.where(own, pltpu.roll(thin, shift, 1), 0.0)
            results[2 + k] += tails[r][:, (k + 1) * LANES : (k + 2) * LANES].astype(F32)
    steps_ref[...] = results[0].astype(BF16)
    logs_ref[...] = results[1].astype(BF16)
    db_ref[...] = results[2]
    dc_ref[...] = results[3]
    for write in writes:
        write.wait()


def finish(heads, head, placed, sent, tails):
    peers = len(tails)
    tokens, width = sent[0].shape
    thin = jax.ShapeDtypeStruct((tokens, LANES), BF16)
    wide = jax.ShapeDtypeStruct((tokens, LANES), F32)
    return call(
        functools.partial(finish_kernel, heads, peers),
        [jax.ShapeDtypeStruct(placed.shape, BF16), thin, thin, wide, wide],
        (head, placed, *sent, *tails),
        in_specs=[smem()] + [anywhere()] * (1 + peers) + [vmem()] * peers,
        out_specs=[anywhere(), vmem(), vmem(), vmem(), vmem()],
        scratch_shapes=[
            pltpu.VMEM((peers, tokens, width), BF16),
            pltpu.SemaphoreType.DMA((2, peers)),
        ],
        input_output_aliases={1: 0},
        compiler_params=one_step(8),
        cost_estimate=LITTLE,
        name="finish",
    )


HALVES = 2


def body(inputs, grad_out, steps, log_decay, input_map, output_map, skip_gain):
    blocks, peers = lax.axis_size("ctx"), lax.axis_size("head")
    inner = inputs.shape[1] // peers
    heads = steps.shape[1] // peers
    width = inner // HALVES
    at = lax.axis_index("head").astype(jnp.int32).reshape(1)

    riders = (steps, log_decay, input_map, output_map)
    low = pack(at, inputs, grad_out, riders, peers, 0, width, ())
    high = pack(at, inputs, grad_out, (), peers, width, width, (low[0],))
    low, high = swap(low), swap(high)
    skip = jnp.broadcast_to(jnp.pad(skip_gain, (0, LANES - heads))[None], (8, LANES))
    half = heads // HALVES

    def begin(low):
        scalars, rows, sums = opening(at, low, heads, blocks, width)
        col_part, row_part, b, c = scalars[0], scalars[1], scalars[6], scalars[7]
        reached = across(sums)
        pairs = inside(rows, width, b, c, col_part, row_part, 0)
        return scalars, rows, pairs, reached

    def empty(low):
        return jax.tree.map(lambda a: jnp.zeros(a.shape, a.dtype), jax.eval_shape(begin, low))

    scalars, rows, pairs, reached = lax.cond(at[0] < peers, begin, empty, low)
    col_part, row_part, into, out_of, dt, tot, b, c, b_t, c_t = scalars
    dxi, ui, vi, dbi, dci = pairs

    begun = scan_blocks(reached, 0, (dxi, *high[1:]))
    carry = across(begun)
    rows_high, sums = states(at, into, out_of, b_t, c_t, tot, high, blocks, width, half, (begun,))
    reached = across(sums)
    dxi_high, ui_high, vi_high, dbi, dci = inside(
        rows_high, width, b, c, col_part, row_part, half, dbi, dci
    )
    begun = scan_blocks(reached, half, (dxi_high,))
    carry_high = across(begun)
    dx_low = channels(peers, 0, at, rows, dxi, carry, into, b, skip, (begun,))
    sent_low = swap(dx_low)
    added = others(
        heads, peers, 0, at, rows, width, carry, into, out_of, b, c, dt, tot, ui, vi, [], dx_low[0]
    )
    dx_high = channels(
        peers, half, at, rows_high, dxi_high, carry_high, into, b, skip, (added[0], *sent_low[1:])
    )
    sent_high = swap(dx_high)
    tails = others(
        heads, peers, half, at, rows_high, width, carry_high, into, out_of, b, c, dt, tot, ui_high,
        vi_high, [*added, dbi, dci], dx_high[0],
    )
    placed = place(at, sent_low, tails[0])
    return tuple(finish(heads, at, placed, sent_high, swap(tails)))


def solution(mesh):
    rows = P(("ctx", "head"), None)
    return jax.shard_map(
        body,
        mesh=mesh,
        in_specs=(rows,) * 6 + (P("head"),),
        out_specs=(rows,) * 5,
        check_vma=False,
    )
```

```python
import functools

import jax
import jax.numpy as jnp
from jax import lax
from jax.experimental import pallas as pl
from jax.experimental.pallas import tpu as pltpu
from jax.sharding import PartitionSpec as P

F32 = jnp.float32
BF16 = jnp.bfloat16
LANES = 128
WIDTH = 64
COLS = 256
WIDE = 512
LOG2E = 1.4426950408889634
NT = (((1,), (1,)), ((), ()))
MIB = 1024 * 1024
LITTLE = pl.CostEstimate(flops=1000, bytes_accessed=1000, transcendentals=0)


def dot(a, b):
    return jnp.dot(a, b, preferred_element_type=F32)


def dot_nt(a, b):
    return lax.dot_general(a, b, NT, preferred_element_type=F32)


def pieces(a, count):
    terms = []
    for _ in range(count):
        term = a.astype(BF16)
        terms.append(term)
        a = a - term.astype(F32)
    return terms


def selector(rows, cols, first):
    row = lax.broadcasted_iota(jnp.int32, (rows, cols), 0)
    col = lax.broadcasted_iota(jnp.int32, (rows, cols), 1)
    return jnp.where((col // WIDTH) + first == row, 1.0, 0.0).astype(BF16)


def spread(a, select, count=2):
    return sum(dot(term, select) for term in pieces(a, count))


def gather(a, select, count=2):
    return sum(dot_nt(term, select) for term in pieces(a, count))


def params(mib):
    return pltpu.CompilerParams(dimension_semantics=("arbitrary",), vmem_limit_bytes=mib * MIB)


def whole(*shape):
    return pl.BlockSpec(shape, lambda *g: (0,) * len(shape))


def columns(rows, first=0, cols=COLS):
    return pl.BlockSpec((rows, cols), lambda g: (0, g + first // cols))


def call(kernel, out_shape, operands, **options):
    operands = [
        a if a.dtype == jnp.int32 else pltpu.with_memory_space_constraint(a, pltpu.HBM)
        for a in operands
    ]
    out_shape = [pltpu.HBM(one.shape, one.dtype) for one in out_shape]
    return pl.pallas_call(kernel, out_shape=out_shape, **options)(*operands)


def smem():
    return pl.BlockSpec(memory_space=pltpu.SMEM)


def anywhere():
    return pl.BlockSpec(memory_space=pl.ANY)


def vmem():
    return pl.BlockSpec(memory_space=pltpu.VMEM)


def one_step(mib):
    return pltpu.CompilerParams(vmem_limit_bytes=mib * MIB)


def swap(parts):
    peers = lax.axis_size("head")
    got = [parts[0]] + [None] * (peers - 1)
    for r in range(peers - 1, 0, -1):
        got[r] = lax.ppermute(parts[r], "head", [(i, i ^ r) for i in range(peers)])
    return got


def pack_kernel(peers, first, width, at_ref, *rest):
    sources, outs, (held, sems) = rest[: -peers - 2], rest[-peers - 2 : -2], rest[-2:]
    inner = sources[0].shape[1] // peers
    order = list(range(peers - 1, -1, -1))
    parts, at = [], 0
    for k, source in enumerate(sources):
        size = width if k < 2 else source.shape[1]
        parts.append((source, at, size))
        at += size
    reads = {}
    for r in order:
        start = pl.multiple_of((at_ref[0] ^ r) * inner + first, LANES)
        for k, (source, at, size) in enumerate(parts):
            chosen = source.at[:, pl.ds(start, size)] if k < 2 else source
            reads[r, k] = pltpu.make_async_copy(
                chosen, held.at[r, :, pl.ds(at, size)], sems.at[0, r, k]
            )
            reads[r, k].start()
    writes = []
    for r in order:
        for k in range(len(parts)):
            reads[r, k].wait()
        writes.append(pltpu.make_async_copy(held.at[r], outs[r], sems.at[1, r, 0]))
        writes[-1].start()
    for write in writes:
        write.wait()


def pack(at, x, dy, riders, peers, first, width, behind):
    tokens = x.shape[0]
    full = 2 * width + sum(rider.shape[1] for rider in riders)
    count = 2 + len(riders)

    def kernel(at_ref, *rest):
        pack_kernel(peers, first, width, at_ref, *rest[:count], *rest[count + len(behind) :])

    return call(
        kernel,
        [jax.ShapeDtypeStruct((tokens, full), BF16)] * peers,
        (at, x, dy, *riders, *behind),
        in_specs=[smem()] + [anywhere()] * (count + len(behind)),
        out_specs=[anywhere()] * peers,
        scratch_shapes=[
            pltpu.VMEM((peers, tokens, full), BF16),
            pltpu.SemaphoreType.DMA((2, peers, count)),
        ],
        compiler_params=one_step(10),
        cost_estimate=LITTLE,
        name="pack",
    )


def prepare(heads, at_ref, small_ref, outs):
    col_ref, row_ref, in_ref, out_ref, dt_ref, tot_ref, b_ref, c_ref, bt_ref, ct_ref = outs
    length = small_ref.shape[0]
    shift = lax.rem(LANES - at_ref[0] * heads, LANES)
    steps = pltpu.roll(small_ref[:, 0:LANES].astype(F32), shift, 1)
    logs = pltpu.roll(small_ref[:, LANES : 2 * LANES].astype(F32), shift, 1)
    row = lax.broadcasted_iota(jnp.int32, (length, length), 0)
    col = lax.broadcasted_iota(jnp.int32, (length, length), 1)
    lower = jnp.where(row >= col, 1.0, 0.0).astype(BF16)
    cum = dot(lower, logs.astype(BF16)) * LOG2E
    total = cum[length - 1 : length, :]
    col_ref[...] = cum - jnp.log(steps) * LOG2E
    turned = cum.T
    per_group = row_ref.shape[1]
    for group in range(row_ref.shape[0]):
        row_ref[group] = turned[group * per_group : (group + 1) * per_group, :]
    in_ref[...] = jnp.exp2(total - cum) * steps
    out_ref[...] = jnp.exp2(cum)
    dt_ref[...] = steps
    tot_ref[...] = jnp.broadcast_to(total, tot_ref.shape)
    b = small_ref[:, 2 * LANES : 3 * LANES]
    c = small_ref[:, 3 * LANES : 4 * LANES]
    b_ref[...] = b
    c_ref[...] = c
    bt_ref[...] = b.astype(F32).T.astype(BF16)
    ct_ref[...] = c.astype(F32).T.astype(BF16)


def prepared(length, heads):
    tall = jax.ShapeDtypeStruct((length, LANES), F32)
    thin = jax.ShapeDtypeStruct((length, LANES), BF16)
    flat = jax.ShapeDtypeStruct((LANES, length), BF16)
    groups = jax.ShapeDtypeStruct((heads * WIDTH // COLS, COLS // WIDTH, length), F32)
    total = jax.ShapeDtypeStruct((8, LANES), F32)
    return [tall, groups, tall, tall, tall, total, thin, thin, flat, flat]


def put_in_order(head_ref, parts, rows_ref, sems):
    tokens = parts[0].shape[0]
    copies = []
    for r, part in enumerate(parts):
        start = pl.multiple_of((head_ref[0] ^ r) * tokens, tokens)
        copies.append(pltpu.make_async_copy(part, rows_ref.at[pl.ds(start, tokens), :], sems.at[r]))
        copies[-1].start()
    for copy in copies:
        copy.wait()


def add_up(first, weight_refs, map_refs, tot_ref, rows_ref, sum_ref):
    blocks, rows, inner = sum_ref.shape
    rows, inner = rows // 2, inner - LANES
    row = lax.broadcasted_iota(jnp.int32, (2 * rows, LANES), 0)
    total = jnp.zeros((2 * rows, LANES), F32)
    for k, term in enumerate(pieces(tot_ref[0:1, :], 3)):
        total = jnp.where(row == k, term.astype(F32), total)
    for block in range(blocks):
        sum_ref[block, :, inner:] = total.astype(BF16)
    weights = [pieces(ref[...], 2) for ref in weight_refs]
    for group in range(inner // COLS):
        here = slice(group * COLS, (group + 1) * COLS)
        select = selector(LANES, COLS, first + group * (COLS // WIDTH))
        for k in range(2):
            there = slice(k * inner + group * COLS, k * inner + (group + 1) * COLS)
            weight = sum(dot(term, select) for term in weights[k])
            weighted = rows_ref[:, there].astype(F32) * weight
            added = sum(dot(map_refs[k][...], term) for term in pieces(weighted, 2)).astype(BF16)
            for block in range(blocks):
                sum_ref[block, k * rows : (k + 1) * rows, here] = added[
                    block * rows : (block + 1) * rows, :
                ]


def opening_kernel(heads, peers, head_ref, *rest):
    parts, (rows_ref, sum_ref, sems) = rest[:peers], rest[-3:]
    outs = rest[peers : peers + 10]
    width = rows_ref.shape[1] - 4 * LANES
    put_in_order(head_ref, parts, rows_ref, sems)
    prepare(heads, head_ref, rows_ref.at[:, width:], outs)
    _, _, in_ref, out_ref, _, tot_ref, _, _, bt_ref, ct_ref = outs
    add_up(0, (in_ref, out_ref), (bt_ref, ct_ref), tot_ref, rows_ref, sum_ref)


def sum_shape(blocks, inner):
    return jax.ShapeDtypeStruct((blocks, 2 * LANES // blocks, inner + LANES), BF16)


def opening(head, parts, heads, blocks, inner):
    peers = len(parts)
    tokens, full = parts[0].shape
    rows = jax.ShapeDtypeStruct((tokens * peers, full), BF16)
    got = call(
        functools.partial(opening_kernel, heads, peers),
        prepared(tokens * peers, heads) + [rows, sum_shape(blocks, inner)],
        (head, *parts),
        in_specs=[smem()] + [anywhere()] * peers,
        scratch_shapes=[pltpu.SemaphoreType.DMA((peers,))],
        compiler_params=one_step(20),
        cost_estimate=LITTLE,
        name="opening",
    )
    return got[:10], got[10], got[11]


def states_kernel(first, peers, head_ref, in_ref, out_ref, bt_ref, ct_ref, tot_ref, *rest):
    parts, (rows_ref, sum_ref, sems) = rest[:peers], rest[-3:]
    put_in_order(head_ref, parts, rows_ref, sems)
    add_up(first, (in_ref, out_ref), (bt_ref, ct_ref), tot_ref, rows_ref, sum_ref)


def states(head, into, out_of, b_t, c_t, tot, parts, blocks, inner, first, behind):
    peers = len(parts)
    tokens, full = parts[0].shape
    rows = jax.ShapeDtypeStruct((tokens * peers, full), BF16)
    return call(
        functools.partial(states_kernel, first, peers),
        [rows, sum_shape(blocks, inner)],
        (head, into, out_of, b_t, c_t, tot, *parts, *behind),
        in_specs=[smem()] + [vmem()] * 5 + [anywhere()] * (peers + len(behind)),
        scratch_shapes=[pltpu.SemaphoreType.DMA((peers,))],
        compiler_params=one_step(16),
        cost_estimate=LITTLE,
        name="states",
    )


def decays(first, in_ref, select):
    blocks, _, full = in_ref.shape
    totals = [
        jnp.sum(in_ref[block, :, full - LANES :].astype(F32), axis=0, keepdims=True)
        for block in range(blocks)
    ]
    return spread(jnp.exp2(jnp.concatenate(totals, axis=0)), select, 3)


def total_kernel(first, at_ref, in_ref, *rest):
    out_ref = rest[-1]
    blocks, rows, inner = in_ref.shape
    rows, inner = rows // 2, inner - LANES
    decay = decays(first, in_ref, selector(LANES, inner, first))
    running = []
    for k, order in enumerate((range(blocks), range(blocks - 1, -1, -1))):
        here = slice(k * rows, (k + 1) * rows)
        value = jnp.zeros((rows, inner), F32)
        for block in order:
            step = decay[block : block + 1, :]
            value = step * value + in_ref[block, here, 0:inner].astype(F32)
        running.append(value)
    out_ref[...] = jnp.where(at_ref[0] < blocks, running[0], running[1])


def total_blocks(at, sums, first, behind):
    blocks, rows, inner = sums.shape
    return call(
        functools.partial(total_kernel, first),
        [jax.ShapeDtypeStruct((rows // 2, inner - LANES), F32)],
        (at, sums, *behind),
        in_specs=[smem(), vmem()] + [anywhere()] * len(behind),
        compiler_params=one_step(8),
        cost_estimate=LITTLE,
        name="total_blocks",
    )[0]


def scan_kernel(first, at_ref, in_ref, far_ref, *rest):
    out_ref, kept_ref = rest[-2:]
    blocks, rows, inner = in_ref.shape
    rows, inner = rows // 2, inner - LANES
    select = selector(LANES, inner, first)
    decay = decays(first, in_ref, select)
    second = at_ref[0] >= blocks
    through = []
    for k, order in enumerate((range(blocks), range(blocks - 1, -1, -1))):
        here = slice(k * rows, (k + 1) * rows)
        running = jnp.where(second == (k == 0), far_ref[...], 0.0)
        for block in order:
            out_ref[block, here, 0:inner] = running.astype(BF16)
            if k == 0:
                kept_ref[block] = running
            else:
                through.append(jnp.sum(kept_ref[block] * running, axis=0, keepdims=True))
            step = decay[block : block + 1, :]
            running = step * running + in_ref[block, here, 0:inner].astype(F32)
    link = gather(jnp.concatenate(through[::-1], axis=0), select, 3)
    high, low = (term.astype(F32) for term in pieces(link, 2))
    row = lax.broadcasted_iota(jnp.int32, (2 * rows, LANES), 0)
    for block in range(blocks):
        here = slice(block, block + 1)
        both = jnp.where(row == 0, high[here, :], jnp.where(row == 1, low[here, :], 0.0))
        out_ref[block, :, inner:] = both.astype(BF16)


def scan_blocks(at, sums, far, first, behind):
    blocks, rows, inner = sums.shape
    return call(
        functools.partial(scan_kernel, first),
        [jax.ShapeDtypeStruct(sums.shape, BF16)],
        (at, sums, far, *behind),
        scratch_shapes=[pltpu.VMEM((blocks, rows // 2, inner - LANES), F32)],
        in_specs=[smem(), vmem(), vmem()] + [anywhere()] * len(behind),
        compiler_params=one_step(8),
        cost_estimate=LITTLE,
        name="scan_blocks",
    )[0]


def across(sums):
    blocks = sums.shape[0]
    groups = [list(range(blocks)), list(range(blocks, 2 * blocks))]
    return lax.all_to_all(
        sums, "ctx", split_axis=0, concat_axis=0, tiled=True, axis_index_groups=groups
    )


def over(total):
    blocks = lax.axis_size("ctx")
    return lax.ppermute(total, "ctx", [(i, (i + blocks // 2) % blocks) for i in range(blocks)])


def stacked(ref, k):
    blocks, rows, _ = ref.shape
    rows //= 2
    return jnp.concatenate(
        [ref[block, k * rows : (k + 1) * rows, :] for block in range(blocks)], axis=0
    )


def inside_kernel(first, x_ref, dy_ref, b_ref, c_ref, col_ref, row_ref, *rest):
    added, (dx_ref, u_ref, v_ref, db_ref, dc_ref, s_ref, ds_ref) = rest[:-7], rest[-7:]
    length = x_ref.shape[0]
    tiles = length // LANES
    heads = COLS // WIDTH
    group = pl.program_id(0)
    from_k = lax.broadcasted_iota(jnp.int32, (length, length), 0)
    to_q = lax.broadcasted_iota(jnp.int32, (length, length), 1)

    @pl.when(group == 0)
    def _():
        s_ref[...] = jnp.where(to_q >= from_k, dot_nt(b_ref[...], c_ref[...]), 0.0)
        ds_ref[...] = jnp.zeros_like(ds_ref)
        v_ref[...] = jnp.zeros_like(v_ref)

    turned = pltpu.roll(col_ref[...], lax.rem(LANES - first - group * heads, LANES), 1)
    lane = lax.broadcasted_iota(jnp.int32, (LANES, LANES), 1)
    for j in range(tiles):
        low = j * LANES
        here = slice(low, low + LANES)
        for pair in range(heads // 2):
            across = slice(pair * LANES, (pair + 1) * LANES)
            xs = x_ref[here, across]
            dys = dy_ref[low:, across]
            side = lax.broadcasted_iota(jnp.int32, dys.shape, 1) // WIDTH
            total = None
            for half in range(2):
                local = pair * 2 + half
                head = first + group * heads + local
                own_x = jnp.where(lane // WIDTH == half, xs, jnp.zeros_like(xs))
                own_dy = jnp.where(side == half, dys, jnp.zeros_like(dys))
                products = dot_nt(own_x, dys)
                behind = turned[here, local : local + 1]
                kept = []
                v_sum = None
                for i in range(j, tiles):
                    there = slice(i * LANES, (i + 1) * LANES)
                    ahead = row_ref[0, local : local + 1, there]
                    decay = jnp.exp2(jnp.minimum(ahead - behind, 64.0))
                    product = products[:, (i - j) * LANES : (i - j + 1) * LANES]
                    score = s_ref[here, there] * decay
                    kept.append(score.astype(BF16))
                    ds_ref[here, there] += decay * product
                    both = score * product
                    v_sum = both if v_sum is None else v_sum + both
                    u_sum = jnp.sum(both, axis=0, keepdims=True)
                    if j > 0:
                        u_sum += u_ref[0, local : local + 1, there]
                    u_ref[0, local : local + 1, there] = u_sum
                v_col = jnp.sum(v_sum, axis=1, keepdims=True)
                v_ref[here, :] = jnp.where(lane == head, v_col, v_ref[here, :])
                scores = jnp.concatenate(kept, axis=1) if len(kept) > 1 else kept[0]
                part = dot(scores, own_dy)
                total = part if total is None else total + part
            dx_ref[here, across] = total

    @pl.when(group == pl.num_programs(0) - 1)
    def _():
        grads = jnp.where(to_q >= from_k, ds_ref[...], 0.0)
        db = sum(dot(term, c_ref[...]) for term in pieces(grads, 2))
        dc = sum(dot(term, b_ref[...]) for term in pieces(grads.T, 2))
        db_ref[...] = db + added[0][...] if added else db
        dc_ref[...] = dc + added[1][...] if added else dc


def inside(rows, inner, b, c, col_part, row_part, first, *added):
    added = [a for a in added if a is not None]
    length = rows.shape[0]
    tall = jax.ShapeDtypeStruct((length, LANES), F32)
    pairs = length * length * inner
    offset = first * WIDTH // COLS
    by_group = pl.BlockSpec((1,) + row_part.shape[1:], lambda g: (g + offset, 0, 0))
    own_group = pl.BlockSpec((1,) + row_part.shape[1:], lambda g: (g, 0, 0))
    return call(
        functools.partial(inside_kernel, first),
        (
            jax.ShapeDtypeStruct((length, inner), F32),
            jax.ShapeDtypeStruct((inner // COLS,) + row_part.shape[1:], F32),
            tall,
            tall,
            tall,
        ),
        (rows, rows, b, c, col_part, row_part, *added),
        grid=(inner // COLS,),
        in_specs=[
            columns(length),
            columns(length, inner),
            whole(length, LANES),
            whole(length, LANES),
            whole(length, LANES),
            by_group,
        ]
        + [whole(length, LANES)] * len(added),
        out_specs=(
            columns(length),
            own_group,
            whole(length, LANES),
            whole(length, LANES),
            whole(length, LANES),
        ),
        scratch_shapes=[pltpu.VMEM((length, length), F32), pltpu.VMEM((length, length), F32)],
        compiler_params=params(20),
        cost_estimate=LITTLE,
        name="inside",
    )


def by_columns(shape):
    return pl.BlockSpec(shape[:2] + (WIDE,), lambda g: (0, 0, g))


def channels_kernel(peers, first, at_ref, dy_ref, dxi_ref, carry_ref, weight_ref, b_ref, skip_ref, *rest):
    outs, dx_ref = rest[-1 - peers : -1], rest[-1]
    tokens = dy_ref.shape[0] // peers
    select = selector(LANES, WIDE, first + pl.program_id(0) * (WIDE // WIDTH))
    carried = spread(weight_ref[...], select) * dot(b_ref[...], stacked(carry_ref, 1))
    gain = spread(skip_ref[...], select, 3)[0:1, :]
    dx_ref[...] = (dxi_ref[...] + carried + gain * dy_ref[...].astype(F32)).astype(BF16)
    for r in range(peers):
        start = pl.multiple_of((at_ref[0] ^ r) * tokens, tokens)
        outs[r][...] = dx_ref[pl.ds(start, tokens), :]


def channels(peers, first, at, rows, dxi, carry, weight, b, skip, behind):
    length, inner = dxi.shape
    tokens = length // peers
    tall = whole(length, LANES)
    return call(
        functools.partial(channels_kernel, peers, first),
        [jax.ShapeDtypeStruct((tokens, inner), BF16)] * peers,
        (at, rows, dxi, carry, weight, b, skip, *behind),
        grid=(inner // WIDE,),
        in_specs=[
            smem(),
            columns(length, inner, WIDE),
            columns(length, 0, WIDE),
            by_columns(carry.shape),
            tall,
            tall,
            whole(8, LANES),
        ]
        + [anywhere()] * len(behind),
        out_specs=[columns(tokens, 0, WIDE)] * peers,
        scratch_shapes=[pltpu.VMEM((length, WIDE), BF16)],
        compiler_params=params(16),
        cost_estimate=LITTLE,
        name="channels",
    )


def others_kernel(
    heads,
    peers,
    first,
    last,
    at_ref,
    x_ref,
    dy_ref,
    carry_ref,
    through_ref,
    into_ref,
    out_of_ref,
    b_ref,
    c_ref,
    dt_ref,
    tot_ref,
    ui_ref,
    vi_ref,
    *rest,
):
    if last:
        added = rest[:5]
    outs = rest[-5 - (peers if last else 3) : -5]
    db_ref, dc_ref, u_ref, v_ref, tail_ref = rest[-5:]
    length = x_ref.shape[0]
    tokens = length // peers
    group = pl.program_id(0)

    @pl.when(group == 0)
    def _():
        db_ref[...] = jnp.zeros_like(db_ref)
        dc_ref[...] = jnp.zeros_like(dc_ref)
        u_ref[...] = jnp.zeros_like(u_ref)
        v_ref[...] = jnp.zeros_like(v_ref)

    select = selector(LANES, WIDE, first + group * (WIDE // WIDTH))
    for source, weight_ref, k, near_ref, sum_ref, head_ref in (
        (x_ref, into_ref, 1, b_ref, db_ref, v_ref),
        (dy_ref, out_of_ref, 0, c_ref, dc_ref, u_ref),
    ):
        weighted = source[...].astype(F32) * spread(weight_ref[...], select)
        far = stacked(carry_ref, k)
        sum_ref[...] += dot_nt(weighted.astype(BF16), far)
        head_ref[...] += gather(weighted * dot(near_ref[...], far), select)

    @pl.when(group == pl.num_programs(0) - 1)
    def _():
        inner_v, outer_v = vi_ref[...], v_ref[...]
        steps = (inner_v + outer_v) / dt_ref[...]
        rows = [ui_ref[at] for at in range(ui_ref.shape[0])]
        if first > 0:
            rows.insert(0, jnp.zeros((first, length), F32))
        rows.append(jnp.zeros((LANES - sum(part.shape[0] for part in rows), length), F32))
        net = jnp.concatenate(rows, axis=0).T + u_ref[...] - inner_v - outer_v
        row = lax.broadcasted_iota(jnp.int32, (length, length), 0)
        col = lax.broadcasted_iota(jnp.int32, (length, length), 1)
        upper = jnp.where(col >= row, 1.0, 0.0).astype(BF16)
        later = sum(dot(upper, term) for term in pieces(net, 3))
        whole_block = jnp.sum(outer_v, axis=0, keepdims=True)
        link = sum(through_ref[block].astype(F32) for block in range(through_ref.shape[0]))
        link = jnp.sum(link, axis=0, keepdims=True)
        logs = later + whole_block + jnp.exp2(tot_ref[0:1, :]) * link
        thin = steps + pltpu.roll(logs, heads, 1)
        if not last:
            outs[0][...] = thin
            outs[1][...] = db_ref[...]
            outs[2][...] = dc_ref[...]
        else:
            thin_ref, dbo_ref, dco_ref, dbi_ref, dci_ref = added
            tail_ref[:, 0:LANES] = (thin + thin_ref[...]).astype(BF16)
            tail_ref[:, LANES : 2 * LANES] = (db_ref[...] + dbo_ref[...] + dbi_ref[...]).astype(BF16)
            tail_ref[:, 2 * LANES :] = (dc_ref[...] + dco_ref[...] + dci_ref[...]).astype(BF16)
            for r in range(peers):
                start = pl.multiple_of((at_ref[0] ^ r) * tokens, tokens)
                outs[r][...] = tail_ref[pl.ds(start, tokens), :]


def others(
    heads, peers, first, at, rows, inner, carry, into, out_of, b, c, dt, tot, ui, vi, added, behind
):
    length = rows.shape[0]
    tokens = length // peers
    tall = whole(length, LANES)
    last = len(added) > 0
    tall_shape = jax.ShapeDtypeStruct((length, LANES), F32)
    tail_shape = jax.ShapeDtypeStruct((tokens, 3 * LANES), BF16)
    return call(
        functools.partial(others_kernel, heads, peers, first, last),
        [tail_shape] * peers if last else [tall_shape] * 3,
        (at, rows, rows, carry, carry, into, out_of, b, c, dt, tot, ui, vi, *added, *behind),
        grid=(inner // WIDE,),
        in_specs=[
            smem(),
            columns(length, 0, WIDE),
            columns(length, inner, WIDE),
            by_columns(carry.shape),
            pl.BlockSpec(carry.shape[:2] + (LANES,), lambda g: (0, 0, inner // LANES)),
            tall,
            tall,
            tall,
            tall,
            tall,
            whole(8, LANES),
            whole(*ui.shape),
            tall,
        ]
        + [tall] * len(added)
        + [anywhere()] * len(behind),
        out_specs=[whole(tokens, 3 * LANES)] * peers if last else [tall] * 3,
        scratch_shapes=[pltpu.VMEM((length, LANES), F32)] * 4
        + [pltpu.VMEM((length, 3 * LANES), BF16)],
        compiler_params=params(24),
        cost_estimate=LITTLE,
        name="others",
    )


def put_columns(peers, half, head_ref, sent, held_ref, dx_ref, sems):
    width = sent[0].shape[1]
    reads = [
        pltpu.make_async_copy(sent[r], held_ref.at[r], sems.at[0, r]) for r in range(peers)
    ]
    for read in reads:
        read.start()
    writes = []
    for r in range(peers):
        reads[r].wait()
        start = pl.multiple_of(((head_ref[0] ^ r) * HALVES + half) * width, LANES)
        writes.append(
            pltpu.make_async_copy(
                held_ref.at[r], dx_ref.at[:, pl.ds(start, width)], sems.at[1, r]
            )
        )
        writes[-1].start()
    return writes


def place_kernel(peers, head_ref, *rest):
    dx_ref, held_ref, sems = rest[-3:]
    for write in put_columns(peers, 0, head_ref, rest[:peers], held_ref, dx_ref, sems):
        write.wait()


def place(head, sent, behind):
    peers = len(sent)
    tokens, width = sent[0].shape
    return call(
        functools.partial(place_kernel, peers),
        [jax.ShapeDtypeStruct((tokens, width * HALVES * peers), BF16)],
        (head, *sent, behind),
        in_specs=[smem()] + [anywhere()] * (peers + 1),
        out_specs=[anywhere()],
        scratch_shapes=[
            pltpu.VMEM((peers, tokens, width), BF16),
            pltpu.SemaphoreType.DMA((2, peers)),
        ],
        compiler_params=one_step(8),
        cost_estimate=LITTLE,
        name="place",
    )[0]


def finish_kernel(heads, peers, head_ref, _, *rest):
    sent, tails = rest[:peers], rest[peers : 2 * peers]
    dx_ref, steps_ref, logs_ref, db_ref, dc_ref, held_ref, sems = rest[2 * peers :]
    tokens = sent[0].shape[0]
    writes = put_columns(peers, 1, head_ref, sent, held_ref, dx_ref, sems)
    lane = lax.broadcasted_iota(jnp.int32, (tokens, LANES), 1)
    results = [jnp.zeros((tokens, LANES), F32) for _ in range(4)]
    for r in range(peers):
        source = head_ref[0] ^ r
        own = lane // heads == source
        thin = tails[r][:, 0:LANES].astype(F32)
        for k in range(2):
            shift = lax.rem((source - k) * heads + LANES, LANES)
            results[k] += jnp.where(own, pltpu.roll(thin, shift, 1), 0.0)
            results[2 + k] += tails[r][:, (k + 1) * LANES : (k + 2) * LANES].astype(F32)
    steps_ref[...] = results[0].astype(BF16)
    logs_ref[...] = results[1].astype(BF16)
    db_ref[...] = results[2]
    dc_ref[...] = results[3]
    for write in writes:
        write.wait()


def finish(heads, head, placed, sent, tails):
    peers = len(tails)
    tokens, width = sent[0].shape
    thin = jax.ShapeDtypeStruct((tokens, LANES), BF16)
    wide = jax.ShapeDtypeStruct((tokens, LANES), F32)
    return call(
        functools.partial(finish_kernel, heads, peers),
        [jax.ShapeDtypeStruct(placed.shape, BF16), thin, thin, wide, wide],
        (head, placed, *sent, *tails),
        in_specs=[smem()] + [anywhere()] * (1 + peers) + [vmem()] * peers,
        out_specs=[anywhere(), vmem(), vmem(), vmem(), vmem()],
        scratch_shapes=[
            pltpu.VMEM((peers, tokens, width), BF16),
            pltpu.SemaphoreType.DMA((2, peers)),
        ],
        input_output_aliases={1: 0},
        compiler_params=one_step(8),
        cost_estimate=LITTLE,
        name="finish",
    )


HALVES = 2


def body(inputs, grad_out, steps, log_decay, input_map, output_map, skip_gain):
    blocks, peers = lax.axis_size("ctx") // 2, lax.axis_size("head")
    inner = inputs.shape[1] // peers
    heads = steps.shape[1] // peers
    width = inner // HALVES
    head = lax.axis_index("head").astype(jnp.int32).reshape(1)
    at = lax.axis_index("ctx").astype(jnp.int32).reshape(1)

    riders = (steps, log_decay, input_map, output_map)
    low = pack(head, inputs, grad_out, riders, peers, 0, width, ())
    high = pack(head, inputs, grad_out, (), peers, width, width, (low[0],))
    low, high = swap(low), swap(high)
    skip = jnp.broadcast_to(jnp.pad(skip_gain, (0, LANES - heads))[None], (8, LANES))
    half = heads // HALVES

    def begin(low):
        scalars, rows, sums = opening(head, low, heads, blocks, width)
        col_part, row_part, b, c = scalars[0], scalars[1], scalars[6], scalars[7]
        reached = across(sums)
        return scalars, rows, inside(rows, width, b, c, col_part, row_part, 0), reached

    def empty(low):
        return jax.tree.map(lambda a: jnp.zeros(a.shape, a.dtype), jax.eval_shape(begin, low))

    scalars, rows, pairs, reached = lax.cond(head[0] < peers, begin, empty, low)
    col_part, row_part, into, out_of, dt, tot, b, c, b_t, c_t = scalars
    dxi, ui, vi, dbi, dci = pairs

    total = total_blocks(at, reached, 0, (dxi, *high[1:]))
    far = over(total)
    rows_high, sums = states(head, into, out_of, b_t, c_t, tot, high, blocks, width, half, (total,))
    reached_high = across(sums)
    dxi_high, ui_high, vi_high, dbi, dci = inside(
        rows_high, width, b, c, col_part, row_part, half, dbi, dci
    )
    total = total_blocks(at, reached_high, half, (dxi_high,))
    far_high = over(total)
    begun = scan_blocks(at, reached, far, 0, (total,))
    carry = across(begun)
    begun = scan_blocks(at, reached_high, far_high, half, (begun,))
    carry_high = across(begun)
    dx_low = channels(peers, 0, head, rows, dxi, carry, into, b, skip, (begun,))
    sent_low = swap(dx_low)
    added = others(
        heads, peers, 0, head, rows, width, carry, into, out_of, b, c, dt, tot, ui, vi, [],
        (dx_low[0],),
    )
    dx_high = channels(
        peers, half, head, rows_high, dxi_high, carry_high, into, b, skip, (added[0],)
    )
    sent_high = swap(dx_high)
    tails = others(
        heads, peers, half, head, rows_high, width, carry_high, into, out_of, b, c, dt, tot,
        ui_high, vi_high, [*added, dbi, dci], (dx_high[0], *sent_low[1:]),
    )
    placed = place(head, sent_low, tails[0])
    return tuple(finish(heads, head, placed, sent_high, swap(tails)))


def solution(mesh):
    rows = P(("ctx", "head"), None)
    return jax.shard_map(
        body,
        mesh=mesh,
        in_specs=(rows,) * 6 + (P("head"),),
        out_specs=(rows,) * 5,
        check_vma=False,
    )
```

```python
import functools

import jax
import jax.numpy as jnp
from jax import lax
from jax.experimental import pallas as pl
from jax.experimental.pallas import tpu as pltpu
from jax.sharding import PartitionSpec as P

F32 = jnp.float32
BF16 = jnp.bfloat16
LANES = 128
WIDTH = 64
COLS = 256
WIDE = 512
LOG2E = 1.4426950408889634
NT = (((1,), (1,)), ((), ()))
MIB = 1024 * 1024
LITTLE = pl.CostEstimate(flops=1000, bytes_accessed=1000, transcendentals=0)


def dot(a, b):
    return jnp.dot(a, b, preferred_element_type=F32)


def dot_nt(a, b):
    return lax.dot_general(a, b, NT, preferred_element_type=F32)


def pieces(a, count):
    terms = []
    for _ in range(count):
        term = a.astype(BF16)
        terms.append(term)
        a = a - term.astype(F32)
    return terms


def selector(rows, cols, first):
    row = lax.broadcasted_iota(jnp.int32, (rows, cols), 0)
    col = lax.broadcasted_iota(jnp.int32, (rows, cols), 1)
    return jnp.where((col // WIDTH) + first == row, 1.0, 0.0).astype(BF16)


def spread(a, select, count=2):
    return sum(dot(term, select) for term in pieces(a, count))


def gather(a, select, count=2):
    return sum(dot_nt(term, select) for term in pieces(a, count))


def params(mib):
    return pltpu.CompilerParams(dimension_semantics=("arbitrary",), vmem_limit_bytes=mib * MIB)


def whole(*shape):
    return pl.BlockSpec(shape, lambda *g: (0,) * len(shape))


def columns(rows, first=0, cols=COLS):
    return pl.BlockSpec((rows, cols), lambda g: (0, g + first // cols))


def call(kernel, out_shape, operands, free=(), **options):
    operands = [
        a
        if a.dtype == jnp.int32 or at in free
        else pltpu.with_memory_space_constraint(a, pltpu.HBM)
        for at, a in enumerate(operands)
    ]
    out_shape = [pltpu.HBM(one.shape, one.dtype) for one in out_shape]
    return pl.pallas_call(kernel, out_shape=out_shape, **options)(*operands)


def smem():
    return pl.BlockSpec(memory_space=pltpu.SMEM)


def anywhere():
    return pl.BlockSpec(memory_space=pl.ANY)


def vmem():
    return pl.BlockSpec(memory_space=pltpu.VMEM)


def one_step(mib):
    return pltpu.CompilerParams(vmem_limit_bytes=mib * MIB)


def swap(parts):
    peers = lax.axis_size("head")
    got = [parts[0]] + [None] * (peers - 1)
    for r in range(peers - 1, 0, -1):
        got[r] = lax.ppermute(parts[r], "head", [(i, i ^ r) for i in range(peers)])
    return got


def pack_kernel(peers, first, width, at_ref, *rest):
    sources, outs, (held, sems) = rest[: -peers - 2], rest[-peers - 2 : -2], rest[-2:]
    inner = sources[0].shape[1] // peers
    order = list(range(peers - 1, -1, -1))
    parts, at = [], 0
    for k, source in enumerate(sources):
        size = width if k < 2 else source.shape[1]
        parts.append((source, at, size))
        at += size
    reads = {}
    for r in order:
        start = pl.multiple_of((at_ref[0] ^ r) * inner + first, LANES)
        for k, (source, at, size) in enumerate(parts):
            chosen = source.at[:, pl.ds(start, size)] if k < 2 else source
            reads[r, k] = pltpu.make_async_copy(
                chosen, held.at[r, :, pl.ds(at, size)], sems.at[0, r, k]
            )
            reads[r, k].start()
    writes = []
    for r in order:
        for k in range(len(parts)):
            reads[r, k].wait()
        writes.append(pltpu.make_async_copy(held.at[r], outs[r], sems.at[1, r, 0]))
        writes[-1].start()
    for write in writes:
        write.wait()


def pack(at, x, dy, riders, peers, first, width, behind):
    tokens = x.shape[0]
    full = 2 * width + sum(rider.shape[1] for rider in riders)
    count = 2 + len(riders)

    def kernel(at_ref, *rest):
        pack_kernel(peers, first, width, at_ref, *rest[:count], *rest[count + len(behind) :])

    return call(
        kernel,
        [jax.ShapeDtypeStruct((tokens, full), BF16)] * peers,
        (at, x, dy, *riders, *behind),
        in_specs=[smem()] + [anywhere()] * (count + len(behind)),
        out_specs=[anywhere()] * peers,
        scratch_shapes=[
            pltpu.VMEM((peers, tokens, full), BF16),
            pltpu.SemaphoreType.DMA((2, peers, count)),
        ],
        compiler_params=one_step(10),
        cost_estimate=LITTLE,
        name="pack",
    )


def prepare(heads, at_ref, small_ref, outs):
    col_ref, row_ref, in_ref, out_ref, dt_ref, tot_ref, b_ref, c_ref, bt_ref, ct_ref = outs
    length = small_ref.shape[0]
    shift = lax.rem(LANES - at_ref[0] * heads, LANES)
    steps = pltpu.roll(small_ref[:, 0:LANES].astype(F32), shift, 1)
    logs = pltpu.roll(small_ref[:, LANES : 2 * LANES].astype(F32), shift, 1)
    row = lax.broadcasted_iota(jnp.int32, (length, length), 0)
    col = lax.broadcasted_iota(jnp.int32, (length, length), 1)
    lower = jnp.where(row >= col, 1.0, 0.0).astype(BF16)
    cum = dot(lower, logs.astype(BF16)) * LOG2E
    total = cum[length - 1 : length, :]
    col_ref[...] = cum - jnp.log(steps) * LOG2E
    turned = cum.T
    per_group = row_ref.shape[1]
    for group in range(row_ref.shape[0]):
        row_ref[group] = turned[group * per_group : (group + 1) * per_group, :]
    in_ref[...] = jnp.exp2(total - cum) * steps
    out_ref[...] = jnp.exp2(cum)
    dt_ref[...] = steps
    tot_ref[...] = jnp.broadcast_to(total, tot_ref.shape)
    b = small_ref[:, 2 * LANES : 3 * LANES]
    c = small_ref[:, 3 * LANES : 4 * LANES]
    b_ref[...] = b
    c_ref[...] = c
    bt_ref[...] = b.astype(F32).T.astype(BF16)
    ct_ref[...] = c.astype(F32).T.astype(BF16)


def prepared(length, heads):
    tall = jax.ShapeDtypeStruct((length, LANES), F32)
    thin = jax.ShapeDtypeStruct((length, LANES), BF16)
    flat = jax.ShapeDtypeStruct((LANES, length), BF16)
    groups = jax.ShapeDtypeStruct((heads * WIDTH // COLS, COLS // WIDTH, length), F32)
    total = jax.ShapeDtypeStruct((8, LANES), F32)
    return [tall, groups, tall, tall, tall, total, thin, thin, flat, flat]


def put_in_order(head_ref, parts, rows_ref, sems):
    tokens = parts[0].shape[0]
    copies = []
    for r, part in enumerate(parts):
        start = pl.multiple_of((head_ref[0] ^ r) * tokens, tokens)
        copies.append(pltpu.make_async_copy(part, rows_ref.at[pl.ds(start, tokens), :], sems.at[r]))
        copies[-1].start()
    for copy in copies:
        copy.wait()


def add_up(first, weight_refs, map_refs, tot_ref, rows_ref, sum_ref):
    blocks, rows, inner = sum_ref.shape
    rows, inner = rows // 2, inner - LANES
    row = lax.broadcasted_iota(jnp.int32, (2 * rows, LANES), 0)
    total = jnp.zeros((2 * rows, LANES), F32)
    for k, term in enumerate(pieces(tot_ref[0:1, :], 3)):
        total = jnp.where(row == k, term.astype(F32), total)
    for block in range(blocks):
        sum_ref[block, :, inner:] = total.astype(BF16)
    weights = [pieces(ref[...], 2) for ref in weight_refs]
    for group in range(inner // COLS):
        here = slice(group * COLS, (group + 1) * COLS)
        select = selector(LANES, COLS, first + group * (COLS // WIDTH))
        for k in range(2):
            there = slice(k * inner + group * COLS, k * inner + (group + 1) * COLS)
            weight = sum(dot(term, select) for term in weights[k])
            weighted = rows_ref[:, there].astype(F32) * weight
            added = sum(dot(map_refs[k][...], term) for term in pieces(weighted, 2)).astype(BF16)
            for block in range(blocks):
                sum_ref[block, k * rows : (k + 1) * rows, here] = added[
                    block * rows : (block + 1) * rows, :
                ]


def opening_kernel(heads, peers, head_ref, *rest):
    parts, (rows_ref, sum_ref, sems) = rest[:peers], rest[-3:]
    outs = rest[peers : peers + 10]
    width = rows_ref.shape[1] - 4 * LANES
    put_in_order(head_ref, parts, rows_ref, sems)
    prepare(heads, head_ref, rows_ref.at[:, width:], outs)
    _, _, in_ref, out_ref, _, tot_ref, _, _, bt_ref, ct_ref = outs
    add_up(0, (in_ref, out_ref), (bt_ref, ct_ref), tot_ref, rows_ref, sum_ref)


def sum_shape(blocks, inner):
    return jax.ShapeDtypeStruct((blocks, 2 * LANES // blocks, inner + LANES), BF16)


def opening(head, parts, heads, blocks, inner):
    peers = len(parts)
    tokens, full = parts[0].shape
    rows = jax.ShapeDtypeStruct((tokens * peers, full), BF16)
    got = call(
        functools.partial(opening_kernel, heads, peers),
        prepared(tokens * peers, heads) + [rows, sum_shape(blocks, inner)],
        (head, *parts),
        in_specs=[smem()] + [anywhere()] * peers,
        scratch_shapes=[pltpu.SemaphoreType.DMA((peers,))],
        compiler_params=one_step(20),
        cost_estimate=LITTLE,
        name="opening",
    )
    return got[:10], got[10], got[11]


def states_kernel(first, peers, head_ref, in_ref, out_ref, bt_ref, ct_ref, tot_ref, *rest):
    parts, (rows_ref, sum_ref, sems) = rest[:peers], rest[-3:]
    put_in_order(head_ref, parts, rows_ref, sems)
    add_up(first, (in_ref, out_ref), (bt_ref, ct_ref), tot_ref, rows_ref, sum_ref)


def states(head, into, out_of, b_t, c_t, tot, parts, blocks, inner, first, behind):
    peers = len(parts)
    tokens, full = parts[0].shape
    rows = jax.ShapeDtypeStruct((tokens * peers, full), BF16)
    return call(
        functools.partial(states_kernel, first, peers),
        [rows, sum_shape(blocks, inner)],
        (head, into, out_of, b_t, c_t, tot, *parts, *behind),
        in_specs=[smem()] + [vmem()] * 5 + [anywhere()] * (peers + len(behind)),
        scratch_shapes=[pltpu.SemaphoreType.DMA((peers,))],
        compiler_params=one_step(16),
        cost_estimate=LITTLE,
        name="states",
    )


def decays(first, in_ref, select):
    blocks, _, full = in_ref.shape
    totals = [
        jnp.sum(in_ref[block, :, full - LANES :].astype(F32), axis=0, keepdims=True)
        for block in range(blocks)
    ]
    return spread(jnp.exp2(jnp.concatenate(totals, axis=0)), select, 3)


def total_kernel(first, at_ref, in_ref, *rest):
    out_ref = rest[-1]
    blocks, rows, inner = in_ref.shape
    rows, inner = rows // 2, inner - LANES
    decay = decays(first, in_ref, selector(LANES, inner, first))
    running = []
    for k, order in enumerate((range(blocks), range(blocks - 1, -1, -1))):
        here = slice(k * rows, (k + 1) * rows)
        value = jnp.zeros((rows, inner), F32)
        for block in order:
            step = decay[block : block + 1, :]
            value = step * value + in_ref[block, here, 0:inner].astype(F32)
        running.append(value)
    out_ref[...] = jnp.where(at_ref[0] < blocks, running[0], running[1])


def total_blocks(at, sums, first, behind):
    blocks, rows, inner = sums.shape
    return call(
        functools.partial(total_kernel, first),
        [jax.ShapeDtypeStruct((rows // 2, inner - LANES), F32)],
        (at, sums, *behind),
        free=(1,),
        in_specs=[smem(), vmem()] + [anywhere()] * len(behind),
        compiler_params=one_step(8),
        cost_estimate=LITTLE,
        name="total_blocks",
    )[0]


def scan_kernel(first, at_ref, in_ref, far_ref, *rest):
    out_ref, kept_ref = rest[-2:]
    blocks, rows, inner = in_ref.shape
    rows, inner = rows // 2, inner - LANES
    select = selector(LANES, inner, first)
    decay = decays(first, in_ref, select)
    second = at_ref[0] >= blocks
    through = []
    for k, order in enumerate((range(blocks), range(blocks - 1, -1, -1))):
        here = slice(k * rows, (k + 1) * rows)
        running = jnp.where(second == (k == 0), far_ref[...], 0.0)
        for block in order:
            out_ref[block, here, 0:inner] = running.astype(BF16)
            if k == 0:
                kept_ref[block] = running
            else:
                through.append(jnp.sum(kept_ref[block] * running, axis=0, keepdims=True))
            step = decay[block : block + 1, :]
            running = step * running + in_ref[block, here, 0:inner].astype(F32)
    link = gather(jnp.concatenate(through[::-1], axis=0), select, 3)
    high, low = (term.astype(F32) for term in pieces(link, 2))
    row = lax.broadcasted_iota(jnp.int32, (2 * rows, LANES), 0)
    for block in range(blocks):
        here = slice(block, block + 1)
        both = jnp.where(row == 0, high[here, :], jnp.where(row == 1, low[here, :], 0.0))
        out_ref[block, :, inner:] = both.astype(BF16)


def scan_blocks(at, sums, far, first, behind):
    blocks, rows, inner = sums.shape
    return call(
        functools.partial(scan_kernel, first),
        [jax.ShapeDtypeStruct(sums.shape, BF16)],
        (at, sums, far, *behind),
        scratch_shapes=[pltpu.VMEM((blocks, rows // 2, inner - LANES), F32)],
        free=(1, 2),
        in_specs=[smem(), vmem(), vmem()] + [anywhere()] * len(behind),
        compiler_params=one_step(8),
        cost_estimate=LITTLE,
        name="scan_blocks",
    )[0]


def across(sums):
    blocks = sums.shape[0]
    groups = [list(range(blocks)), list(range(blocks, 2 * blocks))]
    return lax.all_to_all(
        sums, "ctx", split_axis=0, concat_axis=0, tiled=True, axis_index_groups=groups
    )


def over(total):
    blocks = lax.axis_size("ctx")
    return lax.ppermute(total, "ctx", [(i, (i + blocks // 2) % blocks) for i in range(blocks)])


def stacked(ref, k):
    blocks, rows, _ = ref.shape
    rows //= 2
    return jnp.concatenate(
        [ref[block, k * rows : (k + 1) * rows, :] for block in range(blocks)], axis=0
    )


def inside_kernel(first, x_ref, dy_ref, b_ref, c_ref, col_ref, row_ref, *rest):
    added, (dx_ref, u_ref, v_ref, db_ref, dc_ref, s_ref, ds_ref) = rest[:-7], rest[-7:]
    length = x_ref.shape[0]
    tiles = length // LANES
    heads = COLS // WIDTH
    group = pl.program_id(0)
    from_k = lax.broadcasted_iota(jnp.int32, (length, length), 0)
    to_q = lax.broadcasted_iota(jnp.int32, (length, length), 1)

    @pl.when(group == 0)
    def _():
        s_ref[...] = jnp.where(to_q >= from_k, dot_nt(b_ref[...], c_ref[...]), 0.0)
        ds_ref[...] = jnp.zeros_like(ds_ref)
        v_ref[...] = jnp.zeros_like(v_ref)

    turned = pltpu.roll(col_ref[...], lax.rem(LANES - first - group * heads, LANES), 1)
    lane = lax.broadcasted_iota(jnp.int32, (LANES, LANES), 1)
    nothing = jnp.zeros((LANES, LANES), BF16)
    for first_tile in range(0, tiles, 2):
        low = first_tile * LANES
        both_tiles = slice(low, low + 2 * LANES)
        for pair in range(heads // 2):
            across = slice(pair * LANES, (pair + 1) * LANES)
            xs = x_ref[both_tiles, across]
            dys = dy_ref[low:, across]
            x_side = lax.broadcasted_iota(jnp.int32, xs.shape, 1) // WIDTH
            dy_side = lax.broadcasted_iota(jnp.int32, dys.shape, 1) // WIDTH
            own_x = [jnp.where(x_side == half, xs, jnp.zeros_like(xs)) for half in range(2)]
            products = dot_nt(jnp.concatenate(own_x, axis=0), dys)
            total = None
            for half in range(2):
                local = pair * 2 + half
                head = first + group * heads + local
                rows = []
                for sub in range(2):
                    j = first_tile + sub
                    here = slice(j * LANES, (j + 1) * LANES)
                    from_row = (half * 2 + sub) * LANES
                    behind = turned[here, local : local + 1]
                    kept = [nothing] * sub
                    v_sum = None
                    for i in range(j, tiles):
                        there = slice(i * LANES, (i + 1) * LANES)
                        at = (i - first_tile) * LANES
                        ahead = row_ref[0, local : local + 1, there]
                        decay = jnp.exp2(jnp.minimum(ahead - behind, 64.0))
                        product = products[from_row : from_row + LANES, at : at + LANES]
                        score = s_ref[here, there] * decay
                        kept.append(score.astype(BF16))
                        ds_ref[here, there] += decay * product
                        both = score * product
                        v_sum = both if v_sum is None else v_sum + both
                        u_sum = jnp.sum(both, axis=0, keepdims=True)
                        if j > 0:
                            u_sum += u_ref[0, local : local + 1, there]
                        u_ref[0, local : local + 1, there] = u_sum
                    v_col = jnp.sum(v_sum, axis=1, keepdims=True)
                    v_ref[here, :] = jnp.where(lane == head, v_col, v_ref[here, :])
                    rows.append(jnp.concatenate(kept, axis=1))
                own_dy = jnp.where(dy_side == half, dys, jnp.zeros_like(dys))
                part = dot(jnp.concatenate(rows, axis=0), own_dy)
                total = part if total is None else total + part
            dx_ref[both_tiles, across] = total

    @pl.when(group == pl.num_programs(0) - 1)
    def _():
        grads = jnp.where(to_q >= from_k, ds_ref[...], 0.0)
        db = sum(dot(term, c_ref[...]) for term in pieces(grads, 2))
        dc = sum(dot(term, b_ref[...]) for term in pieces(grads.T, 2))
        db_ref[...] = db + added[0][...] if added else db
        dc_ref[...] = dc + added[1][...] if added else dc


def inside(rows, inner, b, c, col_part, row_part, first, *added):
    added, behind = added[:2], added[2:]
    length = rows.shape[0]
    tall = jax.ShapeDtypeStruct((length, LANES), F32)
    pairs = length * length * inner
    offset = first * WIDTH // COLS
    by_group = pl.BlockSpec((1,) + row_part.shape[1:], lambda g: (g + offset, 0, 0))
    own_group = pl.BlockSpec((1,) + row_part.shape[1:], lambda g: (g, 0, 0))
    return call(
        functools.partial(inside_kernel, first),
        (
            jax.ShapeDtypeStruct((length, inner), F32),
            jax.ShapeDtypeStruct((inner // COLS,) + row_part.shape[1:], F32),
            tall,
            tall,
            tall,
        ),
        (rows, rows, b, c, col_part, row_part, *added, *behind),
        grid=(inner // COLS,),
        in_specs=[
            columns(length),
            columns(length, inner),
            whole(length, LANES),
            whole(length, LANES),
            whole(length, LANES),
            by_group,
        ]
        + [whole(length, LANES)] * len(added)
        + [anywhere()] * len(behind),
        out_specs=(
            columns(length),
            own_group,
            whole(length, LANES),
            whole(length, LANES),
            whole(length, LANES),
        ),
        scratch_shapes=[pltpu.VMEM((length, length), F32), pltpu.VMEM((length, length), F32)],
        compiler_params=params(20),
        cost_estimate=LITTLE,
        name="inside",
    )


def by_columns(shape):
    return pl.BlockSpec(shape[:2] + (WIDE,), lambda g: (0, 0, g))


def channels_kernel(peers, first, at_ref, dy_ref, dxi_ref, carry_ref, weight_ref, b_ref, skip_ref, *rest):
    outs, dx_ref = rest[-1 - peers : -1], rest[-1]
    tokens = dy_ref.shape[0] // peers
    select = selector(LANES, WIDE, first + pl.program_id(0) * (WIDE // WIDTH))
    carried = spread(weight_ref[...], select) * dot(b_ref[...], stacked(carry_ref, 1))
    gain = spread(skip_ref[...], select, 3)[0:1, :]
    dx_ref[...] = (dxi_ref[...] + carried + gain * dy_ref[...].astype(F32)).astype(BF16)
    for r in range(peers):
        start = pl.multiple_of((at_ref[0] ^ r) * tokens, tokens)
        outs[r][...] = dx_ref[pl.ds(start, tokens), :]


def channels(peers, first, at, rows, dxi, carry, weight, b, skip, behind):
    length, inner = dxi.shape
    tokens = length // peers
    tall = whole(length, LANES)
    return call(
        functools.partial(channels_kernel, peers, first),
        [jax.ShapeDtypeStruct((tokens, inner), BF16)] * peers,
        (at, rows, dxi, carry, weight, b, skip, *behind),
        grid=(inner // WIDE,),
        in_specs=[
            smem(),
            columns(length, inner, WIDE),
            columns(length, 0, WIDE),
            by_columns(carry.shape),
            tall,
            tall,
            whole(8, LANES),
        ]
        + [anywhere()] * len(behind),
        out_specs=[columns(tokens, 0, WIDE)] * peers,
        scratch_shapes=[pltpu.VMEM((length, WIDE), BF16)],
        compiler_params=params(16),
        cost_estimate=LITTLE,
        name="channels",
    )


def others_kernel(
    heads,
    peers,
    first,
    last,
    at_ref,
    x_ref,
    dy_ref,
    carry_ref,
    through_ref,
    into_ref,
    out_of_ref,
    b_ref,
    c_ref,
    dt_ref,
    tot_ref,
    ui_ref,
    vi_ref,
    *rest,
):
    if last:
        added = rest[:5]
    outs = rest[-5 - (peers if last else 3) : -5]
    db_ref, dc_ref, u_ref, v_ref, tail_ref = rest[-5:]
    length = x_ref.shape[0]
    tokens = length // peers
    group = pl.program_id(0)

    @pl.when(group == 0)
    def _():
        db_ref[...] = jnp.zeros_like(db_ref)
        dc_ref[...] = jnp.zeros_like(dc_ref)
        u_ref[...] = jnp.zeros_like(u_ref)
        v_ref[...] = jnp.zeros_like(v_ref)

    select = selector(LANES, WIDE, first + group * (WIDE // WIDTH))
    for source, weight_ref, k, near_ref, sum_ref, head_ref in (
        (x_ref, into_ref, 1, b_ref, db_ref, v_ref),
        (dy_ref, out_of_ref, 0, c_ref, dc_ref, u_ref),
    ):
        weighted = source[...].astype(F32) * spread(weight_ref[...], select)
        far = stacked(carry_ref, k)
        sum_ref[...] += dot_nt(weighted.astype(BF16), far)
        head_ref[...] += gather(weighted * dot(near_ref[...], far), select)

    @pl.when(group == pl.num_programs(0) - 1)
    def _():
        inner_v, outer_v = vi_ref[...], v_ref[...]
        steps = (inner_v + outer_v) / dt_ref[...]
        rows = [ui_ref[at] for at in range(ui_ref.shape[0])]
        if first > 0:
            rows.insert(0, jnp.zeros((first, length), F32))
        rows.append(jnp.zeros((LANES - sum(part.shape[0] for part in rows), length), F32))
        net = jnp.concatenate(rows, axis=0).T + u_ref[...] - inner_v - outer_v
        row = lax.broadcasted_iota(jnp.int32, (length, length), 0)
        col = lax.broadcasted_iota(jnp.int32, (length, length), 1)
        upper = jnp.where(col >= row, 1.0, 0.0).astype(BF16)
        later = sum(dot(upper, term) for term in pieces(net, 3))
        whole_block = jnp.sum(outer_v, axis=0, keepdims=True)
        link = sum(through_ref[block].astype(F32) for block in range(through_ref.shape[0]))
        link = jnp.sum(link, axis=0, keepdims=True)
        logs = later + whole_block + jnp.exp2(tot_ref[0:1, :]) * link
        thin = steps + pltpu.roll(logs, heads, 1)
        if not last:
            outs[0][...] = thin
            outs[1][...] = db_ref[...]
            outs[2][...] = dc_ref[...]
        else:
            thin_ref, dbo_ref, dco_ref, dbi_ref, dci_ref = added
            tail_ref[:, 0:LANES] = (thin + thin_ref[...]).astype(BF16)
            tail_ref[:, LANES : 2 * LANES] = (db_ref[...] + dbo_ref[...] + dbi_ref[...]).astype(BF16)
            tail_ref[:, 2 * LANES :] = (dc_ref[...] + dco_ref[...] + dci_ref[...]).astype(BF16)
            for r in range(peers):
                start = pl.multiple_of((at_ref[0] ^ r) * tokens, tokens)
                outs[r][...] = tail_ref[pl.ds(start, tokens), :]


def others(
    heads, peers, first, at, rows, inner, carry, into, out_of, b, c, dt, tot, ui, vi, added, behind
):
    length = rows.shape[0]
    tokens = length // peers
    tall = whole(length, LANES)
    last = len(added) > 0
    tall_shape = jax.ShapeDtypeStruct((length, LANES), F32)
    tail_shape = jax.ShapeDtypeStruct((tokens, 3 * LANES), BF16)
    return call(
        functools.partial(others_kernel, heads, peers, first, last),
        [tail_shape] * peers if last else [tall_shape] * 3,
        (at, rows, rows, carry, carry, into, out_of, b, c, dt, tot, ui, vi, *added, *behind),
        grid=(inner // WIDE,),
        in_specs=[
            smem(),
            columns(length, 0, WIDE),
            columns(length, inner, WIDE),
            by_columns(carry.shape),
            pl.BlockSpec(carry.shape[:2] + (LANES,), lambda g: (0, 0, inner // LANES)),
            tall,
            tall,
            tall,
            tall,
            tall,
            whole(8, LANES),
            whole(*ui.shape),
            tall,
        ]
        + [tall] * len(added)
        + [anywhere()] * len(behind),
        out_specs=[whole(tokens, 3 * LANES)] * peers if last else [tall] * 3,
        scratch_shapes=[pltpu.VMEM((length, LANES), F32)] * 4
        + [pltpu.VMEM((length, 3 * LANES), BF16)],
        compiler_params=params(24),
        cost_estimate=LITTLE,
        name="others",
    )


def put_columns(peers, half, head_ref, sent, held_ref, dx_ref, sems):
    width = sent[0].shape[1]
    reads = [
        pltpu.make_async_copy(sent[r], held_ref.at[r], sems.at[0, r]) for r in range(peers)
    ]
    for read in reads:
        read.start()
    writes = []
    for r in range(peers):
        reads[r].wait()
        start = pl.multiple_of(((head_ref[0] ^ r) * HALVES + half) * width, LANES)
        writes.append(
            pltpu.make_async_copy(
                held_ref.at[r], dx_ref.at[:, pl.ds(start, width)], sems.at[1, r]
            )
        )
        writes[-1].start()
    return writes


def place_kernel(peers, head_ref, *rest):
    dx_ref, held_ref, sems = rest[-3:]
    for write in put_columns(peers, 0, head_ref, rest[:peers], held_ref, dx_ref, sems):
        write.wait()


def place(head, sent, behind):
    peers = len(sent)
    tokens, width = sent[0].shape
    return call(
        functools.partial(place_kernel, peers),
        [jax.ShapeDtypeStruct((tokens, width * HALVES * peers), BF16)],
        (head, *sent, behind),
        in_specs=[smem()] + [anywhere()] * (peers + 1),
        out_specs=[anywhere()],
        scratch_shapes=[
            pltpu.VMEM((peers, tokens, width), BF16),
            pltpu.SemaphoreType.DMA((2, peers)),
        ],
        compiler_params=one_step(8),
        cost_estimate=LITTLE,
        name="place",
    )[0]


def finish_kernel(heads, peers, head_ref, _, *rest):
    sent, tails = rest[:peers], rest[peers : 2 * peers]
    dx_ref, steps_ref, logs_ref, db_ref, dc_ref, held_ref, sems, tail_ref, tail_sems = rest[
        2 * peers :
    ]
    tokens = sent[0].shape[0]
    reads = [
        pltpu.make_async_copy(tails[r], tail_ref.at[r], tail_sems.at[r]) for r in range(peers)
    ]
    for read in reads:
        read.start()
    writes = put_columns(peers, 1, head_ref, sent, held_ref, dx_ref, sems)
    lane = lax.broadcasted_iota(jnp.int32, (tokens, LANES), 1)
    results = [jnp.zeros((tokens, LANES), F32) for _ in range(4)]
    for r in range(peers):
        source = head_ref[0] ^ r
        own = lane // heads == source
        reads[r].wait()
        thin = tail_ref[r, :, 0:LANES].astype(F32)
        for k in range(2):
            shift = lax.rem((source - k) * heads + LANES, LANES)
            results[k] += jnp.where(own, pltpu.roll(thin, shift, 1), 0.0)
            results[2 + k] += tail_ref[r, :, (k + 1) * LANES : (k + 2) * LANES].astype(F32)
    steps_ref[...] = results[0].astype(BF16)
    logs_ref[...] = results[1].astype(BF16)
    db_ref[...] = results[2]
    dc_ref[...] = results[3]
    for write in writes:
        write.wait()


def finish(heads, head, placed, sent, tails):
    peers = len(tails)
    tokens, width = sent[0].shape
    thin = jax.ShapeDtypeStruct((tokens, LANES), BF16)
    wide = jax.ShapeDtypeStruct((tokens, LANES), F32)
    return call(
        functools.partial(finish_kernel, heads, peers),
        [jax.ShapeDtypeStruct(placed.shape, BF16), thin, thin, wide, wide],
        (head, placed, *sent, *tails),
        free=tuple(range(2, 2 + 2 * peers)),
        in_specs=[smem()] + [anywhere()] * (1 + 2 * peers),
        out_specs=[anywhere(), vmem(), vmem(), vmem(), vmem()],
        scratch_shapes=[
            pltpu.VMEM((peers, tokens, width), BF16),
            pltpu.SemaphoreType.DMA((2, peers)),
            pltpu.VMEM((peers,) + tails[0].shape, BF16),
            pltpu.SemaphoreType.DMA((peers,)),
        ],
        input_output_aliases={1: 0},
        compiler_params=one_step(8),
        cost_estimate=LITTLE,
        name="finish",
    )


HALVES = 2


def body(inputs, grad_out, steps, log_decay, input_map, output_map, skip_gain):
    blocks, peers = lax.axis_size("ctx") // 2, lax.axis_size("head")
    inner = inputs.shape[1] // peers
    heads = steps.shape[1] // peers
    width = inner // HALVES
    head = lax.axis_index("head").astype(jnp.int32).reshape(1)
    at = lax.axis_index("ctx").astype(jnp.int32).reshape(1)

    riders = (steps, log_decay, input_map, output_map)
    low = pack(head, inputs, grad_out, riders, peers, 0, width, ())
    high = pack(head, inputs, grad_out, (), peers, width, width, (low[0],))
    low, high = swap(low), swap(high)
    skip = jnp.broadcast_to(jnp.pad(skip_gain, (0, LANES - heads))[None], (8, LANES))
    half = heads // HALVES

    def begin(low):
        scalars, rows, sums = opening(head, low, heads, blocks, width)
        col_part, row_part, b, c = scalars[0], scalars[1], scalars[6], scalars[7]
        reached = across(sums)
        return scalars, rows, inside(rows, width, b, c, col_part, row_part, 0), reached

    def empty(low):
        return jax.tree.map(lambda a: jnp.zeros(a.shape, a.dtype), jax.eval_shape(begin, low))

    scalars, rows, pairs, reached = lax.cond(head[0] < peers, begin, empty, low)
    col_part, row_part, into, out_of, dt, tot, b, c, b_t, c_t = scalars
    dxi, ui, vi, dbi, dci = pairs

    total = total_blocks(at, reached, 0, (dxi, *high[1:]))
    far = over(total)
    rows_high, sums = states(head, into, out_of, b_t, c_t, tot, high, blocks, width, half, (total,))
    reached_high = across(sums)
    begun = scan_blocks(at, reached, far, 0, (sums,))
    total = total_blocks(at, reached_high, half, (begun,))
    far_high = over(total)
    carry = across(begun)
    dxi_high, ui_high, vi_high, dbi, dci = inside(
        rows_high, width, b, c, col_part, row_part, half, dbi, dci, total
    )
    begun = scan_blocks(at, reached_high, far_high, half, (dxi_high,))
    carry_high = across(begun)
    dx_low = channels(peers, 0, head, rows, dxi, carry, into, b, skip, (begun,))
    sent_low = swap(dx_low)
    added = others(
        heads, peers, 0, head, rows, width, carry, into, out_of, b, c, dt, tot, ui, vi, [],
        (dx_low[0],),
    )
    dx_high = channels(
        peers, half, head, rows_high, dxi_high, carry_high, into, b, skip, (added[0],)
    )
    sent_high = swap(dx_high)
    tails = others(
        heads, peers, half, head, rows_high, width, carry_high, into, out_of, b, c, dt, tot,
        ui_high, vi_high, [*added, dbi, dci], (dx_high[0], *sent_low[1:]),
    )
    placed = place(head, sent_low, tails[0])
    return tuple(finish(heads, head, placed, sent_high, swap(tails)))


def solution(mesh):
    rows = P(("ctx", "head"), None)
    return jax.shard_map(
        body,
        mesh=mesh,
        in_specs=(rows,) * 6 + (P("head"),),
        out_specs=(rows,) * 5,
        check_vma=False,
    )
```

```python
import functools

import jax
import jax.numpy as jnp
from jax import lax
from jax.experimental import pallas as pl
from jax.experimental.pallas import tpu as pltpu
from jax.sharding import PartitionSpec as P

F32 = jnp.float32
BF16 = jnp.bfloat16
LANES = 128
WIDTH = 64
COLS = 256
WIDE = 512
LOG2E = 1.4426950408889634
NT = (((1,), (1,)), ((), ()))
MIB = 1024 * 1024
LITTLE = pl.CostEstimate(flops=1000, bytes_accessed=1000, transcendentals=0)


def dot(a, b):
    return jnp.dot(a, b, preferred_element_type=F32)


def dot_nt(a, b):
    return lax.dot_general(a, b, NT, preferred_element_type=F32)


def pieces(a, count):
    terms = []
    for _ in range(count):
        term = a.astype(BF16)
        terms.append(term)
        a = a - term.astype(F32)
    return terms


def selector(rows, cols, first):
    row = lax.broadcasted_iota(jnp.int32, (rows, cols), 0)
    col = lax.broadcasted_iota(jnp.int32, (rows, cols), 1)
    return jnp.where((col // WIDTH) + first == row, 1.0, 0.0).astype(BF16)


def spread(a, select, count=2):
    return sum(dot(term, select) for term in pieces(a, count))


def gather(a, select, count=2):
    return sum(dot_nt(term, select) for term in pieces(a, count))


def params(mib):
    return pltpu.CompilerParams(dimension_semantics=("arbitrary",), vmem_limit_bytes=mib * MIB)


def whole(*shape):
    return pl.BlockSpec(shape, lambda *g: (0,) * len(shape))


def columns(rows, first=0, cols=COLS):
    return pl.BlockSpec((rows, cols), lambda g: (0, g + first // cols))


def call(kernel, out_shape, operands, free=(), **options):
    operands = [
        a
        if a.dtype == jnp.int32 or at in free
        else pltpu.with_memory_space_constraint(a, pltpu.HBM)
        for at, a in enumerate(operands)
    ]
    out_shape = [pltpu.HBM(one.shape, one.dtype) for one in out_shape]
    return pl.pallas_call(kernel, out_shape=out_shape, **options)(*operands)


def smem():
    return pl.BlockSpec(memory_space=pltpu.SMEM)


def anywhere():
    return pl.BlockSpec(memory_space=pl.ANY)


def vmem():
    return pl.BlockSpec(memory_space=pltpu.VMEM)


def one_step(mib):
    return pltpu.CompilerParams(vmem_limit_bytes=mib * MIB)


def swap(parts):
    peers = lax.axis_size("head")
    got = [parts[0]] + [None] * (peers - 1)
    for r in range(peers - 1, 0, -1):
        got[r] = lax.ppermute(parts[r], "head", [(i, i ^ r) for i in range(peers)])
    return got


def pack(head, x, dy, riders, peers, width, jobs, behind):
    tokens = x.shape[0]
    inner = x.shape[1] // peers
    rider = sum(one.shape[1] for one in riders)
    shapes = [(tokens, 2 * width + (0 if first else rider)) for _, first in jobs]
    count, fan = 2 + len(riders), len(jobs)

    def kernel(head_ref, *rest):
        sources, outs = rest[:count], rest[count + len(behind) : count + len(behind) + fan]
        helds, sems = rest[-fan - 1 : -1], rest[-1]
        reads = []
        for to, (r, first) in enumerate(jobs):
            start = pl.multiple_of((head_ref[0] ^ r) * inner + first, LANES)
            at, own = 0, []
            for k, source in enumerate(sources[: 2 if first else count]):
                size = width if k < 2 else source.shape[1]
                chosen = source.at[:, pl.ds(start, size)] if k < 2 else source
                target = helds[to].at[:, pl.ds(at, size)]
                own.append(pltpu.make_async_copy(chosen, target, sems.at[0, to, k]))
                own[-1].start()
                at += size
            reads.append(own)
        writes = []
        for to, own in enumerate(reads):
            for read in own:
                read.wait()
            writes.append(pltpu.make_async_copy(helds[to], outs[to], sems.at[1, to, 0]))
            writes[-1].start()
        for write in writes:
            write.wait()

    return call(
        kernel,
        [jax.ShapeDtypeStruct(shape, BF16) for shape in shapes],
        (head, x, dy, *riders, *behind),
        in_specs=[smem()] + [anywhere()] * (count + len(behind)),
        out_specs=[anywhere()] * fan,
        scratch_shapes=[pltpu.VMEM(shape, BF16) for shape in shapes]
        + [pltpu.SemaphoreType.DMA((2, fan, count))],
        compiler_params=one_step(10),
        cost_estimate=LITTLE,
        name="pack",
    )


def prepare(heads, at_ref, small_ref, outs):
    col_ref, row_ref, in_ref, out_ref, dt_ref, tot_ref, b_ref, c_ref, bt_ref, ct_ref = outs
    length = small_ref.shape[0]
    shift = lax.rem(LANES - at_ref[0] * heads, LANES)
    steps = pltpu.roll(small_ref[:, 0:LANES].astype(F32), shift, 1)
    logs = pltpu.roll(small_ref[:, LANES : 2 * LANES].astype(F32), shift, 1)
    row = lax.broadcasted_iota(jnp.int32, (length, length), 0)
    col = lax.broadcasted_iota(jnp.int32, (length, length), 1)
    lower = jnp.where(row >= col, 1.0, 0.0).astype(BF16)
    cum = dot(lower, logs.astype(BF16)) * LOG2E
    total = cum[length - 1 : length, :]
    col_ref[...] = cum - jnp.log(steps) * LOG2E
    turned = cum.T
    per_group = row_ref.shape[1]
    for group in range(row_ref.shape[0]):
        row_ref[group] = turned[group * per_group : (group + 1) * per_group, :]
    in_ref[...] = jnp.exp2(total - cum) * steps
    out_ref[...] = jnp.exp2(cum)
    dt_ref[...] = steps
    tot_ref[...] = jnp.broadcast_to(total, tot_ref.shape)
    b = small_ref[:, 2 * LANES : 3 * LANES]
    c = small_ref[:, 3 * LANES : 4 * LANES]
    b_ref[...] = b
    c_ref[...] = c
    bt_ref[...] = b.astype(F32).T.astype(BF16)
    ct_ref[...] = c.astype(F32).T.astype(BF16)


def prepared(length, heads):
    tall = jax.ShapeDtypeStruct((length, LANES), F32)
    thin = jax.ShapeDtypeStruct((length, LANES), BF16)
    flat = jax.ShapeDtypeStruct((LANES, length), BF16)
    groups = jax.ShapeDtypeStruct((heads * WIDTH // COLS, COLS // WIDTH, length), F32)
    total = jax.ShapeDtypeStruct((8, LANES), F32)
    return [tall, groups, tall, tall, tall, total, thin, thin, flat, flat]


class Arrivals:
    def __init__(self, head_ref, parts, held_ref, rows_ref, ranges, sems):
        tokens = parts[0].shape[0]
        self.ranges, self.held_ref, self.rows_ref, self.sems = ranges, held_ref, rows_ref, sems
        self.reads, self.writes = {}, []
        for k, (at, size) in enumerate(ranges):
            for r, part in enumerate(parts):
                start = pl.multiple_of((head_ref[0] ^ r) * tokens, tokens)
                self.reads[k, r] = pltpu.make_async_copy(
                    part.at[:, pl.ds(at, size)],
                    held_ref.at[pl.ds(start, tokens), pl.ds(at, size)],
                    sems.at[k, r],
                )
                self.reads[k, r].start()
        self.peers = len(parts)

    def wait(self, k):
        for r in range(self.peers):
            self.reads[k, r].wait()
        chosen = pl.ds(*self.ranges[k])
        self.writes.append(
            pltpu.make_async_copy(
                self.held_ref.at[:, chosen], self.rows_ref.at[:, chosen], self.sems.at[k, self.peers]
            )
        )
        self.writes[-1].start()

    def close(self):
        for write in self.writes:
            write.wait()


def add_up(first, weight_refs, map_refs, tot_ref, held_ref, sum_ref, arrivals):
    blocks, rows, inner = sum_ref.shape
    rows, inner = rows // 2, inner - LANES
    row = lax.broadcasted_iota(jnp.int32, (2 * rows, LANES), 0)
    total = jnp.zeros((2 * rows, LANES), F32)
    for k, term in enumerate(pieces(tot_ref[0:1, :], 3)):
        total = jnp.where(row == k, term.astype(F32), total)
    for block in range(blocks):
        sum_ref[block, :, inner:] = total.astype(BF16)
    weights = [pieces(ref[...], 2) for ref in weight_refs]
    for k in range(2):
        arrivals.wait(k)
        for group in range(inner // COLS):
            here = slice(group * COLS, (group + 1) * COLS)
            there = slice(k * inner + group * COLS, k * inner + (group + 1) * COLS)
            select = selector(LANES, COLS, first + group * (COLS // WIDTH))
            weight = sum(dot(term, select) for term in weights[k])
            weighted = held_ref[:, there].astype(F32) * weight
            added = sum(dot(map_refs[k][...], term) for term in pieces(weighted, 2)).astype(BF16)
            for block in range(blocks):
                sum_ref[block, k * rows : (k + 1) * rows, here] = added[
                    block * rows : (block + 1) * rows, :
                ]


def opening_kernel(heads, peers, head_ref, *rest):
    parts, (rows_ref, sum_ref, held_ref, sems) = rest[:peers], rest[-4:]
    outs = rest[peers : peers + 10]
    width = (held_ref.shape[1] - 4 * LANES) // 2
    ranges = ((0, width), (width, width), (2 * width, 4 * LANES))
    arrivals = Arrivals(head_ref, parts, held_ref, rows_ref, ranges, sems)
    arrivals.wait(2)
    prepare(heads, head_ref, held_ref.at[:, 2 * width :], outs)
    _, _, in_ref, out_ref, _, tot_ref, _, _, bt_ref, ct_ref = outs
    add_up(0, (in_ref, out_ref), (bt_ref, ct_ref), tot_ref, held_ref, sum_ref, arrivals)
    arrivals.close()


def sum_shape(blocks, inner):
    return jax.ShapeDtypeStruct((blocks, 2 * LANES // blocks, inner + LANES), BF16)


def opening(head, parts, heads, blocks, inner):
    peers = len(parts)
    tokens, full = parts[0].shape
    rows = jax.ShapeDtypeStruct((tokens * peers, full), BF16)
    got = call(
        functools.partial(opening_kernel, heads, peers),
        prepared(tokens * peers, heads) + [rows, sum_shape(blocks, inner)],
        (head, *parts),
        in_specs=[smem()] + [anywhere()] * peers,
        out_specs=[vmem()] * 10 + [anywhere(), vmem()],
        scratch_shapes=[
            pltpu.VMEM(rows.shape, BF16),
            pltpu.SemaphoreType.DMA((3, peers + 1)),
        ],
        compiler_params=one_step(20),
        cost_estimate=LITTLE,
        name="opening",
    )
    return got[:10], got[10], got[11]


def states_kernel(first, peers, head_ref, in_ref, out_ref, bt_ref, ct_ref, tot_ref, *rest):
    parts, (rows_ref, sum_ref, held_ref, sems) = rest[:peers], rest[-4:]
    width = held_ref.shape[1] // 2
    ranges = ((0, width), (width, width))
    arrivals = Arrivals(head_ref, parts, held_ref, rows_ref, ranges, sems)
    weights, maps = (in_ref, out_ref), (bt_ref, ct_ref)
    add_up(first, weights, maps, tot_ref, held_ref, sum_ref, arrivals)
    arrivals.close()


def states(head, into, out_of, b_t, c_t, tot, parts, blocks, inner, first, behind):
    peers = len(parts)
    tokens, full = parts[0].shape
    rows = jax.ShapeDtypeStruct((tokens * peers, full), BF16)
    return call(
        functools.partial(states_kernel, first, peers),
        [rows, sum_shape(blocks, inner)],
        (head, into, out_of, b_t, c_t, tot, *parts, *behind),
        in_specs=[smem()] + [vmem()] * 5 + [anywhere()] * (peers + len(behind)),
        out_specs=[anywhere(), vmem()],
        scratch_shapes=[
            pltpu.VMEM(rows.shape, BF16),
            pltpu.SemaphoreType.DMA((2, peers + 1)),
        ],
        compiler_params=one_step(16),
        cost_estimate=LITTLE,
        name="states",
    )


def decays(first, in_ref, select):
    blocks, _, full = in_ref.shape
    totals = [
        jnp.sum(in_ref[block, :, full - LANES :].astype(F32), axis=0, keepdims=True)
        for block in range(blocks)
    ]
    return spread(jnp.exp2(jnp.concatenate(totals, axis=0)), select, 3)


def total_kernel(first, at_ref, in_ref, *rest):
    out_ref = rest[-1]
    blocks, rows, inner = in_ref.shape
    rows, inner = rows // 2, inner - LANES
    decay = decays(first, in_ref, selector(LANES, inner, first))
    running = []
    for k, order in enumerate((range(blocks), range(blocks - 1, -1, -1))):
        here = slice(k * rows, (k + 1) * rows)
        value = jnp.zeros((rows, inner), F32)
        for block in order:
            step = decay[block : block + 1, :]
            value = step * value + in_ref[block, here, 0:inner].astype(F32)
        running.append(value)
    out_ref[...] = jnp.where(at_ref[0] < blocks, running[0], running[1])


def total_blocks(at, sums, first, behind):
    blocks, rows, inner = sums.shape
    return call(
        functools.partial(total_kernel, first),
        [jax.ShapeDtypeStruct((rows // 2, inner - LANES), F32)],
        (at, sums, *behind),
        free=(1,),
        in_specs=[smem(), vmem()] + [anywhere()] * len(behind),
        compiler_params=one_step(8),
        cost_estimate=LITTLE,
        name="total_blocks",
    )[0]


def scan_kernel(first, at_ref, in_ref, far_ref, *rest):
    out_ref, kept_ref = rest[-2:]
    blocks, rows, inner = in_ref.shape
    rows, inner = rows // 2, inner - LANES
    select = selector(LANES, inner, first)
    decay = decays(first, in_ref, select)
    second = at_ref[0] >= blocks
    through = []
    for k, order in enumerate((range(blocks), range(blocks - 1, -1, -1))):
        here = slice(k * rows, (k + 1) * rows)
        running = jnp.where(second == (k == 0), far_ref[...], 0.0)
        for block in order:
            out_ref[block, here, 0:inner] = running.astype(BF16)
            if k == 0:
                kept_ref[block] = running
            else:
                through.append(jnp.sum(kept_ref[block] * running, axis=0, keepdims=True))
            step = decay[block : block + 1, :]
            running = step * running + in_ref[block, here, 0:inner].astype(F32)
    link = gather(jnp.concatenate(through[::-1], axis=0), select, 3)
    high, low = (term.astype(F32) for term in pieces(link, 2))
    row = lax.broadcasted_iota(jnp.int32, (2 * rows, LANES), 0)
    for block in range(blocks):
        here = slice(block, block + 1)
        both = jnp.where(row == 0, high[here, :], jnp.where(row == 1, low[here, :], 0.0))
        out_ref[block, :, inner:] = both.astype(BF16)


def scan_blocks(at, sums, far, first, behind):
    blocks, rows, inner = sums.shape
    return call(
        functools.partial(scan_kernel, first),
        [jax.ShapeDtypeStruct(sums.shape, BF16)],
        (at, sums, far, *behind),
        scratch_shapes=[pltpu.VMEM((blocks, rows // 2, inner - LANES), F32)],
        free=(1, 2),
        in_specs=[smem(), vmem(), vmem()] + [anywhere()] * len(behind),
        compiler_params=one_step(8),
        cost_estimate=LITTLE,
        name="scan_blocks",
    )[0]


def across(sums):
    blocks = sums.shape[0]
    groups = [list(range(blocks)), list(range(blocks, 2 * blocks))]
    return lax.all_to_all(
        sums, "ctx", split_axis=0, concat_axis=0, tiled=True, axis_index_groups=groups
    )


def over(total):
    blocks = lax.axis_size("ctx")
    return lax.ppermute(total, "ctx", [(i, (i + blocks // 2) % blocks) for i in range(blocks)])


def stacked(ref, k):
    blocks, rows, _ = ref.shape
    rows //= 2
    return jnp.concatenate(
        [ref[block, k * rows : (k + 1) * rows, :] for block in range(blocks)], axis=0
    )


def inside_kernel(first, x_ref, dy_ref, b_ref, c_ref, col_ref, row_ref, *rest):
    added, (dx_ref, u_ref, v_ref, db_ref, dc_ref, s_ref, ds_ref) = rest[:-7], rest[-7:]
    length = x_ref.shape[0]
    tiles = length // LANES
    heads = COLS // WIDTH
    group = pl.program_id(0)
    from_k = lax.broadcasted_iota(jnp.int32, (length, length), 0)
    to_q = lax.broadcasted_iota(jnp.int32, (length, length), 1)

    @pl.when(group == 0)
    def _():
        s_ref[...] = jnp.where(to_q >= from_k, dot_nt(b_ref[...], c_ref[...]), 0.0)
        ds_ref[...] = jnp.zeros_like(ds_ref)
        v_ref[...] = jnp.zeros_like(v_ref)

    turned = pltpu.roll(col_ref[...], lax.rem(LANES - first - group * heads, LANES), 1)
    lane = lax.broadcasted_iota(jnp.int32, (LANES, LANES), 1)
    nothing = jnp.zeros((LANES, LANES), BF16)
    for first_tile in range(0, tiles, 2):
        low = first_tile * LANES
        both_tiles = slice(low, low + 2 * LANES)
        for pair in range(heads // 2):
            across = slice(pair * LANES, (pair + 1) * LANES)
            xs = x_ref[both_tiles, across]
            dys = dy_ref[low:, across]
            x_side = lax.broadcasted_iota(jnp.int32, xs.shape, 1) // WIDTH
            dy_side = lax.broadcasted_iota(jnp.int32, dys.shape, 1) // WIDTH
            own_x = [jnp.where(x_side == half, xs, jnp.zeros_like(xs)) for half in range(2)]
            products = dot_nt(jnp.concatenate(own_x, axis=0), dys)
            scores = [[], []]
            for sub in range(2):
                j = first_tile + sub
                here = slice(j * LANES, (j + 1) * LANES)
                locals_ = [pair * 2, pair * 2 + 1]
                behind = [
                    jnp.broadcast_to(turned[here, local : local + 1], (LANES, LANES))
                    for local in locals_
                ]
                kept = [[nothing] * sub, [nothing] * sub]
                v_sums = [None, None]
                for i in range(j, tiles):
                    there = slice(i * LANES, (i + 1) * LANES)
                    at = (i - first_tile) * LANES
                    near = s_ref[here, there]
                    change = None
                    for half, local in enumerate(locals_):
                        from_row = (half * 2 + sub) * LANES
                        power = row_ref[0, local : local + 1, there] - behind[half]
                        if i == j:
                            power = jnp.minimum(power, 64.0)
                        decay = jnp.exp2(power)
                        product = products[from_row : from_row + LANES, at : at + LANES]
                        score = near * decay
                        kept[half].append(score.astype(BF16))
                        spread_product = decay * product
                        change = spread_product if change is None else change + spread_product
                        both = score * product
                        v_sums[half] = both if v_sums[half] is None else v_sums[half] + both
                        u_sum = jnp.sum(both, axis=0, keepdims=True)
                        if j > 0:
                            u_sum += u_ref[0, local : local + 1, there]
                        u_ref[0, local : local + 1, there] = u_sum
                    ds_ref[here, there] += change
                v_cols = [jnp.sum(v_sum, axis=1, keepdims=True) for v_sum in v_sums]
                head = first + group * heads + pair * 2
                v_new = jnp.where(lane == head, v_cols[0], v_ref[here, :])
                v_ref[here, :] = jnp.where(lane == head + 1, v_cols[1], v_new)
                for half in range(2):
                    scores[half].append(jnp.concatenate(kept[half], axis=1))
            total = None
            for half in range(2):
                own_dy = jnp.where(dy_side == half, dys, jnp.zeros_like(dys))
                part = dot(jnp.concatenate(scores[half], axis=0), own_dy)
                total = part if total is None else total + part
            dx_ref[both_tiles, across] = total

    @pl.when(group == pl.num_programs(0) - 1)
    def _():
        grads = jnp.where(to_q >= from_k, ds_ref[...], 0.0)
        db = sum(dot(term, c_ref[...]) for term in pieces(grads, 2))
        dc = sum(dot(term, b_ref[...]) for term in pieces(grads.T, 2))
        db_ref[...] = db + added[0][...] if added else db
        dc_ref[...] = dc + added[1][...] if added else dc


def inside(rows, inner, b, c, col_part, row_part, first, *added):
    added, behind = added[:2], added[2:]
    length = rows.shape[0]
    tall = jax.ShapeDtypeStruct((length, LANES), F32)
    pairs = length * length * inner
    offset = first * WIDTH // COLS
    by_group = pl.BlockSpec((1,) + row_part.shape[1:], lambda g: (g + offset, 0, 0))
    own_group = pl.BlockSpec((1,) + row_part.shape[1:], lambda g: (g, 0, 0))
    return call(
        functools.partial(inside_kernel, first),
        (
            jax.ShapeDtypeStruct((length, inner), F32),
            jax.ShapeDtypeStruct((inner // COLS,) + row_part.shape[1:], F32),
            tall,
            tall,
            tall,
        ),
        (rows, rows, b, c, col_part, row_part, *added, *behind),
        grid=(inner // COLS,),
        in_specs=[
            columns(length),
            columns(length, inner),
            whole(length, LANES),
            whole(length, LANES),
            whole(length, LANES),
            by_group,
        ]
        + [whole(length, LANES)] * len(added)
        + [anywhere()] * len(behind),
        out_specs=(
            columns(length),
            own_group,
            whole(length, LANES),
            whole(length, LANES),
            whole(length, LANES),
        ),
        scratch_shapes=[pltpu.VMEM((length, length), F32), pltpu.VMEM((length, length), F32)],
        compiler_params=params(20),
        cost_estimate=LITTLE,
        name="inside",
    )


def by_columns(shape):
    return pl.BlockSpec(shape[:2] + (WIDE,), lambda g: (0, 0, g))


def channels_kernel(peers, first, at_ref, dy_ref, dxi_ref, carry_ref, weight_ref, b_ref, skip_ref, *rest):
    outs, dx_ref = rest[-1 - peers : -1], rest[-1]
    tokens = dy_ref.shape[0] // peers
    select = selector(LANES, WIDE, first + pl.program_id(0) * (WIDE // WIDTH))
    carried = spread(weight_ref[...], select) * dot(b_ref[...], stacked(carry_ref, 1))
    gain = spread(skip_ref[...], select, 3)[0:1, :]
    dx_ref[...] = (dxi_ref[...] + carried + gain * dy_ref[...].astype(F32)).astype(BF16)
    for r in range(peers):
        start = pl.multiple_of((at_ref[0] ^ r) * tokens, tokens)
        outs[r][...] = dx_ref[pl.ds(start, tokens), :]


def channels(peers, first, at, rows, dxi, carry, weight, b, skip, behind):
    length, inner = dxi.shape
    tokens = length // peers
    tall = whole(length, LANES)
    return call(
        functools.partial(channels_kernel, peers, first),
        [jax.ShapeDtypeStruct((tokens, inner), BF16)] * peers,
        (at, rows, dxi, carry, weight, b, skip, *behind),
        free=(3,),
        grid=(inner // WIDE,),
        in_specs=[
            smem(),
            columns(length, inner, WIDE),
            columns(length, 0, WIDE),
            by_columns(carry.shape),
            tall,
            tall,
            whole(8, LANES),
        ]
        + [anywhere()] * len(behind),
        out_specs=[columns(tokens, 0, WIDE)] * peers,
        scratch_shapes=[pltpu.VMEM((length, WIDE), BF16)],
        compiler_params=params(16),
        cost_estimate=LITTLE,
        name="channels",
    )


def others_kernel(
    heads,
    peers,
    first,
    last,
    at_ref,
    x_ref,
    dy_ref,
    carry_ref,
    through_ref,
    into_ref,
    out_of_ref,
    b_ref,
    c_ref,
    dt_ref,
    tot_ref,
    ui_ref,
    vi_ref,
    *rest,
):
    if last:
        added = rest[:5]
    outs = rest[-5 - (peers if last else 3) : -5]
    db_ref, dc_ref, u_ref, v_ref, tail_ref = rest[-5:]
    length = x_ref.shape[0]
    tokens = length // peers
    group = pl.program_id(0)

    @pl.when(group == 0)
    def _():
        db_ref[...] = jnp.zeros_like(db_ref)
        dc_ref[...] = jnp.zeros_like(dc_ref)
        u_ref[...] = jnp.zeros_like(u_ref)
        v_ref[...] = jnp.zeros_like(v_ref)

    select = selector(LANES, WIDE, first + group * (WIDE // WIDTH))
    for source, weight_ref, k, near_ref, sum_ref, head_ref in (
        (x_ref, into_ref, 1, b_ref, db_ref, v_ref),
        (dy_ref, out_of_ref, 0, c_ref, dc_ref, u_ref),
    ):
        weighted = source[...].astype(F32) * spread(weight_ref[...], select)
        far = stacked(carry_ref, k)
        sum_ref[...] += dot_nt(weighted.astype(BF16), far)
        head_ref[...] += gather(weighted * dot(near_ref[...], far), select)

    @pl.when(group == pl.num_programs(0) - 1)
    def _():
        inner_v, outer_v = vi_ref[...], v_ref[...]
        steps = (inner_v + outer_v) / dt_ref[...]
        rows = [ui_ref[at] for at in range(ui_ref.shape[0])]
        if first > 0:
            rows.insert(0, jnp.zeros((first, length), F32))
        rows.append(jnp.zeros((LANES - sum(part.shape[0] for part in rows), length), F32))
        net = jnp.concatenate(rows, axis=0).T + u_ref[...] - inner_v - outer_v
        row = lax.broadcasted_iota(jnp.int32, (length, length), 0)
        col = lax.broadcasted_iota(jnp.int32, (length, length), 1)
        upper = jnp.where(col >= row, 1.0, 0.0).astype(BF16)
        later = sum(dot(upper, term) for term in pieces(net, 3))
        whole_block = jnp.sum(outer_v, axis=0, keepdims=True)
        link = sum(through_ref[block].astype(F32) for block in range(through_ref.shape[0]))
        link = jnp.sum(link, axis=0, keepdims=True)
        logs = later + whole_block + jnp.exp2(tot_ref[0:1, :]) * link
        thin = steps + pltpu.roll(logs, heads, 1)
        if not last:
            outs[0][...] = thin
            outs[1][...] = db_ref[...]
            outs[2][...] = dc_ref[...]
        else:
            thin_ref, dbo_ref, dco_ref, dbi_ref, dci_ref = added
            tail_ref[:, 0:LANES] = (thin + thin_ref[...]).astype(BF16)
            tail_ref[:, LANES : 2 * LANES] = (db_ref[...] + dbo_ref[...] + dbi_ref[...]).astype(BF16)
            tail_ref[:, 2 * LANES :] = (dc_ref[...] + dco_ref[...] + dci_ref[...]).astype(BF16)
            for r in range(peers):
                start = pl.multiple_of((at_ref[0] ^ r) * tokens, tokens)
                outs[r][...] = tail_ref[pl.ds(start, tokens), :]


def others(
    heads, peers, first, at, rows, inner, carry, into, out_of, b, c, dt, tot, ui, vi, added, behind
):
    length = rows.shape[0]
    tokens = length // peers
    tall = whole(length, LANES)
    last = len(added) > 0
    tall_shape = jax.ShapeDtypeStruct((length, LANES), F32)
    tail_shape = jax.ShapeDtypeStruct((tokens, 3 * LANES), BF16)
    return call(
        functools.partial(others_kernel, heads, peers, first, last),
        [tail_shape] * peers if last else [tall_shape] * 3,
        (at, rows, rows, carry, carry, into, out_of, b, c, dt, tot, ui, vi, *added, *behind),
        grid=(inner // WIDE,),
        in_specs=[
            smem(),
            columns(length, 0, WIDE),
            columns(length, inner, WIDE),
            by_columns(carry.shape),
            pl.BlockSpec(carry.shape[:2] + (LANES,), lambda g: (0, 0, inner // LANES)),
            tall,
            tall,
            tall,
            tall,
            tall,
            whole(8, LANES),
            whole(*ui.shape),
            tall,
        ]
        + [tall] * len(added)
        + [anywhere()] * len(behind),
        out_specs=[whole(tokens, 3 * LANES)] * peers if last else [tall] * 3,
        scratch_shapes=[pltpu.VMEM((length, LANES), F32)] * 4
        + [pltpu.VMEM((length, 3 * LANES), BF16)],
        compiler_params=params(24),
        cost_estimate=LITTLE,
        name="others",
    )


def put_columns(peers, half, head_ref, sent, held_ref, dx_ref, sems):
    width = sent[0].shape[1]
    reads = [
        pltpu.make_async_copy(sent[r], held_ref.at[r], sems.at[0, r]) for r in range(peers)
    ]
    for read in reads:
        read.start()
    writes = []
    for r in range(peers):
        reads[r].wait()
        start = pl.multiple_of(((head_ref[0] ^ r) * HALVES + half) * width, LANES)
        writes.append(
            pltpu.make_async_copy(
                held_ref.at[r], dx_ref.at[:, pl.ds(start, width)], sems.at[1, r]
            )
        )
        writes[-1].start()
    return writes


def place_kernel(peers, head_ref, *rest):
    dx_ref, held_ref, sems = rest[-3:]
    for write in put_columns(peers, 0, head_ref, rest[:peers], held_ref, dx_ref, sems):
        write.wait()


def place(head, sent, behind):
    peers = len(sent)
    tokens, width = sent[0].shape
    return call(
        functools.partial(place_kernel, peers),
        [jax.ShapeDtypeStruct((tokens, width * HALVES * peers), BF16)],
        (head, *sent, behind),
        in_specs=[smem()] + [anywhere()] * (peers + 1),
        out_specs=[anywhere()],
        scratch_shapes=[
            pltpu.VMEM((peers, tokens, width), BF16),
            pltpu.SemaphoreType.DMA((2, peers)),
        ],
        compiler_params=one_step(8),
        cost_estimate=LITTLE,
        name="place",
    )[0]


def finish_kernel(heads, peers, head_ref, _, *rest):
    sent, tails = rest[:peers], rest[peers : 2 * peers]
    dx_ref, steps_ref, logs_ref, db_ref, dc_ref, held_ref, sems, tail_ref, tail_sems = rest[
        2 * peers :
    ]
    tokens = sent[0].shape[0]
    reads = [
        pltpu.make_async_copy(tails[r], tail_ref.at[r], tail_sems.at[r]) for r in range(peers)
    ]
    for read in reads:
        read.start()
    writes = put_columns(peers, 1, head_ref, sent, held_ref, dx_ref, sems)
    lane = lax.broadcasted_iota(jnp.int32, (tokens, LANES), 1)
    results = [jnp.zeros((tokens, LANES), F32) for _ in range(4)]
    for r in range(peers):
        source = head_ref[0] ^ r
        own = lane // heads == source
        reads[r].wait()
        thin = tail_ref[r, :, 0:LANES].astype(F32)
        for k in range(2):
            shift = lax.rem((source - k) * heads + LANES, LANES)
            results[k] += jnp.where(own, pltpu.roll(thin, shift, 1), 0.0)
            results[2 + k] += tail_ref[r, :, (k + 1) * LANES : (k + 2) * LANES].astype(F32)
    steps_ref[...] = results[0].astype(BF16)
    logs_ref[...] = results[1].astype(BF16)
    db_ref[...] = results[2]
    dc_ref[...] = results[3]
    for write in writes:
        write.wait()


def finish(heads, head, placed, sent, tails):
    peers = len(tails)
    tokens, width = sent[0].shape
    thin = jax.ShapeDtypeStruct((tokens, LANES), BF16)
    wide = jax.ShapeDtypeStruct((tokens, LANES), F32)
    return call(
        functools.partial(finish_kernel, heads, peers),
        [jax.ShapeDtypeStruct(placed.shape, BF16), thin, thin, wide, wide],
        (head, placed, *sent, *tails),
        free=tuple(range(2, 2 + 2 * peers)),
        in_specs=[smem()] + [anywhere()] * (1 + 2 * peers),
        out_specs=[anywhere(), vmem(), vmem(), vmem(), vmem()],
        scratch_shapes=[
            pltpu.VMEM((peers, tokens, width), BF16),
            pltpu.SemaphoreType.DMA((2, peers)),
            pltpu.VMEM((peers,) + tails[0].shape, BF16),
            pltpu.SemaphoreType.DMA((peers,)),
        ],
        input_output_aliases={1: 0},
        compiler_params=one_step(8),
        cost_estimate=LITTLE,
        name="finish",
    )


HALVES = 2


def body(inputs, grad_out, steps, log_decay, input_map, output_map, skip_gain):
    blocks, peers = lax.axis_size("ctx") // 2, lax.axis_size("head")
    inner = inputs.shape[1] // peers
    heads = steps.shape[1] // peers
    width = inner // HALVES
    head = lax.axis_index("head").astype(jnp.int32).reshape(1)
    at = lax.axis_index("ctx").astype(jnp.int32).reshape(1)

    riders = (steps, log_decay, input_map, output_map)
    near, distant = tuple(range(min(2, peers))), tuple(range(2, peers))
    jobs = [(r, 0) for r in distant]
    low = pack(head, inputs, grad_out, riders, peers, width, jobs, ()) if distant else []
    jobs = [(r, 0) for r in near] + [(r, width) for r in near + distant]
    rest = pack(head, inputs, grad_out, riders, peers, width, jobs, tuple(low[:1]))
    low, high = [*rest[: len(near)], *low], rest[len(near) :]
    low, high = swap(low), swap(high)
    skip = jnp.broadcast_to(jnp.pad(skip_gain, (0, LANES - heads))[None], (8, LANES))
    half = heads // HALVES

    def begin(low):
        scalars, rows, sums = opening(head, low, heads, blocks, width)
        col_part, row_part, b, c = scalars[0], scalars[1], scalars[6], scalars[7]
        reached = across(sums)
        return scalars, rows, inside(rows, width, b, c, col_part, row_part, 0), reached

    def empty(low):
        return jax.tree.map(lambda a: jnp.zeros(a.shape, a.dtype), jax.eval_shape(begin, low))

    scalars, rows, pairs, reached = lax.cond(head[0] < peers, begin, empty, low)
    col_part, row_part, into, out_of, dt, tot, b, c, b_t, c_t = scalars
    dxi, ui, vi, dbi, dci = pairs

    total = total_blocks(at, reached, 0, (dxi, *high[1:]))
    far = over(total)
    rows_high, sums = states(head, into, out_of, b_t, c_t, tot, high, blocks, width, half, (total,))
    reached_high = across(sums)
    begun = scan_blocks(at, reached, far, 0, (sums,))
    total = total_blocks(at, reached_high, half, (begun,))
    far_high = over(total)
    carry = across(begun)
    dxi_high, ui_high, vi_high, dbi, dci = inside(
        rows_high, width, b, c, col_part, row_part, half, dbi, dci, total
    )
    begun = scan_blocks(at, reached_high, far_high, half, (dxi_high,))
    carry_high = across(begun)
    dx_low = channels(peers, 0, head, rows, dxi, carry, into, b, skip, (begun,))
    sent_low = swap(dx_low)
    added = others(
        heads, peers, 0, head, rows, width, carry, into, out_of, b, c, dt, tot, ui, vi, [],
        (dx_low[0],),
    )
    dx_high = channels(
        peers, half, head, rows_high, dxi_high, carry_high, into, b, skip, (added[0],)
    )
    sent_high = swap(dx_high)
    tails = others(
        heads, peers, half, head, rows_high, width, carry_high, into, out_of, b, c, dt, tot,
        ui_high, vi_high, [*added, dbi, dci], (dx_high[0], *sent_low[1:]),
    )
    placed = place(head, sent_low, tails[0])
    return tuple(finish(heads, head, placed, sent_high, swap(tails)))


def solution(mesh):
    rows = P(("ctx", "head"), None)
    return jax.shard_map(
        body,
        mesh=mesh,
        in_specs=(rows,) * 6 + (P("head"),),
        out_specs=(rows,) * 5,
        check_vma=False,
    )
```

```python
import functools

import jax
import jax.numpy as jnp
from jax import lax
from jax.experimental import pallas as pl
from jax.experimental.pallas import tpu as pltpu
from jax.sharding import PartitionSpec as P

F32 = jnp.float32
BF16 = jnp.bfloat16
LANES = 128
WIDTH = 64
COLS = 256
WIDE = 512
LOG2E = 1.4426950408889634
NT = (((1,), (1,)), ((), ()))
MIB = 1024 * 1024
LITTLE = pl.CostEstimate(flops=1000, bytes_accessed=1000, transcendentals=0)


def dot(a, b):
    return jnp.dot(a, b, preferred_element_type=F32)


def dot_nt(a, b):
    return lax.dot_general(a, b, NT, preferred_element_type=F32)


def pieces(a, count):
    terms = []
    for _ in range(count):
        term = a.astype(BF16)
        terms.append(term)
        a = a - term.astype(F32)
    return terms


def selector(rows, cols, first):
    row = lax.broadcasted_iota(jnp.int32, (rows, cols), 0)
    col = lax.broadcasted_iota(jnp.int32, (rows, cols), 1)
    return jnp.where((col // WIDTH) + first == row, 1.0, 0.0).astype(BF16)


def spread(a, select, count=2):
    return sum(dot(term, select) for term in pieces(a, count))


def gather(a, select, count=2):
    return sum(dot_nt(term, select) for term in pieces(a, count))


def params(mib):
    return pltpu.CompilerParams(dimension_semantics=("arbitrary",), vmem_limit_bytes=mib * MIB)


def whole(*shape):
    return pl.BlockSpec(shape, lambda *g: (0,) * len(shape))


def columns(rows, first=0, cols=COLS):
    return pl.BlockSpec((rows, cols), lambda g: (0, g + first // cols))


def call(kernel, out_shape, operands, free=(), **options):
    operands = [
        a
        if a.dtype == jnp.int32 or at in free
        else pltpu.with_memory_space_constraint(a, pltpu.HBM)
        for at, a in enumerate(operands)
    ]
    out_shape = [pltpu.HBM(one.shape, one.dtype) for one in out_shape]
    return pl.pallas_call(kernel, out_shape=out_shape, **options)(*operands)


def smem():
    return pl.BlockSpec(memory_space=pltpu.SMEM)


def anywhere():
    return pl.BlockSpec(memory_space=pl.ANY)


def vmem():
    return pl.BlockSpec(memory_space=pltpu.VMEM)


def one_step(mib):
    return pltpu.CompilerParams(vmem_limit_bytes=mib * MIB)


def swap(parts):
    peers = lax.axis_size("head")
    got = [parts[0]] + [None] * (peers - 1)
    for r in range(peers - 1, 0, -1):
        got[r] = lax.ppermute(parts[r], "head", [(i, i ^ r) for i in range(peers)])
    return got


def pack(head, x, dy, riders, peers, width, jobs, behind):
    tokens = x.shape[0]
    inner = x.shape[1] // peers
    rider = sum(one.shape[1] for one in riders)
    shapes = [(tokens, 2 * width + (0 if first else rider)) for _, first in jobs]
    count, fan = 2 + len(riders), len(jobs)

    def kernel(head_ref, *rest):
        sources, outs = rest[:count], rest[count + len(behind) : count + len(behind) + fan]
        helds, sems = rest[-fan - 1 : -1], rest[-1]
        reads = []
        for to, (r, first) in enumerate(jobs):
            start = pl.multiple_of((head_ref[0] ^ r) * inner + first, LANES)
            at, own = 0, []
            for k, source in enumerate(sources[: 2 if first else count]):
                size = width if k < 2 else source.shape[1]
                chosen = source.at[:, pl.ds(start, size)] if k < 2 else source
                target = helds[to].at[:, pl.ds(at, size)]
                own.append(pltpu.make_async_copy(chosen, target, sems.at[0, to, k]))
                own[-1].start()
                at += size
            reads.append(own)
        writes = []
        for to, own in enumerate(reads):
            for read in own:
                read.wait()
            writes.append(pltpu.make_async_copy(helds[to], outs[to], sems.at[1, to, 0]))
            writes[-1].start()
        for write in writes:
            write.wait()

    return call(
        kernel,
        [jax.ShapeDtypeStruct(shape, BF16) for shape in shapes],
        (head, x, dy, *riders, *behind),
        in_specs=[smem()] + [anywhere()] * (count + len(behind)),
        out_specs=[anywhere()] * fan,
        scratch_shapes=[pltpu.VMEM(shape, BF16) for shape in shapes]
        + [pltpu.SemaphoreType.DMA((2, fan, count))],
        compiler_params=one_step(10),
        cost_estimate=LITTLE,
        name="pack",
    )


def prepare(heads, at_ref, small_ref, outs):
    col_ref, row_ref, in_ref, out_ref, dt_ref, tot_ref, b_ref, c_ref, bt_ref, ct_ref = outs
    length = small_ref.shape[0]
    shift = lax.rem(LANES - at_ref[0] * heads, LANES)
    steps = pltpu.roll(small_ref[:, 0:LANES].astype(F32), shift, 1)
    logs = pltpu.roll(small_ref[:, LANES : 2 * LANES].astype(F32), shift, 1)
    row = lax.broadcasted_iota(jnp.int32, (length, length), 0)
    col = lax.broadcasted_iota(jnp.int32, (length, length), 1)
    lower = jnp.where(row >= col, 1.0, 0.0).astype(BF16)
    cum = dot(lower, logs.astype(BF16)) * LOG2E
    total = cum[length - 1 : length, :]
    col_ref[...] = cum - jnp.log(steps) * LOG2E
    turned = cum.T
    per_group = row_ref.shape[1]
    for group in range(row_ref.shape[0]):
        row_ref[group] = turned[group * per_group : (group + 1) * per_group, :]
    in_ref[...] = jnp.exp2(total - cum) * steps
    out_ref[...] = jnp.exp2(cum)
    dt_ref[...] = steps
    tot_ref[...] = jnp.broadcast_to(total, tot_ref.shape)
    b = small_ref[:, 2 * LANES : 3 * LANES]
    c = small_ref[:, 3 * LANES : 4 * LANES]
    b_ref[...] = b
    c_ref[...] = c
    bt_ref[...] = b.astype(F32).T.astype(BF16)
    ct_ref[...] = c.astype(F32).T.astype(BF16)


def prepared(length, heads):
    tall = jax.ShapeDtypeStruct((length, LANES), F32)
    thin = jax.ShapeDtypeStruct((length, LANES), BF16)
    flat = jax.ShapeDtypeStruct((LANES, length), BF16)
    groups = jax.ShapeDtypeStruct((heads * WIDTH // COLS, COLS // WIDTH, length), F32)
    total = jax.ShapeDtypeStruct((8, LANES), F32)
    return [tall, groups, tall, tall, tall, total, thin, thin, flat, flat]


class Arrivals:
    def __init__(self, head_ref, parts, held_ref, rows_ref, ranges, sems):
        tokens = parts[0].shape[0]
        self.ranges, self.held_ref, self.rows_ref, self.sems = ranges, held_ref, rows_ref, sems
        self.reads, self.writes = {}, []
        for k in sorted(range(len(ranges)), key=lambda k: ranges[k][1]):
            at, size = ranges[k]
            for r, part in enumerate(parts):
                start = pl.multiple_of((head_ref[0] ^ r) * tokens, tokens)
                self.reads[k, r] = pltpu.make_async_copy(
                    part.at[:, pl.ds(at, size)],
                    held_ref.at[pl.ds(start, tokens), pl.ds(at, size)],
                    sems.at[k, r],
                )
                self.reads[k, r].start()
        self.peers = len(parts)

    def wait(self, k):
        for r in range(self.peers):
            self.reads[k, r].wait()
        chosen = pl.ds(*self.ranges[k])
        self.writes.append(
            pltpu.make_async_copy(
                self.held_ref.at[:, chosen], self.rows_ref.at[:, chosen], self.sems.at[k, self.peers]
            )
        )
        self.writes[-1].start()

    def close(self):
        for write in self.writes:
            write.wait()


def add_up(first, weight_refs, map_refs, tot_ref, held_ref, sum_ref, arrivals):
    blocks, rows, inner = sum_ref.shape
    rows, inner = rows // 2, inner - LANES
    row = lax.broadcasted_iota(jnp.int32, (2 * rows, LANES), 0)
    total = jnp.zeros((2 * rows, LANES), F32)
    for k, term in enumerate(pieces(tot_ref[0:1, :], 3)):
        total = jnp.where(row == k, term.astype(F32), total)
    for block in range(blocks):
        sum_ref[block, :, inner:] = total.astype(BF16)
    weights = [pieces(ref[...], 2) for ref in weight_refs]
    for k in range(2):
        arrivals.wait(k)
        for group in range(inner // COLS):
            here = slice(group * COLS, (group + 1) * COLS)
            there = slice(k * inner + group * COLS, k * inner + (group + 1) * COLS)
            select = selector(LANES, COLS, first + group * (COLS // WIDTH))
            weight = sum(dot(term, select) for term in weights[k])
            weighted = held_ref[:, there].astype(F32) * weight
            added = sum(dot(map_refs[k][...], term) for term in pieces(weighted, 2)).astype(BF16)
            for block in range(blocks):
                sum_ref[block, k * rows : (k + 1) * rows, here] = added[
                    block * rows : (block + 1) * rows, :
                ]


def opening_kernel(heads, peers, head_ref, *rest):
    parts, (rows_ref, sum_ref, held_ref, sems) = rest[:peers], rest[-4:]
    outs = rest[peers : peers + 10]
    width = (held_ref.shape[1] - 4 * LANES) // 2
    ranges = ((0, width), (width, width), (2 * width, 4 * LANES))
    arrivals = Arrivals(head_ref, parts, held_ref, rows_ref, ranges, sems)
    arrivals.wait(2)
    prepare(heads, head_ref, held_ref.at[:, 2 * width :], outs)
    _, _, in_ref, out_ref, _, tot_ref, _, _, bt_ref, ct_ref = outs
    add_up(0, (in_ref, out_ref), (bt_ref, ct_ref), tot_ref, held_ref, sum_ref, arrivals)
    arrivals.close()


def sum_shape(blocks, inner):
    return jax.ShapeDtypeStruct((blocks, 2 * LANES // blocks, inner + LANES), BF16)


def opening(head, parts, heads, blocks, inner):
    peers = len(parts)
    tokens, full = parts[0].shape
    rows = jax.ShapeDtypeStruct((tokens * peers, full), BF16)
    got = call(
        functools.partial(opening_kernel, heads, peers),
        prepared(tokens * peers, heads) + [rows, sum_shape(blocks, inner)],
        (head, *parts),
        in_specs=[smem()] + [anywhere()] * peers,
        out_specs=[vmem()] * 10 + [anywhere(), vmem()],
        scratch_shapes=[
            pltpu.VMEM(rows.shape, BF16),
            pltpu.SemaphoreType.DMA((3, peers + 1)),
        ],
        compiler_params=one_step(20),
        cost_estimate=LITTLE,
        name="opening",
    )
    return got[:10], got[10], got[11]


def states_kernel(first, peers, head_ref, in_ref, out_ref, bt_ref, ct_ref, tot_ref, *rest):
    parts, (rows_ref, sum_ref, held_ref, sems) = rest[:peers], rest[-4:]
    width = held_ref.shape[1] // 2
    ranges = ((0, width), (width, width))
    arrivals = Arrivals(head_ref, parts, held_ref, rows_ref, ranges, sems)
    weights, maps = (in_ref, out_ref), (bt_ref, ct_ref)
    add_up(first, weights, maps, tot_ref, held_ref, sum_ref, arrivals)
    arrivals.close()


def states(head, into, out_of, b_t, c_t, tot, parts, blocks, inner, first, behind):
    peers = len(parts)
    tokens, full = parts[0].shape
    rows = jax.ShapeDtypeStruct((tokens * peers, full), BF16)
    return call(
        functools.partial(states_kernel, first, peers),
        [rows, sum_shape(blocks, inner)],
        (head, into, out_of, b_t, c_t, tot, *parts, *behind),
        in_specs=[smem()] + [vmem()] * 5 + [anywhere()] * (peers + len(behind)),
        out_specs=[anywhere(), vmem()],
        scratch_shapes=[
            pltpu.VMEM(rows.shape, BF16),
            pltpu.SemaphoreType.DMA((2, peers + 1)),
        ],
        compiler_params=one_step(16),
        cost_estimate=LITTLE,
        name="states",
    )


def decays(first, in_ref, select):
    blocks, _, full = in_ref.shape
    totals = [
        jnp.sum(in_ref[block, :, full - LANES :].astype(F32), axis=0, keepdims=True)
        for block in range(blocks)
    ]
    return spread(jnp.exp2(jnp.concatenate(totals, axis=0)), select, 3)


def total_kernel(first, at_ref, in_ref, *rest):
    out_ref = rest[-1]
    blocks, rows, inner = in_ref.shape
    rows, inner = rows // 2, inner - LANES
    decay = decays(first, in_ref, selector(LANES, inner, first))
    running = []
    for k, order in enumerate((range(blocks), range(blocks - 1, -1, -1))):
        here = slice(k * rows, (k + 1) * rows)
        value = jnp.zeros((rows, inner), F32)
        for block in order:
            step = decay[block : block + 1, :]
            value = step * value + in_ref[block, here, 0:inner].astype(F32)
        running.append(value)
    out_ref[...] = jnp.where(at_ref[0] < blocks, running[0], running[1])


def total_blocks(at, sums, first, behind):
    blocks, rows, inner = sums.shape
    return call(
        functools.partial(total_kernel, first),
        [jax.ShapeDtypeStruct((rows // 2, inner - LANES), F32)],
        (at, sums, *behind),
        free=(1,),
        in_specs=[smem(), vmem()] + [anywhere()] * len(behind),
        compiler_params=one_step(8),
        cost_estimate=LITTLE,
        name="total_blocks",
    )[0]


def scan_kernel(first, at_ref, in_ref, far_ref, *rest):
    out_ref, kept_ref = rest[-2:]
    blocks, rows, inner = in_ref.shape
    rows, inner = rows // 2, inner - LANES
    select = selector(LANES, inner, first)
    decay = decays(first, in_ref, select)
    second = at_ref[0] >= blocks
    through = []
    for k, order in enumerate((range(blocks), range(blocks - 1, -1, -1))):
        here = slice(k * rows, (k + 1) * rows)
        running = jnp.where(second == (k == 0), far_ref[...], 0.0)
        for block in order:
            out_ref[block, here, 0:inner] = running.astype(BF16)
            if k == 0:
                kept_ref[block] = running
            else:
                through.append(jnp.sum(kept_ref[block] * running, axis=0, keepdims=True))
            step = decay[block : block + 1, :]
            running = step * running + in_ref[block, here, 0:inner].astype(F32)
    link = gather(jnp.concatenate(through[::-1], axis=0), select, 3)
    high, low = (term.astype(F32) for term in pieces(link, 2))
    row = lax.broadcasted_iota(jnp.int32, (2 * rows, LANES), 0)
    for block in range(blocks):
        here = slice(block, block + 1)
        both = jnp.where(row == 0, high[here, :], jnp.where(row == 1, low[here, :], 0.0))
        out_ref[block, :, inner:] = both.astype(BF16)


def scan_blocks(at, sums, far, first, behind):
    blocks, rows, inner = sums.shape
    return call(
        functools.partial(scan_kernel, first),
        [jax.ShapeDtypeStruct(sums.shape, BF16)],
        (at, sums, far, *behind),
        scratch_shapes=[pltpu.VMEM((blocks, rows // 2, inner - LANES), F32)],
        free=(1, 2),
        in_specs=[smem(), vmem(), vmem()] + [anywhere()] * len(behind),
        compiler_params=one_step(8),
        cost_estimate=LITTLE,
        name="scan_blocks",
    )[0]


def across(sums):
    blocks = sums.shape[0]
    groups = [list(range(blocks)), list(range(blocks, 2 * blocks))]
    return lax.all_to_all(
        sums, "ctx", split_axis=0, concat_axis=0, tiled=True, axis_index_groups=groups
    )


def over(total):
    blocks = lax.axis_size("ctx")
    return lax.ppermute(total, "ctx", [(i, (i + blocks // 2) % blocks) for i in range(blocks)])


def stacked(ref, k):
    blocks, rows, _ = ref.shape
    rows //= 2
    return jnp.concatenate(
        [ref[block, k * rows : (k + 1) * rows, :] for block in range(blocks)], axis=0
    )


def inside_kernel(first, x_ref, dy_ref, b_ref, c_ref, col_ref, row_ref, *rest):
    added, (dx_ref, u_ref, v_ref, db_ref, dc_ref, s_ref, ds_ref) = rest[:3], rest[-7:]
    added = added if len(rest) >= 10 else ()
    length = x_ref.shape[0]
    tiles = length // LANES
    heads = COLS // WIDTH
    group = pl.program_id(0)
    from_k = lax.broadcasted_iota(jnp.int32, (length, length), 0)
    to_q = lax.broadcasted_iota(jnp.int32, (length, length), 1)

    @pl.when(group == 0)
    def _():
        s_ref[...] = jnp.where(to_q >= from_k, dot_nt(b_ref[...], c_ref[...]), 0.0)
        ds_ref[...] = jnp.zeros_like(ds_ref)
        v_ref[...] = added[2][...] if added else jnp.zeros_like(v_ref)

    turned = pltpu.roll(col_ref[...], lax.rem(LANES - first - group * heads, LANES), 1)
    lane = lax.broadcasted_iota(jnp.int32, (LANES, LANES), 1)
    nothing = jnp.zeros((LANES, LANES), BF16)
    for first_tile in range(0, tiles, 2):
        low = first_tile * LANES
        both_tiles = slice(low, low + 2 * LANES)
        for pair in range(heads // 2):
            across = slice(pair * LANES, (pair + 1) * LANES)
            xs = x_ref[both_tiles, across]
            dys = dy_ref[low:, across]
            x_side = lax.broadcasted_iota(jnp.int32, xs.shape, 1) // WIDTH
            dy_side = lax.broadcasted_iota(jnp.int32, dys.shape, 1) // WIDTH
            own_x = [jnp.where(x_side == half, xs, jnp.zeros_like(xs)) for half in range(2)]
            products = dot_nt(jnp.concatenate(own_x, axis=0), dys)
            scores = [[], []]
            for sub in range(2):
                j = first_tile + sub
                here = slice(j * LANES, (j + 1) * LANES)
                locals_ = [pair * 2, pair * 2 + 1]
                behind = [
                    jnp.broadcast_to(turned[here, local : local + 1], (LANES, LANES))
                    for local in locals_
                ]
                kept = [[nothing] * sub, [nothing] * sub]
                v_sums = [None, None]
                for i in range(j, tiles):
                    there = slice(i * LANES, (i + 1) * LANES)
                    at = (i - first_tile) * LANES
                    near = s_ref[here, there]
                    change = None
                    for half, local in enumerate(locals_):
                        from_row = (half * 2 + sub) * LANES
                        power = row_ref[0, local : local + 1, there] - behind[half]
                        if i == j:
                            power = jnp.minimum(power, 64.0)
                        decay = jnp.exp2(power)
                        product = products[from_row : from_row + LANES, at : at + LANES]
                        score = near * decay
                        kept[half].append(score.astype(BF16))
                        spread_product = decay * product
                        change = spread_product if change is None else change + spread_product
                        both = score * product
                        v_sums[half] = both if v_sums[half] is None else v_sums[half] + both
                        u_sum = jnp.sum(both, axis=0, keepdims=True)
                        if j > 0:
                            u_sum += u_ref[0, local : local + 1, there]
                        u_ref[0, local : local + 1, there] = u_sum
                    ds_ref[here, there] += change
                v_cols = [jnp.sum(v_sum, axis=1, keepdims=True) for v_sum in v_sums]
                head = first + group * heads + pair * 2
                v_new = jnp.where(lane == head, v_cols[0], v_ref[here, :])
                v_ref[here, :] = jnp.where(lane == head + 1, v_cols[1], v_new)
                for half in range(2):
                    scores[half].append(jnp.concatenate(kept[half], axis=1))
            total = None
            for half in range(2):
                own_dy = jnp.where(dy_side == half, dys, jnp.zeros_like(dys))
                part = dot(jnp.concatenate(scores[half], axis=0), own_dy)
                total = part if total is None else total + part
            dx_ref[both_tiles, across] = total

    @pl.when(group == pl.num_programs(0) - 1)
    def _():
        grads = jnp.where(to_q >= from_k, ds_ref[...], 0.0)
        db = sum(dot(term, c_ref[...]) for term in pieces(grads, 2))
        dc = sum(dot(term, b_ref[...]) for term in pieces(grads.T, 2))
        db_ref[...] = db + added[0][...] if added else db
        dc_ref[...] = dc + added[1][...] if added else dc


def inside(rows, inner, b, c, col_part, row_part, first, start, count, added, held, behind):
    length = rows.shape[0]
    tall = jax.ShapeDtypeStruct((length, LANES), F32)
    own = row_part.shape[1:]
    offset = first * WIDTH // COLS + start
    by_group = pl.BlockSpec((1,) + own, lambda g: (g + offset, 0, 0))
    own_group = pl.BlockSpec((1,) + own, lambda g: (g + start, 0, 0))
    far = whole(length, LANES)
    named = 6 + len(added)
    return call(
        functools.partial(inside_kernel, first + start * (COLS // WIDTH)),
        [
            jax.ShapeDtypeStruct((length, inner), F32),
            jax.ShapeDtypeStruct((inner // COLS,) + own, F32),
            tall,
            tall,
            tall,
        ],
        (rows, rows, b, c, col_part, row_part, *added, *held, *behind),
        grid=(count,),
        in_specs=[
            columns(length, start * COLS),
            columns(length, inner + start * COLS),
            far,
            far,
            far,
            by_group,
        ]
        + [far] * len(added)
        + [anywhere()] * (len(held) + len(behind)),
        out_specs=[columns(length, start * COLS), own_group, far, far, far],
        scratch_shapes=[pltpu.VMEM((length, length), F32), pltpu.VMEM((length, length), F32)],
        input_output_aliases={named + k: k for k in range(len(held))},
        compiler_params=params(20),
        cost_estimate=LITTLE,
        name="inside",
    )


def by_columns(shape):
    return pl.BlockSpec(shape[:2] + (WIDE,), lambda g: (0, 0, g))


def channels_kernel(peers, first, at_ref, dy_ref, dxi_ref, carry_ref, weight_ref, b_ref, skip_ref, *rest):
    outs, dx_ref = rest[-1 - peers : -1], rest[-1]
    tokens = dy_ref.shape[0] // peers
    select = selector(LANES, WIDE, first + pl.program_id(0) * (WIDE // WIDTH))
    carried = spread(weight_ref[...], select) * dot(b_ref[...], stacked(carry_ref, 1))
    gain = spread(skip_ref[...], select, 3)[0:1, :]
    dx_ref[...] = (dxi_ref[...] + carried + gain * dy_ref[...].astype(F32)).astype(BF16)
    for r in range(peers):
        start = pl.multiple_of((at_ref[0] ^ r) * tokens, tokens)
        outs[r][...] = dx_ref[pl.ds(start, tokens), :]


def channels(peers, first, at, rows, dxi, carry, weight, b, skip, behind):
    length, inner = dxi.shape
    tokens = length // peers
    tall = whole(length, LANES)
    return call(
        functools.partial(channels_kernel, peers, first),
        [jax.ShapeDtypeStruct((tokens, inner), BF16)] * peers,
        (at, rows, dxi, carry, weight, b, skip, *behind),
        free=(3,),
        grid=(inner // WIDE,),
        in_specs=[
            smem(),
            columns(length, inner, WIDE),
            columns(length, 0, WIDE),
            by_columns(carry.shape),
            tall,
            tall,
            whole(8, LANES),
        ]
        + [anywhere()] * len(behind),
        out_specs=[columns(tokens, 0, WIDE)] * peers,
        scratch_shapes=[pltpu.VMEM((length, WIDE), BF16)],
        compiler_params=params(16),
        cost_estimate=LITTLE,
        name="channels",
    )


def others_kernel(
    heads,
    peers,
    first,
    last,
    at_ref,
    x_ref,
    dy_ref,
    carry_ref,
    through_ref,
    into_ref,
    out_of_ref,
    b_ref,
    c_ref,
    dt_ref,
    tot_ref,
    ui_ref,
    vi_ref,
    *rest,
):
    if last:
        added = rest[:5]
    outs = rest[-5 - (peers if last else 3) : -5]
    db_ref, dc_ref, u_ref, v_ref, tail_ref = rest[-5:]
    length = x_ref.shape[0]
    tokens = length // peers
    group = pl.program_id(0)

    @pl.when(group == 0)
    def _():
        db_ref[...] = jnp.zeros_like(db_ref)
        dc_ref[...] = jnp.zeros_like(dc_ref)
        u_ref[...] = jnp.zeros_like(u_ref)
        v_ref[...] = jnp.zeros_like(v_ref)

    select = selector(LANES, WIDE, first + group * (WIDE // WIDTH))
    for source, weight_ref, k, near_ref, sum_ref, head_ref in (
        (x_ref, into_ref, 1, b_ref, db_ref, v_ref),
        (dy_ref, out_of_ref, 0, c_ref, dc_ref, u_ref),
    ):
        weighted = source[...].astype(F32) * spread(weight_ref[...], select)
        far = stacked(carry_ref, k)
        sum_ref[...] += dot_nt(weighted.astype(BF16), far)
        head_ref[...] += gather(weighted * dot(near_ref[...], far), select)

    @pl.when(group == pl.num_programs(0) - 1)
    def _():
        inner_v, outer_v = vi_ref[...], v_ref[...]
        steps = (inner_v + outer_v) / dt_ref[...]
        rows = [ui_ref[at] for at in range(ui_ref.shape[0])]
        if first > 0:
            rows.insert(0, jnp.zeros((first, length), F32))
        rows.append(jnp.zeros((LANES - sum(part.shape[0] for part in rows), length), F32))
        net = jnp.concatenate(rows, axis=0).T + u_ref[...] - inner_v - outer_v
        row = lax.broadcasted_iota(jnp.int32, (length, length), 0)
        col = lax.broadcasted_iota(jnp.int32, (length, length), 1)
        upper = jnp.where(col >= row, 1.0, 0.0).astype(BF16)
        later = sum(dot(upper, term) for term in pieces(net, 3))
        whole_block = jnp.sum(outer_v, axis=0, keepdims=True)
        link = sum(through_ref[block].astype(F32) for block in range(through_ref.shape[0]))
        link = jnp.sum(link, axis=0, keepdims=True)
        logs = later + whole_block + jnp.exp2(tot_ref[0:1, :]) * link
        thin = steps + pltpu.roll(logs, heads, 1)
        if not last:
            outs[0][...] = thin
            outs[1][...] = db_ref[...]
            outs[2][...] = dc_ref[...]
        else:
            thin_ref, dbo_ref, dco_ref, dbi_ref, dci_ref = added
            tail_ref[:, 0:LANES] = (thin + thin_ref[...]).astype(BF16)
            tail_ref[:, LANES : 2 * LANES] = (db_ref[...] + dbo_ref[...] + dbi_ref[...]).astype(BF16)
            tail_ref[:, 2 * LANES :] = (dc_ref[...] + dco_ref[...] + dci_ref[...]).astype(BF16)
            for r in range(peers):
                start = pl.multiple_of((at_ref[0] ^ r) * tokens, tokens)
                outs[r][...] = tail_ref[pl.ds(start, tokens), :]


def others(
    heads, peers, first, at, rows, inner, carry, into, out_of, b, c, dt, tot, ui, vi, added, behind
):
    length = rows.shape[0]
    tokens = length // peers
    tall = whole(length, LANES)
    last = len(added) > 0
    tall_shape = jax.ShapeDtypeStruct((length, LANES), F32)
    tail_shape = jax.ShapeDtypeStruct((tokens, 3 * LANES), BF16)
    return call(
        functools.partial(others_kernel, heads, peers, first, last),
        [tail_shape] * peers if last else [tall_shape] * 3,
        (at, rows, rows, carry, carry, into, out_of, b, c, dt, tot, ui, vi, *added, *behind),
        grid=(inner // WIDE,),
        in_specs=[
            smem(),
            columns(length, 0, WIDE),
            columns(length, inner, WIDE),
            by_columns(carry.shape),
            pl.BlockSpec(carry.shape[:2] + (LANES,), lambda g: (0, 0, inner // LANES)),
            tall,
            tall,
            tall,
            tall,
            tall,
            whole(8, LANES),
            whole(*ui.shape),
            tall,
        ]
        + [tall] * len(added)
        + [anywhere()] * len(behind),
        out_specs=[whole(tokens, 3 * LANES)] * peers if last else [tall] * 3,
        scratch_shapes=[pltpu.VMEM((length, LANES), F32)] * 4
        + [pltpu.VMEM((length, 3 * LANES), BF16)],
        compiler_params=params(24),
        cost_estimate=LITTLE,
        name="others",
    )


def put_columns(peers, half, head_ref, sent, held_ref, dx_ref, sems):
    width = sent[0].shape[1]
    reads = [
        pltpu.make_async_copy(sent[r], held_ref.at[r], sems.at[0, r]) for r in range(peers)
    ]
    for read in reads:
        read.start()
    writes = []
    for r in range(peers):
        reads[r].wait()
        start = pl.multiple_of(((head_ref[0] ^ r) * HALVES + half) * width, LANES)
        writes.append(
            pltpu.make_async_copy(
                held_ref.at[r], dx_ref.at[:, pl.ds(start, width)], sems.at[1, r]
            )
        )
        writes[-1].start()
    return writes


def place_kernel(peers, head_ref, *rest):
    dx_ref, held_ref, sems = rest[-3:]
    for write in put_columns(peers, 0, head_ref, rest[:peers], held_ref, dx_ref, sems):
        write.wait()


def place(head, sent, behind):
    peers = len(sent)
    tokens, width = sent[0].shape
    return call(
        functools.partial(place_kernel, peers),
        [jax.ShapeDtypeStruct((tokens, width * HALVES * peers), BF16)],
        (head, *sent, behind),
        in_specs=[smem()] + [anywhere()] * (peers + 1),
        out_specs=[anywhere()],
        scratch_shapes=[
            pltpu.VMEM((peers, tokens, width), BF16),
            pltpu.SemaphoreType.DMA((2, peers)),
        ],
        compiler_params=one_step(8),
        cost_estimate=LITTLE,
        name="place",
    )[0]


def finish_kernel(heads, peers, head_ref, _, *rest):
    sent, tails = rest[:peers], rest[peers : 2 * peers]
    dx_ref, steps_ref, logs_ref, db_ref, dc_ref, held_ref, sems, tail_ref, tail_sems = rest[
        2 * peers :
    ]
    tokens = sent[0].shape[0]
    reads = [
        pltpu.make_async_copy(tails[r], tail_ref.at[r], tail_sems.at[r]) for r in range(peers)
    ]
    for read in reads:
        read.start()
    writes = put_columns(peers, 1, head_ref, sent, held_ref, dx_ref, sems)
    lane = lax.broadcasted_iota(jnp.int32, (tokens, LANES), 1)
    results = [jnp.zeros((tokens, LANES), F32) for _ in range(4)]
    for r in range(peers):
        source = head_ref[0] ^ r
        own = lane // heads == source
        reads[r].wait()
        thin = tail_ref[r, :, 0:LANES].astype(F32)
        for k in range(2):
            shift = lax.rem((source - k) * heads + LANES, LANES)
            results[k] += jnp.where(own, pltpu.roll(thin, shift, 1), 0.0)
            results[2 + k] += tail_ref[r, :, (k + 1) * LANES : (k + 2) * LANES].astype(F32)
    steps_ref[...] = results[0].astype(BF16)
    logs_ref[...] = results[1].astype(BF16)
    db_ref[...] = results[2]
    dc_ref[...] = results[3]
    for write in writes:
        write.wait()


def finish(heads, head, placed, sent, tails):
    peers = len(tails)
    tokens, width = sent[0].shape
    thin = jax.ShapeDtypeStruct((tokens, LANES), BF16)
    wide = jax.ShapeDtypeStruct((tokens, LANES), F32)
    return call(
        functools.partial(finish_kernel, heads, peers),
        [jax.ShapeDtypeStruct(placed.shape, BF16), thin, thin, wide, wide],
        (head, placed, *sent, *tails),
        free=tuple(range(2, 2 + 2 * peers)),
        in_specs=[smem()] + [anywhere()] * (1 + 2 * peers),
        out_specs=[anywhere(), vmem(), vmem(), vmem(), vmem()],
        scratch_shapes=[
            pltpu.VMEM((peers, tokens, width), BF16),
            pltpu.SemaphoreType.DMA((2, peers)),
            pltpu.VMEM((peers,) + tails[0].shape, BF16),
            pltpu.SemaphoreType.DMA((peers,)),
        ],
        input_output_aliases={1: 0},
        compiler_params=one_step(8),
        cost_estimate=LITTLE,
        name="finish",
    )


HALVES = 2


def body(inputs, grad_out, steps, log_decay, input_map, output_map, skip_gain):
    blocks, peers = lax.axis_size("ctx") // 2, lax.axis_size("head")
    inner = inputs.shape[1] // peers
    heads = steps.shape[1] // peers
    width = inner // HALVES
    head = lax.axis_index("head").astype(jnp.int32).reshape(1)
    at = lax.axis_index("ctx").astype(jnp.int32).reshape(1)

    riders = (steps, log_decay, input_map, output_map)
    everyone = tuple(range(peers - 1, -1, -1))
    low = pack(head, inputs, grad_out, riders, peers, width, [(r, 0) for r in everyone], ())
    high = pack(
        head, inputs, grad_out, (), peers, width, [(r, width) for r in everyone], (low[0],)
    )
    low, high = low[::-1], high[::-1]
    low, high = swap(low), swap(high)
    skip = jnp.broadcast_to(jnp.pad(skip_gain, (0, LANES - heads))[None], (8, LANES))
    half = heads // HALVES

    steps_low = width // COLS
    early = steps_low // 2

    def begin(low):
        scalars, rows, sums = opening(head, low, heads, blocks, width)
        col_part, row_part, b, c = scalars[0], scalars[1], scalars[6], scalars[7]
        reached = across(sums)
        pairs = inside(rows, width, b, c, col_part, row_part, 0, 0, early, (), (), ())
        return scalars, rows, pairs, reached

    def empty(low):
        return jax.tree.map(lambda a: jnp.zeros(a.shape, a.dtype), jax.eval_shape(begin, low))

    scalars, rows, pairs, reached = lax.cond(head[0] < peers, begin, empty, low)
    col_part, row_part, into, out_of, dt, tot, b, c, b_t, c_t = scalars
    dxi, ui, vi, dbi, dci = pairs

    rows_high, sums = states(
        head, into, out_of, b_t, c_t, tot, high, blocks, width, half, (reached, dxi)
    )
    total = total_blocks(at, reached, 0, (sums,))
    far = over(total)
    reached_high = across(sums)
    dxi, ui, vi, dbi, dci = inside(
        rows, width, b, c, col_part, row_part, 0, early, steps_low - early, (dbi, dci, vi),
        (dxi, ui), (total,),
    )
    begun = scan_blocks(at, reached, far, 0, (dxi,))
    total = total_blocks(at, reached_high, half, (begun,))
    far_high = over(total)
    carry = across(begun)
    dxi_high, ui_high, vi_high, dbi, dci = inside(
        rows_high, width, b, c, col_part, row_part, half, 0, steps_low,
        (dbi, dci, jnp.zeros_like(vi)), (), (total,),
    )
    begun = scan_blocks(at, reached_high, far_high, half, (dxi_high,))
    carry_high = across(begun)
    dx_low = channels(peers, 0, head, rows, dxi, carry, into, b, skip, (begun,))
    sent_low = swap(dx_low)
    added = others(
        heads, peers, 0, head, rows, width, carry, into, out_of, b, c, dt, tot, ui, vi, [],
        (dx_low[0],),
    )
    dx_high = channels(
        peers, half, head, rows_high, dxi_high, carry_high, into, b, skip, (added[0],)
    )
    sent_high = swap(dx_high)
    tails = others(
        heads, peers, half, head, rows_high, width, carry_high, into, out_of, b, c, dt, tot,
        ui_high, vi_high, [*added, dbi, dci], (dx_high[0], *sent_low[1:]),
    )
    placed = place(head, sent_low, tails[0])
    return tuple(finish(heads, head, placed, sent_high, swap(tails)))


def solution(mesh):
    rows = P(("ctx", "head"), None)
    return jax.shard_map(
        body,
        mesh=mesh,
        in_specs=(rows,) * 6 + (P("head"),),
        out_specs=(rows,) * 5,
        check_vma=False,
    )
```

```python
import functools

import jax
import jax.numpy as jnp
from jax import lax
from jax.experimental import pallas as pl
from jax.experimental.pallas import tpu as pltpu
from jax.sharding import PartitionSpec as P

F32 = jnp.float32
BF16 = jnp.bfloat16
LANES = 128
WIDTH = 64
COLS = 256
WIDE = 512
LOG2E = 1.4426950408889634
NT = (((1,), (1,)), ((), ()))
MIB = 1024 * 1024
LITTLE = pl.CostEstimate(flops=1000, bytes_accessed=1000, transcendentals=0)


def dot(a, b):
    return jnp.dot(a, b, preferred_element_type=F32)


def dot_nt(a, b):
    return lax.dot_general(a, b, NT, preferred_element_type=F32)


def pieces(a, count):
    terms = []
    for _ in range(count):
        term = a.astype(BF16)
        terms.append(term)
        a = a - term.astype(F32)
    return terms


def selector(rows, cols, first):
    row = lax.broadcasted_iota(jnp.int32, (rows, cols), 0)
    col = lax.broadcasted_iota(jnp.int32, (rows, cols), 1)
    return jnp.where((col // WIDTH) + first == row, 1.0, 0.0).astype(BF16)


def beside(a, count):
    return jnp.concatenate(pieces(a, count), axis=1)


def below(select, count):
    return jnp.concatenate([select] * count, axis=0)


def spread(a, select, count=2):
    return dot(beside(a, count), below(select, count))


def gather(a, select, count=2):
    return sum(dot_nt(term, select) for term in pieces(a, count))


def params(mib):
    return pltpu.CompilerParams(dimension_semantics=("arbitrary",), vmem_limit_bytes=mib * MIB)


def whole(*shape):
    return pl.BlockSpec(shape, lambda *g: (0,) * len(shape))


def columns(rows, first=0, cols=COLS):
    return pl.BlockSpec((rows, cols), lambda g: (0, g + first // cols))


def call(kernel, out_shape, operands, free=(), **options):
    operands = [
        a
        if a.dtype == jnp.int32 or at in free
        else pltpu.with_memory_space_constraint(a, pltpu.HBM)
        for at, a in enumerate(operands)
    ]
    out_shape = [pltpu.HBM(one.shape, one.dtype) for one in out_shape]
    return pl.pallas_call(kernel, out_shape=out_shape, **options)(*operands)


def smem():
    return pl.BlockSpec(memory_space=pltpu.SMEM)


def anywhere():
    return pl.BlockSpec(memory_space=pl.ANY)


def vmem():
    return pl.BlockSpec(memory_space=pltpu.VMEM)


def one_step(mib):
    return pltpu.CompilerParams(vmem_limit_bytes=mib * MIB)


def swap(parts):
    peers = lax.axis_size("head")
    got = [parts[0]] + [None] * (peers - 1)
    for r in range(peers - 1, 0, -1):
        got[r] = lax.ppermute(parts[r], "head", [(i, i ^ r) for i in range(peers)])
    return got


def pack(head, x, dy, riders, peers, width, jobs, behind):
    tokens = x.shape[0]
    inner = x.shape[1] // peers
    rider = sum(one.shape[1] for one in riders)
    shapes = [(tokens, 2 * width + (0 if first else rider)) for _, first in jobs]
    count, fan = 2 + len(riders), len(jobs)

    def kernel(head_ref, *rest):
        sources, outs = rest[:count], rest[count + len(behind) : count + len(behind) + fan]
        helds, sems = rest[-fan - 1 : -1], rest[-1]
        reads = []
        for to, (r, first) in enumerate(jobs):
            start = pl.multiple_of((head_ref[0] ^ r) * inner + first, LANES)
            at, own = 0, []
            for k, source in enumerate(sources[: 2 if first else count]):
                size = width if k < 2 else source.shape[1]
                chosen = source.at[:, pl.ds(start, size)] if k < 2 else source
                target = helds[to].at[:, pl.ds(at, size)]
                own.append(pltpu.make_async_copy(chosen, target, sems.at[0, to, k]))
                own[-1].start()
                at += size
            reads.append(own)
        writes = []
        for to, own in enumerate(reads):
            for read in own:
                read.wait()
            writes.append(pltpu.make_async_copy(helds[to], outs[to], sems.at[1, to, 0]))
            writes[-1].start()
        for write in writes:
            write.wait()

    return call(
        kernel,
        [jax.ShapeDtypeStruct(shape, BF16) for shape in shapes],
        (head, x, dy, *riders, *behind),
        in_specs=[smem()] + [anywhere()] * (count + len(behind)),
        out_specs=[anywhere()] * fan,
        scratch_shapes=[pltpu.VMEM(shape, BF16) for shape in shapes]
        + [pltpu.SemaphoreType.DMA((2, fan, count))],
        compiler_params=one_step(10),
        cost_estimate=LITTLE,
        name="pack",
    )


def prepare(heads, at_ref, small_ref, outs):
    col_ref, row_ref, in_ref, out_ref, dt_ref, tot_ref, b_ref, c_ref, bt_ref, ct_ref = outs
    length = small_ref.shape[0]
    shift = lax.rem(LANES - at_ref[0] * heads, LANES)
    steps = pltpu.roll(small_ref[:, 0:LANES].astype(F32), shift, 1)
    logs = pltpu.roll(small_ref[:, LANES : 2 * LANES].astype(F32), shift, 1)
    row = lax.broadcasted_iota(jnp.int32, (length, length), 0)
    col = lax.broadcasted_iota(jnp.int32, (length, length), 1)
    lower = jnp.where(row >= col, 1.0, 0.0).astype(BF16)
    cum = dot(lower, logs.astype(BF16)) * LOG2E
    total = cum[length - 1 : length, :]
    col_ref[...] = cum - jnp.log(steps) * LOG2E
    turned = cum.T
    per_group = row_ref.shape[1]
    for group in range(row_ref.shape[0]):
        row_ref[group] = turned[group * per_group : (group + 1) * per_group, :]
    in_ref[...] = jnp.exp2(total - cum) * steps
    out_ref[...] = jnp.exp2(cum)
    dt_ref[...] = steps
    tot_ref[...] = jnp.broadcast_to(total, tot_ref.shape)
    b = small_ref[:, 2 * LANES : 3 * LANES]
    c = small_ref[:, 3 * LANES : 4 * LANES]
    b_ref[...] = b
    c_ref[...] = c
    bt_ref[...] = b.astype(F32).T.astype(BF16)
    ct_ref[...] = c.astype(F32).T.astype(BF16)


def prepared(length, heads):
    tall = jax.ShapeDtypeStruct((length, LANES), F32)
    thin = jax.ShapeDtypeStruct((length, LANES), BF16)
    flat = jax.ShapeDtypeStruct((LANES, length), BF16)
    groups = jax.ShapeDtypeStruct((heads * WIDTH // COLS, COLS // WIDTH, length), F32)
    total = jax.ShapeDtypeStruct((8, LANES), F32)
    return [tall, groups, tall, tall, tall, total, thin, thin, flat, flat]


class Arrivals:
    def __init__(self, head_ref, parts, held_ref, rows_ref, ranges, sems):
        tokens = parts[0].shape[0]
        self.ranges, self.held_ref, self.rows_ref, self.sems = ranges, held_ref, rows_ref, sems
        self.reads, self.writes = {}, []
        for k in sorted(range(len(ranges)), key=lambda k: ranges[k][1]):
            at, size = ranges[k]
            for r, part in enumerate(parts):
                start = pl.multiple_of((head_ref[0] ^ r) * tokens, tokens)
                self.reads[k, r] = pltpu.make_async_copy(
                    part.at[:, pl.ds(at, size)],
                    held_ref.at[pl.ds(start, tokens), pl.ds(at, size)],
                    sems.at[k, r],
                )
                self.reads[k, r].start()
        self.peers = len(parts)

    def wait(self, k):
        for r in range(self.peers):
            self.reads[k, r].wait()
        chosen = pl.ds(*self.ranges[k])
        self.writes.append(
            pltpu.make_async_copy(
                self.held_ref.at[:, chosen], self.rows_ref.at[:, chosen], self.sems.at[k, self.peers]
            )
        )
        self.writes[-1].start()

    def close(self):
        for write in self.writes:
            write.wait()


def add_up(first, weight_refs, map_refs, tot_ref, held_ref, sum_ref, arrivals):
    blocks, rows, inner = sum_ref.shape
    rows, inner = rows // 2, inner - LANES
    row = lax.broadcasted_iota(jnp.int32, (2 * rows, LANES), 0)
    total = jnp.zeros((2 * rows, LANES), F32)
    for k, term in enumerate(pieces(tot_ref[0:1, :], 3)):
        total = jnp.where(row == k, term.astype(F32), total)
    for block in range(blocks):
        sum_ref[block, :, inner:] = total.astype(BF16)
    weights = [beside(ref[...], 2) for ref in weight_refs]
    for k in range(2):
        arrivals.wait(k)
        for group in range(inner // COLS):
            here = slice(group * COLS, (group + 1) * COLS)
            there = slice(k * inner + group * COLS, k * inner + (group + 1) * COLS)
            select = selector(LANES, COLS, first + group * (COLS // WIDTH))
            weight = dot(weights[k], below(select, 2))
            weighted = held_ref[:, there].astype(F32) * weight
            added = sum(dot(map_refs[k][...], term) for term in pieces(weighted, 2)).astype(BF16)
            for block in range(blocks):
                sum_ref[block, k * rows : (k + 1) * rows, here] = added[
                    block * rows : (block + 1) * rows, :
                ]


def opening_kernel(heads, peers, head_ref, *rest):
    parts, (rows_ref, sum_ref, held_ref, sems) = rest[:peers], rest[-4:]
    outs = rest[peers : peers + 10]
    width = (held_ref.shape[1] - 4 * LANES) // 2
    ranges = ((0, width), (width, width), (2 * width, 4 * LANES))
    arrivals = Arrivals(head_ref, parts, held_ref, rows_ref, ranges, sems)
    arrivals.wait(2)
    prepare(heads, head_ref, held_ref.at[:, 2 * width :], outs)
    _, _, in_ref, out_ref, _, tot_ref, _, _, bt_ref, ct_ref = outs
    add_up(0, (in_ref, out_ref), (bt_ref, ct_ref), tot_ref, held_ref, sum_ref, arrivals)
    arrivals.close()


def sum_shape(blocks, inner):
    return jax.ShapeDtypeStruct((blocks, 2 * LANES // blocks, inner + LANES), BF16)


def opening(head, parts, heads, blocks, inner):
    peers = len(parts)
    tokens, full = parts[0].shape
    rows = jax.ShapeDtypeStruct((tokens * peers, full), BF16)
    got = call(
        functools.partial(opening_kernel, heads, peers),
        prepared(tokens * peers, heads) + [rows, sum_shape(blocks, inner)],
        (head, *parts),
        in_specs=[smem()] + [anywhere()] * peers,
        out_specs=[vmem()] * 10 + [anywhere(), vmem()],
        scratch_shapes=[
            pltpu.VMEM(rows.shape, BF16),
            pltpu.SemaphoreType.DMA((3, peers + 1)),
        ],
        compiler_params=one_step(20),
        cost_estimate=LITTLE,
        name="opening",
    )
    return got[:10], got[10], got[11]


def states_kernel(first, peers, head_ref, in_ref, out_ref, bt_ref, ct_ref, tot_ref, *rest):
    parts, (rows_ref, sum_ref, held_ref, sems) = rest[:peers], rest[-4:]
    width = held_ref.shape[1] // 2
    ranges = ((0, width), (width, width))
    arrivals = Arrivals(head_ref, parts, held_ref, rows_ref, ranges, sems)
    weights, maps = (in_ref, out_ref), (bt_ref, ct_ref)
    add_up(first, weights, maps, tot_ref, held_ref, sum_ref, arrivals)
    arrivals.close()


def states(head, into, out_of, b_t, c_t, tot, parts, blocks, inner, first, behind):
    peers = len(parts)
    tokens, full = parts[0].shape
    rows = jax.ShapeDtypeStruct((tokens * peers, full), BF16)
    return call(
        functools.partial(states_kernel, first, peers),
        [rows, sum_shape(blocks, inner)],
        (head, into, out_of, b_t, c_t, tot, *parts, *behind),
        in_specs=[smem()] + [vmem()] * 5 + [anywhere()] * (peers + len(behind)),
        out_specs=[anywhere(), vmem()],
        scratch_shapes=[
            pltpu.VMEM(rows.shape, BF16),
            pltpu.SemaphoreType.DMA((2, peers + 1)),
        ],
        compiler_params=one_step(16),
        cost_estimate=LITTLE,
        name="states",
    )


def decays(first, in_ref, select):
    blocks, _, full = in_ref.shape
    totals = [
        jnp.sum(in_ref[block, :, full - LANES :].astype(F32), axis=0, keepdims=True)
        for block in range(blocks)
    ]
    return spread(jnp.exp2(jnp.concatenate(totals, axis=0)), select, 3)


def total_kernel(first, at_ref, in_ref, *rest):
    out_ref = rest[-1]
    blocks, rows, inner = in_ref.shape
    rows, inner = rows // 2, inner - LANES
    decay = decays(first, in_ref, selector(LANES, inner, first))
    running = []
    for k, order in enumerate((range(blocks), range(blocks - 1, -1, -1))):
        here = slice(k * rows, (k + 1) * rows)
        value = jnp.zeros((rows, inner), F32)
        for block in order:
            step = decay[block : block + 1, :]
            value = step * value + in_ref[block, here, 0:inner].astype(F32)
        running.append(value)
    out_ref[...] = jnp.where(at_ref[0] < blocks, running[0], running[1])


def total_blocks(at, sums, first, behind):
    blocks, rows, inner = sums.shape
    return call(
        functools.partial(total_kernel, first),
        [jax.ShapeDtypeStruct((rows // 2, inner - LANES), F32)],
        (at, sums, *behind),
        free=(1,),
        in_specs=[smem(), vmem()] + [anywhere()] * len(behind),
        compiler_params=one_step(8),
        cost_estimate=LITTLE,
        name="total_blocks",
    )[0]


def scan_kernel(first, at_ref, in_ref, far_ref, *rest):
    out_ref, kept_ref = rest[-2:]
    blocks, rows, inner = in_ref.shape
    rows, inner = rows // 2, inner - LANES
    select = selector(LANES, inner, first)
    decay = decays(first, in_ref, select)
    second = at_ref[0] >= blocks
    through = []
    for k, order in enumerate((range(blocks), range(blocks - 1, -1, -1))):
        here = slice(k * rows, (k + 1) * rows)
        running = jnp.where(second == (k == 0), far_ref[...], 0.0)
        for block in order:
            out_ref[block, here, 0:inner] = running.astype(BF16)
            if k == 0:
                kept_ref[block] = running
            else:
                through.append(jnp.sum(kept_ref[block] * running, axis=0, keepdims=True))
            step = decay[block : block + 1, :]
            running = step * running + in_ref[block, here, 0:inner].astype(F32)
    link = gather(jnp.concatenate(through[::-1], axis=0), select, 3)
    high, low = (term.astype(F32) for term in pieces(link, 2))
    row = lax.broadcasted_iota(jnp.int32, (2 * rows, LANES), 0)
    for block in range(blocks):
        here = slice(block, block + 1)
        both = jnp.where(row == 0, high[here, :], jnp.where(row == 1, low[here, :], 0.0))
        out_ref[block, :, inner:] = both.astype(BF16)


def scan_blocks(at, sums, far, first, behind):
    blocks, rows, inner = sums.shape
    return call(
        functools.partial(scan_kernel, first),
        [jax.ShapeDtypeStruct(sums.shape, BF16)],
        (at, sums, far, *behind),
        scratch_shapes=[pltpu.VMEM((blocks, rows // 2, inner - LANES), F32)],
        free=(1, 2),
        in_specs=[smem(), vmem(), vmem()] + [anywhere()] * len(behind),
        compiler_params=one_step(8),
        cost_estimate=LITTLE,
        name="scan_blocks",
    )[0]


def across(sums):
    blocks = sums.shape[0]
    groups = [list(range(blocks)), list(range(blocks, 2 * blocks))]
    return lax.all_to_all(
        sums, "ctx", split_axis=0, concat_axis=0, tiled=True, axis_index_groups=groups
    )


def over(total):
    blocks = lax.axis_size("ctx")
    return lax.ppermute(total, "ctx", [(i, (i + blocks // 2) % blocks) for i in range(blocks)])


def stacked(ref, k):
    blocks, rows, _ = ref.shape
    rows //= 2
    return jnp.concatenate(
        [ref[block, k * rows : (k + 1) * rows, :] for block in range(blocks)], axis=0
    )


def inside_kernel(first, going_on, x_ref, dy_ref, b_ref, c_ref, col_ref, row_ref, *rest):
    added, (dx_ref, u_ref, v_ref, db_ref, dc_ref, s_ref, ds_ref) = rest[:3], rest[-7:]
    added = added if len(rest) >= 10 else ()
    length = x_ref.shape[0]
    tiles = length // LANES
    heads = COLS // WIDTH
    group = pl.program_id(0)
    from_k = lax.broadcasted_iota(jnp.int32, (length, length), 0)
    to_q = lax.broadcasted_iota(jnp.int32, (length, length), 1)

    @pl.when(group == 0)
    def _():
        s_ref[...] = jnp.where(to_q >= from_k, dot_nt(b_ref[...], c_ref[...]), 0.0)
        ds_ref[...] = jnp.zeros_like(ds_ref)
        v_ref[...] = added[2][...] if added and going_on else jnp.zeros_like(v_ref)

    turned = pltpu.roll(col_ref[...], lax.rem(LANES - first - group * heads, LANES), 1)
    lane = lax.broadcasted_iota(jnp.int32, (LANES, LANES), 1)
    nothing = jnp.zeros((LANES, LANES), BF16)
    for first_tile in range(0, tiles, 2):
        low = first_tile * LANES
        both_tiles = slice(low, low + 2 * LANES)
        for pair in range(heads // 2):
            across = slice(pair * LANES, (pair + 1) * LANES)
            xs = x_ref[both_tiles, across]
            dys = dy_ref[low:, across]
            x_side = lax.broadcasted_iota(jnp.int32, xs.shape, 1) // WIDTH
            dy_side = lax.broadcasted_iota(jnp.int32, dys.shape, 1) // WIDTH
            own_x = [jnp.where(x_side == half, xs, jnp.zeros_like(xs)) for half in range(2)]
            products = dot_nt(jnp.concatenate(own_x, axis=0), dys)
            scores = [[], []]
            for sub in range(2):
                j = first_tile + sub
                here = slice(j * LANES, (j + 1) * LANES)
                locals_ = [pair * 2, pair * 2 + 1]
                behind = [
                    jnp.broadcast_to(turned[here, local : local + 1], (LANES, LANES))
                    for local in locals_
                ]
                kept = [[nothing] * sub, [nothing] * sub]
                v_sums = [None, None]
                for i in range(j, tiles):
                    there = slice(i * LANES, (i + 1) * LANES)
                    at = (i - first_tile) * LANES
                    near = s_ref[here, there]
                    change = None
                    for half, local in enumerate(locals_):
                        from_row = (half * 2 + sub) * LANES
                        power = row_ref[0, local : local + 1, there] - behind[half]
                        if i == j:
                            power = jnp.minimum(power, 64.0)
                        decay = jnp.exp2(power)
                        product = products[from_row : from_row + LANES, at : at + LANES]
                        score = near * decay
                        kept[half].append(score.astype(BF16))
                        spread_product = decay * product
                        change = spread_product if change is None else change + spread_product
                        both = score * product
                        v_sums[half] = both if v_sums[half] is None else v_sums[half] + both
                        u_sum = jnp.sum(both, axis=0, keepdims=True)
                        if j > 0:
                            u_sum += u_ref[0, local : local + 1, there]
                        u_ref[0, local : local + 1, there] = u_sum
                    ds_ref[here, there] += change
                v_cols = [jnp.sum(v_sum, axis=1, keepdims=True) for v_sum in v_sums]
                head = first + group * heads + pair * 2
                v_new = jnp.where(lane == head, v_cols[0], v_ref[here, :])
                v_ref[here, :] = jnp.where(lane == head + 1, v_cols[1], v_new)
                for half in range(2):
                    scores[half].append(jnp.concatenate(kept[half], axis=1))
            total = None
            for half in range(2):
                own_dy = jnp.where(dy_side == half, dys, jnp.zeros_like(dys))
                part = dot(jnp.concatenate(scores[half], axis=0), own_dy)
                total = part if total is None else total + part
            dx_ref[both_tiles, across] = total

    @pl.when(group == pl.num_programs(0) - 1)
    def _():
        grads = jnp.where(to_q >= from_k, ds_ref[...], 0.0)
        db = sum(dot(term, c_ref[...]) for term in pieces(grads, 2))
        dc = sum(dot(term, b_ref[...]) for term in pieces(grads.T, 2))
        db_ref[...] = db + added[0][...] if added else db
        dc_ref[...] = dc + added[1][...] if added else dc


def inside(rows, inner, b, c, col_part, row_part, first, start, count, added, held, behind):
    length = rows.shape[0]
    tall = jax.ShapeDtypeStruct((length, LANES), F32)
    own = row_part.shape[1:]
    offset = first * WIDTH // COLS + start
    by_group = pl.BlockSpec((1,) + own, lambda g: (g + offset, 0, 0))
    own_group = pl.BlockSpec((1,) + own, lambda g: (g + start, 0, 0))
    far = whole(length, LANES)
    named = 6 + len(added)
    return call(
        functools.partial(inside_kernel, first + start * (COLS // WIDTH), start > 0),
        [
            jax.ShapeDtypeStruct((length, inner), F32),
            jax.ShapeDtypeStruct((inner // COLS,) + own, F32),
            tall,
            tall,
            tall,
        ],
        (rows, rows, b, c, col_part, row_part, *added, *held, *behind),
        grid=(count,),
        in_specs=[
            columns(length, start * COLS),
            columns(length, inner + start * COLS),
            far,
            far,
            far,
            by_group,
        ]
        + [far] * len(added)
        + [anywhere()] * (len(held) + len(behind)),
        out_specs=[columns(length, start * COLS), own_group, far, far, far],
        scratch_shapes=[pltpu.VMEM((length, length), F32), pltpu.VMEM((length, length), F32)],
        input_output_aliases={named + k: k for k in range(len(held))},
        compiler_params=params(20),
        cost_estimate=LITTLE,
        name="inside",
    )


def by_columns(shape):
    return pl.BlockSpec(shape[:2] + (WIDE,), lambda g: (0, 0, g))


def channels_kernel(peers, first, at_ref, dy_ref, dxi_ref, carry_ref, weight_ref, b_ref, skip_ref, *rest):
    outs, dx_ref = rest[-1 - peers : -1], rest[-1]
    tokens = dy_ref.shape[0] // peers
    select = selector(LANES, WIDE, first + pl.program_id(0) * (WIDE // WIDTH))
    carried = spread(weight_ref[...], select) * dot(b_ref[...], stacked(carry_ref, 1))
    heads = skip_ref.shape[1]
    own = selector(heads, WIDE, first + pl.program_id(0) * (WIDE // WIDTH))
    gains = jnp.broadcast_to(skip_ref[...], (8, heads))
    gain = sum(dot(term, own) for term in pieces(gains, 3))[0:1, :]
    dx_ref[...] = (dxi_ref[...] + carried + gain * dy_ref[...].astype(F32)).astype(BF16)
    for r in range(peers):
        start = pl.multiple_of((at_ref[0] ^ r) * tokens, tokens)
        outs[r][...] = dx_ref[pl.ds(start, tokens), :]


def channels(peers, first, at, rows, dxi, carry, weight, b, skip, behind):
    length, inner = dxi.shape
    tokens = length // peers
    tall = whole(length, LANES)
    return call(
        functools.partial(channels_kernel, peers, first),
        [jax.ShapeDtypeStruct((tokens, inner), BF16)] * peers,
        (at, rows, dxi, carry, weight, b, skip, *behind),
        free=(3,),
        grid=(inner // WIDE,),
        in_specs=[
            smem(),
            columns(length, inner, WIDE),
            columns(length, 0, WIDE),
            by_columns(carry.shape),
            tall,
            tall,
            whole(*skip.shape),
        ]
        + [anywhere()] * len(behind),
        out_specs=[columns(tokens, 0, WIDE)] * peers,
        scratch_shapes=[pltpu.VMEM((length, WIDE), BF16)],
        compiler_params=params(16),
        cost_estimate=LITTLE,
        name="channels",
    )


def others_kernel(
    heads,
    peers,
    first,
    last,
    at_ref,
    x_ref,
    dy_ref,
    carry_ref,
    through_ref,
    into_ref,
    out_of_ref,
    b_ref,
    c_ref,
    dt_ref,
    tot_ref,
    ui_ref,
    vi_ref,
    *rest,
):
    if last:
        added = rest[:5]
    outs = rest[-5 - (peers if last else 3) : -5]
    db_ref, dc_ref, u_ref, v_ref, tail_ref = rest[-5:]
    length = x_ref.shape[0]
    tokens = length // peers
    group = pl.program_id(0)

    @pl.when(group == 0)
    def _():
        db_ref[...] = jnp.zeros_like(db_ref)
        dc_ref[...] = jnp.zeros_like(dc_ref)
        u_ref[...] = jnp.zeros_like(u_ref)
        v_ref[...] = jnp.zeros_like(v_ref)

    select = selector(LANES, WIDE, first + group * (WIDE // WIDTH))
    for source, weight_ref, k, near_ref, sum_ref, head_ref in (
        (x_ref, into_ref, 1, b_ref, db_ref, v_ref),
        (dy_ref, out_of_ref, 0, c_ref, dc_ref, u_ref),
    ):
        weighted = source[...].astype(F32) * spread(weight_ref[...], select)
        far = stacked(carry_ref, k)
        sum_ref[...] += dot_nt(weighted.astype(BF16), far)
        head_ref[...] += gather(weighted * dot(near_ref[...], far), select)

    @pl.when(group == pl.num_programs(0) - 1)
    def _():
        inner_v, outer_v = vi_ref[...], v_ref[...]
        steps = (inner_v + outer_v) / dt_ref[...]
        rows = [ui_ref[at] for at in range(ui_ref.shape[0])]
        if first > 0:
            rows.insert(0, jnp.zeros((first, length), F32))
        rows.append(jnp.zeros((LANES - sum(part.shape[0] for part in rows), length), F32))
        net = jnp.concatenate(rows, axis=0).T + u_ref[...] - inner_v - outer_v
        row = lax.broadcasted_iota(jnp.int32, (length, length), 0)
        col = lax.broadcasted_iota(jnp.int32, (length, length), 1)
        upper = jnp.where(col >= row, 1.0, 0.0).astype(BF16)
        later = sum(dot(upper, term) for term in pieces(net, 3))
        whole_block = jnp.sum(outer_v, axis=0, keepdims=True)
        link = sum(through_ref[block].astype(F32) for block in range(through_ref.shape[0]))
        link = jnp.sum(link, axis=0, keepdims=True)
        logs = later + whole_block + jnp.exp2(tot_ref[0:1, :]) * link
        thin = steps + pltpu.roll(logs, heads, 1)
        if not last:
            outs[0][...] = thin
            outs[1][...] = db_ref[...]
            outs[2][...] = dc_ref[...]
        else:
            thin_ref, dbo_ref, dco_ref, dbi_ref, dci_ref = added
            tail_ref[:, 0:LANES] = (thin + thin_ref[...]).astype(BF16)
            tail_ref[:, LANES : 2 * LANES] = (db_ref[...] + dbo_ref[...] + dbi_ref[...]).astype(BF16)
            tail_ref[:, 2 * LANES :] = (dc_ref[...] + dco_ref[...] + dci_ref[...]).astype(BF16)
            for r in range(peers):
                start = pl.multiple_of((at_ref[0] ^ r) * tokens, tokens)
                outs[r][...] = tail_ref[pl.ds(start, tokens), :]


def others(
    heads, peers, first, at, rows, inner, carry, into, out_of, b, c, dt, tot, ui, vi, added, behind
):
    length = rows.shape[0]
    tokens = length // peers
    tall = whole(length, LANES)
    last = len(added) > 0
    tall_shape = jax.ShapeDtypeStruct((length, LANES), F32)
    tail_shape = jax.ShapeDtypeStruct((tokens, 3 * LANES), BF16)
    return call(
        functools.partial(others_kernel, heads, peers, first, last),
        [tail_shape] * peers if last else [tall_shape] * 3,
        (at, rows, rows, carry, carry, into, out_of, b, c, dt, tot, ui, vi, *added, *behind),
        grid=(inner // WIDE,),
        in_specs=[
            smem(),
            columns(length, 0, WIDE),
            columns(length, inner, WIDE),
            by_columns(carry.shape),
            pl.BlockSpec(carry.shape[:2] + (LANES,), lambda g: (0, 0, inner // LANES)),
            tall,
            tall,
            tall,
            tall,
            tall,
            whole(8, LANES),
            whole(*ui.shape),
            tall,
        ]
        + [tall] * len(added)
        + [anywhere()] * len(behind),
        out_specs=[whole(tokens, 3 * LANES)] * peers if last else [tall] * 3,
        scratch_shapes=[pltpu.VMEM((length, LANES), F32)] * 4
        + [pltpu.VMEM((length, 3 * LANES), BF16)],
        compiler_params=params(24),
        cost_estimate=LITTLE,
        name="others",
    )


def put_columns(peers, half, head_ref, sent, held_ref, dx_ref, sems):
    width = sent[0].shape[1]
    reads = [
        pltpu.make_async_copy(sent[r], held_ref.at[r], sems.at[0, r]) for r in range(peers)
    ]
    for read in reads:
        read.start()
    writes = []
    for r in range(peers):
        reads[r].wait()
        start = pl.multiple_of(((head_ref[0] ^ r) * HALVES + half) * width, LANES)
        writes.append(
            pltpu.make_async_copy(
                held_ref.at[r], dx_ref.at[:, pl.ds(start, width)], sems.at[1, r]
            )
        )
        writes[-1].start()
    return writes


def place_kernel(peers, head_ref, *rest):
    dx_ref, held_ref, sems = rest[-3:]
    for write in put_columns(peers, 0, head_ref, rest[:peers], held_ref, dx_ref, sems):
        write.wait()


def place(head, sent, behind):
    peers = len(sent)
    tokens, width = sent[0].shape
    return call(
        functools.partial(place_kernel, peers),
        [jax.ShapeDtypeStruct((tokens, width * HALVES * peers), BF16)],
        (head, *sent, behind),
        in_specs=[smem()] + [anywhere()] * (peers + 1),
        out_specs=[anywhere()],
        scratch_shapes=[
            pltpu.VMEM((peers, tokens, width), BF16),
            pltpu.SemaphoreType.DMA((2, peers)),
        ],
        compiler_params=one_step(8),
        cost_estimate=LITTLE,
        name="place",
    )[0]


def finish_kernel(heads, peers, head_ref, _, *rest):
    sent, tails = rest[:peers], rest[peers : 2 * peers]
    dx_ref, steps_ref, logs_ref, db_ref, dc_ref, held_ref, sems, tail_ref, tail_sems = rest[
        2 * peers :
    ]
    tokens = sent[0].shape[0]
    reads = [
        pltpu.make_async_copy(tails[r], tail_ref.at[r], tail_sems.at[r]) for r in range(peers)
    ]
    for read in reads:
        read.start()
    writes = put_columns(peers, 1, head_ref, sent, held_ref, dx_ref, sems)
    lane = lax.broadcasted_iota(jnp.int32, (tokens, LANES), 1)
    results = [jnp.zeros((tokens, LANES), F32) for _ in range(4)]
    for r in range(peers):
        source = head_ref[0] ^ r
        own = lane // heads == source
        reads[r].wait()
        thin = tail_ref[r, :, 0:LANES].astype(F32)
        for k in range(2):
            shift = lax.rem((source - k) * heads + LANES, LANES)
            results[k] += jnp.where(own, pltpu.roll(thin, shift, 1), 0.0)
            results[2 + k] += tail_ref[r, :, (k + 1) * LANES : (k + 2) * LANES].astype(F32)
    steps_ref[...] = results[0].astype(BF16)
    logs_ref[...] = results[1].astype(BF16)
    db_ref[...] = results[2]
    dc_ref[...] = results[3]
    for write in writes:
        write.wait()


def finish(heads, head, placed, sent, tails):
    peers = len(tails)
    tokens, width = sent[0].shape
    thin = jax.ShapeDtypeStruct((tokens, LANES), BF16)
    wide = jax.ShapeDtypeStruct((tokens, LANES), F32)
    return call(
        functools.partial(finish_kernel, heads, peers),
        [jax.ShapeDtypeStruct(placed.shape, BF16), thin, thin, wide, wide],
        (head, placed, *sent, *tails),
        free=tuple(range(2, 2 + 2 * peers)),
        in_specs=[smem()] + [anywhere()] * (1 + 2 * peers),
        out_specs=[anywhere(), vmem(), vmem(), vmem(), vmem()],
        scratch_shapes=[
            pltpu.VMEM((peers, tokens, width), BF16),
            pltpu.SemaphoreType.DMA((2, peers)),
            pltpu.VMEM((peers,) + tails[0].shape, BF16),
            pltpu.SemaphoreType.DMA((peers,)),
        ],
        input_output_aliases={1: 0},
        compiler_params=one_step(8),
        cost_estimate=LITTLE,
        name="finish",
    )


HALVES = 2


def body(inputs, grad_out, steps, log_decay, input_map, output_map, skip_gain):
    blocks, peers = lax.axis_size("ctx") // 2, lax.axis_size("head")
    inner = inputs.shape[1] // peers
    heads = steps.shape[1] // peers
    width = inner // HALVES
    head = lax.axis_index("head").astype(jnp.int32).reshape(1)
    at = lax.axis_index("ctx").astype(jnp.int32).reshape(1)

    riders = (steps, log_decay, input_map, output_map)
    everyone = tuple(range(peers - 1, -1, -1))
    low = pack(head, inputs, grad_out, riders, peers, width, [(r, 0) for r in everyone], ())
    high = pack(
        head, inputs, grad_out, (), peers, width, [(r, width) for r in everyone], (low[0],)
    )
    low, high = low[::-1], high[::-1]
    low, high = swap(low), swap(high)
    skip = skip_gain[None]
    half = heads // HALVES

    steps_low = width // COLS
    early = steps_low // 2

    def begin(low):
        scalars, rows, sums = opening(head, low, heads, blocks, width)
        col_part, row_part, b, c = scalars[0], scalars[1], scalars[6], scalars[7]
        reached = across(sums)
        pairs = inside(rows, width, b, c, col_part, row_part, 0, 0, early, (), (), ())
        return scalars, rows, pairs, reached

    def empty(low):
        return jax.tree.map(lambda a: jnp.zeros(a.shape, a.dtype), jax.eval_shape(begin, low))

    scalars, rows, pairs, reached = lax.cond(head[0] < peers, begin, empty, low)
    col_part, row_part, into, out_of, dt, tot, b, c, b_t, c_t = scalars
    dxi, ui, vi, dbi, dci = pairs

    rows_high, sums = states(
        head, into, out_of, b_t, c_t, tot, high, blocks, width, half, (reached, dxi)
    )
    total = total_blocks(at, reached, 0, (sums,))
    far = over(total)
    reached_high = across(sums)
    dxi, ui, vi, dbi, dci = inside(
        rows, width, b, c, col_part, row_part, 0, early, steps_low - early, (dbi, dci, vi),
        (dxi, ui), (total,),
    )
    begun = scan_blocks(at, reached, far, 0, (dxi,))
    total = total_blocks(at, reached_high, half, (begun,))
    far_high = over(total)
    carry = across(begun)
    dxi_high, ui_high, vi_high, dbi, dci = inside(
        rows_high, width, b, c, col_part, row_part, half, 0, steps_low,
        (dbi, dci, vi), (), (total,),
    )
    begun = scan_blocks(at, reached_high, far_high, half, (dxi_high,))
    carry_high = across(begun)
    dx_low = channels(peers, 0, head, rows, dxi, carry, into, b, skip, (begun,))
    sent_low = swap(dx_low)
    added = others(
        heads, peers, 0, head, rows, width, carry, into, out_of, b, c, dt, tot, ui, vi, [],
        (dx_low[0],),
    )
    dx_high = channels(
        peers, half, head, rows_high, dxi_high, carry_high, into, b, skip, (added[0],)
    )
    sent_high = swap(dx_high)
    tails = others(
        heads, peers, half, head, rows_high, width, carry_high, into, out_of, b, c, dt, tot,
        ui_high, vi_high, [*added, dbi, dci], (dx_high[0], *sent_low[1:]),
    )
    placed = place(head, sent_low, tails[0])
    return tuple(finish(heads, head, placed, sent_high, swap(tails)))


def solution(mesh):
    rows = P(("ctx", "head"), None)
    return jax.shard_map(
        body,
        mesh=mesh,
        in_specs=(rows,) * 6 + (P("head"),),
        out_specs=(rows,) * 5,
        check_vma=False,
    )
```

```python
import functools

import jax
import jax.numpy as jnp
from jax import lax
from jax.experimental import pallas as pl
from jax.experimental.pallas import tpu as pltpu
from jax.sharding import PartitionSpec as P

F32 = jnp.float32
BF16 = jnp.bfloat16
LANES = 128
WIDTH = 64
COLS = 256
WIDE = 512
LOG2E = 1.4426950408889634
NT = (((1,), (1,)), ((), ()))
MIB = 1024 * 1024
LITTLE = pl.CostEstimate(flops=1000, bytes_accessed=1000, transcendentals=0)


def dot(a, b):
    return jnp.dot(a, b, preferred_element_type=F32)


def dot_nt(a, b):
    return lax.dot_general(a, b, NT, preferred_element_type=F32)


def pieces(a, count):
    terms = []
    for _ in range(count):
        term = a.astype(BF16)
        terms.append(term)
        a = a - term.astype(F32)
    return terms


def selector(rows, cols, first):
    row = lax.broadcasted_iota(jnp.int32, (rows, cols), 0)
    col = lax.broadcasted_iota(jnp.int32, (rows, cols), 1)
    return jnp.where((col // WIDTH) + first == row, 1.0, 0.0).astype(BF16)


def beside(a, count):
    return jnp.concatenate(pieces(a, count), axis=1)


def below(select, count):
    return jnp.concatenate([select] * count, axis=0)


def spread(a, select, count=2):
    return dot(beside(a, count), below(select, count))


def gather(a, select, count=2):
    return sum(dot_nt(term, select) for term in pieces(a, count))


def params(mib):
    return pltpu.CompilerParams(dimension_semantics=("arbitrary",), vmem_limit_bytes=mib * MIB)


def whole(*shape):
    return pl.BlockSpec(shape, lambda *g: (0,) * len(shape))


def columns(rows, first=0, cols=COLS):
    return pl.BlockSpec((rows, cols), lambda g: (0, g + first // cols))


def call(kernel, out_shape, operands, free=(), **options):
    operands = [
        a
        if a.dtype == jnp.int32 or at in free
        else pltpu.with_memory_space_constraint(a, pltpu.HBM)
        for at, a in enumerate(operands)
    ]
    out_shape = [pltpu.HBM(one.shape, one.dtype) for one in out_shape]
    return pl.pallas_call(kernel, out_shape=out_shape, **options)(*operands)


def smem():
    return pl.BlockSpec(memory_space=pltpu.SMEM)


def anywhere():
    return pl.BlockSpec(memory_space=pl.ANY)


def vmem():
    return pl.BlockSpec(memory_space=pltpu.VMEM)


def one_step(mib):
    return pltpu.CompilerParams(vmem_limit_bytes=mib * MIB)


def swap(parts):
    peers = lax.axis_size("head")
    got = [parts[0]] + [None] * (peers - 1)
    for r in range(peers - 1, 0, -1):
        got[r] = lax.ppermute(parts[r], "head", [(i, i ^ r) for i in range(peers)])
    return got


def pack(head, x, dy, riders, peers, width, jobs, behind):
    tokens = x.shape[0]
    inner = x.shape[1] // peers
    rider = sum(one.shape[1] for one in riders)
    shapes = [(tokens, 2 * width + (0 if first else rider)) for _, first in jobs]
    count, fan = 2 + len(riders), len(jobs)

    def kernel(head_ref, *rest):
        sources, outs = rest[:count], rest[count + len(behind) : count + len(behind) + fan]
        helds, sems = rest[-fan - 1 : -1], rest[-1]
        reads = []
        for to, (r, first) in enumerate(jobs):
            start = pl.multiple_of((head_ref[0] ^ r) * inner + first, LANES)
            at, own = 0, []
            for k, source in enumerate(sources[: 2 if first else count]):
                size = width if k < 2 else source.shape[1]
                chosen = source.at[:, pl.ds(start, size)] if k < 2 else source
                target = helds[to].at[:, pl.ds(at, size)]
                own.append(pltpu.make_async_copy(chosen, target, sems.at[0, to, k]))
                own[-1].start()
                at += size
            reads.append(own)
        writes = []
        for to, own in enumerate(reads):
            for read in own:
                read.wait()
            writes.append(pltpu.make_async_copy(helds[to], outs[to], sems.at[1, to, 0]))
            writes[-1].start()
        for write in writes:
            write.wait()

    return call(
        kernel,
        [jax.ShapeDtypeStruct(shape, BF16) for shape in shapes],
        (head, x, dy, *riders, *behind),
        in_specs=[smem()] + [anywhere()] * (count + len(behind)),
        out_specs=[anywhere()] * fan,
        scratch_shapes=[pltpu.VMEM(shape, BF16) for shape in shapes]
        + [pltpu.SemaphoreType.DMA((2, fan, count))],
        compiler_params=one_step(10),
        cost_estimate=LITTLE,
        name="pack",
    )


def prepare(heads, at_ref, small_ref, outs):
    col_ref, row_ref, in_ref, out_ref, dt_ref, tot_ref, b_ref, c_ref, bt_ref, ct_ref = outs
    length = small_ref.shape[0]
    shift = lax.rem(LANES - at_ref[0] * heads, LANES)
    steps = pltpu.roll(small_ref[:, 0:LANES].astype(F32), shift, 1)
    logs = pltpu.roll(small_ref[:, LANES : 2 * LANES].astype(F32), shift, 1)
    row = lax.broadcasted_iota(jnp.int32, (length, length), 0)
    col = lax.broadcasted_iota(jnp.int32, (length, length), 1)
    lower = jnp.where(row >= col, 1.0, 0.0).astype(BF16)
    cum = dot(lower, logs.astype(BF16)) * LOG2E
    total = cum[length - 1 : length, :]
    col_ref[...] = cum - jnp.log(steps) * LOG2E
    turned = cum.T
    per_group = row_ref.shape[1]
    for group in range(row_ref.shape[0]):
        row_ref[group] = turned[group * per_group : (group + 1) * per_group, :]
    in_ref[...] = jnp.exp2(total - cum) * steps
    out_ref[...] = jnp.exp2(cum)
    dt_ref[...] = steps
    tot_ref[...] = jnp.broadcast_to(total, tot_ref.shape)
    b = small_ref[:, 2 * LANES : 3 * LANES]
    c = small_ref[:, 3 * LANES : 4 * LANES]
    b_ref[...] = b
    c_ref[...] = c
    bt_ref[...] = b.astype(F32).T.astype(BF16)
    ct_ref[...] = c.astype(F32).T.astype(BF16)


def prepared(length, heads):
    tall = jax.ShapeDtypeStruct((length, LANES), F32)
    thin = jax.ShapeDtypeStruct((length, LANES), BF16)
    flat = jax.ShapeDtypeStruct((LANES, length), BF16)
    groups = jax.ShapeDtypeStruct((heads * WIDTH // COLS, COLS // WIDTH, length), F32)
    total = jax.ShapeDtypeStruct((8, LANES), F32)
    return [tall, groups, tall, tall, tall, total, thin, thin, flat, flat]


class Arrivals:
    def __init__(self, head_ref, parts, held_ref, rows_ref, ranges, sems):
        tokens = parts[0].shape[0]
        self.ranges, self.held_ref, self.rows_ref, self.sems = ranges, held_ref, rows_ref, sems
        self.reads, self.writes = {}, []
        for k in sorted(range(len(ranges)), key=lambda k: ranges[k][1]):
            at, size = ranges[k]
            for r, part in enumerate(parts):
                start = pl.multiple_of((head_ref[0] ^ r) * tokens, tokens)
                self.reads[k, r] = pltpu.make_async_copy(
                    part.at[:, pl.ds(at, size)],
                    held_ref.at[pl.ds(start, tokens), pl.ds(at, size)],
                    sems.at[k, r],
                )
                self.reads[k, r].start()
        self.peers = len(parts)

    def wait(self, k):
        for r in range(self.peers):
            self.reads[k, r].wait()
        chosen = pl.ds(*self.ranges[k])
        self.writes.append(
            pltpu.make_async_copy(
                self.held_ref.at[:, chosen], self.rows_ref.at[:, chosen], self.sems.at[k, self.peers]
            )
        )
        self.writes[-1].start()

    def close(self):
        for write in self.writes:
            write.wait()


def add_up(first, weight_refs, map_refs, tot_ref, held_ref, sum_ref, arrivals):
    blocks, rows, inner = sum_ref.shape
    rows, inner = rows // 2, inner - LANES
    row = lax.broadcasted_iota(jnp.int32, (2 * rows, LANES), 0)
    total = jnp.zeros((2 * rows, LANES), F32)
    for k, term in enumerate(pieces(tot_ref[0:1, :], 3)):
        total = jnp.where(row == k, term.astype(F32), total)
    for block in range(blocks):
        sum_ref[block, :, inner:] = total.astype(BF16)
    weights = [beside(ref[...], 2) for ref in weight_refs]
    for k in range(2):
        arrivals.wait(k)
        for group in range(inner // COLS):
            here = slice(group * COLS, (group + 1) * COLS)
            there = slice(k * inner + group * COLS, k * inner + (group + 1) * COLS)
            select = selector(LANES, COLS, first + group * (COLS // WIDTH))
            weight = dot(weights[k], below(select, 2))
            weighted = held_ref[:, there].astype(F32) * weight
            added = sum(dot(map_refs[k][...], term) for term in pieces(weighted, 2)).astype(BF16)
            for block in range(blocks):
                sum_ref[block, k * rows : (k + 1) * rows, here] = added[
                    block * rows : (block + 1) * rows, :
                ]


def opening_kernel(heads, peers, head_ref, *rest):
    parts, (rows_ref, sum_ref, held_ref, sems) = rest[:peers], rest[-4:]
    outs = rest[peers : peers + 10]
    width = (held_ref.shape[1] - 4 * LANES) // 2
    ranges = ((0, width), (width, width), (2 * width, 4 * LANES))
    arrivals = Arrivals(head_ref, parts, held_ref, rows_ref, ranges, sems)
    arrivals.wait(2)
    prepare(heads, head_ref, held_ref.at[:, 2 * width :], outs)
    _, _, in_ref, out_ref, _, tot_ref, _, _, bt_ref, ct_ref = outs
    add_up(0, (in_ref, out_ref), (bt_ref, ct_ref), tot_ref, held_ref, sum_ref, arrivals)
    arrivals.close()


def sum_shape(blocks, inner):
    return jax.ShapeDtypeStruct((blocks, 2 * LANES // blocks, inner + LANES), BF16)


def opening(head, parts, heads, blocks, inner):
    peers = len(parts)
    tokens, full = parts[0].shape
    rows = jax.ShapeDtypeStruct((tokens * peers, full), BF16)
    got = call(
        functools.partial(opening_kernel, heads, peers),
        prepared(tokens * peers, heads) + [rows, sum_shape(blocks, inner)],
        (head, *parts),
        in_specs=[smem()] + [anywhere()] * peers,
        out_specs=[vmem()] * 10 + [anywhere(), vmem()],
        scratch_shapes=[
            pltpu.VMEM(rows.shape, BF16),
            pltpu.SemaphoreType.DMA((3, peers + 1)),
        ],
        compiler_params=one_step(20),
        cost_estimate=LITTLE,
        name="opening",
    )
    return got[:10], got[10], got[11]


def states_kernel(first, peers, head_ref, in_ref, out_ref, bt_ref, ct_ref, tot_ref, *rest):
    parts, (rows_ref, sum_ref, held_ref, sems) = rest[:peers], rest[-4:]
    width = held_ref.shape[1] // 2
    ranges = ((0, width), (width, width))
    arrivals = Arrivals(head_ref, parts, held_ref, rows_ref, ranges, sems)
    weights, maps = (in_ref, out_ref), (bt_ref, ct_ref)
    add_up(first, weights, maps, tot_ref, held_ref, sum_ref, arrivals)
    arrivals.close()


def states(head, into, out_of, b_t, c_t, tot, parts, blocks, inner, first, behind):
    peers = len(parts)
    tokens, full = parts[0].shape
    rows = jax.ShapeDtypeStruct((tokens * peers, full), BF16)
    return call(
        functools.partial(states_kernel, first, peers),
        [rows, sum_shape(blocks, inner)],
        (head, into, out_of, b_t, c_t, tot, *parts, *behind),
        in_specs=[smem()] + [vmem()] * 5 + [anywhere()] * (peers + len(behind)),
        out_specs=[anywhere(), vmem()],
        scratch_shapes=[
            pltpu.VMEM(rows.shape, BF16),
            pltpu.SemaphoreType.DMA((2, peers + 1)),
        ],
        compiler_params=one_step(16),
        cost_estimate=LITTLE,
        name="states",
    )


def decays(first, in_ref, select):
    blocks, _, full = in_ref.shape
    totals = [
        jnp.sum(in_ref[block, :, full - LANES :].astype(F32), axis=0, keepdims=True)
        for block in range(blocks)
    ]
    return spread(jnp.exp2(jnp.concatenate(totals, axis=0)), select, 3)


def total_kernel(first, at_ref, in_ref, *rest):
    out_ref = rest[-1]
    blocks, rows, inner = in_ref.shape
    rows, inner = rows // 2, inner - LANES
    decay = decays(first, in_ref, selector(LANES, inner, first))
    running = []
    for k, order in enumerate((range(blocks), range(blocks - 1, -1, -1))):
        here = slice(k * rows, (k + 1) * rows)
        value = jnp.zeros((rows, inner), F32)
        for block in order:
            step = decay[block : block + 1, :]
            value = step * value + in_ref[block, here, 0:inner].astype(F32)
        running.append(value)
    out_ref[...] = jnp.where(at_ref[0] < blocks, running[0], running[1])


def total_blocks(at, sums, first, behind):
    blocks, rows, inner = sums.shape
    return call(
        functools.partial(total_kernel, first),
        [jax.ShapeDtypeStruct((rows // 2, inner - LANES), F32)],
        (at, sums, *behind),
        free=(1,),
        in_specs=[smem(), vmem()] + [anywhere()] * len(behind),
        compiler_params=one_step(8),
        cost_estimate=LITTLE,
        name="total_blocks",
    )[0]


def scan_kernel(first, at_ref, in_ref, far_ref, *rest):
    out_ref, kept_ref = rest[-2:]
    blocks, rows, inner = in_ref.shape
    rows, inner = rows // 2, inner - LANES
    select = selector(LANES, inner, first)
    decay = decays(first, in_ref, select)
    second = at_ref[0] >= blocks
    through = []
    for k, order in enumerate((range(blocks), range(blocks - 1, -1, -1))):
        here = slice(k * rows, (k + 1) * rows)
        running = jnp.where(second == (k == 0), far_ref[...], 0.0)
        for block in order:
            out_ref[block, here, 0:inner] = running.astype(BF16)
            if k == 0:
                kept_ref[block] = running
            else:
                through.append(jnp.sum(kept_ref[block] * running, axis=0, keepdims=True))
            step = decay[block : block + 1, :]
            running = step * running + in_ref[block, here, 0:inner].astype(F32)
    link = gather(jnp.concatenate(through[::-1], axis=0), select, 3)
    high, low = (term.astype(F32) for term in pieces(link, 2))
    row = lax.broadcasted_iota(jnp.int32, (2 * rows, LANES), 0)
    for block in range(blocks):
        here = slice(block, block + 1)
        both = jnp.where(row == 0, high[here, :], jnp.where(row == 1, low[here, :], 0.0))
        out_ref[block, :, inner:] = both.astype(BF16)


def scan_blocks(at, sums, far, first, behind):
    blocks, rows, inner = sums.shape
    return call(
        functools.partial(scan_kernel, first),
        [jax.ShapeDtypeStruct(sums.shape, BF16)],
        (at, sums, far, *behind),
        scratch_shapes=[pltpu.VMEM((blocks, rows // 2, inner - LANES), F32)],
        free=(1, 2),
        in_specs=[smem(), vmem(), vmem()] + [anywhere()] * len(behind),
        compiler_params=one_step(8),
        cost_estimate=LITTLE,
        name="scan_blocks",
    )[0]


def across(sums):
    blocks = sums.shape[0]
    groups = [list(range(blocks)), list(range(blocks, 2 * blocks))]
    return lax.all_to_all(
        sums, "ctx", split_axis=0, concat_axis=0, tiled=True, axis_index_groups=groups
    )


def over(total):
    blocks = lax.axis_size("ctx")
    return lax.ppermute(total, "ctx", [(i, (i + blocks // 2) % blocks) for i in range(blocks)])


def stacked(ref, k):
    blocks, rows, _ = ref.shape
    rows //= 2
    return jnp.concatenate(
        [ref[block, k * rows : (k + 1) * rows, :] for block in range(blocks)], axis=0
    )


def inside_kernel(first, going_on, x_ref, dy_ref, b_ref, c_ref, col_ref, row_ref, *rest):
    added, (dx_ref, u_ref, v_ref, db_ref, dc_ref, s_ref, ds_ref, u8_ref) = rest[:3], rest[-8:]
    added = added if len(rest) >= 11 else ()
    length = x_ref.shape[0]
    tiles = length // LANES
    heads = COLS // WIDTH
    group = pl.program_id(0)
    from_k = lax.broadcasted_iota(jnp.int32, (length, length), 0)
    to_q = lax.broadcasted_iota(jnp.int32, (length, length), 1)

    @pl.when(group == 0)
    def _():
        s_ref[...] = jnp.where(to_q >= from_k, dot_nt(b_ref[...], c_ref[...]), 0.0)
        ds_ref[...] = jnp.zeros_like(ds_ref)
        v_ref[...] = added[2][...] if added and going_on else jnp.zeros_like(v_ref)

    turned = pltpu.roll(col_ref[...], lax.rem(LANES - first - group * heads, LANES), 1)
    lane = lax.broadcasted_iota(jnp.int32, (LANES, LANES), 1)
    nothing = jnp.zeros((LANES, LANES), BF16)
    for first_tile in range(0, tiles, 2):
        low = first_tile * LANES
        both_tiles = slice(low, low + 2 * LANES)
        for pair in range(heads // 2):
            across = slice(pair * LANES, (pair + 1) * LANES)
            xs = x_ref[both_tiles, across]
            dys = dy_ref[low:, across]
            x_side = lax.broadcasted_iota(jnp.int32, xs.shape, 1) // WIDTH
            dy_side = lax.broadcasted_iota(jnp.int32, dys.shape, 1) // WIDTH
            own_x = [jnp.where(x_side == half, xs, jnp.zeros_like(xs)) for half in range(2)]
            products = dot_nt(jnp.concatenate(own_x, axis=0), dys)
            scores = [[], []]
            for sub in range(2):
                j = first_tile + sub
                here = slice(j * LANES, (j + 1) * LANES)
                locals_ = [pair * 2, pair * 2 + 1]
                behind = [
                    jnp.broadcast_to(turned[here, local : local + 1], (LANES, LANES))
                    for local in locals_
                ]
                kept = [[nothing] * sub, [nothing] * sub]
                v_sums = [None, None]
                for i in range(j, tiles):
                    there = slice(i * LANES, (i + 1) * LANES)
                    at = (i - first_tile) * LANES
                    near = s_ref[here, there]
                    change = None
                    for half, local in enumerate(locals_):
                        from_row = (half * 2 + sub) * LANES
                        power = row_ref[0, local : local + 1, there] - behind[half]
                        if i == j:
                            power = jnp.minimum(power, 64.0)
                        decay = jnp.exp2(power)
                        product = products[from_row : from_row + LANES, at : at + LANES]
                        score = near * decay
                        kept[half].append(score.astype(BF16))
                        spread_product = decay * product
                        change = spread_product if change is None else change + spread_product
                        both = score * product
                        v_sums[half] = both if v_sums[half] is None else v_sums[half] + both
                        eight = slice(local * 8, local * 8 + 8)
                        u_sum = jnp.sum(both.reshape(LANES // 8, 8, LANES), axis=0)
                        if j > 0:
                            u_sum += u8_ref[eight, there]
                        u8_ref[eight, there] = u_sum
                    ds_ref[here, there] += change
                v_cols = [jnp.sum(v_sum, axis=1, keepdims=True) for v_sum in v_sums]
                head = first + group * heads + pair * 2
                v_new = jnp.where(lane == head, v_cols[0], v_ref[here, :])
                v_ref[here, :] = jnp.where(lane == head + 1, v_cols[1], v_new)
                for half in range(2):
                    scores[half].append(jnp.concatenate(kept[half], axis=1))
            total = None
            for half in range(2):
                own_dy = jnp.where(dy_side == half, dys, jnp.zeros_like(dys))
                part = dot(jnp.concatenate(scores[half], axis=0), own_dy)
                total = part if total is None else total + part
            dx_ref[both_tiles, across] = total
    for local in range(heads):
        part = u8_ref[local * 8 : local * 8 + 8, :]
        u_ref[0, local : local + 1, :] = jnp.sum(part, axis=0, keepdims=True)

    @pl.when(group == pl.num_programs(0) - 1)
    def _():
        grads = jnp.where(to_q >= from_k, ds_ref[...], 0.0)
        db = sum(dot(term, c_ref[...]) for term in pieces(grads, 2))
        dc = sum(dot(term, b_ref[...]) for term in pieces(grads.T, 2))
        db_ref[...] = db + added[0][...] if added else db
        dc_ref[...] = dc + added[1][...] if added else dc


def inside(rows, inner, b, c, col_part, row_part, first, start, count, added, held, behind):
    length = rows.shape[0]
    tall = jax.ShapeDtypeStruct((length, LANES), F32)
    own = row_part.shape[1:]
    offset = first * WIDTH // COLS + start
    by_group = pl.BlockSpec((1,) + own, lambda g: (g + offset, 0, 0))
    own_group = pl.BlockSpec((1,) + own, lambda g: (g + start, 0, 0))
    far = whole(length, LANES)
    named = 6 + len(added)
    return call(
        functools.partial(inside_kernel, first + start * (COLS // WIDTH), start > 0),
        [
            jax.ShapeDtypeStruct((length, inner), F32),
            jax.ShapeDtypeStruct((inner // COLS,) + own, F32),
            tall,
            tall,
            tall,
        ],
        (rows, rows, b, c, col_part, row_part, *added, *held, *behind),
        grid=(count,),
        in_specs=[
            columns(length, start * COLS),
            columns(length, inner + start * COLS),
            far,
            far,
            far,
            by_group,
        ]
        + [far] * len(added)
        + [anywhere()] * (len(held) + len(behind)),
        out_specs=[columns(length, start * COLS), own_group, far, far, far],
        scratch_shapes=[
            pltpu.VMEM((length, length), F32),
            pltpu.VMEM((length, length), F32),
            pltpu.VMEM((COLS // WIDTH * 8, length), F32),
        ],
        input_output_aliases={named + k: k for k in range(len(held))},
        compiler_params=params(20),
        cost_estimate=LITTLE,
        name="inside",
    )


def by_columns(shape):
    return pl.BlockSpec(shape[:2] + (WIDE,), lambda g: (0, 0, g))


def channels_kernel(peers, first, at_ref, dy_ref, dxi_ref, carry_ref, weight_ref, b_ref, skip_ref, *rest):
    outs, dx_ref = rest[-1 - peers : -1], rest[-1]
    tokens = dy_ref.shape[0] // peers
    select = selector(LANES, WIDE, first + pl.program_id(0) * (WIDE // WIDTH))
    carried = spread(weight_ref[...], select) * dot(b_ref[...], stacked(carry_ref, 1))
    heads = skip_ref.shape[1]
    own = selector(heads, WIDE, first + pl.program_id(0) * (WIDE // WIDTH))
    gains = jnp.broadcast_to(skip_ref[...], (8, heads))
    gain = sum(dot(term, own) for term in pieces(gains, 3))[0:1, :]
    dx_ref[...] = (dxi_ref[...] + carried + gain * dy_ref[...].astype(F32)).astype(BF16)
    for r in range(peers):
        start = pl.multiple_of((at_ref[0] ^ r) * tokens, tokens)
        outs[r][...] = dx_ref[pl.ds(start, tokens), :]


def channels(peers, first, at, rows, dxi, carry, weight, b, skip, behind):
    length, inner = dxi.shape
    tokens = length // peers
    tall = whole(length, LANES)
    return call(
        functools.partial(channels_kernel, peers, first),
        [jax.ShapeDtypeStruct((tokens, inner), BF16)] * peers,
        (at, rows, dxi, carry, weight, b, skip, *behind),
        free=(3,),
        grid=(inner // WIDE,),
        in_specs=[
            smem(),
            columns(length, inner, WIDE),
            columns(length, 0, WIDE),
            by_columns(carry.shape),
            tall,
            tall,
            whole(*skip.shape),
        ]
        + [anywhere()] * len(behind),
        out_specs=[columns(tokens, 0, WIDE)] * peers,
        scratch_shapes=[pltpu.VMEM((length, WIDE), BF16)],
        compiler_params=params(16),
        cost_estimate=LITTLE,
        name="channels",
    )


def others_kernel(
    heads,
    peers,
    first,
    last,
    at_ref,
    x_ref,
    dy_ref,
    carry_ref,
    through_ref,
    into_ref,
    out_of_ref,
    b_ref,
    c_ref,
    dt_ref,
    tot_ref,
    ui_ref,
    vi_ref,
    *rest,
):
    if last:
        added = rest[:5]
    outs = rest[-5 - (peers if last else 3) : -5]
    db_ref, dc_ref, u_ref, v_ref, tail_ref = rest[-5:]
    length = x_ref.shape[0]
    tokens = length // peers
    group = pl.program_id(0)

    @pl.when(group == 0)
    def _():
        db_ref[...] = jnp.zeros_like(db_ref)
        dc_ref[...] = jnp.zeros_like(dc_ref)
        u_ref[...] = jnp.zeros_like(u_ref)
        v_ref[...] = jnp.zeros_like(v_ref)

    select = selector(LANES, WIDE, first + group * (WIDE // WIDTH))
    for source, weight_ref, k, near_ref, sum_ref, head_ref in (
        (x_ref, into_ref, 1, b_ref, db_ref, v_ref),
        (dy_ref, out_of_ref, 0, c_ref, dc_ref, u_ref),
    ):
        weighted = source[...].astype(F32) * spread(weight_ref[...], select)
        far = stacked(carry_ref, k)
        sum_ref[...] += dot_nt(weighted.astype(BF16), far)
        head_ref[...] += gather(weighted * dot(near_ref[...], far), select)

    @pl.when(group == pl.num_programs(0) - 1)
    def _():
        inner_v, outer_v = vi_ref[...], v_ref[...]
        steps = (inner_v + outer_v) / dt_ref[...]
        rows = [ui_ref[at] for at in range(ui_ref.shape[0])]
        if first > 0:
            rows.insert(0, jnp.zeros((first, length), F32))
        rows.append(jnp.zeros((LANES - sum(part.shape[0] for part in rows), length), F32))
        net = jnp.concatenate(rows, axis=0).T + u_ref[...] - inner_v - outer_v
        row = lax.broadcasted_iota(jnp.int32, (length, length), 0)
        col = lax.broadcasted_iota(jnp.int32, (length, length), 1)
        upper = jnp.where(col >= row, 1.0, 0.0).astype(BF16)
        later = sum(dot(upper, term) for term in pieces(net, 3))
        whole_block = jnp.sum(outer_v, axis=0, keepdims=True)
        link = sum(through_ref[block].astype(F32) for block in range(through_ref.shape[0]))
        link = jnp.sum(link, axis=0, keepdims=True)
        logs = later + whole_block + jnp.exp2(tot_ref[0:1, :]) * link
        thin = steps + pltpu.roll(logs, heads, 1)
        if not last:
            outs[0][...] = thin
            outs[1][...] = db_ref[...]
            outs[2][...] = dc_ref[...]
        else:
            thin_ref, dbo_ref, dco_ref, dbi_ref, dci_ref = added
            tail_ref[:, 0:LANES] = (thin + thin_ref[...]).astype(BF16)
            tail_ref[:, LANES : 2 * LANES] = (db_ref[...] + dbo_ref[...] + dbi_ref[...]).astype(BF16)
            tail_ref[:, 2 * LANES :] = (dc_ref[...] + dco_ref[...] + dci_ref[...]).astype(BF16)
            for r in range(peers):
                start = pl.multiple_of((at_ref[0] ^ r) * tokens, tokens)
                outs[r][...] = tail_ref[pl.ds(start, tokens), :]


def others(
    heads, peers, first, at, rows, inner, carry, into, out_of, b, c, dt, tot, ui, vi, added, behind
):
    length = rows.shape[0]
    tokens = length // peers
    tall = whole(length, LANES)
    last = len(added) > 0
    tall_shape = jax.ShapeDtypeStruct((length, LANES), F32)
    tail_shape = jax.ShapeDtypeStruct((tokens, 3 * LANES), BF16)
    return call(
        functools.partial(others_kernel, heads, peers, first, last),
        [tail_shape] * peers if last else [tall_shape] * 3,
        (at, rows, rows, carry, carry, into, out_of, b, c, dt, tot, ui, vi, *added, *behind),
        grid=(inner // WIDE,),
        in_specs=[
            smem(),
            columns(length, 0, WIDE),
            columns(length, inner, WIDE),
            by_columns(carry.shape),
            pl.BlockSpec(carry.shape[:2] + (LANES,), lambda g: (0, 0, inner // LANES)),
            tall,
            tall,
            tall,
            tall,
            tall,
            whole(8, LANES),
            whole(*ui.shape),
            tall,
        ]
        + [tall] * len(added)
        + [anywhere()] * len(behind),
        out_specs=[whole(tokens, 3 * LANES)] * peers if last else [tall] * 3,
        scratch_shapes=[pltpu.VMEM((length, LANES), F32)] * 4
        + [pltpu.VMEM((length, 3 * LANES), BF16)],
        compiler_params=params(24),
        cost_estimate=LITTLE,
        name="others",
    )


def put_columns(peers, half, head_ref, sent, held_ref, dx_ref, sems):
    width = sent[0].shape[1]
    reads = [
        pltpu.make_async_copy(sent[r], held_ref.at[r], sems.at[0, r]) for r in range(peers)
    ]
    for read in reads:
        read.start()
    writes = []
    for r in range(peers):
        reads[r].wait()
        start = pl.multiple_of(((head_ref[0] ^ r) * HALVES + half) * width, LANES)
        writes.append(
            pltpu.make_async_copy(
                held_ref.at[r], dx_ref.at[:, pl.ds(start, width)], sems.at[1, r]
            )
        )
        writes[-1].start()
    return writes


def place_kernel(peers, head_ref, *rest):
    dx_ref, held_ref, sems = rest[-3:]
    for write in put_columns(peers, 0, head_ref, rest[:peers], held_ref, dx_ref, sems):
        write.wait()


def place(head, sent, behind):
    peers = len(sent)
    tokens, width = sent[0].shape
    return call(
        functools.partial(place_kernel, peers),
        [jax.ShapeDtypeStruct((tokens, width * HALVES * peers), BF16)],
        (head, *sent, behind),
        in_specs=[smem()] + [anywhere()] * (peers + 1),
        out_specs=[anywhere()],
        scratch_shapes=[
            pltpu.VMEM((peers, tokens, width), BF16),
            pltpu.SemaphoreType.DMA((2, peers)),
        ],
        compiler_params=one_step(8),
        cost_estimate=LITTLE,
        name="place",
    )[0]


def finish_kernel(heads, peers, head_ref, _, *rest):
    sent, tails = rest[:peers], rest[peers : 2 * peers]
    dx_ref, steps_ref, logs_ref, db_ref, dc_ref, held_ref, sems, tail_ref, tail_sems = rest[
        2 * peers :
    ]
    tokens = sent[0].shape[0]
    reads = [
        pltpu.make_async_copy(tails[r], tail_ref.at[r], tail_sems.at[r]) for r in range(peers)
    ]
    for read in reads:
        read.start()
    writes = put_columns(peers, 1, head_ref, sent, held_ref, dx_ref, sems)
    lane = lax.broadcasted_iota(jnp.int32, (tokens, LANES), 1)
    results = [jnp.zeros((tokens, LANES), F32) for _ in range(4)]
    for r in range(peers):
        source = head_ref[0] ^ r
        own = lane // heads == source
        reads[r].wait()
        thin = tail_ref[r, :, 0:LANES].astype(F32)
        for k in range(2):
            shift = lax.rem((source - k) * heads + LANES, LANES)
            results[k] += jnp.where(own, pltpu.roll(thin, shift, 1), 0.0)
            results[2 + k] += tail_ref[r, :, (k + 1) * LANES : (k + 2) * LANES].astype(F32)
    steps_ref[...] = results[0].astype(BF16)
    logs_ref[...] = results[1].astype(BF16)
    db_ref[...] = results[2]
    dc_ref[...] = results[3]
    for write in writes:
        write.wait()


def finish(heads, head, placed, sent, tails):
    peers = len(tails)
    tokens, width = sent[0].shape
    thin = jax.ShapeDtypeStruct((tokens, LANES), BF16)
    wide = jax.ShapeDtypeStruct((tokens, LANES), F32)
    return call(
        functools.partial(finish_kernel, heads, peers),
        [jax.ShapeDtypeStruct(placed.shape, BF16), thin, thin, wide, wide],
        (head, placed, *sent, *tails),
        free=tuple(range(2, 2 + 2 * peers)),
        in_specs=[smem()] + [anywhere()] * (1 + 2 * peers),
        out_specs=[anywhere(), vmem(), vmem(), vmem(), vmem()],
        scratch_shapes=[
            pltpu.VMEM((peers, tokens, width), BF16),
            pltpu.SemaphoreType.DMA((2, peers)),
            pltpu.VMEM((peers,) + tails[0].shape, BF16),
            pltpu.SemaphoreType.DMA((peers,)),
        ],
        input_output_aliases={1: 0},
        compiler_params=one_step(8),
        cost_estimate=LITTLE,
        name="finish",
    )


HALVES = 2


def body(inputs, grad_out, steps, log_decay, input_map, output_map, skip_gain):
    blocks, peers = lax.axis_size("ctx") // 2, lax.axis_size("head")
    inner = inputs.shape[1] // peers
    heads = steps.shape[1] // peers
    width = inner // HALVES
    head = lax.axis_index("head").astype(jnp.int32).reshape(1)
    at = lax.axis_index("ctx").astype(jnp.int32).reshape(1)

    riders = (steps, log_decay, input_map, output_map)
    everyone = tuple(range(peers - 1, -1, -1))
    low = pack(head, inputs, grad_out, riders, peers, width, [(r, 0) for r in everyone], ())
    high = pack(
        head, inputs, grad_out, (), peers, width, [(r, width) for r in everyone], (low[0],)
    )
    low, high = low[::-1], high[::-1]
    low, high = swap(low), swap(high)
    skip = skip_gain[None]
    half = heads // HALVES

    steps_low = width // COLS
    early = steps_low // 2

    def begin(low):
        scalars, rows, sums = opening(head, low, heads, blocks, width)
        col_part, row_part, b, c = scalars[0], scalars[1], scalars[6], scalars[7]
        reached = across(sums)
        pairs = inside(rows, width, b, c, col_part, row_part, 0, 0, early, (), (), ())
        return scalars, rows, pairs, reached

    def empty(low):
        return jax.tree.map(lambda a: jnp.zeros(a.shape, a.dtype), jax.eval_shape(begin, low))

    scalars, rows, pairs, reached = lax.cond(head[0] < peers, begin, empty, low)
    col_part, row_part, into, out_of, dt, tot, b, c, b_t, c_t = scalars
    dxi, ui, vi, dbi, dci = pairs

    rows_high, sums = states(
        head, into, out_of, b_t, c_t, tot, high, blocks, width, half, (reached, dxi)
    )
    total = total_blocks(at, reached, 0, (sums,))
    far = over(total)
    reached_high = across(sums)
    dxi, ui, vi, dbi, dci = inside(
        rows, width, b, c, col_part, row_part, 0, early, steps_low - early, (dbi, dci, vi),
        (dxi, ui), (total,),
    )
    begun = scan_blocks(at, reached, far, 0, (dxi,))
    total = total_blocks(at, reached_high, half, (begun,))
    far_high = over(total)
    carry = across(begun)
    dxi_high, ui_high, vi_high, dbi, dci = inside(
        rows_high, width, b, c, col_part, row_part, half, 0, steps_low,
        (dbi, dci, vi), (), (total,),
    )
    begun = scan_blocks(at, reached_high, far_high, half, (dxi_high,))
    carry_high = across(begun)
    dx_low = channels(peers, 0, head, rows, dxi, carry, into, b, skip, (begun,))
    sent_low = swap(dx_low)
    added = others(
        heads, peers, 0, head, rows, width, carry, into, out_of, b, c, dt, tot, ui, vi, [],
        (dx_low[0],),
    )
    dx_high = channels(
        peers, half, head, rows_high, dxi_high, carry_high, into, b, skip, (added[0],)
    )
    sent_high = swap(dx_high)
    tails = others(
        heads, peers, half, head, rows_high, width, carry_high, into, out_of, b, c, dt, tot,
        ui_high, vi_high, [*added, dbi, dci], (dx_high[0], *sent_low[1:]),
    )
    placed = place(head, sent_low, tails[0])
    return tuple(finish(heads, head, placed, sent_high, swap(tails)))


def solution(mesh):
    rows = P(("ctx", "head"), None)
    return jax.shard_map(
        body,
        mesh=mesh,
        in_specs=(rows,) * 6 + (P("head"),),
        out_specs=(rows,) * 5,
        check_vma=False,
    )
```
